32 devices in a mesh: dp: 16 (over z, y, core), cp: 2 (over x).
Axes of the slice: x: 2, y: 2, z: 4, core: 2. Of those that a mesh axis runs over, the one named last changes fastest.
Arguments:
- tokens: bfloat16 [4096, 768], P(('dp', 'cp')), may hold values from -6 to 6
- segment_ids: int32 [4096], P(('dp', 'cp')), may hold values from 0 to 2, as said below
- cotangent: bfloat16 [4096, 768], P(('dp', 'cp')), may hold values from -6 to 6
- qkv_weight: bfloat16 [2, 768, 2304], P(None, ('dp', 'cp')), may hold values from -0.21875 to 0.21875
- qkv_bias: bfloat16 [2, 2304], P(None, ('dp', 'cp')), may hold values from -3 to 3
- attn_weight: bfloat16 [2, 768, 768], P(None, ('dp', 'cp')), may hold values from -1.75 to 1.75
- attn_bias: bfloat16 [2, 768], P(None, ('dp', 'cp')), may hold values from -2 to 2
- up_weight: bfloat16 [2, 768, 3072], P(None, ('dp', 'cp')), may hold values from -0.21875 to 0.21875
- up_bias: bfloat16 [2, 3072], P(None, ('dp', 'cp')), may hold values from -3 to 3
- down_weight: bfloat16 [2, 3072, 768], P(None, ('dp', 'cp')), may hold values from -0.109375 to 0.109375
- down_bias: bfloat16 [2, 768], P(None, ('dp', 'cp')), may hold values from -2 to 2
- attn_gain: bfloat16 [2, 768], P(None, ('dp', 'cp')), may hold values from 0.5 to 1.5
- attn_shift: bfloat16 [2, 768], P(None, ('dp', 'cp')), may hold values from -2 to 2
- mlp_gain: bfloat16 [2, 768], P(None, ('dp', 'cp')), may hold values from 0.5 to 1.5
- mlp_shift: bfloat16 [2, 768], P(None, ('dp', 'cp')), may hold values from -2 to 2
Outputs:
- activations: bfloat16 [4096, 768], P(('dp', 'cp'))
- input_grad: float32 [4096, 768], P(('dp', 'cp'))
- qkv_weight_grad: float32 [2, 768, 2304], P(None, ('dp', 'cp'))
- qkv_bias_grad: float32 [2, 2304], P(None, ('dp', 'cp'))
- attn_weight_grad: float32 [2, 768, 768], P(None, ('dp', 'cp'))
- attn_bias_grad: float32 [2, 768], P(None, ('dp', 'cp'))
- up_weight_grad: float32 [2, 768, 3072], P(None, ('dp', 'cp'))
- up_bias_grad: float32 [2, 3072], P(None, ('dp', 'cp'))
- down_weight_grad: float32 [2, 3072, 768], P(None, ('dp', 'cp'))
- down_bias_grad: float32 [2, 768], P(None, ('dp', 'cp'))
- attn_gain_grad: float32 [2, 768], P(None, ('dp', 'cp'))
- attn_shift_grad: float32 [2, 768], P(None, ('dp', 'cp'))
- mlp_gain_grad: float32 [2, 768], P(None, ('dp', 'cp'))
- mlp_shift_grad: float32 [2, 768], P(None, ('dp', 'cp'))
The draws below stay inside these ranges and needn't reach their ends.
Inputs may be any that keep to these rules, and one draw needn't show every extreme that they name: `segment_ids`: within each group of 256 consecutive tokens the ids never fall; ids 0, 1 and 2 all occur, and id 1 runs from a position before 128 // 8 + 1 to one at or after 256 - 128 // 8 - 1.
All inputs are finite; a program needn't handle non-finite values.
Results may differ from the reference program's by a relative error of at most 0.02.
Values may be sent and summed in bfloat16 or wider, within the bound.
No kernel may reach another device: no remote copies, remote signals or barrier semaphores. Data moves between devices by JAX's collectives and lax.ppermute only.
A program may use at most 192 MiB of HBM per device.

```python
import math
import jax
import jax.numpy as jnp
from jax import lax

D = 768
HEADS = 12
HEAD = 64
FF = 3072
ROT = 16
LAYERS = 2
TOK_DEV = 128
GROUP = 256
TOKENS = 4096


def draw_segment_ids(key, part):
    key = jax.random.fold_in(key, 7)
    head_key, tail_key = jax.random.split(key)
    groups = TOKENS // GROUP
    heads_len = jax.random.randint(head_key, (groups,), 1, TOK_DEV // 8 + 1)
    tails_len = jax.random.randint(tail_key, (groups,), 1, TOK_DEV // 8 + 1)
    positions = jnp.arange(GROUP, dtype=jnp.int32)
    labels = (positions[None, :] >= heads_len[:, None]).astype(jnp.int32)
    labels = labels + (positions[None, :] >= GROUP - tails_len[:, None]).astype(jnp.int32)
    return labels.reshape(TOKENS)


def level_of(stream_key, shape, shards, least, top_value):
    loudness = 1.0
    for position, blocks in shards:
        draws = jax.random.uniform(jax.random.fold_in(jax.random.fold_in(stream_key, 6), position), (blocks,), jnp.float32, least / len(shards), top_value / len(shards))
        loudness = loudness * jnp.repeat(jnp.exp(draws), shape[position] // blocks).reshape((-1,) + (1,) * (len(shape) - 1 - position))
    return loudness


def noise(rng, dims, width, most, cuts=(), kind=jnp.bfloat16):
    level = level_of(rng, dims, cuts, -0.22, 0.18) if cuts else 1.0
    drawn = jax.random.normal(rng, dims, jnp.float32) * width * level
    return jnp.minimum(jnp.maximum(drawn, -most), most).astype(kind)


def setup_inputs(seed: int = 0) -> dict:
    arg_keys = jax.random.split(jax.random.key(seed), 16)
    tokens = noise(arg_keys[0], (TOKENS, D), 1.0, 6.0, ((0, 32),))
    segment_ids = draw_segment_ids(jax.random.fold_in(arg_keys[15], 71), 0)
    cotangent = noise(arg_keys[2], (TOKENS, D), 1.0, 6.0, ((0, 32),))
    qkv_weight = noise(arg_keys[3], (LAYERS, D, 3 * D), D ** -0.5, 0.21875, ((1, 32),))
    qkv_bias = noise(arg_keys[4], (LAYERS, 3 * D), 0.5, 3.0, ((1, 32),))
    attn_weight = noise(arg_keys[5], (LAYERS, D, D), (D // 64) ** -0.5, 1.75, ((1, 32),))
    attn_bias = noise(arg_keys[6], (LAYERS, D), 0.3, 2.0, ((1, 32),))
    up_weight = noise(arg_keys[7], (LAYERS, D, FF), D ** -0.5, 0.21875, ((1, 32),))
    up_bias = noise(arg_keys[8], (LAYERS, FF), 0.5, 3.0, ((1, 32),))
    down_weight = noise(arg_keys[9], (LAYERS, FF, D), FF ** -0.5, 0.109375, ((1, 32),))
    down_bias = noise(arg_keys[10], (LAYERS, D), 0.3, 2.0, ((1, 32),))
    attn_gain = jnp.clip(1.0 + 0.1 * jax.random.normal(arg_keys[11], (LAYERS, D), jnp.float32), 0.5, 1.5).astype(jnp.bfloat16)
    attn_shift = noise(arg_keys[12], (LAYERS, D), 0.3, 2.0, ((1, 32),))
    mlp_gain = jnp.clip(1.0 + 0.1 * jax.random.normal(arg_keys[13], (LAYERS, D), jnp.float32), 0.5, 1.5).astype(jnp.bfloat16)
    mlp_shift = noise(arg_keys[14], (LAYERS, D), 0.3, 2.0, ((1, 32),))
    return dict(tokens=tokens, segment_ids=segment_ids, cotangent=cotangent, qkv_weight=qkv_weight, qkv_bias=qkv_bias, attn_weight=attn_weight, attn_bias=attn_bias, up_weight=up_weight, up_bias=up_bias, down_weight=down_weight, down_bias=down_bias, attn_gain=attn_gain, attn_shift=attn_shift, mlp_gain=mlp_gain, mlp_shift=mlp_shift)


@jax.custom_vjp
def low(v):
    return lax.optimization_barrier(v.astype(jnp.bfloat16)).astype(jnp.float32)

@jax.custom_vjp
def low_back(v):
    return v

def low_keep(v):
    return (low(v), None)

def low_pass(kept, grad):
    return (grad,)

def back_keep(v):
    return (v, None)

def back_low(kept, grad):
    return (low(grad),)
low.defvjp(low_keep, low_pass)
low_back.defvjp(back_keep, back_low)

def matmul(left, right):
    return jnp.dot(left, right, precision=lax.Precision.HIGHEST, preferred_element_type=jnp.float32)

def layer_norm(stream, norm_gain, norm_shift):
    centered = stream - lax.optimization_barrier(jnp.mean(stream, axis=-1, keepdims=True))
    spread = lax.optimization_barrier(jnp.mean(centered * centered, axis=-1, keepdims=True))
    return centered * lax.rsqrt(spread + 1e-05) * norm_gain + norm_shift

def angles(positions):
    inverse = 10000.0 ** (-jnp.arange(0, ROT, 2, dtype=jnp.float32) / ROT)
    phases = positions.astype(jnp.float32)[:, None] * inverse[None, :]
    return (jnp.cos(phases)[:, None, :], jnp.sin(phases)[:, None, :])

def rotate(heads_in, cosine_table, sine_table):
    half_rot = cosine_table.shape[-1]
    first_half = heads_in[..., :half_rot]
    second_half = heads_in[..., half_rot:2 * half_rot]
    untouched = heads_in[..., 2 * half_rot:]
    return jnp.concatenate([first_half * cosine_table - second_half * sine_table, second_half * cosine_table + first_half * sine_table, untouched], axis=-1)

def attend_group(queries, key_rows, values, segment):
    length = queries.shape[0]
    block_rows = min(512, length)
    block_count = length // block_rows
    key_index = jnp.arange(length, dtype=jnp.int32)
    score_scale = 1.0 / math.sqrt(HEAD)

    def attend_block(inputs):
        query_block, offset = inputs
        row_index = offset + jnp.arange(block_rows, dtype=jnp.int32)
        row_segment = lax.dynamic_slice_in_dim(segment, offset, block_rows)
        visible = (key_index[None, :] <= row_index[:, None]) & (segment[None, :] == row_segment[:, None])
        scores = low_back(jnp.einsum('qhd,khd->hqk', query_block, key_rows, precision=lax.Precision.HIGHEST) * score_scale)
        scores = jnp.where(visible[None], scores, -1e+30)
        row_max = lax.optimization_barrier(jnp.max(scores, axis=-1, keepdims=True))
        weights = jnp.exp(scores - row_max)
        weights = weights / lax.optimization_barrier(jnp.sum(weights, axis=-1, keepdims=True))
        return jnp.einsum('hqk,khd->qhd', low(weights), values, precision=lax.Precision.HIGHEST)
    offsets = jnp.arange(block_count, dtype=jnp.int32) * block_rows
    result = lax.map(jax.checkpoint(attend_block), (queries.reshape(block_count, block_rows, HEADS, HEAD), offsets))
    return result.reshape(length, HEADS * HEAD)

def forward_group(stream, segment, params):
    proj_qkv, bias_qkv, proj_attn, bias_attn, proj_up, bias_up, proj_down, bias_down, gain_attn, shift_attn, gain_mlp, shift_mlp = params
    length = stream.shape[0]
    positions = jnp.arange(length, dtype=jnp.int32) - lax.optimization_barrier(jnp.sum((segment[None, :] < segment[:, None]).astype(jnp.int32), axis=1))
    cosine_table, sine_table = angles(positions)
    for depth in range(LAYERS):
        normed_attn = low(layer_norm(stream, gain_attn[depth], shift_attn[depth]))
        normed_mlp = low(layer_norm(stream, gain_mlp[depth], shift_mlp[depth]))
        projected = low_back(matmul(normed_attn, proj_qkv[depth]) + bias_qkv[depth])
        queries = low(rotate(projected[:, :D].reshape(length, HEADS, HEAD), cosine_table, sine_table))
        key_rows = low(rotate(projected[:, D:2 * D].reshape(length, HEADS, HEAD), cosine_table, sine_table))
        values = low(projected[:, 2 * D:].reshape(length, HEADS, HEAD))
        attended = low(low_back(attend_group(queries, key_rows, values, segment)))
        attn_branch = low_back(matmul(attended, proj_attn[depth]) + bias_attn[depth])
        hidden_pre = low_back(matmul(normed_mlp, proj_up[depth]) + bias_up[depth])
        hidden = low(jax.nn.gelu(hidden_pre, approximate=False))
        mlp_branch = low_back(matmul(hidden, proj_down[depth]) + bias_down[depth])
        stream = stream + attn_branch + mlp_branch
    return stream

def reference(tokens, segment_ids, cotangent, qkv_weight, qkv_bias, attn_weight, attn_bias, up_weight, up_bias, down_weight, down_bias, attn_gain, attn_shift, mlp_gain, mlp_shift):
    params = (qkv_weight.astype(jnp.float32), qkv_bias.astype(jnp.float32), attn_weight.astype(jnp.float32), attn_bias.astype(jnp.float32), up_weight.astype(jnp.float32), up_bias.astype(jnp.float32), down_weight.astype(jnp.float32), down_bias.astype(jnp.float32), attn_gain.astype(jnp.float32), attn_shift.astype(jnp.float32), mlp_gain.astype(jnp.float32), mlp_shift.astype(jnp.float32))
    groups = TOKENS // GROUP
    streams = tokens.astype(jnp.float32).reshape(groups, GROUP, D)
    segments = segment_ids.reshape(groups, GROUP)

    def forward(stream_all, param_all):

        def one_group(inputs):
            return forward_group(inputs[0], inputs[1], param_all)
        return lax.map(one_group, (stream_all, segments))
    result, pullback = jax.vjp(forward, streams, params)
    stream_grad, grads = pullback(cotangent.astype(jnp.float32).reshape(groups, GROUP, D))
    return (result.reshape(TOKENS, D).astype(jnp.bfloat16), stream_grad.reshape(TOKENS, D), grads[0], grads[1], grads[2], grads[3], grads[4], grads[5], grads[6], grads[7], grads[8], grads[9], grads[10], grads[11])
```

```python
from functools import partial
import math

import jax
import jax.numpy as jnp
from jax import lax
from jax.experimental import pallas as pl
from jax.experimental.pallas import tpu as pltpu
from jax.sharding import Mesh, PartitionSpec as P

D = 768
HEADS = 12
HEAD = 64
FF = 3072
ROT = 16
LAYERS = 2


def layer_norm(stream, norm_gain, norm_shift):
    centered = stream - jnp.mean(stream, axis=-1, keepdims=True)
    spread = jnp.mean(centered * centered, axis=-1, keepdims=True)
    return centered * lax.rsqrt(spread + 1e-05) * norm_gain + norm_shift


def both_norms(stream, gain_attn, shift_attn, gain_mlp, shift_mlp):
    return (layer_norm(stream, gain_attn, shift_attn), layer_norm(stream, gain_mlp, shift_mlp))


def angles(positions):
    inverse = 10000.0 ** (-jnp.arange(0, ROT, 2, dtype=jnp.float32) / ROT)
    phases = positions.astype(jnp.float32)[:, None] * inverse[None, :]
    return (jnp.cos(phases)[:, None, :], jnp.sin(phases)[:, None, :])


def rotate(heads_in, cosine_table, sine_table):
    half_rot = cosine_table.shape[-1]
    first_half = heads_in[..., :half_rot]
    second_half = heads_in[..., half_rot : 2 * half_rot]
    untouched = heads_in[..., 2 * half_rot :]
    return jnp.concatenate(
        [
            first_half * cosine_table - second_half * sine_table,
            second_half * cosine_table + first_half * sine_table,
            untouched,
        ],
        axis=-1,
    )


def split_blocks(update, running, key_piece, value_piece, offset):
    piece_rows = key_piece.shape[0]
    block_rows = 512 if piece_rows > 512 and piece_rows % 512 == 0 else piece_rows
    block_count = piece_rows // block_rows
    if block_count == 1:
        return update(running, key_piece, value_piece, offset)

    def advance(state, inputs):
        key_block, value_block, start = inputs
        return (update(state, key_block, value_block, offset + start), None)

    starts = jnp.arange(block_count, dtype=jnp.int32) * block_rows
    state, _ = lax.scan(
        advance,
        running,
        (
            key_piece.reshape(block_count, block_rows, -1),
            value_piece.reshape(block_count, block_rows, -1),
            starts,
        ),
    )
    return state


def stack_layers(per_layer, member):
    return jnp.stack([layer_entry[member] for layer_entry in per_layer])


def flatten_rows(matrix):
    return matrix.reshape(matrix.shape[:-2] + (-1, 128))


def local(
    tokens,
    segment_ids,
    cotangent,
    qkv_weight,
    qkv_bias,
    attn_weight,
    attn_bias,
    up_weight,
    up_bias,
    down_weight,
    down_bias,
    attn_gain,
    attn_shift,
    mlp_gain,
    mlp_shift,
):
    tok_rows = tokens.shape[0]
    group_rows = tok_rows * lax.axis_size("cp")
    score_scale = 1.0 / math.sqrt(HEAD)
    all_segments = lax.all_gather(segment_ids, "cp", axis=0, tiled=True)
    row_index = lax.axis_index("cp") * tok_rows + jnp.arange(tok_rows, dtype=jnp.int32)
    positions = row_index - jnp.sum(
        (all_segments[None, :] < segment_ids[:, None]).astype(jnp.int32), axis=1
    )
    cosine_table, sine_table = angles(positions)

    def visible_mask(offset, block_rows):
        key_index = offset + jnp.arange(block_rows, dtype=jnp.int32)
        key_segment = lax.dynamic_slice_in_dim(all_segments, offset, block_rows)
        return (key_index[None, :] <= row_index[:, None]) & (
            key_segment[None, :] == segment_ids[:, None]
        )

    def online_step(query_heads, running, key_block, value_block, offset):
        row_max, denominator, weighted = running
        block_rows = key_block.shape[0]
        key_heads = key_block.reshape(block_rows, HEADS, HEAD)
        value_heads = value_block.reshape(block_rows, HEADS, HEAD)
        scores = (
            jnp.einsum("qhd,khd->hqk", query_heads, key_heads, preferred_element_type=jnp.float32)
            * score_scale
        )
        visible = visible_mask(offset, block_rows)
        scores = jnp.where(visible[None], scores, -1e30)
        new_max = jnp.maximum(row_max, jnp.max(scores, axis=-1))
        rescale = jnp.exp(row_max - new_max)
        weights = jnp.where(visible[None], jnp.exp(scores - new_max[..., None]), 0.0)
        denominator = denominator * rescale + jnp.sum(weights, axis=-1)
        weighted = weighted * rescale[..., None] + jnp.einsum(
            "hqk,khd->hqd",
            weights.astype(jnp.bfloat16),
            value_heads,
            preferred_element_type=jnp.float32,
        )
        return (new_max, denominator, weighted)

    stream = tokens.astype(jnp.float32)
    stored = []
    for depth in range(LAYERS):
        params = (
            lax.all_gather(qkv_weight[depth], ("dp", "cp"), axis=0, tiled=True),
            lax.all_gather(qkv_bias[depth], ("dp", "cp"), axis=0, tiled=True),
            lax.all_gather(attn_weight[depth], ("dp", "cp"), axis=0, tiled=True),
            lax.all_gather(attn_bias[depth], ("dp", "cp"), axis=0, tiled=True),
            lax.all_gather(up_weight[depth], ("dp", "cp"), axis=0, tiled=True),
            lax.all_gather(up_bias[depth], ("dp", "cp"), axis=0, tiled=True),
            lax.all_gather(down_weight[depth], ("dp", "cp"), axis=0, tiled=True),
            lax.all_gather(down_bias[depth], ("dp", "cp"), axis=0, tiled=True),
            lax.all_gather(attn_gain[depth], ("dp", "cp"), axis=0, tiled=True),
            lax.all_gather(attn_shift[depth], ("dp", "cp"), axis=0, tiled=True),
            lax.all_gather(mlp_gain[depth], ("dp", "cp"), axis=0, tiled=True),
            lax.all_gather(mlp_shift[depth], ("dp", "cp"), axis=0, tiled=True),
        )
        (
            proj_qkv,
            bias_qkv,
            proj_attn,
            bias_attn,
            proj_up,
            bias_up,
            proj_down,
            bias_down,
            gain_attn,
            shift_attn,
            gain_mlp,
            shift_mlp,
        ) = params
        normed_attn, normed_mlp = both_norms(
            stream,
            gain_attn.astype(jnp.float32),
            shift_attn.astype(jnp.float32),
            gain_mlp.astype(jnp.float32),
            shift_mlp.astype(jnp.float32),
        )
        normed_attn = normed_attn.astype(jnp.bfloat16)
        normed_mlp = normed_mlp.astype(jnp.bfloat16)
        projected = jnp.dot(
            normed_attn, proj_qkv, preferred_element_type=jnp.float32
        ) + bias_qkv.astype(jnp.float32)
        queries = rotate(
            projected[:, :D].reshape(tok_rows, HEADS, HEAD), cosine_table, sine_table
        ).astype(jnp.bfloat16)
        key_rows = (
            rotate(projected[:, D : 2 * D].reshape(tok_rows, HEADS, HEAD), cosine_table, sine_table)
            .astype(jnp.bfloat16)
            .reshape(tok_rows, D)
        )
        values = projected[:, 2 * D :].astype(jnp.bfloat16)
        initial = (
            jnp.full((HEADS, tok_rows), -1e30, jnp.float32),
            jnp.zeros((HEADS, tok_rows), jnp.float32),
            jnp.zeros((HEADS, tok_rows, HEAD), jnp.float32),
        )
        row_max, denominator, weighted = split_blocks(
            partial(online_step, queries),
            initial,
            lax.all_gather(key_rows, "cp", axis=0, tiled=True),
            lax.all_gather(values, "cp", axis=0, tiled=True),
            jnp.int32(0),
        )
        attended = jnp.transpose(weighted / denominator[..., None], (1, 0, 2)).reshape(tok_rows, D)
        log_total = row_max + jnp.log(denominator)
        attended_low = attended.astype(jnp.bfloat16)
        attn_branch = jnp.dot(
            attended_low, proj_attn, preferred_element_type=jnp.float32
        ) + bias_attn.astype(jnp.float32)
        hidden_pre = jnp.dot(
            normed_mlp, proj_up, preferred_element_type=jnp.float32
        ) + bias_up.astype(jnp.float32)
        hidden = jax.nn.gelu(hidden_pre, approximate=False).astype(jnp.bfloat16)
        mlp_branch = jnp.dot(
            hidden, proj_down, preferred_element_type=jnp.float32
        ) + bias_down.astype(jnp.float32)
        stored.append(
            (
                stream,
                normed_attn,
                normed_mlp,
                queries,
                key_rows,
                values,
                attended,
                attended_low,
                log_total,
                hidden_pre,
                hidden,
            )
        )
        stream = stream + attn_branch + mlp_branch
    grad_stream = cotangent.astype(jnp.float32)
    per_layer = [None] * LAYERS
    for depth in reversed(range(LAYERS)):
        (
            saved_stream,
            normed_attn,
            normed_mlp,
            queries,
            key_rows,
            values,
            attended,
            attended_low,
            log_total,
            hidden_pre,
            hidden,
        ) = stored[depth]
        params = (
            lax.all_gather(qkv_weight[depth], ("dp", "cp"), axis=0, tiled=True),
            lax.all_gather(qkv_bias[depth], ("dp", "cp"), axis=0, tiled=True),
            lax.all_gather(attn_weight[depth], ("dp", "cp"), axis=0, tiled=True),
            lax.all_gather(attn_bias[depth], ("dp", "cp"), axis=0, tiled=True),
            lax.all_gather(up_weight[depth], ("dp", "cp"), axis=0, tiled=True),
            lax.all_gather(up_bias[depth], ("dp", "cp"), axis=0, tiled=True),
            lax.all_gather(down_weight[depth], ("dp", "cp"), axis=0, tiled=True),
            lax.all_gather(down_bias[depth], ("dp", "cp"), axis=0, tiled=True),
            lax.all_gather(attn_gain[depth], ("dp", "cp"), axis=0, tiled=True),
            lax.all_gather(attn_shift[depth], ("dp", "cp"), axis=0, tiled=True),
            lax.all_gather(mlp_gain[depth], ("dp", "cp"), axis=0, tiled=True),
            lax.all_gather(mlp_shift[depth], ("dp", "cp"), axis=0, tiled=True),
        )
        (
            proj_qkv,
            bias_qkv,
            proj_attn,
            bias_attn,
            proj_up,
            bias_up,
            proj_down,
            bias_down,
            gain_attn,
            shift_attn,
            gain_mlp,
            shift_mlp,
        ) = params
        grad_low = grad_stream.astype(jnp.bfloat16)
        bias_grad = jnp.sum(grad_low.astype(jnp.float32), axis=0)
        attn_weight_grad = jnp.einsum(
            "td,te->de", attended_low, grad_low, preferred_element_type=jnp.float32
        )
        down_weight_grad = jnp.einsum(
            "tf,te->fe", hidden, grad_low, preferred_element_type=jnp.float32
        )
        grad_attended = jnp.einsum(
            "te,de->td", grad_low, proj_attn, preferred_element_type=jnp.float32
        ).astype(jnp.bfloat16)
        grad_hidden = jnp.einsum(
            "te,fe->tf", grad_low, proj_down, preferred_element_type=jnp.float32
        )
        _, gelu_pull = jax.vjp(partial(jax.nn.gelu, approximate=False), hidden_pre)
        grad_pre = gelu_pull(grad_hidden)[0].astype(jnp.bfloat16)
        up_weight_grad = jnp.einsum(
            "td,tf->df", normed_mlp, grad_pre, preferred_element_type=jnp.float32
        )
        up_bias_grad = jnp.sum(grad_pre.astype(jnp.float32), axis=0)
        grad_normed_mlp = jnp.einsum(
            "tf,df->td", grad_pre, proj_up, preferred_element_type=jnp.float32
        )
        all_keys, all_values = (
            lax.all_gather(key_rows, "cp", axis=0, tiled=True),
            lax.all_gather(values, "cp", axis=0, tiled=True),
        )
        grad_heads = grad_attended.reshape(tok_rows, HEADS, HEAD)
        row_dot = jnp.transpose(
            jnp.sum(
                grad_heads.astype(jnp.float32) * attended.reshape(tok_rows, HEADS, HEAD), axis=-1
            )
        )
        block_rows = 512 if group_rows > 512 and group_rows % 512 == 0 else group_rows
        block_count = group_rows // block_rows
        starts = jnp.arange(block_count, dtype=jnp.int32) * block_rows

        def back_step(grad_query, inputs):
            key_block, value_block, offset = inputs
            key_heads = key_block.reshape(block_rows, HEADS, HEAD)
            value_heads = value_block.reshape(block_rows, HEADS, HEAD)
            scores = (
                jnp.einsum("qhd,khd->hqk", queries, key_heads, preferred_element_type=jnp.float32)
                * score_scale
            )
            visible = visible_mask(offset, block_rows)
            weights = jnp.where(visible[None], jnp.exp(scores - log_total[..., None]), 0.0)
            grad_weights = jnp.einsum(
                "qhd,khd->hqk", grad_heads, value_heads, preferred_element_type=jnp.float32
            )
            grad_scores = (weights * (grad_weights - row_dot[..., None])).astype(jnp.bfloat16)
            grad_query = grad_query + jnp.einsum(
                "hqk,khd->hqd", grad_scores, key_heads, preferred_element_type=jnp.float32
            )
            key_grad = (
                jnp.einsum("hqk,qhd->khd", grad_scores, queries, preferred_element_type=jnp.float32)
                * score_scale
            )
            value_grad = jnp.einsum(
                "hqk,qhd->khd",
                weights.astype(jnp.bfloat16),
                grad_heads,
                preferred_element_type=jnp.float32,
            )
            return (
                grad_query,
                (key_grad.reshape(block_rows, D), value_grad.reshape(block_rows, D)),
            )

        grad_query, (key_grads, value_grads) = lax.scan(
            back_step,
            jnp.zeros((HEADS, tok_rows, HEAD), jnp.float32),
            (
                all_keys.reshape(block_count, block_rows, D),
                all_values.reshape(block_count, block_rows, D),
                starts,
            ),
        )
        local_key_grad, local_value_grad = (
            lax.psum_scatter(
                key_grads.reshape(group_rows, D).astype(jnp.bfloat16),
                "cp",
                scatter_dimension=0,
                tiled=True,
            ).astype(jnp.float32),
            lax.psum_scatter(
                value_grads.reshape(group_rows, D).astype(jnp.bfloat16),
                "cp",
                scatter_dimension=0,
                tiled=True,
            ).astype(jnp.float32),
        )
        query_raw = rotate(
            jnp.transpose(grad_query * score_scale, (1, 0, 2)), cosine_table, -sine_table
        )
        key_raw = rotate(local_key_grad.reshape(tok_rows, HEADS, HEAD), cosine_table, -sine_table)
        grad_projected = jnp.concatenate(
            [query_raw.reshape(tok_rows, D), key_raw.reshape(tok_rows, D), local_value_grad], axis=1
        ).astype(jnp.bfloat16)
        qkv_weight_grad = jnp.einsum(
            "td,te->de", normed_attn, grad_projected, preferred_element_type=jnp.float32
        )
        qkv_bias_grad = jnp.sum(grad_projected.astype(jnp.float32), axis=0)
        grad_normed_attn = jnp.einsum(
            "te,de->td", grad_projected, proj_qkv, preferred_element_type=jnp.float32
        )
        _, norm_pull = jax.vjp(
            both_norms,
            saved_stream,
            gain_attn.astype(jnp.float32),
            shift_attn.astype(jnp.float32),
            gain_mlp.astype(jnp.float32),
            shift_mlp.astype(jnp.float32),
        )
        grad_input, attn_gain_grad, attn_shift_grad, mlp_gain_grad, mlp_shift_grad = norm_pull(
            (grad_normed_attn, grad_normed_mlp)
        )
        grad_stream = grad_stream + grad_input
        summed = (
            lax.psum_scatter(
                flatten_rows(qkv_weight_grad), ("dp", "cp"), scatter_dimension=0, tiled=True
            ),
            lax.psum_scatter(qkv_bias_grad, ("dp", "cp"), scatter_dimension=0, tiled=True),
            lax.psum_scatter(
                flatten_rows(attn_weight_grad), ("dp", "cp"), scatter_dimension=0, tiled=True
            ),
            lax.psum_scatter(bias_grad, ("dp", "cp"), scatter_dimension=0, tiled=True),
            lax.psum_scatter(
                flatten_rows(up_weight_grad), ("dp", "cp"), scatter_dimension=0, tiled=True
            ),
            lax.psum_scatter(up_bias_grad, ("dp", "cp"), scatter_dimension=0, tiled=True),
            lax.psum_scatter(
                flatten_rows(down_weight_grad), ("dp", "cp"), scatter_dimension=0, tiled=True
            ),
            lax.psum_scatter(bias_grad, ("dp", "cp"), scatter_dimension=0, tiled=True),
            lax.psum_scatter(attn_gain_grad, ("dp", "cp"), scatter_dimension=0, tiled=True),
            lax.psum_scatter(attn_shift_grad, ("dp", "cp"), scatter_dimension=0, tiled=True),
            lax.psum_scatter(mlp_gain_grad, ("dp", "cp"), scatter_dimension=0, tiled=True),
            lax.psum_scatter(mlp_shift_grad, ("dp", "cp"), scatter_dimension=0, tiled=True),
        )
        per_layer[depth] = (
            summed[0].reshape(-1, 3 * D),
            summed[1],
            summed[2].reshape(-1, D),
            summed[3],
            summed[4].reshape(-1, FF),
            summed[5],
            summed[6].reshape(-1, D),
            summed[7],
            summed[8],
            summed[9],
            summed[10],
            summed[11],
        )
    stacked = [stack_layers(per_layer, member) for member in range(12)]
    return (
        stream.astype(jnp.bfloat16),
        grad_stream,
        stacked[0],
        stacked[1],
        stacked[2],
        stacked[3],
        stacked[4],
        stacked[5],
        stacked[6],
        stacked[7],
        stacked[8],
        stacked[9],
        stacked[10],
        stacked[11],
    )


TEAM = 4
TEAM_AXES = ("core", "x")
LINE_AXES = ("z", "y")
MINE = (3 * D) // TEAM
HCOLS = D // TEAM
UCOLS = FF // TEAM
VMEM_BYTES = 56 * 1024 * 1024
BF = jnp.bfloat16
F32 = jnp.float32


def call(body, out_shape, name, operands, scratch=()):
    return pl.pallas_call(
        body,
        out_shape=out_shape,
        scratch_shapes=list(scratch),
        compiler_params=pltpu.CompilerParams(vmem_limit_bytes=VMEM_BYTES),
        name=name,
    )(*operands)


def shape(dims, kind):
    return jax.ShapeDtypeStruct(dims, kind)


def mm(left, right):
    return jnp.dot(left, right, preferred_element_type=F32)


def mm_t(left, right):
    return lax.dot_general(left, right, (((1,), (1,)), ((), ())), preferred_element_type=F32)


def t_mm(left, right):
    return lax.dot_general(left, right, (((0,), (0,)), ((), ())), preferred_element_type=F32)


def pick(member, slot, pieces, wanted):
    chosen = pieces[0]
    for s in range(1, TEAM):
        chosen = jnp.where((member ^ s) == wanted, pieces[s], chosen)
    return chosen


def pack_body(me_ref, qkv_ref, up_ref, small_ref, *outs):
    me = me_ref[0]
    for depth in range(LAYERS):
        rows = qkv_ref.shape[1]
        qkv = qkv_ref[depth].astype(F32)
        up = up_ref[depth].astype(F32)
        blocks = up.shape[1] // (TEAM * 96)
        parts = []
        for p in range(TEAM):
            up_p = jnp.concatenate(
                [up[:, 96 * (TEAM * b + p) : 96 * (TEAM * b + p + 1)] for b in range(blocks)], axis=1
            )
            qkv_p = jnp.concatenate(
                [qkv[:, D * t + HCOLS * p : D * t + HCOLS * (p + 1)] for t in range(3)]
                + [jnp.zeros((rows, UCOLS - MINE), F32)],
                axis=1,
            )
            parts.append(jnp.concatenate([up_p, qkv_p], axis=0))
        small = small_ref[depth].astype(F32)
        for s in range(TEAM):
            dest = me ^ s
            chosen = parts[0]
            for p in range(1, TEAM):
                chosen = jnp.where(dest == p, parts[p], chosen)
            outs[depth * TEAM + s][...] = jnp.concatenate([chosen, small], axis=0).astype(BF)


def assemble_body(me_ref, p0, p1, p2, p3, attn_ref, down_ref, q_ref, m_ref):
    me = me_ref[0]
    slots = [r[...].astype(F32) for r in (p0, p1, p2, p3)]
    ordered = [pick(me, None, slots, p) for p in range(TEAM)]
    up = jnp.concatenate([piece[0:24] for piece in ordered], axis=0)
    qkv = jnp.concatenate([piece[24:48] for piece in ordered], axis=0)
    small = jnp.concatenate([piece[48:56] for piece in ordered], axis=0)
    q_ref[0:96] = qkv[:, :MINE].astype(BF)
    q_ref[96:128] = small[:, :MINE].astype(BF)
    m_ref[0:96] = up.astype(BF)
    m_ref[96:192] = down_ref[...]
    m_ref[192:224] = jnp.concatenate(
        [attn_ref[...].astype(F32), jnp.zeros((8, D), F32)], axis=0
    ).astype(BF)


def norm_parts(stream):
    centered = stream - jnp.mean(stream, axis=-1, keepdims=True)
    spread = jnp.mean(centered * centered, axis=-1, keepdims=True)
    inverse = lax.rsqrt(spread + 1e-05)
    return centered * inverse, inverse


def two_slots(first, second):
    return jnp.concatenate([first[0:TOK].astype(F32), second[0:TOK].astype(F32)], axis=0)


TOK = 128
PAIR = 2 * TOK


def turn(block, cosine, sine):
    lane = lax.broadcasted_iota(jnp.int32, (block.shape[0], 128), 1) % HEAD
    tiles = []
    for t in range(block.shape[1] // 128):
        tile = block[:, 128 * t : 128 * (t + 1)]
        swapped = jnp.where(
            lane < ROT // 2, pltpu.roll(tile, 128 - ROT // 2, 1), pltpu.roll(tile, ROT // 2, 1)
        )
        tiles.append(tile * cosine + swapped * sine)
    return jnp.concatenate(tiles, axis=1)


def head_mask(rows, head):
    lane = lax.broadcasted_iota(jnp.int32, (rows, HCOLS), 1)
    return (lane >= head * HEAD) & (lane < (head + 1) * HEAD)


def attend_body(
    x0, x1, x2, x3, w_ref, b_ref, vec_ref, cos_ref, sin_ref, mask_ref,
    a_ref, q_ref, k_ref, v_ref, o_ref,
):
    weight = w_ref[:, 0:96, :].reshape(D, MINE)
    for g, (first, second) in enumerate(((x0, x1), (x2, x3))):
        rows = pl.ds(PAIR * g, PAIR)
        scaled, _ = norm_parts(two_slots(first[0:TOK], second[0:TOK]))
        normed = (scaled * vec_ref[2:3] + vec_ref[3:4]).astype(BF)
        a_ref[rows, :] = normed
        projected = mm(normed, weight) + b_ref[...]
        turned = turn(projected[:, : 2 * HCOLS], cos_ref[rows, :], sin_ref[rows, :])
        queries = (turned[:, :HCOLS].astype(BF) * 0.125).astype(BF)
        keys = turned[:, HCOLS:].astype(BF)
        values = projected[:, 2 * HCOLS :].astype(BF)
        q_ref[rows, :] = queries
        k_ref[rows, :] = keys
        v_ref[rows, :] = values
        total = jnp.zeros((PAIR, HCOLS), F32)
        for head in range(HEADS // TEAM):
            owned = head_mask(PAIR, head)
            scores = mm_t(jnp.where(owned, queries, jnp.zeros_like(queries)), keys) + mask_ref[g]
            weights = jnp.exp(scores - jnp.max(scores, axis=-1, keepdims=True))
            below = jnp.sum(weights, axis=-1, keepdims=True)
            total = total + jnp.where(owned, mm(weights.astype(BF), values) / below, 0.0)
        o_ref[rows, :] = total.astype(BF)


def attn_rows(w_ref):
    return w_ref[:, 192:224, :].astype(F32)[:, :24].reshape(HCOLS, D).astype(BF)


def gelu_parts(u):
    cdf = 0.5 * (1.0 + lax.erf(u * (1.0 / math.sqrt(2.0))))
    density = jnp.exp(-0.5 * u * u) * (1.0 / math.sqrt(2.0 * math.pi))
    return u * cdf, cdf + u * density


def mlp_body(x0, x1, x2, x3, w_ref, b_ref, vec_ref, o_ref, c_ref, u_ref, y0, y1, y2, y3):
    up = w_ref[:, 0:96, :].reshape(D, UCOLS)
    down = w_ref[:, 96:192, :].reshape(UCOLS, D)
    attn = attn_rows(w_ref)
    for g, (first, second, y_first, y_second) in enumerate(((x0, x1, y0, y1), (x2, x3, y2, y3))):
        rows = pl.ds(PAIR * g, PAIR)
        scaled, _ = norm_parts(two_slots(first[0:TOK], second[0:TOK]))
        normed = (scaled * vec_ref[4:5] + vec_ref[5:6]).astype(BF)
        c_ref[rows, :] = normed
        before = mm(normed, up) + b_ref[...]
        u_ref[rows, :] = before
        hidden = (before * (0.5 * (1.0 + lax.erf(before * (1.0 / math.sqrt(2.0)))))).astype(BF)
        result = mm(hidden, down) + mm(o_ref[rows, :], attn)
        y_first[...] = result[0:TOK].astype(y_first.dtype)
        y_second[...] = result[TOK:].astype(y_second.dtype)


def mlp_back_body(
    x0, x1, x2, x3, g0, g1, g2, g3, w_ref, vec_ref, o_ref, c_ref, u_ref,
    grad_ref, do_ref, dn_ref, sum_ref, hid_s, du_s, gb_s,
):
    up = w_ref[:, 0:96, :].reshape(D, UCOLS)
    down = w_ref[:, 96:192, :].reshape(UCOLS, D)
    attn = attn_rows(w_ref)
    gain_sum = jnp.zeros((1, D), F32)
    shift_sum = jnp.zeros((1, D), F32)
    bias_sum = jnp.zeros((1, D), F32)
    up_sum = jnp.zeros((1, UCOLS), F32)
    for g, (first, second, g_first, g_second) in enumerate(((x0, x1, g0, g1), (x2, x3, g2, g3))):
        rows = pl.ds(PAIR * g, PAIR)
        low = jnp.concatenate([g_first[...], g_second[...]], axis=0)
        gb_s[rows, :] = low
        do_ref[rows, :] = mm_t(low, attn).astype(BF)
        hidden, slope = gelu_parts(u_ref[rows, :])
        hid_s[rows, :] = hidden.astype(BF)
        du = (mm_t(low, down) * slope).astype(BF)
        du_s[rows, :] = du
        dc = mm_t(du, up)
        scaled, _ = norm_parts(two_slots(first[0:TOK], second[0:TOK]))
        dn_ref[rows, :] = dc * vec_ref[4:5]
        gain_sum = gain_sum + jnp.sum(dc * scaled, axis=0, keepdims=True)
        shift_sum = shift_sum + jnp.sum(dc, axis=0, keepdims=True)
        bias_sum = bias_sum + jnp.sum(low.astype(F32), axis=0, keepdims=True)
        up_sum = up_sum + jnp.sum(du.astype(F32), axis=0, keepdims=True)
    grad_ref[:, 0:96, :] = t_mm(c_ref[...], du_s[...]).reshape(-1, 96, UCOLS).astype(BF)
    grad_ref[:, 96:192, :] = t_mm(hid_s[...], gb_s[...]).reshape(-1, 96, D).astype(BF)
    attn_grad = t_mm(o_ref[...], gb_s[...]).reshape(-1, 24, D)
    grad_ref[:, 192:224, :] = jnp.concatenate(
        [attn_grad, jnp.zeros((attn_grad.shape[0], 8, D), F32)], axis=1
    ).astype(BF)
    sum_ref[...] = jnp.concatenate(
        [bias_sum, up_sum, gain_sum, shift_sum, jnp.zeros((4, D), F32)], axis=0
    )


def attend_back_body(
    x0, x1, x2, x3, w_ref, vec_ref, cos_ref, sin_ref, mask_ref,
    a_ref, q_ref, k_ref, v_ref, do_ref, dn_ref,
    grad_ref, sum_ref, bias_ref, y0, y1, y2, y3, dp_s,
):
    weight = w_ref[:, 0:96, :].reshape(D, MINE)
    gain_sum = jnp.zeros((1, D), F32)
    shift_sum = jnp.zeros((1, D), F32)
    bias_sum = jnp.zeros((1, MINE), F32)
    for g, (first, second, y_first, y_second) in enumerate(((x0, x1, y0, y1), (x2, x3, y2, y3))):
        rows = pl.ds(PAIR * g, PAIR)
        queries, keys, values = q_ref[rows, :], k_ref[rows, :], v_ref[rows, :]
        grad_o = do_ref[rows, :]
        zero = jnp.zeros_like(queries)
        dq = jnp.zeros((PAIR, HCOLS), F32)
        dk = jnp.zeros((PAIR, HCOLS), F32)
        dv = jnp.zeros((PAIR, HCOLS), F32)
        for head in range(HEADS // TEAM):
            owned = head_mask(PAIR, head)
            scores = mm_t(jnp.where(owned, queries, zero), keys) + mask_ref[g]
            weights = jnp.exp(scores - jnp.max(scores, axis=-1, keepdims=True))
            weights = weights / jnp.sum(weights, axis=-1, keepdims=True)
            dweights = mm_t(jnp.where(owned, grad_o, zero), values)
            delta = jnp.sum(weights * dweights, axis=-1, keepdims=True)
            dscores = (weights * (dweights - delta)).astype(BF)
            dq = dq + jnp.where(owned, mm(dscores, keys), 0.0)
            dk = dk + jnp.where(owned, t_mm(dscores, queries), 0.0)
            dv = dv + jnp.where(owned, t_mm(weights.astype(BF), grad_o), 0.0)
        both = turn(
            jnp.concatenate([dq * 0.125, dk], axis=1), cos_ref[rows, :], -sin_ref[rows, :]
        )
        dproj = jnp.concatenate([both, dv], axis=1).astype(BF)
        dp_s[rows, :] = dproj
        bias_sum = bias_sum + jnp.sum(dproj.astype(F32), axis=0, keepdims=True)
        da = mm_t(dproj, weight)
        scaled, _ = norm_parts(two_slots(first[0:TOK], second[0:TOK]))
        gain_sum = gain_sum + jnp.sum(da * scaled, axis=0, keepdims=True)
        shift_sum = shift_sum + jnp.sum(da, axis=0, keepdims=True)
        dn = dn_ref[rows, :] + da * vec_ref[2:3]
        y_first[...] = dn[0:TOK].astype(y_first.dtype)
        y_second[...] = dn[TOK:].astype(y_second.dtype)
    grad_ref[...] = t_mm(a_ref[...], dp_s[...]).reshape(-1, 96, MINE).astype(BF)
    sum_ref[...] = jnp.concatenate([gain_sum, shift_sum, jnp.zeros((6, D), F32)], axis=0)
    bias_ref[...] = jnp.concatenate([bias_sum, jnp.zeros((7, MINE), F32)], axis=0)


def norm_back_body(x_ref, g_ref, n0, n1, n2, n3, out_ref, low_ref):
    scaled, inverse = norm_parts(x_ref[...].astype(F32))
    dn = n0[...] + n1[...].astype(F32) + n2[...].astype(F32) + n3[...].astype(F32)
    centered = dn - jnp.mean(dn, axis=-1, keepdims=True)
    moment = jnp.mean(dn * scaled, axis=-1, keepdims=True)
    result = g_ref[...].astype(F32) + inverse * (centered - scaled * moment)
    out_ref[...] = result
    low_ref[...] = result.astype(BF)


def split_body(me_ref, m_ref, q_ref, o0, o1, o2, o3):
    me = me_ref[0]
    up = m_ref[0:96].astype(F32)
    qkv = jnp.concatenate(
        [q_ref[...].astype(F32), jnp.zeros((96, UCOLS - MINE), F32)], axis=1
    )
    for s, out in enumerate((o0, o1, o2, o3)):
        dest = me ^ s
        piece = jnp.concatenate([up[0:24], qkv[0:24]], axis=0)
        for p in range(1, TEAM):
            rows = slice(24 * p, 24 * (p + 1))
            piece = jnp.where(dest == p, jnp.concatenate([up[rows], qkv[rows]], axis=0), piece)
        out[...] = piece.astype(BF)


def unpack_body(me_ref, *refs):
    me = me_ref[0]
    qkv_ref, up_ref = refs[-2:]
    for depth in range(LAYERS):
        slots = [refs[depth * TEAM + s][...].astype(F32) for s in range(TEAM)]
        ordered = [pick(me, None, slots, p) for p in range(TEAM)]
        blocks = FF // (96 * TEAM)
        up_ref[depth] = jnp.concatenate(
            [ordered[p][0:24, 96 * b : 96 * (b + 1)] for b in range(blocks) for p in range(TEAM)],
            axis=1,
        )
        qkv_ref[depth] = jnp.concatenate(
            [
                ordered[p][24:48, HCOLS * t : HCOLS * (t + 1)]
                for t in range(3)
                for p in range(TEAM)
            ],
            axis=1,
        )


def team_send(piece, slot):
    flips = [(m, m ^ slot) for m in range(TEAM)]
    return lax.ppermute(piece, TEAM_AXES, flips)


def local_team(
    tokens, segment_ids, cotangent, qkv_weight, qkv_bias, attn_weight, attn_bias,
    up_weight, up_bias, down_weight, down_bias, attn_gain, attn_shift, mlp_gain, mlp_shift,
):
    lines = lax.axis_size("z") * lax.axis_size("y")
    world = lines * TEAM
    team = lax.axis_index("z") * lax.axis_size("y") + lax.axis_index("y")
    member = lax.axis_index("core") * 2 + lax.axis_index("x")
    me = jnp.reshape(member, (1,)).astype(jnp.int32)
    everywhere = LINE_AXES + TEAM_AXES

    def row(vector):
        return jnp.pad(vector, ((0, 0), (0, UCOLS - vector.shape[1])))[:, None, :]

    small = jnp.concatenate(
        [row(v) for v in (qkv_bias, up_bias, attn_gain, attn_shift, mlp_gain, mlp_shift, attn_bias, down_bias)],
        axis=1,
    )
    def with_member(body, out_shape, name, operands):
        return pl.pallas_call(
            body,
            out_shape=out_shape,
            in_specs=[pl.BlockSpec(memory_space=pltpu.SMEM)]
            + [pl.BlockSpec(memory_space=pltpu.VMEM)] * len(operands),
            compiler_params=pltpu.CompilerParams(vmem_limit_bytes=VMEM_BYTES),
            name=name,
        )(me, *operands)

    packed = with_member(
        pack_body,
        [shape((56, UCOLS), BF)] * (LAYERS * TEAM),
        "pack_weights",
        (qkv_weight, up_weight, small),
    )

    spread = [(i, TEAM * (i % lines) + i // lines) for i in range(world)]
    gather_back = [(b, a) for a, b in spread]
    attn_piece = lax.ppermute(attn_weight, everywhere, spread)

    gathered = []
    for depth in range(LAYERS):
        mine = packed[depth * TEAM : (depth + 1) * TEAM]
        pieces = [mine[0]] + [team_send(mine[s], s) for s in range(1, TEAM)]
        q_part, m_part = with_member(
            assemble_body,
            [shape((128, MINE), BF), shape((224, D), BF)],
            "assemble_weights",
            (*pieces, attn_piece[depth], down_weight[depth]),
        )
        gathered.append(
            (
                lax.all_gather(q_part, LINE_AXES, axis=0),
                lax.all_gather(m_part, LINE_AXES, axis=0),
            )
        )

    token_slots = [tokens] + [team_send(tokens, s) for s in range(1, TEAM)]
    segment_slots = [segment_ids] + [team_send(segment_ids, s) for s in range(1, TEAM)]
    low_cotangent = [cotangent] + [team_send(cotangent, s) for s in range(1, TEAM)]
    here = lax.axis_index("x")
    rows = jnp.arange(TOK, dtype=jnp.int32)
    places = jnp.concatenate([here * TOK + rows, (1 - here) * TOK + rows])
    masks, cosines, sines = [], [], []
    lane = jnp.arange(128, dtype=jnp.int32) % HEAD
    inverse = 10000.0 ** (-(lane % (ROT // 2) * 2).astype(F32) / ROT)
    for g in range(2):
        ids = jnp.concatenate(segment_slots[2 * g : 2 * g + 2])
        visible = (places[None, :] <= places[:, None]) & (ids[None, :] == ids[:, None])
        masks.append(jnp.where(visible, 0.0, -1e30).astype(F32))
        position = places - jnp.sum((ids[None, :] < ids[:, None]).astype(jnp.int32), axis=1)
        phases = position.astype(F32)[:, None] * inverse[None, :]
        cosines.append(jnp.where(lane[None, :] < ROT, jnp.cos(phases), 1.0))
        sign = jnp.where(lane < ROT // 2, -1.0, jnp.where(lane < ROT, 1.0, 0.0))
        sines.append(jnp.sin(phases) * sign[None, :])
    mask = jnp.stack(masks)
    cosine, sine = jnp.concatenate(cosines), jnp.concatenate(sines)

    def vectors(depth):
        block = gathered[depth][0][:, 96:128, :128].reshape(lines, TEAM, 8, 128)
        wide = block[:, :, 2:8, :24].transpose(2, 0, 1, 3).reshape(6, D).astype(F32)
        whole = jnp.concatenate([jnp.zeros((2, D), F32), wide], axis=0)
        up_b = lax.dynamic_index_in_dim(block[:, :, 1, :96], member, 1, keepdims=False)
        qkv_b = lax.dynamic_index_in_dim(
            block[:, :, 0, :72].reshape(3, TEAM, HCOLS), member, 1, keepdims=False
        )
        return whole, up_b.reshape(1, UCOLS).astype(F32), qkv_b.reshape(1, MINE).astype(F32)

    tok_all = TEAM * TOK
    stream = tokens
    slots = token_slots
    kept = []
    activations = None
    for depth in range(LAYERS):
        q_all, m_all = gathered[depth]
        whole, up_b, qkv_b = vectors(depth)
        a, q, k, v, o = call(
            attend_body,
            [shape((tok_all, D), BF)] + [shape((tok_all, HCOLS), BF)] * 4,
            "attend_forward",
            (*slots, q_all, qkv_b, whole, cosine, sine, mask),
        )
        c, u, y0, y1, y2, y3 = call(
            mlp_body,
            [shape((tok_all, D), BF), shape((tok_all, UCOLS), F32), shape((TOK, D), F32)]
            + [shape((TOK, D), BF)] * 3,
            "mlp_forward",
            (*slots, m_all, up_b, whole, o),
        )
        kept.append((stream, slots, a, q, k, v, o, c, u, whole))
        total = y0
        for s, y in ((1, y1), (2, y2), (3, y3)):
            total = total + team_send(y, s).astype(F32)
        stream = stream.astype(F32) + total + (whole[6:7] + whole[7:8])
        low = stream.astype(BF)
        if depth < LAYERS - 1:
            slots = [low] + [team_send(low, s) for s in range(1, TEAM)]
        else:
            activations = low

    grad = cotangent
    grad_slots = low_cotangent
    outs, sums = [None] * LAYERS, [None] * LAYERS
    for depth in reversed(range(LAYERS)):
        q_all, m_all = gathered[depth]
        stream, slots, a, q, k, v, o, c, u, whole = kept[depth]
        m_grad, do, dn, sum_m = call(
            mlp_back_body,
            [
                shape((lines, 224, D), BF),
                shape((tok_all, HCOLS), BF),
                shape((tok_all, D), F32),
                shape((8, D), F32),
            ],
            "mlp_backward",
            (*slots, *grad_slots, m_all, whole, o, c, u),
            [pltpu.VMEM((tok_all, UCOLS), BF), pltpu.VMEM((tok_all, UCOLS), BF), pltpu.VMEM((tok_all, D), BF)],
        )
        m_sum = lax.psum_scatter(m_grad, LINE_AXES, scatter_dimension=0, tiled=False)
        q_grad, sum_q, bias_q, n0, n1, n2, n3 = call(
            attend_back_body,
            [
                shape((lines, 96, MINE), BF),
                shape((8, D), F32),
                shape((8, MINE), F32),
                shape((TOK, D), F32),
            ]
            + [shape((TOK, D), BF)] * 3,
            "attend_backward",
            (*slots, q_all, whole, cosine, sine, mask, a, q, k, v, do, dn),
            [pltpu.VMEM((tok_all, MINE), BF)],
        )
        q_sum = lax.psum_scatter(q_grad, LINE_AXES, scatter_dimension=0, tiled=False)
        received = [n0] + [team_send(n, s) for s, n in ((1, n1), (2, n2), (3, n3))]
        grad, low = call(
            norm_back_body,
            [shape((TOK, D), F32), shape((TOK, D), BF)],
            "norm_backward",
            (stream, grad, *received),
        )
        if depth > 0:
            grad_slots = [low] + [team_send(low, s) for s in range(1, TEAM)]
        mine = with_member(
            split_body, [shape((48, UCOLS), BF)] * TEAM, "split_gradients", (m_sum, q_sum)
        )
        outs[depth] = (
            [mine[0]] + [team_send(mine[s], s) for s in range(1, TEAM)],
            m_sum[96:192].astype(F32),
            m_sum[192:216],
        )
        qkv_full = lax.dynamic_update_index_in_dim(
            jnp.zeros((3, TEAM, HCOLS), F32), bias_q[0].reshape(3, HCOLS), member, 1
        )
        up_full = lax.dynamic_update_index_in_dim(
            jnp.zeros((lines, TEAM, 96), F32), sum_m[1].reshape(lines, 96), member, 1
        )
        bias_full = jnp.where(member == 0, sum_m[0], 0.0)
        sums[depth] = jnp.concatenate(
            [
                qkv_full.reshape(world, 72),
                up_full.reshape(world, 96),
                *(
                    vector.reshape(world, 24)
                    for vector in (bias_full, sum_q[0], sum_q[1], sum_m[2], sum_m[3])
                ),
            ],
            axis=1,
        )
    qkv_grad, up_grad = with_member(
        unpack_body,
        [shape((LAYERS, 24, 3 * D), F32), shape((LAYERS, 24, FF), F32)],
        "unpack_gradients",
        [piece for depth in range(LAYERS) for piece in outs[depth][0]],
    )
    down_grad = jnp.stack([outs[depth][1] for depth in range(LAYERS)])
    attn_grad = lax.ppermute(
        jnp.stack([outs[depth][2] for depth in range(LAYERS)]), everywhere, gather_back
    ).astype(F32)
    tally = jnp.stack(sums)
    tally = tally + sum(team_send(tally, s) for s in range(1, TEAM))
    tally = tally + lax.ppermute(tally, "y", [(0, 1), (1, 0)])
    depth_z = lax.axis_size("z")
    tally = tally + sum(
        lax.ppermute(tally, "z", [(i, (i + s) % depth_z) for i in range(depth_z)])
        for s in range(1, depth_z)
    )
    own = lax.dynamic_index_in_dim(tally, team * TEAM + member, 1, keepdims=False)
    cuts = [0, 72, 168, 192, 216, 240, 264, 288]
    qkv_b, up_b, bias, ga, sa, gm, sm = (own[:, lo:hi] for lo, hi in zip(cuts[:-1], cuts[1:]))
    return (
        activations, grad, qkv_grad, qkv_b, attn_grad, bias, up_grad, up_b,
        down_grad, bias, ga, sa, gm, sm,
    )


def whole_mesh_solution(mesh):
    in_specs = (
        P(("dp", "cp"), None),
        P(("dp", "cp")),
        P(("dp", "cp"), None),
        P(None, ("dp", "cp"), None),
        P(None, ("dp", "cp")),
        P(None, ("dp", "cp"), None),
        P(None, ("dp", "cp")),
        P(None, ("dp", "cp"), None),
        P(None, ("dp", "cp")),
        P(None, ("dp", "cp"), None),
        P(None, ("dp", "cp")),
        P(None, ("dp", "cp")),
        P(None, ("dp", "cp")),
        P(None, ("dp", "cp")),
        P(None, ("dp", "cp")),
    )
    out_specs = (
        P(("dp", "cp"), None),
        P(("dp", "cp"), None),
        P(None, ("dp", "cp"), None),
        P(None, ("dp", "cp")),
        P(None, ("dp", "cp"), None),
        P(None, ("dp", "cp")),
        P(None, ("dp", "cp"), None),
        P(None, ("dp", "cp")),
        P(None, ("dp", "cp"), None),
        P(None, ("dp", "cp")),
        P(None, ("dp", "cp")),
        P(None, ("dp", "cp")),
        P(None, ("dp", "cp")),
        P(None, ("dp", "cp")),
    )
    return jax.shard_map(local, mesh=mesh, in_specs=in_specs, out_specs=out_specs, check_vma=False)


def solution(mesh):
    teams = mesh.shape["dp"] // 2
    if mesh.shape["cp"] != 2 or teams * TEAM * 24 != D:
        return whole_mesh_solution(mesh)
    split_mesh = Mesh(mesh.devices.reshape(teams // 2, 2, 2, 2), ("z", "y", "core", "x"))
    every = ("z", "y", "core", "x")
    row = P(every, None)
    matrix, vector = P(None, every, None), P(None, every)
    in_specs = (row, P(every), row) + (matrix, vector) * 4 + (vector,) * 4
    out_specs = (row, row) + (matrix, vector) * 4 + (vector,) * 4
    return jax.shard_map(
        local_team, mesh=split_mesh, in_specs=in_specs, out_specs=out_specs, check_vma=False
    )
```

```python
from functools import partial
import math

import jax
import jax.numpy as jnp
from jax import lax
from jax.experimental import pallas as pl
from jax.experimental.pallas import tpu as pltpu
from jax.sharding import Mesh, PartitionSpec as P

D = 768
HEADS = 12
HEAD = 64
FF = 3072
ROT = 16
LAYERS = 2


def layer_norm(stream, norm_gain, norm_shift):
    centered = stream - jnp.mean(stream, axis=-1, keepdims=True)
    spread = jnp.mean(centered * centered, axis=-1, keepdims=True)
    return centered * lax.rsqrt(spread + 1e-05) * norm_gain + norm_shift


def both_norms(stream, gain_attn, shift_attn, gain_mlp, shift_mlp):
    return (layer_norm(stream, gain_attn, shift_attn), layer_norm(stream, gain_mlp, shift_mlp))


def angles(positions):
    inverse = 10000.0 ** (-jnp.arange(0, ROT, 2, dtype=jnp.float32) / ROT)
    phases = positions.astype(jnp.float32)[:, None] * inverse[None, :]
    return (jnp.cos(phases)[:, None, :], jnp.sin(phases)[:, None, :])


def rotate(heads_in, cosine_table, sine_table):
    half_rot = cosine_table.shape[-1]
    first_half = heads_in[..., :half_rot]
    second_half = heads_in[..., half_rot : 2 * half_rot]
    untouched = heads_in[..., 2 * half_rot :]
    return jnp.concatenate(
        [
            first_half * cosine_table - second_half * sine_table,
            second_half * cosine_table + first_half * sine_table,
            untouched,
        ],
        axis=-1,
    )


def split_blocks(update, running, key_piece, value_piece, offset):
    piece_rows = key_piece.shape[0]
    block_rows = 512 if piece_rows > 512 and piece_rows % 512 == 0 else piece_rows
    block_count = piece_rows // block_rows
    if block_count == 1:
        return update(running, key_piece, value_piece, offset)

    def advance(state, inputs):
        key_block, value_block, start = inputs
        return (update(state, key_block, value_block, offset + start), None)

    starts = jnp.arange(block_count, dtype=jnp.int32) * block_rows
    state, _ = lax.scan(
        advance,
        running,
        (
            key_piece.reshape(block_count, block_rows, -1),
            value_piece.reshape(block_count, block_rows, -1),
            starts,
        ),
    )
    return state


def stack_layers(per_layer, member):
    return jnp.stack([layer_entry[member] for layer_entry in per_layer])


def flatten_rows(matrix):
    return matrix.reshape(matrix.shape[:-2] + (-1, 128))


def local(
    tokens,
    segment_ids,
    cotangent,
    qkv_weight,
    qkv_bias,
    attn_weight,
    attn_bias,
    up_weight,
    up_bias,
    down_weight,
    down_bias,
    attn_gain,
    attn_shift,
    mlp_gain,
    mlp_shift,
):
    tok_rows = tokens.shape[0]
    group_rows = tok_rows * lax.axis_size("cp")
    score_scale = 1.0 / math.sqrt(HEAD)
    all_segments = lax.all_gather(segment_ids, "cp", axis=0, tiled=True)
    row_index = lax.axis_index("cp") * tok_rows + jnp.arange(tok_rows, dtype=jnp.int32)
    positions = row_index - jnp.sum(
        (all_segments[None, :] < segment_ids[:, None]).astype(jnp.int32), axis=1
    )
    cosine_table, sine_table = angles(positions)

    def visible_mask(offset, block_rows):
        key_index = offset + jnp.arange(block_rows, dtype=jnp.int32)
        key_segment = lax.dynamic_slice_in_dim(all_segments, offset, block_rows)
        return (key_index[None, :] <= row_index[:, None]) & (
            key_segment[None, :] == segment_ids[:, None]
        )

    def online_step(query_heads, running, key_block, value_block, offset):
        row_max, denominator, weighted = running
        block_rows = key_block.shape[0]
        key_heads = key_block.reshape(block_rows, HEADS, HEAD)
        value_heads = value_block.reshape(block_rows, HEADS, HEAD)
        scores = (
            jnp.einsum("qhd,khd->hqk", query_heads, key_heads, preferred_element_type=jnp.float32)
            * score_scale
        )
        visible = visible_mask(offset, block_rows)
        scores = jnp.where(visible[None], scores, -1e30)
        new_max = jnp.maximum(row_max, jnp.max(scores, axis=-1))
        rescale = jnp.exp(row_max - new_max)
        weights = jnp.where(visible[None], jnp.exp(scores - new_max[..., None]), 0.0)
        denominator = denominator * rescale + jnp.sum(weights, axis=-1)
        weighted = weighted * rescale[..., None] + jnp.einsum(
            "hqk,khd->hqd",
            weights.astype(jnp.bfloat16),
            value_heads,
            preferred_element_type=jnp.float32,
        )
        return (new_max, denominator, weighted)

    stream = tokens.astype(jnp.float32)
    stored = []
    for depth in range(LAYERS):
        params = (
            lax.all_gather(qkv_weight[depth], ("dp", "cp"), axis=0, tiled=True),
            lax.all_gather(qkv_bias[depth], ("dp", "cp"), axis=0, tiled=True),
            lax.all_gather(attn_weight[depth], ("dp", "cp"), axis=0, tiled=True),
            lax.all_gather(attn_bias[depth], ("dp", "cp"), axis=0, tiled=True),
            lax.all_gather(up_weight[depth], ("dp", "cp"), axis=0, tiled=True),
            lax.all_gather(up_bias[depth], ("dp", "cp"), axis=0, tiled=True),
            lax.all_gather(down_weight[depth], ("dp", "cp"), axis=0, tiled=True),
            lax.all_gather(down_bias[depth], ("dp", "cp"), axis=0, tiled=True),
            lax.all_gather(attn_gain[depth], ("dp", "cp"), axis=0, tiled=True),
            lax.all_gather(attn_shift[depth], ("dp", "cp"), axis=0, tiled=True),
            lax.all_gather(mlp_gain[depth], ("dp", "cp"), axis=0, tiled=True),
            lax.all_gather(mlp_shift[depth], ("dp", "cp"), axis=0, tiled=True),
        )
        (
            proj_qkv,
            bias_qkv,
            proj_attn,
            bias_attn,
            proj_up,
            bias_up,
            proj_down,
            bias_down,
            gain_attn,
            shift_attn,
            gain_mlp,
            shift_mlp,
        ) = params
        normed_attn, normed_mlp = both_norms(
            stream,
            gain_attn.astype(jnp.float32),
            shift_attn.astype(jnp.float32),
            gain_mlp.astype(jnp.float32),
            shift_mlp.astype(jnp.float32),
        )
        normed_attn = normed_attn.astype(jnp.bfloat16)
        normed_mlp = normed_mlp.astype(jnp.bfloat16)
        projected = jnp.dot(
            normed_attn, proj_qkv, preferred_element_type=jnp.float32
        ) + bias_qkv.astype(jnp.float32)
        queries = rotate(
            projected[:, :D].reshape(tok_rows, HEADS, HEAD), cosine_table, sine_table
        ).astype(jnp.bfloat16)
        key_rows = (
            rotate(projected[:, D : 2 * D].reshape(tok_rows, HEADS, HEAD), cosine_table, sine_table)
            .astype(jnp.bfloat16)
            .reshape(tok_rows, D)
        )
        values = projected[:, 2 * D :].astype(jnp.bfloat16)
        initial = (
            jnp.full((HEADS, tok_rows), -1e30, jnp.float32),
            jnp.zeros((HEADS, tok_rows), jnp.float32),
            jnp.zeros((HEADS, tok_rows, HEAD), jnp.float32),
        )
        row_max, denominator, weighted = split_blocks(
            partial(online_step, queries),
            initial,
            lax.all_gather(key_rows, "cp", axis=0, tiled=True),
            lax.all_gather(values, "cp", axis=0, tiled=True),
            jnp.int32(0),
        )
        attended = jnp.transpose(weighted / denominator[..., None], (1, 0, 2)).reshape(tok_rows, D)
        log_total = row_max + jnp.log(denominator)
        attended_low = attended.astype(jnp.bfloat16)
        attn_branch = jnp.dot(
            attended_low, proj_attn, preferred_element_type=jnp.float32
        ) + bias_attn.astype(jnp.float32)
        hidden_pre = jnp.dot(
            normed_mlp, proj_up, preferred_element_type=jnp.float32
        ) + bias_up.astype(jnp.float32)
        hidden = jax.nn.gelu(hidden_pre, approximate=False).astype(jnp.bfloat16)
        mlp_branch = jnp.dot(
            hidden, proj_down, preferred_element_type=jnp.float32
        ) + bias_down.astype(jnp.float32)
        stored.append(
            (
                stream,
                normed_attn,
                normed_mlp,
                queries,
                key_rows,
                values,
                attended,
                attended_low,
                log_total,
                hidden_pre,
                hidden,
            )
        )
        stream = stream + attn_branch + mlp_branch
    grad_stream = cotangent.astype(jnp.float32)
    per_layer = [None] * LAYERS
    for depth in reversed(range(LAYERS)):
        (
            saved_stream,
            normed_attn,
            normed_mlp,
            queries,
            key_rows,
            values,
            attended,
            attended_low,
            log_total,
            hidden_pre,
            hidden,
        ) = stored[depth]
        params = (
            lax.all_gather(qkv_weight[depth], ("dp", "cp"), axis=0, tiled=True),
            lax.all_gather(qkv_bias[depth], ("dp", "cp"), axis=0, tiled=True),
            lax.all_gather(attn_weight[depth], ("dp", "cp"), axis=0, tiled=True),
            lax.all_gather(attn_bias[depth], ("dp", "cp"), axis=0, tiled=True),
            lax.all_gather(up_weight[depth], ("dp", "cp"), axis=0, tiled=True),
            lax.all_gather(up_bias[depth], ("dp", "cp"), axis=0, tiled=True),
            lax.all_gather(down_weight[depth], ("dp", "cp"), axis=0, tiled=True),
            lax.all_gather(down_bias[depth], ("dp", "cp"), axis=0, tiled=True),
            lax.all_gather(attn_gain[depth], ("dp", "cp"), axis=0, tiled=True),
            lax.all_gather(attn_shift[depth], ("dp", "cp"), axis=0, tiled=True),
            lax.all_gather(mlp_gain[depth], ("dp", "cp"), axis=0, tiled=True),
            lax.all_gather(mlp_shift[depth], ("dp", "cp"), axis=0, tiled=True),
        )
        (
            proj_qkv,
            bias_qkv,
            proj_attn,
            bias_attn,
            proj_up,
            bias_up,
            proj_down,
            bias_down,
            gain_attn,
            shift_attn,
            gain_mlp,
            shift_mlp,
        ) = params
        grad_low = grad_stream.astype(jnp.bfloat16)
        bias_grad = jnp.sum(grad_low.astype(jnp.float32), axis=0)
        attn_weight_grad = jnp.einsum(
            "td,te->de", attended_low, grad_low, preferred_element_type=jnp.float32
        )
        down_weight_grad = jnp.einsum(
            "tf,te->fe", hidden, grad_low, preferred_element_type=jnp.float32
        )
        grad_attended = jnp.einsum(
            "te,de->td", grad_low, proj_attn, preferred_element_type=jnp.float32
        ).astype(jnp.bfloat16)
        grad_hidden = jnp.einsum(
            "te,fe->tf", grad_low, proj_down, preferred_element_type=jnp.float32
        )
        _, gelu_pull = jax.vjp(partial(jax.nn.gelu, approximate=False), hidden_pre)
        grad_pre = gelu_pull(grad_hidden)[0].astype(jnp.bfloat16)
        up_weight_grad = jnp.einsum(
            "td,tf->df", normed_mlp, grad_pre, preferred_element_type=jnp.float32
        )
        up_bias_grad = jnp.sum(grad_pre.astype(jnp.float32), axis=0)
        grad_normed_mlp = jnp.einsum(
            "tf,df->td", grad_pre, proj_up, preferred_element_type=jnp.float32
        )
        all_keys, all_values = (
            lax.all_gather(key_rows, "cp", axis=0, tiled=True),
            lax.all_gather(values, "cp", axis=0, tiled=True),
        )
        grad_heads = grad_attended.reshape(tok_rows, HEADS, HEAD)
        row_dot = jnp.transpose(
            jnp.sum(
                grad_heads.astype(jnp.float32) * attended.reshape(tok_rows, HEADS, HEAD), axis=-1
            )
        )
        block_rows = 512 if group_rows > 512 and group_rows % 512 == 0 else group_rows
        block_count = group_rows // block_rows
        starts = jnp.arange(block_count, dtype=jnp.int32) * block_rows

        def back_step(grad_query, inputs):
            key_block, value_block, offset = inputs
            key_heads = key_block.reshape(block_rows, HEADS, HEAD)
            value_heads = value_block.reshape(block_rows, HEADS, HEAD)
            scores = (
                jnp.einsum("qhd,khd->hqk", queries, key_heads, preferred_element_type=jnp.float32)
                * score_scale
            )
            visible = visible_mask(offset, block_rows)
            weights = jnp.where(visible[None], jnp.exp(scores - log_total[..., None]), 0.0)
            grad_weights = jnp.einsum(
                "qhd,khd->hqk", grad_heads, value_heads, preferred_element_type=jnp.float32
            )
            grad_scores = (weights * (grad_weights - row_dot[..., None])).astype(jnp.bfloat16)
            grad_query = grad_query + jnp.einsum(
                "hqk,khd->hqd", grad_scores, key_heads, preferred_element_type=jnp.float32
            )
            key_grad = (
                jnp.einsum("hqk,qhd->khd", grad_scores, queries, preferred_element_type=jnp.float32)
                * score_scale
            )
            value_grad = jnp.einsum(
                "hqk,qhd->khd",
                weights.astype(jnp.bfloat16),
                grad_heads,
                preferred_element_type=jnp.float32,
            )
            return (
                grad_query,
                (key_grad.reshape(block_rows, D), value_grad.reshape(block_rows, D)),
            )

        grad_query, (key_grads, value_grads) = lax.scan(
            back_step,
            jnp.zeros((HEADS, tok_rows, HEAD), jnp.float32),
            (
                all_keys.reshape(block_count, block_rows, D),
                all_values.reshape(block_count, block_rows, D),
                starts,
            ),
        )
        local_key_grad, local_value_grad = (
            lax.psum_scatter(
                key_grads.reshape(group_rows, D).astype(jnp.bfloat16),
                "cp",
                scatter_dimension=0,
                tiled=True,
            ).astype(jnp.float32),
            lax.psum_scatter(
                value_grads.reshape(group_rows, D).astype(jnp.bfloat16),
                "cp",
                scatter_dimension=0,
                tiled=True,
            ).astype(jnp.float32),
        )
        query_raw = rotate(
            jnp.transpose(grad_query * score_scale, (1, 0, 2)), cosine_table, -sine_table
        )
        key_raw = rotate(local_key_grad.reshape(tok_rows, HEADS, HEAD), cosine_table, -sine_table)
        grad_projected = jnp.concatenate(
            [query_raw.reshape(tok_rows, D), key_raw.reshape(tok_rows, D), local_value_grad], axis=1
        ).astype(jnp.bfloat16)
        qkv_weight_grad = jnp.einsum(
            "td,te->de", normed_attn, grad_projected, preferred_element_type=jnp.float32
        )
        qkv_bias_grad = jnp.sum(grad_projected.astype(jnp.float32), axis=0)
        grad_normed_attn = jnp.einsum(
            "te,de->td", grad_projected, proj_qkv, preferred_element_type=jnp.float32
        )
        _, norm_pull = jax.vjp(
            both_norms,
            saved_stream,
            gain_attn.astype(jnp.float32),
            shift_attn.astype(jnp.float32),
            gain_mlp.astype(jnp.float32),
            shift_mlp.astype(jnp.float32),
        )
        grad_input, attn_gain_grad, attn_shift_grad, mlp_gain_grad, mlp_shift_grad = norm_pull(
            (grad_normed_attn, grad_normed_mlp)
        )
        grad_stream = grad_stream + grad_input
        summed = (
            lax.psum_scatter(
                flatten_rows(qkv_weight_grad), ("dp", "cp"), scatter_dimension=0, tiled=True
            ),
            lax.psum_scatter(qkv_bias_grad, ("dp", "cp"), scatter_dimension=0, tiled=True),
            lax.psum_scatter(
                flatten_rows(attn_weight_grad), ("dp", "cp"), scatter_dimension=0, tiled=True
            ),
            lax.psum_scatter(bias_grad, ("dp", "cp"), scatter_dimension=0, tiled=True),
            lax.psum_scatter(
                flatten_rows(up_weight_grad), ("dp", "cp"), scatter_dimension=0, tiled=True
            ),
            lax.psum_scatter(up_bias_grad, ("dp", "cp"), scatter_dimension=0, tiled=True),
            lax.psum_scatter(
                flatten_rows(down_weight_grad), ("dp", "cp"), scatter_dimension=0, tiled=True
            ),
            lax.psum_scatter(bias_grad, ("dp", "cp"), scatter_dimension=0, tiled=True),
            lax.psum_scatter(attn_gain_grad, ("dp", "cp"), scatter_dimension=0, tiled=True),
            lax.psum_scatter(attn_shift_grad, ("dp", "cp"), scatter_dimension=0, tiled=True),
            lax.psum_scatter(mlp_gain_grad, ("dp", "cp"), scatter_dimension=0, tiled=True),
            lax.psum_scatter(mlp_shift_grad, ("dp", "cp"), scatter_dimension=0, tiled=True),
        )
        per_layer[depth] = (
            summed[0].reshape(-1, 3 * D),
            summed[1],
            summed[2].reshape(-1, D),
            summed[3],
            summed[4].reshape(-1, FF),
            summed[5],
            summed[6].reshape(-1, D),
            summed[7],
            summed[8],
            summed[9],
            summed[10],
            summed[11],
        )
    stacked = [stack_layers(per_layer, member) for member in range(12)]
    return (
        stream.astype(jnp.bfloat16),
        grad_stream,
        stacked[0],
        stacked[1],
        stacked[2],
        stacked[3],
        stacked[4],
        stacked[5],
        stacked[6],
        stacked[7],
        stacked[8],
        stacked[9],
        stacked[10],
        stacked[11],
    )


TEAM = 4
TEAM_AXES = ("core", "x")
LINE_AXES = ("z", "y")
LINE = 4
MINE = (3 * D) // TEAM
HCOLS = D // TEAM
UCOLS = FF // TEAM
VMEM_BYTES = 56 * 1024 * 1024
BF = jnp.bfloat16
F32 = jnp.float32


def call(body, out_shape, name, operands, scratch=()):
    return pl.pallas_call(
        body,
        out_shape=out_shape,
        scratch_shapes=list(scratch),
        compiler_params=pltpu.CompilerParams(vmem_limit_bytes=VMEM_BYTES),
        name=name,
    )(*operands)


def shape(dims, kind):
    return jax.ShapeDtypeStruct(dims, kind)


def mm(left, right):
    return jnp.dot(left, right, preferred_element_type=F32)


def mm_t(left, right):
    return lax.dot_general(left, right, (((1,), (1,)), ((), ())), preferred_element_type=F32)


def t_mm(left, right):
    return lax.dot_general(left, right, (((0,), (0,)), ((), ())), preferred_element_type=F32)


def pick(member, pieces, wanted):
    chosen = pieces[0]
    for s in range(1, TEAM):
        chosen = jnp.where((member ^ s) == wanted, pieces[s], chosen)
    return chosen


def small_rows(vectors, depth):
    rows = []
    for vector in vectors:
        values = vector[depth : depth + 1].astype(F32)
        rows.append(
            jnp.concatenate([values, jnp.zeros((1, 128 - values.shape[1]), F32)], axis=1)
        )
    return jnp.concatenate(rows, axis=0)


def pack_body(me_ref, qkv_ref, up_ref, *refs):
    vectors, outs = [r[...] for r in refs[:8]], refs[8:]
    me = me_ref[0]
    small = jnp.concatenate([small_rows(vectors, depth) for depth in range(LAYERS)], axis=0)
    small = jnp.concatenate([small, jnp.zeros((small.shape[0], UCOLS - 128), F32)], axis=1)
    for depth in range(LAYERS):
        rows = qkv_ref.shape[1]
        qkv = qkv_ref[depth].astype(F32)
        up = up_ref[depth].astype(F32)
        blocks = up.shape[1] // (TEAM * 96)
        parts = []
        for p in range(TEAM):
            up_p = jnp.concatenate(
                [up[:, 96 * (TEAM * b + p) : 96 * (TEAM * b + p + 1)] for b in range(blocks)], axis=1
            )
            qkv_p = jnp.concatenate(
                [qkv[:, D * t + HCOLS * p : D * t + HCOLS * (p + 1)] for t in range(3)]
                + [jnp.zeros((rows, UCOLS - MINE), F32)],
                axis=1,
            )
            parts.append(jnp.concatenate([up_p, qkv_p], axis=0))
        for s in range(TEAM):
            dest = me ^ s
            chosen = parts[0]
            for p in range(1, TEAM):
                chosen = jnp.where(dest == p, parts[p], chosen)
            if depth == 0:
                chosen = jnp.concatenate([chosen, small], axis=0)
            outs[depth * TEAM + s][...] = chosen.astype(BF)


def assemble_body(me_ref, p0, p1, p2, p3, attn_ref, down_ref, a_ref, m_ref):
    me = me_ref[0]
    slots = [r[...].astype(F32) for r in (p0, p1, p2, p3)]
    ordered = [pick(me, slots, p) for p in range(TEAM)]
    up = jnp.concatenate([piece[0:24] for piece in ordered], axis=0)
    qkv = jnp.concatenate([piece[24:48] for piece in ordered], axis=0)
    attn = attn_ref[...].astype(F32)
    side = jnp.concatenate([attn[:, HCOLS * n : HCOLS * (n + 1)] for n in range(4)], axis=0)
    a_ref[0:96] = jnp.concatenate([qkv[:, :MINE], side], axis=1).astype(BF)
    if a_ref.shape[0] > 96:
        small = jnp.concatenate(
            [piece[48:64, :128] for piece in ordered] + [jnp.zeros((16, D - 4 * 128), F32)], axis=1
        )
        a_ref[96:112] = small.astype(BF)
    m_ref[0:96] = up.astype(BF)
    m_ref[96:192] = down_ref[...]


def source_team(me_ref, index):
    shift, flip = index % LINE, index // LINE
    return 2 * lax.rem(me_ref[1] + LINE - shift, LINE) + (me_ref[2] ^ flip)


def target_team(me_ref, index):
    shift, flip = index % LINE, index // LINE
    return 2 * lax.rem(me_ref[1] + shift, LINE) + (me_ref[2] ^ flip)


def place(me_ref, pieces, whole):
    for index, piece in enumerate(pieces):
        whole[source_team(me_ref, index)] = piece[...]


def hand_out(me_ref, whole, pieces):
    for index, piece in enumerate(pieces):
        piece[...] = whole[target_team(me_ref, index)]


def layer_vectors(me_ref, whole, depth):
    me = me_ref[0]
    small = [whole[k, 96:112, :].astype(F32) for k in range(2 * LINE)]
    fields = [block[8 * depth : 8 * (depth + 1)] for block in small]
    shared = jnp.concatenate(
        [block[2:8, 128 * p : 128 * p + 24] for block in fields for p in range(TEAM)], axis=1
    )
    up_rows, qkv_rows = [], []
    qkv = jnp.concatenate(
        [block[0:1, 128 * p : 128 * p + 72] for block in fields for p in range(TEAM)], axis=1
    )
    for p in range(TEAM):
        up_rows.append(
            jnp.concatenate([block[1:2, 128 * p : 128 * p + 96] for block in fields], axis=1)
        )
        qkv_rows.append(
            jnp.concatenate(
                [qkv[:, D * t + HCOLS * p : D * t + HCOLS * (p + 1)] for t in range(3)]
                + [jnp.zeros((1, D - MINE), F32)],
                axis=1,
            )
        )
    up_mine, qkv_mine = up_rows[0], qkv_rows[0]
    for p in range(1, TEAM):
        up_mine = jnp.where(me == p, up_rows[p], up_mine)
        qkv_mine = jnp.where(me == p, qkv_rows[p], qkv_mine)
    return jnp.concatenate([shared, up_mine, qkv_mine], axis=0)


def attn_weights(whole):
    qkv = whole[:, 0:96, :][:, :, :MINE].reshape(D, MINE)
    side = whole[:, 0:96, MINE:].astype(F32)
    out = jnp.concatenate(
        [side[:, 24 * n : 24 * (n + 1), :].reshape(HCOLS, HCOLS) for n in range(4)], axis=1
    )
    return qkv, out.astype(BF)


def project(scaled, vec, weight, cosine, sine):
    normed = (scaled * vec[0:1] + vec[1:2]).astype(BF)
    projected = mm(normed, weight) + vec[7:8, :MINE]
    turned = turn(projected[:, : 2 * HCOLS], cosine, sine)
    queries = (turned[:, :HCOLS] * 0.125).astype(BF)
    keys = turned[:, HCOLS:].astype(BF)
    values = projected[:, 2 * HCOLS :].astype(BF)
    return normed, queries, keys, values


def attend_body(me_ref, x0, x1, x2, x3, *refs):
    pieces, (cos_ref, sin_ref, mask_ref, y_ref, vec_ref, whole) = refs[:8], refs[8:]
    place(me_ref, pieces, whole)
    for depth in range(LAYERS):
        vec_ref[depth] = layer_vectors(me_ref, whole, depth)
    vec = vec_ref[0]
    weight, out_weight = attn_weights(whole)
    for g, (first, second) in enumerate(((x0, x1), (x2, x3))):
        rows = pl.ds(PAIR * g, PAIR)
        scaled, _ = norm_parts(two_slots(first[...], second[...]))
        _, queries, keys, values = project(scaled, vec, weight, cos_ref[rows, :], sin_ref[rows, :])
        total = jnp.zeros((PAIR, HCOLS), F32)
        for head in range(HEADS // TEAM):
            owned = head_mask(PAIR, head)
            scores = mm_t(jnp.where(owned, queries, jnp.zeros_like(queries)), keys) + mask_ref[g]
            weights = jnp.exp(scores - jnp.max(scores, axis=-1, keepdims=True))
            below = jnp.sum(weights, axis=-1, keepdims=True)
            total = total + jnp.where(owned, mm(weights.astype(BF), values) / below, 0.0)
        y_ref[rows, :] = mm(total.astype(BF), out_weight)


def mlp_body(me_ref, x0, x1, x2, x3, *refs):
    pieces, (vec_ref, a_ref, y0, y1, y2, y3, whole) = refs[:8], refs[8:]
    place(me_ref, pieces, whole)
    vec = vec_ref[0]
    up = whole[:, 0:96, :].reshape(D, UCOLS)
    down = whole[:, 96:192, :].reshape(UCOLS, D)
    for g, (first, second, y_first, y_second) in enumerate(((x0, x1, y0, y1), (x2, x3, y2, y3))):
        rows = pl.ds(PAIR * g, PAIR)
        scaled, _ = norm_parts(two_slots(first[...], second[...]))
        normed = (scaled * vec[2:3] + vec[3:4]).astype(BF)
        before = mm(normed, up) + vec[6:7]
        hidden = (before * (0.5 * (1.0 + lax.erf(before * (1.0 / math.sqrt(2.0)))))).astype(BF)
        result = mm(hidden, down) + a_ref[rows, :]
        y_first[...] = result[0:TOK].astype(y_first.dtype)
        y_second[...] = result[TOK:].astype(y_second.dtype)


def mlp_both_body(depth, last, me_ref, x0, x1, x2, x3, g0, g1, g2, g3, *refs):
    pieces, vec_ref, blocks = refs[:8], refs[8], refs[9:17]
    dn_ref, sum_ref = refs[17:19]
    whole, grads, c_s, hid_s, du_s, gb_s = refs[-6:]
    place(me_ref, pieces, whole)
    vec = vec_ref[depth]
    up = whole[:, 0:96, :].reshape(D, UCOLS)
    down = whole[:, 96:192, :].reshape(UCOLS, D)
    gain_sum = jnp.zeros((1, D), F32)
    shift_sum = jnp.zeros((1, D), F32)
    bias_sum = jnp.zeros((1, D), F32)
    up_sum = jnp.zeros((1, UCOLS), F32)
    for g, (first, second, g_first, g_second) in enumerate(((x0, x1, g0, g1), (x2, x3, g2, g3))):
        rows = pl.ds(PAIR * g, PAIR)
        scaled, _ = norm_parts(two_slots(first[...], second[...]))
        normed = (scaled * vec[2:3] + vec[3:4]).astype(BF)
        c_s[rows, :] = normed
        low = jnp.concatenate([g_first[...], g_second[...]], axis=0)
        gb_s[rows, :] = low
        hidden, slope = gelu_parts(mm(normed, up) + vec[6:7])
        hidden = hidden.astype(BF)
        hid_s[rows, :] = hidden
        if last:
            refs[19][rows, :] = mm(hidden, down)
        du = (mm_t(low, down) * slope).astype(BF)
        du_s[rows, :] = du
        dc = mm_t(du, up)
        dn_ref[rows, :] = dc * vec[2:3]
        gain_sum = gain_sum + jnp.sum(dc * scaled, axis=0, keepdims=True)
        shift_sum = shift_sum + jnp.sum(dc, axis=0, keepdims=True)
        bias_sum = bias_sum + jnp.sum(low.astype(F32), axis=0, keepdims=True)
        up_sum = up_sum + jnp.sum(du.astype(F32), axis=0, keepdims=True)
    grads[:, 0:96, :] = t_mm(c_s[...], du_s[...]).reshape(-1, 96, UCOLS).astype(BF)
    grads[:, 96:192, :] = t_mm(hid_s[...], gb_s[...]).reshape(-1, 96, D).astype(BF)
    hand_out(me_ref, grads, blocks)
    sum_ref[...] = jnp.concatenate(
        [bias_sum, up_sum, gain_sum, shift_sum, jnp.zeros((4, D), F32)], axis=0
    )


def attend_both_body(depth, last, me_ref, x0, x1, x2, x3, g0, g1, g2, g3, *refs):
    pieces, (vec_ref, cos_ref, sin_ref, mask_ref, dn_ref) = refs[:8], refs[8:13]
    refs = refs[13:]
    if last:
        y_ref, refs = refs[0], refs[1:]
    blocks, (sum_ref, n0, n1, n2, n3) = refs[:8], refs[8:13]
    whole, grads, a_s, dp_s, o_s, gb_s = refs[-6:]
    place(me_ref, pieces, whole)
    vec = vec_ref[depth]
    weight, out_weight = attn_weights(whole)
    gain_sum = jnp.zeros((1, D), F32)
    shift_sum = jnp.zeros((1, D), F32)
    bias_sum = jnp.zeros((1, MINE), F32)
    for g, (first, second, g_first, g_second, n_first, n_second) in enumerate(
        ((x0, x1, g0, g1, n0, n1), (x2, x3, g2, g3, n2, n3))
    ):
        rows = pl.ds(PAIR * g, PAIR)
        cosine, sine = cos_ref[rows, :], sin_ref[rows, :]
        scaled, _ = norm_parts(two_slots(first[...], second[...]))
        normed, queries, keys, values = project(scaled, vec, weight, cosine, sine)
        a_s[rows, :] = normed
        low = jnp.concatenate([g_first[...], g_second[...]], axis=0)
        gb_s[rows, :] = low
        grad_o = mm_t(low, out_weight).astype(BF)
        zero = jnp.zeros_like(queries)
        out = jnp.zeros((PAIR, HCOLS), F32)
        dq = jnp.zeros((PAIR, HCOLS), F32)
        dk = jnp.zeros((PAIR, HCOLS), F32)
        dv = jnp.zeros((PAIR, HCOLS), F32)
        for head in range(HEADS // TEAM):
            owned = head_mask(PAIR, head)
            scores = mm_t(jnp.where(owned, queries, zero), keys) + mask_ref[g]
            weights = jnp.exp(scores - jnp.max(scores, axis=-1, keepdims=True))
            weights = weights / jnp.sum(weights, axis=-1, keepdims=True)
            rounded = weights.astype(BF)
            dweights = mm_t(jnp.where(owned, grad_o, zero), values)
            delta = jnp.sum(weights * dweights, axis=-1, keepdims=True)
            dscores = (weights * (dweights - delta)).astype(BF)
            out = out + jnp.where(owned, mm(rounded, values), 0.0)
            dq = dq + jnp.where(owned, mm(dscores, keys), 0.0)
            dk = dk + jnp.where(owned, t_mm(dscores, queries), 0.0)
            dv = dv + jnp.where(owned, t_mm(rounded, grad_o), 0.0)
        o_s[rows, :] = out.astype(BF)
        both = turn(jnp.concatenate([dq * 0.125, dk], axis=1), cosine, -sine)
        dproj = jnp.concatenate([both, dv], axis=1).astype(BF)
        dp_s[rows, :] = dproj
        bias_sum = bias_sum + jnp.sum(dproj.astype(F32), axis=0, keepdims=True)
        da = mm_t(dproj, weight)
        gain_sum = gain_sum + jnp.sum(da * scaled, axis=0, keepdims=True)
        shift_sum = shift_sum + jnp.sum(da, axis=0, keepdims=True)
        dn = dn_ref[rows, :] + da * vec[0:1]
        n_first[...] = dn[0:TOK].astype(n_first.dtype)
        n_second[...] = dn[TOK:].astype(n_second.dtype)
        if last:
            result = y_ref[rows, :] + mm(out.astype(BF), out_weight)
            y_first, y_second = refs[13 + 2 * g], refs[14 + 2 * g]
            y_first[...] = result[0:TOK].astype(y_first.dtype)
            y_second[...] = result[TOK:].astype(y_second.dtype)
    qkv_grad = t_mm(a_s[...], dp_s[...]).reshape(-1, 96, MINE)
    out_grad = t_mm(o_s[...], gb_s[...])
    side = jnp.concatenate(
        [out_grad[:, HCOLS * n : HCOLS * (n + 1)].reshape(-1, 24, HCOLS) for n in range(4)], axis=1
    )
    grads[...] = jnp.concatenate([qkv_grad, side], axis=2).astype(BF)
    hand_out(me_ref, grads, blocks)
    bias_row = jnp.concatenate([bias_sum, jnp.zeros((1, D - MINE), F32)], axis=1)
    sum_ref[...] = jnp.concatenate([gain_sum, shift_sum, bias_row, jnp.zeros((5, D), F32)], axis=0)


def residual_body(x_ref, y0, y1, y2, y3, vec_ref, out_ref, low_ref):
    depth = 0 if x_ref.dtype == BF else 1
    total = y0[...] + y1[...].astype(F32) + y2[...].astype(F32) + y3[...].astype(F32)
    result = x_ref[...].astype(F32) + total + (vec_ref[depth, 4:5] + vec_ref[depth, 5:6])
    out_ref[...] = result
    low_ref[...] = result.astype(BF)

def norm_parts(stream):
    centered = stream - jnp.mean(stream, axis=-1, keepdims=True)
    spread = jnp.mean(centered * centered, axis=-1, keepdims=True)
    inverse = lax.rsqrt(spread + 1e-05)
    return centered * inverse, inverse


def two_slots(first, second):
    return jnp.concatenate([first[0:TOK].astype(F32), second[0:TOK].astype(F32)], axis=0)


TOK = 128
PAIR = 2 * TOK


def turn(block, cosine, sine):
    lane = lax.broadcasted_iota(jnp.int32, (block.shape[0], 128), 1) % HEAD
    tiles = []
    for t in range(block.shape[1] // 128):
        tile = block[:, 128 * t : 128 * (t + 1)]
        swapped = jnp.where(
            lane < ROT // 2, pltpu.roll(tile, 128 - ROT // 2, 1), pltpu.roll(tile, ROT // 2, 1)
        )
        tiles.append(tile * cosine + swapped * sine)
    return jnp.concatenate(tiles, axis=1)


def head_mask(rows, head):
    lane = lax.broadcasted_iota(jnp.int32, (rows, HCOLS), 1)
    return (lane >= head * HEAD) & (lane < (head + 1) * HEAD)


def gelu_parts(u):
    cdf = 0.5 * (1.0 + lax.erf(u * (1.0 / math.sqrt(2.0))))
    density = jnp.exp(-0.5 * u * u) * (1.0 / math.sqrt(2.0 * math.pi))
    return u * cdf, cdf + u * density


def norm_back_body(x_ref, g_ref, n0, n1, n2, n3, out_ref, low_ref):
    scaled, inverse = norm_parts(x_ref[...].astype(F32))
    dn = n0[...] + n1[...].astype(F32) + n2[...].astype(F32) + n3[...].astype(F32)
    centered = dn - jnp.mean(dn, axis=-1, keepdims=True)
    moment = jnp.mean(dn * scaled, axis=-1, keepdims=True)
    result = g_ref[...].astype(F32) + inverse * (centered - scaled * moment)
    out_ref[...] = result
    low_ref[...] = result.astype(BF)


def split_body(me_ref, m0, m1, m2, m3, m4, a0, a1, a2, a3, a4, o0, o1, o2, o3, down_ref, attn_ref):
    me = me_ref[0]

    def total(refs):
        result = refs[0][...].astype(F32)
        for ref in refs[1:]:
            result = result + ref[...].astype(F32)
        return result

    mlp, attn = total((m0, m1, m2, m3, m4)), total((a0, a1, a2, a3, a4))
    up = mlp[0:96]
    down_ref[...] = mlp[96:192]
    side = attn[:, MINE:]
    attn_ref[...] = jnp.concatenate(
        [side[24 * n : 24 * (n + 1)] for n in range(4)], axis=1
    ).astype(BF)
    qkv = jnp.concatenate([attn[:, :MINE], jnp.zeros((96, UCOLS - MINE), F32)], axis=1)
    for s, out in enumerate((o0, o1, o2, o3)):
        dest = me ^ s
        piece = jnp.concatenate([up[0:24], qkv[0:24]], axis=0)
        for p in range(1, TEAM):
            rows = slice(24 * p, 24 * (p + 1))
            piece = jnp.where(dest == p, jnp.concatenate([up[rows], qkv[rows]], axis=0), piece)
        out[...] = piece.astype(BF)


def unpack_body(me_ref, *refs):
    me = me_ref[0]
    qkv_ref, up_ref = refs[-2:]
    for depth in range(LAYERS):
        slots = [refs[depth * TEAM + s][...].astype(F32) for s in range(TEAM)]
        ordered = [pick(me, slots, p) for p in range(TEAM)]
        blocks = FF // (96 * TEAM)
        up_ref[depth] = jnp.concatenate(
            [ordered[p][0:24, 96 * b : 96 * (b + 1)] for b in range(blocks) for p in range(TEAM)],
            axis=1,
        )
        qkv_ref[depth] = jnp.concatenate(
            [
                ordered[p][24:48, HCOLS * t : HCOLS * (t + 1)]
                for t in range(3)
                for p in range(TEAM)
            ],
            axis=1,
        )


def team_send(piece, slot):
    flips = [(m, m ^ slot) for m in range(TEAM)]
    return lax.ppermute(piece, TEAM_AXES, flips)


def line_shift(piece, shift):
    size = lax.axis_size("z")
    return lax.ppermute(piece, "z", [(i, (i + shift) % size) for i in range(size)])


def line_flip(piece):
    return lax.ppermute(piece, "y", [(0, 1), (1, 0)])


def line_gather(piece):
    near = [piece] + [line_shift(piece, s) for s in range(1, LINE)]
    return near + [line_flip(p) for p in near]


def line_scatter(blocks):
    sums = [None] * LINE
    for s in list(range(1, LINE)) + [0]:
        other = line_flip(blocks[LINE + s])
        if s == 0:
            sums[0] = [blocks[0], other]
        else:
            both = (blocks[s].astype(F32) + other.astype(F32)).astype(BF)
            sums[s] = [line_shift(both, s)]
    return [array for group in sums for array in group]


def local_team(
    tokens, segment_ids, cotangent, qkv_weight, qkv_bias, attn_weight, attn_bias,
    up_weight, up_bias, down_weight, down_bias, attn_gain, attn_shift, mlp_gain, mlp_shift,
):
    lines = lax.axis_size("z") * lax.axis_size("y")
    world = lines * TEAM
    team = lax.axis_index("z") * lax.axis_size("y") + lax.axis_index("y")
    member = lax.axis_index("core") * 2 + lax.axis_index("x")
    me = jnp.stack([member, lax.axis_index("z"), lax.axis_index("y")]).astype(jnp.int32)
    everywhere = LINE_AXES + TEAM_AXES
    tok_all = TEAM * TOK

    def run(body, out_shape, name, operands, scratch=()):
        return pl.pallas_call(
            body,
            out_shape=out_shape,
            in_specs=[pl.BlockSpec(memory_space=pltpu.SMEM)]
            + [pl.BlockSpec(memory_space=pltpu.VMEM)] * len(operands),
            scratch_shapes=[pltpu.VMEM(dims, kind) for dims, kind in scratch],
            compiler_params=pltpu.CompilerParams(vmem_limit_bytes=VMEM_BYTES),
            name=name,
        )(me, *operands)

    small = (
        qkv_bias, up_bias, attn_gain, attn_shift, mlp_gain, mlp_shift, attn_bias, down_bias
    )
    packed = run(
        pack_body,
        [shape((64, UCOLS), BF)] * TEAM + [shape((48, UCOLS), BF)] * TEAM,
        "pack_weights",
        (qkv_weight, up_weight, *small),
    )
    spread = [(i, TEAM * (i % lines) + i // lines) for i in range(world)]
    gather_back = [(b, a) for a, b in spread]
    attn_piece = lax.ppermute(attn_weight, everywhere, spread)

    parts = []
    for depth in range(LAYERS):
        mine = packed[depth * TEAM : (depth + 1) * TEAM]
        pieces = [mine[0]] + [team_send(mine[s], s) for s in range(1, TEAM)]
        parts.append(
            run(
                assemble_body,
                [shape((112 if depth == 0 else 96, D), BF), shape((192, D), BF)],
                "assemble_weights",
                (*pieces, attn_piece[depth], down_weight[depth]),
            )
        )
    a_pieces, m_pieces = [None] * LAYERS, [None] * LAYERS
    a_pieces[0] = line_gather(parts[0][0])
    m_pieces[0] = line_gather(parts[0][1])
    m_pieces[1] = line_gather(parts[1][1])
    a_pieces[1] = line_gather(parts[1][0])

    token_slots = [tokens] + [team_send(tokens, s) for s in range(1, TEAM)]
    segment_slots = [segment_ids] + [team_send(segment_ids, s) for s in range(1, TEAM)]
    low_cotangent = [cotangent] + [team_send(cotangent, s) for s in range(1, TEAM)]
    here = lax.axis_index("x")
    rows = jnp.arange(TOK, dtype=jnp.int32)
    places = jnp.concatenate([here * TOK + rows, (1 - here) * TOK + rows])
    masks, cosines, sines = [], [], []
    lane = jnp.arange(128, dtype=jnp.int32) % HEAD
    inverse = 10000.0 ** (-(lane % (ROT // 2) * 2).astype(F32) / ROT)
    for g in range(2):
        ids = jnp.concatenate(segment_slots[2 * g : 2 * g + 2])
        visible = (places[None, :] <= places[:, None]) & (ids[None, :] == ids[:, None])
        masks.append(jnp.where(visible, 0.0, -1e30).astype(F32))
        position = places - jnp.sum((ids[None, :] < ids[:, None]).astype(jnp.int32), axis=1)
        phases = position.astype(F32)[:, None] * inverse[None, :]
        cosines.append(jnp.where(lane[None, :] < ROT, jnp.cos(phases), 1.0))
        sign = jnp.where(lane < ROT // 2, -1.0, jnp.where(lane < ROT, 1.0, 0.0))
        sines.append(jnp.sin(phases) * sign[None, :])
    mask = jnp.stack(masks)
    cosine, sine = jnp.concatenate(cosines), jnp.concatenate(sines)

    block_a, block_m = shape((96, D), BF), shape((192, D), BF)
    four = [shape((TOK, D), F32)] + [shape((TOK, D), BF)] * 3
    stream_pair = [shape((TOK, D), F32), shape((TOK, D), BF)]
    wide = ((tok_all, D), BF)

    def exchange(blocks):
        return [blocks[0]] + [team_send(blocks[s], s) for s in range(1, TEAM)]

    attn_out, vec = run(
        attend_body,
        [shape((tok_all, D), F32), shape((LAYERS, 8, D), F32)],
        "attend_forward",
        (*token_slots, *a_pieces[0], cosine, sine, mask),
        [((lines, 112, D), BF)],
    )
    y = run(
        mlp_body,
        four,
        "mlp_forward",
        (*token_slots, *m_pieces[0], vec, attn_out),
        [((lines, 192, D), BF)],
    )

    def residual(stream, blocks):
        return call(residual_body, stream_pair, "residual", (stream, *exchange(blocks), vec))

    stream, low = residual(tokens, y)
    streams = [tokens, stream]
    slots = [token_slots, [low] + [team_send(low, s) for s in range(1, TEAM)]]

    grad = cotangent
    grad_slots = low_cotangent
    outs, sums = [None] * LAYERS, [None] * LAYERS
    activations = None
    for depth in reversed(range(LAYERS)):
        last = depth == LAYERS - 1
        result = run(
            partial(mlp_both_body, depth, last),
            [block_m] * 8
            + [shape((tok_all, D), F32), shape((8, D), F32)]
            + ([shape((tok_all, D), F32)] if last else []),
            "mlp_both",
            (*slots[depth], *grad_slots, *m_pieces[depth], vec),
            [((lines, 192, D), BF), ((lines, 192, D), BF), wide, wide, wide, wide],
        )
        m_sum = line_scatter(result[:8])
        dn, sum_m = result[8:10]
        result = run(
            partial(attend_both_body, depth, last),
            [block_a] * 8 + [shape((8, D), F32)] + four + (four if last else []),
            "attend_both",
            (*slots[depth], *grad_slots, *a_pieces[depth], vec, cosine, sine, mask, dn)
            + tuple(result[10:]),
            [
                ((lines, 112 if depth == 0 else 96, D), BF),
                ((lines, 96, D), BF),
                wide,
                ((tok_all, MINE), BF),
                ((tok_all, HCOLS), BF),
                wide,
            ],
        )
        a_sum = line_scatter(result[:8])
        sum_q = result[8]
        grad, low = call(
            norm_back_body,
            stream_pair,
            "norm_backward",
            (streams[depth], grad, *exchange(result[9:13])),
        )
        if depth > 0:
            grad_slots = [low] + [team_send(low, s) for s in range(1, TEAM)]
        if last:
            _, activations = residual(streams[depth], result[13:])
        mine = run(
            split_body,
            [shape((48, UCOLS), BF)] * TEAM + [shape((96, D), F32), shape((24, D), BF)],
            "split_gradients",
            (*m_sum, *a_sum),
        )
        outs[depth] = (exchange(mine[:TEAM]), mine[TEAM], mine[TEAM + 1])
        qkv_full = lax.dynamic_update_index_in_dim(
            jnp.zeros((3, TEAM, HCOLS), F32), sum_q[2, :MINE].reshape(3, HCOLS), member, 1
        )
        up_full = lax.dynamic_update_index_in_dim(
            jnp.zeros((lines, TEAM, 96), F32), sum_m[1].reshape(lines, 96), member, 1
        )
        bias_full = jnp.where(member == 0, sum_m[0], 0.0)
        sums[depth] = jnp.concatenate(
            [
                qkv_full.reshape(world, 72),
                up_full.reshape(world, 96),
                *(
                    vector.reshape(world, 24)
                    for vector in (bias_full, sum_q[0], sum_q[1], sum_m[2], sum_m[3])
                ),
            ],
            axis=1,
        )
    qkv_grad, up_grad = run(
        unpack_body,
        [shape((LAYERS, 24, 3 * D), F32), shape((LAYERS, 24, FF), F32)],
        "unpack_gradients",
        [piece for depth in range(LAYERS) for piece in outs[depth][0]],
    )
    down_grad = jnp.stack([outs[depth][1] for depth in range(LAYERS)])
    attn_grad = lax.ppermute(
        jnp.stack([outs[depth][2] for depth in range(LAYERS)]), everywhere, gather_back
    ).astype(F32)
    tally = jnp.stack(sums)
    tally = tally + sum(team_send(tally, s) for s in range(1, TEAM))
    tally = tally + lax.ppermute(tally, "y", [(0, 1), (1, 0)])
    depth_z = lax.axis_size("z")
    tally = tally + sum(
        lax.ppermute(tally, "z", [(i, (i + s) % depth_z) for i in range(depth_z)])
        for s in range(1, depth_z)
    )
    own = lax.dynamic_index_in_dim(tally, team * TEAM + member, 1, keepdims=False)
    cuts = [0, 72, 168, 192, 216, 240, 264, 288]
    qkv_b, up_b, bias, ga, sa, gm, sm = (own[:, lo:hi] for lo, hi in zip(cuts[:-1], cuts[1:]))
    return (
        activations, grad, qkv_grad, qkv_b, attn_grad, bias, up_grad, up_b,
        down_grad, bias, ga, sa, gm, sm,
    )


def whole_mesh_solution(mesh):
    in_specs = (
        P(("dp", "cp"), None),
        P(("dp", "cp")),
        P(("dp", "cp"), None),
        P(None, ("dp", "cp"), None),
        P(None, ("dp", "cp")),
        P(None, ("dp", "cp"), None),
        P(None, ("dp", "cp")),
        P(None, ("dp", "cp"), None),
        P(None, ("dp", "cp")),
        P(None, ("dp", "cp"), None),
        P(None, ("dp", "cp")),
        P(None, ("dp", "cp")),
        P(None, ("dp", "cp")),
        P(None, ("dp", "cp")),
        P(None, ("dp", "cp")),
    )
    out_specs = (
        P(("dp", "cp"), None),
        P(("dp", "cp"), None),
        P(None, ("dp", "cp"), None),
        P(None, ("dp", "cp")),
        P(None, ("dp", "cp"), None),
        P(None, ("dp", "cp")),
        P(None, ("dp", "cp"), None),
        P(None, ("dp", "cp")),
        P(None, ("dp", "cp"), None),
        P(None, ("dp", "cp")),
        P(None, ("dp", "cp")),
        P(None, ("dp", "cp")),
        P(None, ("dp", "cp")),
        P(None, ("dp", "cp")),
    )
    return jax.shard_map(local, mesh=mesh, in_specs=in_specs, out_specs=out_specs, check_vma=False)


def solution(mesh):
    teams = mesh.shape["dp"] // 2
    if mesh.shape["cp"] != 2 or teams != 2 * LINE or teams * TEAM * 24 != D:
        return whole_mesh_solution(mesh)
    split_mesh = Mesh(mesh.devices.reshape(teams // 2, 2, 2, 2), ("z", "y", "core", "x"))
    every = ("z", "y", "core", "x")
    row = P(every, None)
    matrix, vector = P(None, every, None), P(None, every)
    in_specs = (row, P(every), row) + (matrix, vector) * 4 + (vector,) * 4
    out_specs = (row, row) + (matrix, vector) * 4 + (vector,) * 4
    return jax.shard_map(
        local_team, mesh=split_mesh, in_specs=in_specs, out_specs=out_specs, check_vma=False
    )
```

```python
from functools import partial
import math

import jax
import jax.numpy as jnp
from jax import lax
from jax.experimental import pallas as pl
from jax.experimental.pallas import tpu as pltpu
from jax.sharding import Mesh, PartitionSpec as P

D = 768
HEADS = 12
HEAD = 64
FF = 3072
ROT = 16
LAYERS = 2


def layer_norm(stream, norm_gain, norm_shift):
    centered = stream - jnp.mean(stream, axis=-1, keepdims=True)
    spread = jnp.mean(centered * centered, axis=-1, keepdims=True)
    return centered * lax.rsqrt(spread + 1e-05) * norm_gain + norm_shift


def both_norms(stream, gain_attn, shift_attn, gain_mlp, shift_mlp):
    return (layer_norm(stream, gain_attn, shift_attn), layer_norm(stream, gain_mlp, shift_mlp))


def angles(positions):
    inverse = 10000.0 ** (-jnp.arange(0, ROT, 2, dtype=jnp.float32) / ROT)
    phases = positions.astype(jnp.float32)[:, None] * inverse[None, :]
    return (jnp.cos(phases)[:, None, :], jnp.sin(phases)[:, None, :])


def rotate(heads_in, cosine_table, sine_table):
    half_rot = cosine_table.shape[-1]
    first_half = heads_in[..., :half_rot]
    second_half = heads_in[..., half_rot : 2 * half_rot]
    untouched = heads_in[..., 2 * half_rot :]
    return jnp.concatenate(
        [
            first_half * cosine_table - second_half * sine_table,
            second_half * cosine_table + first_half * sine_table,
            untouched,
        ],
        axis=-1,
    )


def split_blocks(update, running, key_piece, value_piece, offset):
    piece_rows = key_piece.shape[0]
    block_rows = 512 if piece_rows > 512 and piece_rows % 512 == 0 else piece_rows
    block_count = piece_rows // block_rows
    if block_count == 1:
        return update(running, key_piece, value_piece, offset)

    def advance(state, inputs):
        key_block, value_block, start = inputs
        return (update(state, key_block, value_block, offset + start), None)

    starts = jnp.arange(block_count, dtype=jnp.int32) * block_rows
    state, _ = lax.scan(
        advance,
        running,
        (
            key_piece.reshape(block_count, block_rows, -1),
            value_piece.reshape(block_count, block_rows, -1),
            starts,
        ),
    )
    return state


def stack_layers(per_layer, member):
    return jnp.stack([layer_entry[member] for layer_entry in per_layer])


def flatten_rows(matrix):
    return matrix.reshape(matrix.shape[:-2] + (-1, 128))


def local(
    tokens,
    segment_ids,
    cotangent,
    qkv_weight,
    qkv_bias,
    attn_weight,
    attn_bias,
    up_weight,
    up_bias,
    down_weight,
    down_bias,
    attn_gain,
    attn_shift,
    mlp_gain,
    mlp_shift,
):
    tok_rows = tokens.shape[0]
    group_rows = tok_rows * lax.axis_size("cp")
    score_scale = 1.0 / math.sqrt(HEAD)
    all_segments = lax.all_gather(segment_ids, "cp", axis=0, tiled=True)
    row_index = lax.axis_index("cp") * tok_rows + jnp.arange(tok_rows, dtype=jnp.int32)
    positions = row_index - jnp.sum(
        (all_segments[None, :] < segment_ids[:, None]).astype(jnp.int32), axis=1
    )
    cosine_table, sine_table = angles(positions)

    def visible_mask(offset, block_rows):
        key_index = offset + jnp.arange(block_rows, dtype=jnp.int32)
        key_segment = lax.dynamic_slice_in_dim(all_segments, offset, block_rows)
        return (key_index[None, :] <= row_index[:, None]) & (
            key_segment[None, :] == segment_ids[:, None]
        )

    def online_step(query_heads, running, key_block, value_block, offset):
        row_max, denominator, weighted = running
        block_rows = key_block.shape[0]
        key_heads = key_block.reshape(block_rows, HEADS, HEAD)
        value_heads = value_block.reshape(block_rows, HEADS, HEAD)
        scores = (
            jnp.einsum("qhd,khd->hqk", query_heads, key_heads, preferred_element_type=jnp.float32)
            * score_scale
        )
        visible = visible_mask(offset, block_rows)
        scores = jnp.where(visible[None], scores, -1e30)
        new_max = jnp.maximum(row_max, jnp.max(scores, axis=-1))
        rescale = jnp.exp(row_max - new_max)
        weights = jnp.where(visible[None], jnp.exp(scores - new_max[..., None]), 0.0)
        denominator = denominator * rescale + jnp.sum(weights, axis=-1)
        weighted = weighted * rescale[..., None] + jnp.einsum(
            "hqk,khd->hqd",
            weights.astype(jnp.bfloat16),
            value_heads,
            preferred_element_type=jnp.float32,
        )
        return (new_max, denominator, weighted)

    stream = tokens.astype(jnp.float32)
    stored = []
    for depth in range(LAYERS):
        params = (
            lax.all_gather(qkv_weight[depth], ("dp", "cp"), axis=0, tiled=True),
            lax.all_gather(qkv_bias[depth], ("dp", "cp"), axis=0, tiled=True),
            lax.all_gather(attn_weight[depth], ("dp", "cp"), axis=0, tiled=True),
            lax.all_gather(attn_bias[depth], ("dp", "cp"), axis=0, tiled=True),
            lax.all_gather(up_weight[depth], ("dp", "cp"), axis=0, tiled=True),
            lax.all_gather(up_bias[depth], ("dp", "cp"), axis=0, tiled=True),
            lax.all_gather(down_weight[depth], ("dp", "cp"), axis=0, tiled=True),
            lax.all_gather(down_bias[depth], ("dp", "cp"), axis=0, tiled=True),
            lax.all_gather(attn_gain[depth], ("dp", "cp"), axis=0, tiled=True),
            lax.all_gather(attn_shift[depth], ("dp", "cp"), axis=0, tiled=True),
            lax.all_gather(mlp_gain[depth], ("dp", "cp"), axis=0, tiled=True),
            lax.all_gather(mlp_shift[depth], ("dp", "cp"), axis=0, tiled=True),
        )
        (
            proj_qkv,
            bias_qkv,
            proj_attn,
            bias_attn,
            proj_up,
            bias_up,
            proj_down,
            bias_down,
            gain_attn,
            shift_attn,
            gain_mlp,
            shift_mlp,
        ) = params
        normed_attn, normed_mlp = both_norms(
            stream,
            gain_attn.astype(jnp.float32),
            shift_attn.astype(jnp.float32),
            gain_mlp.astype(jnp.float32),
            shift_mlp.astype(jnp.float32),
        )
        normed_attn = normed_attn.astype(jnp.bfloat16)
        normed_mlp = normed_mlp.astype(jnp.bfloat16)
        projected = jnp.dot(
            normed_attn, proj_qkv, preferred_element_type=jnp.float32
        ) + bias_qkv.astype(jnp.float32)
        queries = rotate(
            projected[:, :D].reshape(tok_rows, HEADS, HEAD), cosine_table, sine_table
        ).astype(jnp.bfloat16)
        key_rows = (
            rotate(projected[:, D : 2 * D].reshape(tok_rows, HEADS, HEAD), cosine_table, sine_table)
            .astype(jnp.bfloat16)
            .reshape(tok_rows, D)
        )
        values = projected[:, 2 * D :].astype(jnp.bfloat16)
        initial = (
            jnp.full((HEADS, tok_rows), -1e30, jnp.float32),
            jnp.zeros((HEADS, tok_rows), jnp.float32),
            jnp.zeros((HEADS, tok_rows, HEAD), jnp.float32),
        )
        row_max, denominator, weighted = split_blocks(
            partial(online_step, queries),
            initial,
            lax.all_gather(key_rows, "cp", axis=0, tiled=True),
            lax.all_gather(values, "cp", axis=0, tiled=True),
            jnp.int32(0),
        )
        attended = jnp.transpose(weighted / denominator[..., None], (1, 0, 2)).reshape(tok_rows, D)
        log_total = row_max + jnp.log(denominator)
        attended_low = attended.astype(jnp.bfloat16)
        attn_branch = jnp.dot(
            attended_low, proj_attn, preferred_element_type=jnp.float32
        ) + bias_attn.astype(jnp.float32)
        hidden_pre = jnp.dot(
            normed_mlp, proj_up, preferred_element_type=jnp.float32
        ) + bias_up.astype(jnp.float32)
        hidden = jax.nn.gelu(hidden_pre, approximate=False).astype(jnp.bfloat16)
        mlp_branch = jnp.dot(
            hidden, proj_down, preferred_element_type=jnp.float32
        ) + bias_down.astype(jnp.float32)
        stored.append(
            (
                stream,
                normed_attn,
                normed_mlp,
                queries,
                key_rows,
                values,
                attended,
                attended_low,
                log_total,
                hidden_pre,
                hidden,
            )
        )
        stream = stream + attn_branch + mlp_branch
    grad_stream = cotangent.astype(jnp.float32)
    per_layer = [None] * LAYERS
    for depth in reversed(range(LAYERS)):
        (
            saved_stream,
            normed_attn,
            normed_mlp,
            queries,
            key_rows,
            values,
            attended,
            attended_low,
            log_total,
            hidden_pre,
            hidden,
        ) = stored[depth]
        params = (
            lax.all_gather(qkv_weight[depth], ("dp", "cp"), axis=0, tiled=True),
            lax.all_gather(qkv_bias[depth], ("dp", "cp"), axis=0, tiled=True),
            lax.all_gather(attn_weight[depth], ("dp", "cp"), axis=0, tiled=True),
            lax.all_gather(attn_bias[depth], ("dp", "cp"), axis=0, tiled=True),
            lax.all_gather(up_weight[depth], ("dp", "cp"), axis=0, tiled=True),
            lax.all_gather(up_bias[depth], ("dp", "cp"), axis=0, tiled=True),
            lax.all_gather(down_weight[depth], ("dp", "cp"), axis=0, tiled=True),
            lax.all_gather(down_bias[depth], ("dp", "cp"), axis=0, tiled=True),
            lax.all_gather(attn_gain[depth], ("dp", "cp"), axis=0, tiled=True),
            lax.all_gather(attn_shift[depth], ("dp", "cp"), axis=0, tiled=True),
            lax.all_gather(mlp_gain[depth], ("dp", "cp"), axis=0, tiled=True),
            lax.all_gather(mlp_shift[depth], ("dp", "cp"), axis=0, tiled=True),
        )
        (
            proj_qkv,
            bias_qkv,
            proj_attn,
            bias_attn,
            proj_up,
            bias_up,
            proj_down,
            bias_down,
            gain_attn,
            shift_attn,
            gain_mlp,
            shift_mlp,
        ) = params
        grad_low = grad_stream.astype(jnp.bfloat16)
        bias_grad = jnp.sum(grad_low.astype(jnp.float32), axis=0)
        attn_weight_grad = jnp.einsum(
            "td,te->de", attended_low, grad_low, preferred_element_type=jnp.float32
        )
        down_weight_grad = jnp.einsum(
            "tf,te->fe", hidden, grad_low, preferred_element_type=jnp.float32
        )
        grad_attended = jnp.einsum(
            "te,de->td", grad_low, proj_attn, preferred_element_type=jnp.float32
        ).astype(jnp.bfloat16)
        grad_hidden = jnp.einsum(
            "te,fe->tf", grad_low, proj_down, preferred_element_type=jnp.float32
        )
        _, gelu_pull = jax.vjp(partial(jax.nn.gelu, approximate=False), hidden_pre)
        grad_pre = gelu_pull(grad_hidden)[0].astype(jnp.bfloat16)
        up_weight_grad = jnp.einsum(
            "td,tf->df", normed_mlp, grad_pre, preferred_element_type=jnp.float32
        )
        up_bias_grad = jnp.sum(grad_pre.astype(jnp.float32), axis=0)
        grad_normed_mlp = jnp.einsum(
            "tf,df->td", grad_pre, proj_up, preferred_element_type=jnp.float32
        )
        all_keys, all_values = (
            lax.all_gather(key_rows, "cp", axis=0, tiled=True),
            lax.all_gather(values, "cp", axis=0, tiled=True),
        )
        grad_heads = grad_attended.reshape(tok_rows, HEADS, HEAD)
        row_dot = jnp.transpose(
            jnp.sum(
                grad_heads.astype(jnp.float32) * attended.reshape(tok_rows, HEADS, HEAD), axis=-1
            )
        )
        block_rows = 512 if group_rows > 512 and group_rows % 512 == 0 else group_rows
        block_count = group_rows // block_rows
        starts = jnp.arange(block_count, dtype=jnp.int32) * block_rows

        def back_step(grad_query, inputs):
            key_block, value_block, offset = inputs
            key_heads = key_block.reshape(block_rows, HEADS, HEAD)
            value_heads = value_block.reshape(block_rows, HEADS, HEAD)
            scores = (
                jnp.einsum("qhd,khd->hqk", queries, key_heads, preferred_element_type=jnp.float32)
                * score_scale
            )
            visible = visible_mask(offset, block_rows)
            weights = jnp.where(visible[None], jnp.exp(scores - log_total[..., None]), 0.0)
            grad_weights = jnp.einsum(
                "qhd,khd->hqk", grad_heads, value_heads, preferred_element_type=jnp.float32
            )
            grad_scores = (weights * (grad_weights - row_dot[..., None])).astype(jnp.bfloat16)
            grad_query = grad_query + jnp.einsum(
                "hqk,khd->hqd", grad_scores, key_heads, preferred_element_type=jnp.float32
            )
            key_grad = (
                jnp.einsum("hqk,qhd->khd", grad_scores, queries, preferred_element_type=jnp.float32)
                * score_scale
            )
            value_grad = jnp.einsum(
                "hqk,qhd->khd",
                weights.astype(jnp.bfloat16),
                grad_heads,
                preferred_element_type=jnp.float32,
            )
            return (
                grad_query,
                (key_grad.reshape(block_rows, D), value_grad.reshape(block_rows, D)),
            )

        grad_query, (key_grads, value_grads) = lax.scan(
            back_step,
            jnp.zeros((HEADS, tok_rows, HEAD), jnp.float32),
            (
                all_keys.reshape(block_count, block_rows, D),
                all_values.reshape(block_count, block_rows, D),
                starts,
            ),
        )
        local_key_grad, local_value_grad = (
            lax.psum_scatter(
                key_grads.reshape(group_rows, D).astype(jnp.bfloat16),
                "cp",
                scatter_dimension=0,
                tiled=True,
            ).astype(jnp.float32),
            lax.psum_scatter(
                value_grads.reshape(group_rows, D).astype(jnp.bfloat16),
                "cp",
                scatter_dimension=0,
                tiled=True,
            ).astype(jnp.float32),
        )
        query_raw = rotate(
            jnp.transpose(grad_query * score_scale, (1, 0, 2)), cosine_table, -sine_table
        )
        key_raw = rotate(local_key_grad.reshape(tok_rows, HEADS, HEAD), cosine_table, -sine_table)
        grad_projected = jnp.concatenate(
            [query_raw.reshape(tok_rows, D), key_raw.reshape(tok_rows, D), local_value_grad], axis=1
        ).astype(jnp.bfloat16)
        qkv_weight_grad = jnp.einsum(
            "td,te->de", normed_attn, grad_projected, preferred_element_type=jnp.float32
        )
        qkv_bias_grad = jnp.sum(grad_projected.astype(jnp.float32), axis=0)
        grad_normed_attn = jnp.einsum(
            "te,de->td", grad_projected, proj_qkv, preferred_element_type=jnp.float32
        )
        _, norm_pull = jax.vjp(
            both_norms,
            saved_stream,
            gain_attn.astype(jnp.float32),
            shift_attn.astype(jnp.float32),
            gain_mlp.astype(jnp.float32),
            shift_mlp.astype(jnp.float32),
        )
        grad_input, attn_gain_grad, attn_shift_grad, mlp_gain_grad, mlp_shift_grad = norm_pull(
            (grad_normed_attn, grad_normed_mlp)
        )
        grad_stream = grad_stream + grad_input
        summed = (
            lax.psum_scatter(
                flatten_rows(qkv_weight_grad), ("dp", "cp"), scatter_dimension=0, tiled=True
            ),
            lax.psum_scatter(qkv_bias_grad, ("dp", "cp"), scatter_dimension=0, tiled=True),
            lax.psum_scatter(
                flatten_rows(attn_weight_grad), ("dp", "cp"), scatter_dimension=0, tiled=True
            ),
            lax.psum_scatter(bias_grad, ("dp", "cp"), scatter_dimension=0, tiled=True),
            lax.psum_scatter(
                flatten_rows(up_weight_grad), ("dp", "cp"), scatter_dimension=0, tiled=True
            ),
            lax.psum_scatter(up_bias_grad, ("dp", "cp"), scatter_dimension=0, tiled=True),
            lax.psum_scatter(
                flatten_rows(down_weight_grad), ("dp", "cp"), scatter_dimension=0, tiled=True
            ),
            lax.psum_scatter(bias_grad, ("dp", "cp"), scatter_dimension=0, tiled=True),
            lax.psum_scatter(attn_gain_grad, ("dp", "cp"), scatter_dimension=0, tiled=True),
            lax.psum_scatter(attn_shift_grad, ("dp", "cp"), scatter_dimension=0, tiled=True),
            lax.psum_scatter(mlp_gain_grad, ("dp", "cp"), scatter_dimension=0, tiled=True),
            lax.psum_scatter(mlp_shift_grad, ("dp", "cp"), scatter_dimension=0, tiled=True),
        )
        per_layer[depth] = (
            summed[0].reshape(-1, 3 * D),
            summed[1],
            summed[2].reshape(-1, D),
            summed[3],
            summed[4].reshape(-1, FF),
            summed[5],
            summed[6].reshape(-1, D),
            summed[7],
            summed[8],
            summed[9],
            summed[10],
            summed[11],
        )
    stacked = [stack_layers(per_layer, member) for member in range(12)]
    return (
        stream.astype(jnp.bfloat16),
        grad_stream,
        stacked[0],
        stacked[1],
        stacked[2],
        stacked[3],
        stacked[4],
        stacked[5],
        stacked[6],
        stacked[7],
        stacked[8],
        stacked[9],
        stacked[10],
        stacked[11],
    )


TEAM = 4
TEAM_AXES = ("core", "x")
LINE_AXES = ("z", "y")
LINE = 4
MINE = (3 * D) // TEAM
HCOLS = D // TEAM
UCOLS = FF // TEAM
VMEM_BYTES = 56 * 1024 * 1024
BF = jnp.bfloat16
F32 = jnp.float32


def call(body, out_shape, name, operands, scratch=()):
    return pl.pallas_call(
        body,
        out_shape=out_shape,
        scratch_shapes=list(scratch),
        compiler_params=pltpu.CompilerParams(vmem_limit_bytes=VMEM_BYTES),
        name=name,
    )(*operands)


def shape(dims, kind):
    return jax.ShapeDtypeStruct(dims, kind)


def mm(left, right):
    return jnp.dot(left, right, preferred_element_type=F32)


def mm_t(left, right):
    return lax.dot_general(left, right, (((1,), (1,)), ((), ())), preferred_element_type=F32)


def t_mm(left, right):
    return lax.dot_general(left, right, (((0,), (0,)), ((), ())), preferred_element_type=F32)


def pick(member, pieces, wanted):
    chosen = pieces[0]
    for s in range(1, TEAM):
        chosen = jnp.where((member ^ s) == wanted, pieces[s], chosen)
    return chosen


def small_rows(vectors, depth):
    rows = []
    for vector in vectors:
        values = vector[depth : depth + 1].astype(F32)
        rows.append(
            jnp.concatenate([values, jnp.zeros((1, 128 - values.shape[1]), F32)], axis=1)
        )
    return jnp.concatenate(rows, axis=0)


def pack_body(me_ref, qkv_ref, up_ref, *refs):
    vectors, outs = [r[...] for r in refs[:8]], refs[8:]
    me = me_ref[0]
    small = jnp.concatenate([small_rows(vectors, depth) for depth in range(LAYERS)], axis=0)
    small = jnp.concatenate([small, jnp.zeros((small.shape[0], UCOLS - 128), F32)], axis=1)
    parts = [[] for _ in range(TEAM)]
    for depth in range(LAYERS):
        rows = qkv_ref.shape[1]
        qkv = qkv_ref[depth].astype(F32)
        up = up_ref[depth].astype(F32)
        blocks = up.shape[1] // (TEAM * 96)
        for p in range(TEAM):
            parts[p].append(
                jnp.concatenate(
                    [up[:, 96 * (TEAM * b + p) : 96 * (TEAM * b + p + 1)] for b in range(blocks)],
                    axis=1,
                )
            )
            parts[p].append(
                jnp.concatenate(
                    [qkv[:, D * t + HCOLS * p : D * t + HCOLS * (p + 1)] for t in range(3)]
                    + [jnp.zeros((rows, UCOLS - MINE), F32)],
                    axis=1,
                )
            )
    parts = [jnp.concatenate(group, axis=0) for group in parts]
    for s in range(TEAM):
        chosen = parts[0]
        for p in range(1, TEAM):
            chosen = jnp.where((me ^ s) == p, parts[p], chosen)
        outs[s][...] = jnp.concatenate([chosen, small], axis=0).astype(BF)


def assemble_body(me_ref, p0, p1, p2, p3, attn_ref, down_ref, *outs):
    me = me_ref[0]
    slots = [r[...].astype(F32) for r in (p0, p1, p2, p3)]
    ordered = [pick(me, slots, p) for p in range(TEAM)]
    for depth, out in enumerate(outs):
        base = 48 * depth
        up = jnp.concatenate([piece[base : base + 24] for piece in ordered], axis=0)
        qkv = jnp.concatenate([piece[base + 24 : base + 48] for piece in ordered], axis=0)
        attn = attn_ref[depth].astype(F32)
        side = jnp.concatenate([attn[:, HCOLS * n : HCOLS * (n + 1)] for n in range(4)], axis=0)
        out[0:96] = up.astype(BF)
        out[96:192] = down_ref[depth]
        out[192:288] = jnp.concatenate([qkv[:, :MINE], side], axis=1).astype(BF)
        if out.shape[0] > 288:
            small = jnp.concatenate(
                [piece[96:112, :128] for piece in ordered] + [jnp.zeros((16, D - 4 * 128), F32)],
                axis=1,
            )
            out[288:304] = small.astype(BF)


def source_team(me_ref, index):
    shift, flip = index % LINE, index // LINE
    return 2 * lax.rem(me_ref[1] + LINE - shift, LINE) + (me_ref[2] ^ flip)


def target_team(me_ref, index):
    shift, flip = index % LINE, index // LINE
    return 2 * lax.rem(me_ref[1] + shift, LINE) + (me_ref[2] ^ flip)


def place(me_ref, pieces, whole):
    for index, piece in enumerate(pieces):
        whole[source_team(me_ref, index)] = piece[...]


def hand_out(me_ref, whole, keep, send):
    for s in range(LINE):
        keep[s] = whole[target_team(me_ref, s)]
        send[s] = whole[target_team(me_ref, LINE + s)]


def add_body(me_ref, keep, received, *outs):
    for s, out in enumerate(outs):
        out[...] = (keep[s + 1].astype(F32) + received[s + 1].astype(F32)).astype(BF)


def layer_vectors(me_ref, whole, depth):
    me = me_ref[0]
    small = [whole[k].astype(F32) for k in range(2 * LINE)]
    fields = [block[8 * depth : 8 * (depth + 1)] for block in small]
    shared = jnp.concatenate(
        [block[2:8, 128 * p : 128 * p + 24] for block in fields for p in range(TEAM)], axis=1
    )
    up_rows, qkv_rows = [], []
    qkv = jnp.concatenate(
        [block[0:1, 128 * p : 128 * p + 72] for block in fields for p in range(TEAM)], axis=1
    )
    for p in range(TEAM):
        up_rows.append(
            jnp.concatenate([block[1:2, 128 * p : 128 * p + 96] for block in fields], axis=1)
        )
        qkv_rows.append(
            jnp.concatenate(
                [qkv[:, D * t + HCOLS * p : D * t + HCOLS * (p + 1)] for t in range(3)]
                + [jnp.zeros((1, D - MINE), F32)],
                axis=1,
            )
        )
    up_mine, qkv_mine = up_rows[0], qkv_rows[0]
    for p in range(1, TEAM):
        up_mine = jnp.where(me == p, up_rows[p], up_mine)
        qkv_mine = jnp.where(me == p, qkv_rows[p], qkv_mine)
    return jnp.concatenate([shared, up_mine, qkv_mine], axis=0)


def attn_weights(whole):
    qkv = whole[:, 0:96, :][:, :, :MINE].reshape(D, MINE)
    side = whole[:, 0:96, MINE:].astype(F32)
    out = jnp.concatenate(
        [side[:, 24 * n : 24 * (n + 1), :].reshape(HCOLS, HCOLS) for n in range(4)], axis=1
    )
    return qkv, out.astype(BF)


def project(scaled, vec, weight, cosine, sine):
    normed = (scaled * vec[0:1] + vec[1:2]).astype(BF)
    projected = mm(normed, weight) + vec[7:8, :MINE]
    turned = turn(projected[:, : 2 * HCOLS], cosine, sine)
    queries = (turned[:, :HCOLS] * 0.125).astype(BF)
    keys = turned[:, HCOLS:].astype(BF)
    values = projected[:, 2 * HCOLS :].astype(BF)
    return normed, queries, keys, values


def attend_body(me_ref, x0, x1, x2, x3, *refs):
    pieces, smalls = refs[:8], refs[8:16]
    cos_ref, sin_ref, mask_ref, y_ref, vec_ref, whole, small = refs[16:]
    place(me_ref, pieces, whole)
    place(me_ref, smalls, small)
    for depth in range(LAYERS):
        vec_ref[depth] = layer_vectors(me_ref, small, depth)
    vec = vec_ref[0]
    weight, out_weight = attn_weights(whole)
    for g, (first, second) in enumerate(((x0, x1), (x2, x3))):
        rows = pl.ds(PAIR * g, PAIR)
        scaled, _ = norm_parts(two_slots(first[...], second[...]))
        _, queries, keys, values = project(scaled, vec, weight, cos_ref[rows, :], sin_ref[rows, :])
        total = jnp.zeros((PAIR, HCOLS), F32)
        for head in range(HEADS // TEAM):
            owned = head_mask(PAIR, head)
            scores = mm_t(jnp.where(owned, queries, jnp.zeros_like(queries)), keys) + mask_ref[g]
            weights = jnp.exp(scores - jnp.max(scores, axis=-1, keepdims=True))
            below = jnp.sum(weights, axis=-1, keepdims=True)
            total = total + jnp.where(owned, mm(weights.astype(BF), values) / below, 0.0)
        y_ref[rows, :] = mm(total.astype(BF), out_weight)


def mlp_body(me_ref, x0, x1, x2, x3, *refs):
    pieces, (vec_ref, a_ref, y0, y1, y2, y3, whole) = refs[:8], refs[8:]
    place(me_ref, pieces, whole)
    vec = vec_ref[0]
    up = whole[:, 0:96, :].reshape(D, UCOLS)
    down = whole[:, 96:192, :].reshape(UCOLS, D)
    for g, (first, second, y_first, y_second) in enumerate(((x0, x1, y0, y1), (x2, x3, y2, y3))):
        rows = pl.ds(PAIR * g, PAIR)
        scaled, _ = norm_parts(two_slots(first[...], second[...]))
        normed = (scaled * vec[2:3] + vec[3:4]).astype(BF)
        before = mm(normed, up) + vec[6:7]
        hidden = (before * (0.5 * (1.0 + lax.erf(before * (1.0 / math.sqrt(2.0)))))).astype(BF)
        result = mm(hidden, down) + a_ref[rows, :]
        y_first[...] = result[0:TOK].astype(y_first.dtype)
        y_second[...] = result[TOK:].astype(y_second.dtype)


def mlp_both_body(depth, last, me_ref, x0, x1, x2, x3, g0, g1, g2, g3, *refs):
    pieces, vec_ref, blocks = refs[:8], refs[8], refs[9:11]
    dn_ref, sum_ref = refs[11:13]
    whole, grads, c_s, hid_s, du_s, gb_s = refs[-6:]
    place(me_ref, pieces, whole)
    vec = vec_ref[depth]
    up = whole[:, 0:96, :].reshape(D, UCOLS)
    down = whole[:, 96:192, :].reshape(UCOLS, D)
    gain_sum = jnp.zeros((1, D), F32)
    shift_sum = jnp.zeros((1, D), F32)
    bias_sum = jnp.zeros((1, D), F32)
    up_sum = jnp.zeros((1, UCOLS), F32)
    for g, (first, second, g_first, g_second) in enumerate(((x0, x1, g0, g1), (x2, x3, g2, g3))):
        rows = pl.ds(PAIR * g, PAIR)
        scaled, _ = norm_parts(two_slots(first[...], second[...]))
        normed = (scaled * vec[2:3] + vec[3:4]).astype(BF)
        c_s[rows, :] = normed
        low = jnp.concatenate([g_first[...], g_second[...]], axis=0)
        gb_s[rows, :] = low
        hidden, slope = gelu_parts(mm(normed, up) + vec[6:7])
        hidden = hidden.astype(BF)
        hid_s[rows, :] = hidden
        if last:
            refs[13][rows, :] = mm(hidden, down)
        du = (mm_t(low, down) * slope).astype(BF)
        du_s[rows, :] = du
        dc = mm_t(du, up)
        dn_ref[rows, :] = dc * vec[2:3]
        gain_sum = gain_sum + jnp.sum(dc * scaled, axis=0, keepdims=True)
        shift_sum = shift_sum + jnp.sum(dc, axis=0, keepdims=True)
        bias_sum = bias_sum + jnp.sum(low.astype(F32), axis=0, keepdims=True)
        up_sum = up_sum + jnp.sum(du.astype(F32), axis=0, keepdims=True)
    grads[:, 0:96, :] = t_mm(c_s[...], du_s[...]).reshape(-1, 96, UCOLS).astype(BF)
    grads[:, 96:192, :] = t_mm(hid_s[...], gb_s[...]).reshape(-1, 96, D).astype(BF)
    hand_out(me_ref, grads, *blocks)
    sum_ref[...] = jnp.concatenate(
        [bias_sum, up_sum, gain_sum, shift_sum, jnp.zeros((4, D), F32)], axis=0
    )


def attend_both_body(depth, last, me_ref, x0, x1, x2, x3, g0, g1, g2, g3, *refs):
    pieces, (vec_ref, cos_ref, sin_ref, mask_ref, dn_ref, sum_ref) = refs[:8], refs[8:14]
    refs = refs[14:]
    if last:
        y_ref, refs = refs[0], refs[1:]
    blocks, (n0, n1, n2, n3) = refs[:2], refs[2:6]
    whole, grads, a_s, dp_s, o_s, gb_s = refs[-6:]
    place(me_ref, pieces, whole)
    vec = vec_ref[depth]
    weight, out_weight = attn_weights(whole)
    gain_sum = jnp.zeros((1, D), F32)
    shift_sum = jnp.zeros((1, D), F32)
    bias_sum = jnp.zeros((1, MINE), F32)
    for g, (first, second, g_first, g_second, n_first, n_second) in enumerate(
        ((x0, x1, g0, g1, n0, n1), (x2, x3, g2, g3, n2, n3))
    ):
        rows = pl.ds(PAIR * g, PAIR)
        cosine, sine = cos_ref[rows, :], sin_ref[rows, :]
        scaled, _ = norm_parts(two_slots(first[...], second[...]))
        normed, queries, keys, values = project(scaled, vec, weight, cosine, sine)
        a_s[rows, :] = normed
        low = jnp.concatenate([g_first[...], g_second[...]], axis=0)
        gb_s[rows, :] = low
        grad_o = mm_t(low, out_weight).astype(BF)
        zero = jnp.zeros_like(queries)
        out = jnp.zeros((PAIR, HCOLS), F32)
        dq = jnp.zeros((PAIR, HCOLS), F32)
        dk = jnp.zeros((PAIR, HCOLS), F32)
        dv = jnp.zeros((PAIR, HCOLS), F32)
        for head in range(HEADS // TEAM):
            owned = head_mask(PAIR, head)
            scores = mm_t(jnp.where(owned, queries, zero), keys) + mask_ref[g]
            weights = jnp.exp(scores - jnp.max(scores, axis=-1, keepdims=True))
            weights = weights / jnp.sum(weights, axis=-1, keepdims=True)
            rounded = weights.astype(BF)
            dweights = mm_t(jnp.where(owned, grad_o, zero), values)
            delta = jnp.sum(weights * dweights, axis=-1, keepdims=True)
            dscores = (weights * (dweights - delta)).astype(BF)
            out = out + jnp.where(owned, mm(rounded, values), 0.0)
            dq = dq + jnp.where(owned, mm(dscores, keys), 0.0)
            dk = dk + jnp.where(owned, t_mm(dscores, queries), 0.0)
            dv = dv + jnp.where(owned, t_mm(rounded, grad_o), 0.0)
        o_s[rows, :] = out.astype(BF)
        both = turn(jnp.concatenate([dq * 0.125, dk], axis=1), cosine, -sine)
        dproj = jnp.concatenate([both, dv], axis=1).astype(BF)
        dp_s[rows, :] = dproj
        bias_sum = bias_sum + jnp.sum(dproj.astype(F32), axis=0, keepdims=True)
        da = mm_t(dproj, weight)
        gain_sum = gain_sum + jnp.sum(da * scaled, axis=0, keepdims=True)
        shift_sum = shift_sum + jnp.sum(da, axis=0, keepdims=True)
        dn = dn_ref[rows, :] + da * vec[0:1]
        n_first[...] = dn[0:TOK].astype(n_first.dtype)
        n_second[...] = dn[TOK:].astype(n_second.dtype)
        if last:
            result = y_ref[rows, :] + mm(out.astype(BF), out_weight)
            y_first, y_second = refs[6 + 2 * g], refs[7 + 2 * g]
            y_first[...] = result[0:TOK].astype(y_first.dtype)
            y_second[...] = result[TOK:].astype(y_second.dtype)
    qkv_grad = t_mm(a_s[...], dp_s[...]).reshape(-1, 96, MINE)
    out_grad = t_mm(o_s[...], gb_s[...])
    side = jnp.concatenate(
        [out_grad[:, HCOLS * n : HCOLS * (n + 1)].reshape(-1, 24, HCOLS) for n in range(4)], axis=1
    )
    grads[:, 0:96, :] = jnp.concatenate([qkv_grad, side], axis=2).astype(BF)
    sums = sum_ref[...]
    vectors = jnp.concatenate([sums[0:2], gain_sum, shift_sum, sums[2:4]], axis=0)
    me = me_ref[0]
    spread = jnp.concatenate(
        [
            jnp.where(me == p, bias_sum[:, HCOLS * t : HCOLS * (t + 1)], 0.0)
            for t in range(3)
            for p in range(TEAM)
        ],
        axis=1,
    )
    for k in range(2 * LINE):
        shared = jnp.concatenate(
            [vectors[:, 96 * k : 96 * (k + 1)], jnp.zeros((6, D - 96), F32)], axis=1
        )
        bias = jnp.concatenate(
            [spread[:, 288 * k : 288 * (k + 1)], jnp.zeros((1, D - 288), F32)], axis=1
        )
        grads[k, 96:112, :] = jnp.concatenate([shared, bias, jnp.zeros((9, D), F32)], axis=0).astype(BF)
    hand_out(me_ref, grads, *blocks)


def residual_body(x_ref, y0, y1, y2, y3, vec_ref, out_ref, low_ref):
    depth = 0 if x_ref.dtype == BF else 1
    total = y0[...] + y1[...].astype(F32) + y2[...].astype(F32) + y3[...].astype(F32)
    result = x_ref[...].astype(F32) + total + (vec_ref[depth, 4:5] + vec_ref[depth, 5:6])
    out_ref[...] = result
    low_ref[...] = result.astype(BF)

def norm_parts(stream):
    centered = stream - jnp.mean(stream, axis=-1, keepdims=True)
    spread = jnp.mean(centered * centered, axis=-1, keepdims=True)
    inverse = lax.rsqrt(spread + 1e-05)
    return centered * inverse, inverse


def two_slots(first, second):
    return jnp.concatenate([first[0:TOK].astype(F32), second[0:TOK].astype(F32)], axis=0)


TOK = 128
PAIR = 2 * TOK


def turn(block, cosine, sine):
    lane = lax.broadcasted_iota(jnp.int32, (block.shape[0], 128), 1) % HEAD
    tiles = []
    for t in range(block.shape[1] // 128):
        tile = block[:, 128 * t : 128 * (t + 1)]
        swapped = jnp.where(
            lane < ROT // 2, pltpu.roll(tile, 128 - ROT // 2, 1), pltpu.roll(tile, ROT // 2, 1)
        )
        tiles.append(tile * cosine + swapped * sine)
    return jnp.concatenate(tiles, axis=1)


def head_mask(rows, head):
    lane = lax.broadcasted_iota(jnp.int32, (rows, HCOLS), 1)
    return (lane >= head * HEAD) & (lane < (head + 1) * HEAD)


def gelu_parts(u):
    cdf = 0.5 * (1.0 + lax.erf(u * (1.0 / math.sqrt(2.0))))
    density = jnp.exp(-0.5 * u * u) * (1.0 / math.sqrt(2.0 * math.pi))
    return u * cdf, cdf + u * density


def norm_back_body(x_ref, g_ref, n0, n1, n2, n3, out_ref, low_ref):
    scaled, inverse = norm_parts(x_ref[...].astype(F32))
    dn = n0[...] + n1[...].astype(F32) + n2[...].astype(F32) + n3[...].astype(F32)
    centered = dn - jnp.mean(dn, axis=-1, keepdims=True)
    moment = jnp.mean(dn * scaled, axis=-1, keepdims=True)
    result = g_ref[...].astype(F32) + inverse * (centered - scaled * moment)
    out_ref[...] = result
    low_ref[...] = result.astype(BF)


def split_body(me_ref, *refs):
    me = me_ref[0]

    def total(group):
        result = group[0][0].astype(F32) + group[1][0].astype(F32)
        for ref in group[2:]:
            result = result + ref[...].astype(F32)
        return result

    mlp, attn = total(refs[0:5]), total(refs[5:10])
    outs, (down_ref, attn_ref, small_ref) = refs[10:14], refs[14:]
    up = mlp[0:96]
    down_ref[...] = mlp[96:192]
    side = attn[0:96, MINE:]
    attn_ref[...] = jnp.concatenate(
        [side[24 * n : 24 * (n + 1)] for n in range(4)], axis=1
    ).astype(BF)
    qkv = jnp.concatenate([attn[0:96, :MINE], jnp.zeros((96, UCOLS - MINE), F32)], axis=1)
    small = attn[96:112]
    parts, bias = [], jnp.zeros((1, 24), F32)
    for p in range(TEAM):
        rows = slice(24 * p, 24 * (p + 1))
        gains = jnp.concatenate([small[2:6, rows], jnp.zeros((4, D - 24), F32)], axis=1)
        qkv_bias = jnp.concatenate(
            [small[6:7, 72 * p : 72 * (p + 1)], jnp.zeros((1, D - 72), F32)], axis=1
        )
        parts.append(
            jnp.concatenate([up[rows], qkv[rows], gains, qkv_bias, jnp.zeros((11, D), F32)], axis=0)
        )
        bias = jnp.where(me == p, small[0:1, rows], bias)
    small_ref[...] = jnp.concatenate(
        [
            jnp.concatenate([bias, jnp.zeros((1, 104), F32)], axis=1),
            small[1:2, :128],
            jnp.zeros((6, 128), F32),
        ],
        axis=0,
    )
    for s, out in enumerate(outs):
        piece = parts[0]
        for p in range(1, TEAM):
            piece = jnp.where((me ^ s) == p, parts[p], piece)
        out[...] = piece.astype(BF)


def unpack_body(me_ref, *refs):
    me = me_ref[0]
    (
        qkv_ref, qkv_b_ref, attn_ref, attn_b_ref, up_ref, up_b_ref, down_ref,
        ga_ref, sa_ref, gm_ref, sm_ref,
    ) = refs[7 * LAYERS :]
    gain_refs = (ga_ref, sa_ref, gm_ref, sm_ref)
    for depth in range(LAYERS):
        group = refs[7 * depth : 7 * (depth + 1)]
        slots = [r[...].astype(F32) for r in group[:TEAM]]
        own_small, attn_rows, down_rows = group[TEAM:]
        ordered = [pick(me, slots, p) for p in range(TEAM)]
        blocks = FF // (96 * TEAM)
        up_ref[depth] = jnp.concatenate(
            [ordered[p][0:24, 96 * b : 96 * (b + 1)] for b in range(blocks) for p in range(TEAM)],
            axis=1,
        )
        qkv_ref[depth] = jnp.concatenate(
            [
                ordered[p][24:48, HCOLS * t : HCOLS * (t + 1)]
                for t in range(3)
                for p in range(TEAM)
            ],
            axis=1,
        )
        attn_ref[depth] = attn_rows[...].astype(F32)
        down_ref[depth] = down_rows[...]
        small = slots[0][48:56, :128] + slots[1][48:56, :128]
        small = small + slots[2][48:56, :128] + slots[3][48:56, :128]
        for n, ref in enumerate(gain_refs):
            ref[depth : depth + 1] = small[n : n + 1, :24]
        qkv_b_ref[depth : depth + 1] = small[4:5, :72]
        attn_b_ref[depth : depth + 1] = own_small[0:1, :24]
        up_b_ref[depth : depth + 1] = own_small[1:2, :96]


def team_send(piece, slot):
    flips = [(m, m ^ slot) for m in range(TEAM)]
    return lax.ppermute(piece, TEAM_AXES, flips)


def line_shift(piece, shift):
    size = lax.axis_size("z")
    return lax.ppermute(piece, "z", [(i, (i + shift) % size) for i in range(size)])


def line_flip(piece):
    return lax.ppermute(piece, "y", [(0, 1), (1, 0)])


def after(value, *others):
    return lax.optimization_barrier((value, *others))[0]


def line_near(piece):
    return [piece] + [line_shift(piece, s) for s in range(1, LINE)]


def local_team(
    tokens, segment_ids, cotangent, qkv_weight, qkv_bias, attn_weight, attn_bias,
    up_weight, up_bias, down_weight, down_bias, attn_gain, attn_shift, mlp_gain, mlp_shift,
):
    lines = lax.axis_size("z") * lax.axis_size("y")
    world = lines * TEAM
    member = lax.axis_index("core") * 2 + lax.axis_index("x")
    me = jnp.stack([member, lax.axis_index("z"), lax.axis_index("y")]).astype(jnp.int32)
    everywhere = LINE_AXES + TEAM_AXES
    tok_all = TEAM * TOK
    whole_spec = pl.BlockSpec(memory_space=pltpu.VMEM)

    def run(body, out_shape, name, operands, scratch=()):
        specs = [whole_spec if isinstance(x, jax.Array) else x[1] for x in operands]
        return pl.pallas_call(
            body,
            grid=(1,),
            out_shape=out_shape,
            in_specs=[pl.BlockSpec(memory_space=pltpu.SMEM)] + specs,
            scratch_shapes=[pltpu.VMEM(dims, kind) for dims, kind in scratch],
            compiler_params=pltpu.CompilerParams(vmem_limit_bytes=VMEM_BYTES),
            name=name,
        )(me, *[x if isinstance(x, jax.Array) else x[0] for x in operands])

    def part(rows, start):
        return pl.BlockSpec((rows, D), lambda i: (start // rows, 0))

    def one_of(array, index):
        return (array, pl.BlockSpec((1,) + array.shape[1:], lambda i: (index, 0, 0)))

    def exchange(blocks):
        return [blocks[0]] + [team_send(blocks[s], s) for s in range(1, TEAM)]

    small = (
        qkv_bias, up_bias, attn_gain, attn_shift, mlp_gain, mlp_shift, attn_bias, down_bias
    )
    packed = run(
        pack_body, [shape((112, D), BF)] * TEAM, "pack_weights", (qkv_weight, up_weight, *small)
    )
    spread = [(i, TEAM * (i % lines) + i // lines) for i in range(world)]
    gather_back = [(b, a) for a, b in spread]
    attn_piece = lax.ppermute(attn_weight, everywhere, spread)
    chunks = run(
        assemble_body,
        [shape((304, D), BF), shape((288, D), BF)],
        "assemble_weights",
        (*exchange(packed), attn_piece, down_weight),
    )
    near = line_near(chunks[0])
    pieces = [near + [line_flip(p) for p in near]]
    near = line_near(after(chunks[1], near[2]))
    pieces.append(near + [line_flip(p) for p in near])
    m_parts = [[(p, part(192, 0)) for p in group] for group in pieces]
    a_parts = [[(p, part(96, 192)) for p in group] for group in pieces]
    small_parts = [(p, part(16, 288)) for p in pieces[0]]

    ids_row = jnp.pad(segment_ids.astype(BF)[None, :], ((0, 15), (0, D - TOK)))
    load = jnp.concatenate([tokens, ids_row, cotangent], axis=0)
    loads = [load] + exchange([after(load, chunks[0])] * TEAM)[1:]
    token_slots = [(load, part(TOK, 0)) for load in loads]
    here = lax.axis_index("x")
    rows = jnp.arange(TOK, dtype=jnp.int32)
    places = jnp.concatenate([here * TOK + rows, (1 - here) * TOK + rows])
    masks, cosines, sines = [], [], []
    lane = jnp.arange(128, dtype=jnp.int32) % HEAD
    inverse = 10000.0 ** (-(lane % (ROT // 2) * 2).astype(F32) / ROT)
    for g in range(2):
        ids = jnp.concatenate([load[TOK, :TOK] for load in loads[2 * g : 2 * g + 2]]).astype(F32)
        visible = (places[None, :] <= places[:, None]) & (ids[None, :] == ids[:, None])
        masks.append(jnp.where(visible, 0.0, -1e30).astype(F32))
        position = places - jnp.sum((ids[None, :] < ids[:, None]).astype(jnp.int32), axis=1)
        phases = position.astype(F32)[:, None] * inverse[None, :]
        cosines.append(jnp.where(lane[None, :] < ROT, jnp.cos(phases), 1.0))
        sign = jnp.where(lane < ROT // 2, -1.0, jnp.where(lane < ROT, 1.0, 0.0))
        sines.append(jnp.sin(phases) * sign[None, :])
    mask = jnp.stack(masks)
    cosine, sine = jnp.concatenate(cosines), jnp.concatenate(sines)

    four = [shape((TOK, D), F32)] + [shape((TOK, D), BF)] * 3
    stream_pair = [shape((TOK, D), F32), shape((TOK, D), BF)]
    wide = ((tok_all, D), BF)

    attn_out, vec = run(
        attend_body,
        [shape((tok_all, D), F32), shape((LAYERS, 8, D), F32)],
        "attend_forward",
        (*token_slots, *a_parts[0], *small_parts, cosine, sine, mask),
        [((lines, 96, D), BF), ((lines, 16, D), BF)],
    )
    y = run(
        mlp_body,
        four,
        "mlp_forward",
        (*token_slots, *m_parts[0], vec, attn_out),
        [((lines, 192, D), BF)],
    )

    def residual(stream, blocks):
        return call(residual_body, stream_pair, "residual", (stream, *exchange(blocks), vec))

    stream, low = residual(tokens, y)
    streams = [tokens, stream]
    slots = [token_slots, exchange([low] * TEAM)]

    grad = cotangent
    grad_slots = [load[TOK + 16 :] for load in loads]
    outs = [None] * LAYERS
    block_m, block_a = shape((192, D), BF), shape((112, D), BF)

    def mlp_back(depth, slots, grad_slots):
        last = depth == LAYERS - 1
        result = run(
            partial(mlp_both_body, depth, last),
            [shape((4, 192, D), BF)] * 2
            + [shape((tok_all, D), F32), shape((8, D), F32)]
            + ([shape((tok_all, D), F32)] if last else []),
            "mlp_both",
            (*slots, *grad_slots, *m_parts[depth], vec),
            [((lines, 192, D), BF), ((lines, 192, D), BF), wide, wide, wide, wide],
        )
        return result[0], line_flip(result[1]), result[2:]

    def attend_back(depth, slots, grad_slots, rest):
        last = depth == LAYERS - 1
        result = run(
            partial(attend_both_body, depth, last),
            [shape((4, 112, D), BF)] * 2 + four + (four if last else []),
            "attend_both",
            (*slots, *grad_slots, *a_parts[depth], vec, cosine, sine, mask, *rest),
            [
                ((lines, 96, D), BF),
                ((lines, 112, D), BF),
                wide,
                ((tok_all, MINE), BF),
                ((tok_all, HCOLS), BF),
                wide,
            ],
        )
        return result[0], line_flip(result[1]), result[2:6], result[6:]

    def norm_back(depth, grad, received):
        return call(
            norm_back_body, stream_pair, "norm_backward", (streams[depth], grad, *received)
        )

    def add(kind, keep, other, name):
        return run(add_body, [kind] * 3, name, (keep, other))

    def shifts(sums):
        return [line_shift(piece, s + 1) for s, piece in enumerate(sums)]

    def hand_over(depth, m_keep, m_other, m_sums, a_keep, a_other, a_sums):
        mine = run(
            split_body,
            [shape((64, D), BF)] * TEAM
            + [shape((96, D), F32), shape((24, D), BF), shape((8, 128), F32)],
            "split_gradients",
            (
                one_of(m_keep, 0), one_of(m_other, 0), *m_sums,
                one_of(a_keep, 0), one_of(a_other, 0), *a_sums,
            ),
        )
        attn_rows = lax.ppermute(mine[TEAM + 1], everywhere, gather_back)
        outs[depth] = exchange(mine[:TEAM]) + [mine[TEAM + 2], attn_rows, mine[TEAM]]
        return mine

    m_keep1, m_other1, rest = mlp_back(1, slots[1], grad_slots)
    a_keep1, a_other1, ns, ys = attend_back(1, slots[1], grad_slots, rest)
    received = exchange(ns)
    received[3] = after(received[3], m_other1)
    grad, low = norm_back(1, grad, received)
    m_added1 = add(block_m, m_keep1, after(m_other1, low), "add_mlp")
    m_sums1 = shifts(m_added1)
    grad_slots = exchange([low] * TEAM)
    _, activations = residual(streams[1], [ys[0]] + [after(y, grad_slots[3]) for y in ys[1:]])
    grad_slots[0] = after(grad_slots[0], *m_added1)
    m_keep0, m_other0, rest = mlp_back(0, slots[0], grad_slots)
    a_added1 = add(block_a, a_keep1, after(a_other1, rest[0]), "add_attend")
    a_sums1 = shifts(a_added1)
    a_keep0, a_other0, ns, _ = attend_back(
        0, slots[0], grad_slots, [after(rest[0], *a_added1, *m_sums1), *rest[1:]]
    )
    grad, _ = norm_back(0, grad, exchange(ns))
    mine = hand_over(1, m_keep1, m_other1, m_sums1, a_keep1, a_other1, a_sums1)
    m_added0 = add(block_m, m_keep0, after(m_other0, mine[0]), "add_mlp")
    m_sums0 = shifts(m_added0)
    a_added0 = add(block_a, a_keep0, after(a_other0, *m_added0), "add_attend")
    a_sums0 = shifts(a_added0)
    hand_over(0, m_keep0, m_other0, m_sums0, a_keep0, a_other0, a_sums0)
    row_24 = shape((LAYERS, 24), F32)
    final = run(
        unpack_body,
        [
            shape((LAYERS, 24, 3 * D), F32), shape((LAYERS, 72), F32),
            shape((LAYERS, 24, D), F32), row_24,
            shape((LAYERS, 24, FF), F32), shape((LAYERS, 96), F32),
            shape((LAYERS, 96, D), F32), row_24, row_24, row_24, row_24,
        ],
        "unpack_gradients",
        [array for group in outs for array in group],
    )
    return (activations, grad, *final[:7], final[3], *final[7:])


def whole_mesh_solution(mesh):
    in_specs = (
        P(("dp", "cp"), None),
        P(("dp", "cp")),
        P(("dp", "cp"), None),
        P(None, ("dp", "cp"), None),
        P(None, ("dp", "cp")),
        P(None, ("dp", "cp"), None),
        P(None, ("dp", "cp")),
        P(None, ("dp", "cp"), None),
        P(None, ("dp", "cp")),
        P(None, ("dp", "cp"), None),
        P(None, ("dp", "cp")),
        P(None, ("dp", "cp")),
        P(None, ("dp", "cp")),
        P(None, ("dp", "cp")),
        P(None, ("dp", "cp")),
    )
    out_specs = (
        P(("dp", "cp"), None),
        P(("dp", "cp"), None),
        P(None, ("dp", "cp"), None),
        P(None, ("dp", "cp")),
        P(None, ("dp", "cp"), None),
        P(None, ("dp", "cp")),
        P(None, ("dp", "cp"), None),
        P(None, ("dp", "cp")),
        P(None, ("dp", "cp"), None),
        P(None, ("dp", "cp")),
        P(None, ("dp", "cp")),
        P(None, ("dp", "cp")),
        P(None, ("dp", "cp")),
        P(None, ("dp", "cp")),
    )
    return jax.shard_map(local, mesh=mesh, in_specs=in_specs, out_specs=out_specs, check_vma=False)


def solution(mesh):
    teams = mesh.shape["dp"] // 2
    if mesh.shape["cp"] != 2 or teams != 2 * LINE or teams * TEAM * 24 != D:
        return whole_mesh_solution(mesh)
    split_mesh = Mesh(mesh.devices.reshape(teams // 2, 2, 2, 2), ("z", "y", "core", "x"))
    every = ("z", "y", "core", "x")
    row = P(every, None)
    matrix, vector = P(None, every, None), P(None, every)
    in_specs = (row, P(every), row) + (matrix, vector) * 4 + (vector,) * 4
    out_specs = (row, row) + (matrix, vector) * 4 + (vector,) * 4
    return jax.shard_map(
        local_team, mesh=split_mesh, in_specs=in_specs, out_specs=out_specs, check_vma=False
    )
```

```python
from functools import partial
import math

import jax
import jax.numpy as jnp
from jax import lax
from jax.experimental import pallas as pl
from jax.experimental.pallas import tpu as pltpu
from jax.sharding import Mesh, PartitionSpec as P

D = 768
HEADS = 12
HEAD = 64
FF = 3072
ROT = 16
LAYERS = 2


def layer_norm(stream, norm_gain, norm_shift):
    centered = stream - jnp.mean(stream, axis=-1, keepdims=True)
    spread = jnp.mean(centered * centered, axis=-1, keepdims=True)
    return centered * lax.rsqrt(spread + 1e-05) * norm_gain + norm_shift


def both_norms(stream, gain_attn, shift_attn, gain_mlp, shift_mlp):
    return (layer_norm(stream, gain_attn, shift_attn), layer_norm(stream, gain_mlp, shift_mlp))


def angles(positions):
    inverse = 10000.0 ** (-jnp.arange(0, ROT, 2, dtype=jnp.float32) / ROT)
    phases = positions.astype(jnp.float32)[:, None] * inverse[None, :]
    return (jnp.cos(phases)[:, None, :], jnp.sin(phases)[:, None, :])


def rotate(heads_in, cosine_table, sine_table):
    half_rot = cosine_table.shape[-1]
    first_half = heads_in[..., :half_rot]
    second_half = heads_in[..., half_rot : 2 * half_rot]
    untouched = heads_in[..., 2 * half_rot :]
    return jnp.concatenate(
        [
            first_half * cosine_table - second_half * sine_table,
            second_half * cosine_table + first_half * sine_table,
            untouched,
        ],
        axis=-1,
    )


def split_blocks(update, running, key_piece, value_piece, offset):
    piece_rows = key_piece.shape[0]
    block_rows = 512 if piece_rows > 512 and piece_rows % 512 == 0 else piece_rows
    block_count = piece_rows // block_rows
    if block_count == 1:
        return update(running, key_piece, value_piece, offset)

    def advance(state, inputs):
        key_block, value_block, start = inputs
        return (update(state, key_block, value_block, offset + start), None)

    starts = jnp.arange(block_count, dtype=jnp.int32) * block_rows
    state, _ = lax.scan(
        advance,
        running,
        (
            key_piece.reshape(block_count, block_rows, -1),
            value_piece.reshape(block_count, block_rows, -1),
            starts,
        ),
    )
    return state


def stack_layers(per_layer, member):
    return jnp.stack([layer_entry[member] for layer_entry in per_layer])


def flatten_rows(matrix):
    return matrix.reshape(matrix.shape[:-2] + (-1, 128))


def local(
    tokens,
    segment_ids,
    cotangent,
    qkv_weight,
    qkv_bias,
    attn_weight,
    attn_bias,
    up_weight,
    up_bias,
    down_weight,
    down_bias,
    attn_gain,
    attn_shift,
    mlp_gain,
    mlp_shift,
):
    tok_rows = tokens.shape[0]
    group_rows = tok_rows * lax.axis_size("cp")
    score_scale = 1.0 / math.sqrt(HEAD)
    all_segments = lax.all_gather(segment_ids, "cp", axis=0, tiled=True)
    row_index = lax.axis_index("cp") * tok_rows + jnp.arange(tok_rows, dtype=jnp.int32)
    positions = row_index - jnp.sum(
        (all_segments[None, :] < segment_ids[:, None]).astype(jnp.int32), axis=1
    )
    cosine_table, sine_table = angles(positions)

    def visible_mask(offset, block_rows):
        key_index = offset + jnp.arange(block_rows, dtype=jnp.int32)
        key_segment = lax.dynamic_slice_in_dim(all_segments, offset, block_rows)
        return (key_index[None, :] <= row_index[:, None]) & (
            key_segment[None, :] == segment_ids[:, None]
        )

    def online_step(query_heads, running, key_block, value_block, offset):
        row_max, denominator, weighted = running
        block_rows = key_block.shape[0]
        key_heads = key_block.reshape(block_rows, HEADS, HEAD)
        value_heads = value_block.reshape(block_rows, HEADS, HEAD)
        scores = (
            jnp.einsum("qhd,khd->hqk", query_heads, key_heads, preferred_element_type=jnp.float32)
            * score_scale
        )
        visible = visible_mask(offset, block_rows)
        scores = jnp.where(visible[None], scores, -1e30)
        new_max = jnp.maximum(row_max, jnp.max(scores, axis=-1))
        rescale = jnp.exp(row_max - new_max)
        weights = jnp.where(visible[None], jnp.exp(scores - new_max[..., None]), 0.0)
        denominator = denominator * rescale + jnp.sum(weights, axis=-1)
        weighted = weighted * rescale[..., None] + jnp.einsum(
            "hqk,khd->hqd",
            weights.astype(jnp.bfloat16),
            value_heads,
            preferred_element_type=jnp.float32,
        )
        return (new_max, denominator, weighted)

    stream = tokens.astype(jnp.float32)
    stored = []
    for depth in range(LAYERS):
        params = (
            lax.all_gather(qkv_weight[depth], ("dp", "cp"), axis=0, tiled=True),
            lax.all_gather(qkv_bias[depth], ("dp", "cp"), axis=0, tiled=True),
            lax.all_gather(attn_weight[depth], ("dp", "cp"), axis=0, tiled=True),
            lax.all_gather(attn_bias[depth], ("dp", "cp"), axis=0, tiled=True),
            lax.all_gather(up_weight[depth], ("dp", "cp"), axis=0, tiled=True),
            lax.all_gather(up_bias[depth], ("dp", "cp"), axis=0, tiled=True),
            lax.all_gather(down_weight[depth], ("dp", "cp"), axis=0, tiled=True),
            lax.all_gather(down_bias[depth], ("dp", "cp"), axis=0, tiled=True),
            lax.all_gather(attn_gain[depth], ("dp", "cp"), axis=0, tiled=True),
            lax.all_gather(attn_shift[depth], ("dp", "cp"), axis=0, tiled=True),
            lax.all_gather(mlp_gain[depth], ("dp", "cp"), axis=0, tiled=True),
            lax.all_gather(mlp_shift[depth], ("dp", "cp"), axis=0, tiled=True),
        )
        (
            proj_qkv,
            bias_qkv,
            proj_attn,
            bias_attn,
            proj_up,
            bias_up,
            proj_down,
            bias_down,
            gain_attn,
            shift_attn,
            gain_mlp,
            shift_mlp,
        ) = params
        normed_attn, normed_mlp = both_norms(
            stream,
            gain_attn.astype(jnp.float32),
            shift_attn.astype(jnp.float32),
            gain_mlp.astype(jnp.float32),
            shift_mlp.astype(jnp.float32),
        )
        normed_attn = normed_attn.astype(jnp.bfloat16)
        normed_mlp = normed_mlp.astype(jnp.bfloat16)
        projected = jnp.dot(
            normed_attn, proj_qkv, preferred_element_type=jnp.float32
        ) + bias_qkv.astype(jnp.float32)
        queries = rotate(
            projected[:, :D].reshape(tok_rows, HEADS, HEAD), cosine_table, sine_table
        ).astype(jnp.bfloat16)
        key_rows = (
            rotate(projected[:, D : 2 * D].reshape(tok_rows, HEADS, HEAD), cosine_table, sine_table)
            .astype(jnp.bfloat16)
            .reshape(tok_rows, D)
        )
        values = projected[:, 2 * D :].astype(jnp.bfloat16)
        initial = (
            jnp.full((HEADS, tok_rows), -1e30, jnp.float32),
            jnp.zeros((HEADS, tok_rows), jnp.float32),
            jnp.zeros((HEADS, tok_rows, HEAD), jnp.float32),
        )
        row_max, denominator, weighted = split_blocks(
            partial(online_step, queries),
            initial,
            lax.all_gather(key_rows, "cp", axis=0, tiled=True),
            lax.all_gather(values, "cp", axis=0, tiled=True),
            jnp.int32(0),
        )
        attended = jnp.transpose(weighted / denominator[..., None], (1, 0, 2)).reshape(tok_rows, D)
        log_total = row_max + jnp.log(denominator)
        attended_low = attended.astype(jnp.bfloat16)
        attn_branch = jnp.dot(
            attended_low, proj_attn, preferred_element_type=jnp.float32
        ) + bias_attn.astype(jnp.float32)
        hidden_pre = jnp.dot(
            normed_mlp, proj_up, preferred_element_type=jnp.float32
        ) + bias_up.astype(jnp.float32)
        hidden = jax.nn.gelu(hidden_pre, approximate=False).astype(jnp.bfloat16)
        mlp_branch = jnp.dot(
            hidden, proj_down, preferred_element_type=jnp.float32
        ) + bias_down.astype(jnp.float32)
        stored.append(
            (
                stream,
                normed_attn,
                normed_mlp,
                queries,
                key_rows,
                values,
                attended,
                attended_low,
                log_total,
                hidden_pre,
                hidden,
            )
        )
        stream = stream + attn_branch + mlp_branch
    grad_stream = cotangent.astype(jnp.float32)
    per_layer = [None] * LAYERS
    for depth in reversed(range(LAYERS)):
        (
            saved_stream,
            normed_attn,
            normed_mlp,
            queries,
            key_rows,
            values,
            attended,
            attended_low,
            log_total,
            hidden_pre,
            hidden,
        ) = stored[depth]
        params = (
            lax.all_gather(qkv_weight[depth], ("dp", "cp"), axis=0, tiled=True),
            lax.all_gather(qkv_bias[depth], ("dp", "cp"), axis=0, tiled=True),
            lax.all_gather(attn_weight[depth], ("dp", "cp"), axis=0, tiled=True),
            lax.all_gather(attn_bias[depth], ("dp", "cp"), axis=0, tiled=True),
            lax.all_gather(up_weight[depth], ("dp", "cp"), axis=0, tiled=True),
            lax.all_gather(up_bias[depth], ("dp", "cp"), axis=0, tiled=True),
            lax.all_gather(down_weight[depth], ("dp", "cp"), axis=0, tiled=True),
            lax.all_gather(down_bias[depth], ("dp", "cp"), axis=0, tiled=True),
            lax.all_gather(attn_gain[depth], ("dp", "cp"), axis=0, tiled=True),
            lax.all_gather(attn_shift[depth], ("dp", "cp"), axis=0, tiled=True),
            lax.all_gather(mlp_gain[depth], ("dp", "cp"), axis=0, tiled=True),
            lax.all_gather(mlp_shift[depth], ("dp", "cp"), axis=0, tiled=True),
        )
        (
            proj_qkv,
            bias_qkv,
            proj_attn,
            bias_attn,
            proj_up,
            bias_up,
            proj_down,
            bias_down,
            gain_attn,
            shift_attn,
            gain_mlp,
            shift_mlp,
        ) = params
        grad_low = grad_stream.astype(jnp.bfloat16)
        bias_grad = jnp.sum(grad_low.astype(jnp.float32), axis=0)
        attn_weight_grad = jnp.einsum(
            "td,te->de", attended_low, grad_low, preferred_element_type=jnp.float32
        )
        down_weight_grad = jnp.einsum(
            "tf,te->fe", hidden, grad_low, preferred_element_type=jnp.float32
        )
        grad_attended = jnp.einsum(
            "te,de->td", grad_low, proj_attn, preferred_element_type=jnp.float32
        ).astype(jnp.bfloat16)
        grad_hidden = jnp.einsum(
            "te,fe->tf", grad_low, proj_down, preferred_element_type=jnp.float32
        )
        _, gelu_pull = jax.vjp(partial(jax.nn.gelu, approximate=False), hidden_pre)
        grad_pre = gelu_pull(grad_hidden)[0].astype(jnp.bfloat16)
        up_weight_grad = jnp.einsum(
            "td,tf->df", normed_mlp, grad_pre, preferred_element_type=jnp.float32
        )
        up_bias_grad = jnp.sum(grad_pre.astype(jnp.float32), axis=0)
        grad_normed_mlp = jnp.einsum(
            "tf,df->td", grad_pre, proj_up, preferred_element_type=jnp.float32
        )
        all_keys, all_values = (
            lax.all_gather(key_rows, "cp", axis=0, tiled=True),
            lax.all_gather(values, "cp", axis=0, tiled=True),
        )
        grad_heads = grad_attended.reshape(tok_rows, HEADS, HEAD)
        row_dot = jnp.transpose(
            jnp.sum(
                grad_heads.astype(jnp.float32) * attended.reshape(tok_rows, HEADS, HEAD), axis=-1
            )
        )
        block_rows = 512 if group_rows > 512 and group_rows % 512 == 0 else group_rows
        block_count = group_rows // block_rows
        starts = jnp.arange(block_count, dtype=jnp.int32) * block_rows

        def back_step(grad_query, inputs):
            key_block, value_block, offset = inputs
            key_heads = key_block.reshape(block_rows, HEADS, HEAD)
            value_heads = value_block.reshape(block_rows, HEADS, HEAD)
            scores = (
                jnp.einsum("qhd,khd->hqk", queries, key_heads, preferred_element_type=jnp.float32)
                * score_scale
            )
            visible = visible_mask(offset, block_rows)
            weights = jnp.where(visible[None], jnp.exp(scores - log_total[..., None]), 0.0)
            grad_weights = jnp.einsum(
                "qhd,khd->hqk", grad_heads, value_heads, preferred_element_type=jnp.float32
            )
            grad_scores = (weights * (grad_weights - row_dot[..., None])).astype(jnp.bfloat16)
            grad_query = grad_query + jnp.einsum(
                "hqk,khd->hqd", grad_scores, key_heads, preferred_element_type=jnp.float32
            )
            key_grad = (
                jnp.einsum("hqk,qhd->khd", grad_scores, queries, preferred_element_type=jnp.float32)
                * score_scale
            )
            value_grad = jnp.einsum(
                "hqk,qhd->khd",
                weights.astype(jnp.bfloat16),
                grad_heads,
                preferred_element_type=jnp.float32,
            )
            return (
                grad_query,
                (key_grad.reshape(block_rows, D), value_grad.reshape(block_rows, D)),
            )

        grad_query, (key_grads, value_grads) = lax.scan(
            back_step,
            jnp.zeros((HEADS, tok_rows, HEAD), jnp.float32),
            (
                all_keys.reshape(block_count, block_rows, D),
                all_values.reshape(block_count, block_rows, D),
                starts,
            ),
        )
        local_key_grad, local_value_grad = (
            lax.psum_scatter(
                key_grads.reshape(group_rows, D).astype(jnp.bfloat16),
                "cp",
                scatter_dimension=0,
                tiled=True,
            ).astype(jnp.float32),
            lax.psum_scatter(
                value_grads.reshape(group_rows, D).astype(jnp.bfloat16),
                "cp",
                scatter_dimension=0,
                tiled=True,
            ).astype(jnp.float32),
        )
        query_raw = rotate(
            jnp.transpose(grad_query * score_scale, (1, 0, 2)), cosine_table, -sine_table
        )
        key_raw = rotate(local_key_grad.reshape(tok_rows, HEADS, HEAD), cosine_table, -sine_table)
        grad_projected = jnp.concatenate(
            [query_raw.reshape(tok_rows, D), key_raw.reshape(tok_rows, D), local_value_grad], axis=1
        ).astype(jnp.bfloat16)
        qkv_weight_grad = jnp.einsum(
            "td,te->de", normed_attn, grad_projected, preferred_element_type=jnp.float32
        )
        qkv_bias_grad = jnp.sum(grad_projected.astype(jnp.float32), axis=0)
        grad_normed_attn = jnp.einsum(
            "te,de->td", grad_projected, proj_qkv, preferred_element_type=jnp.float32
        )
        _, norm_pull = jax.vjp(
            both_norms,
            saved_stream,
            gain_attn.astype(jnp.float32),
            shift_attn.astype(jnp.float32),
            gain_mlp.astype(jnp.float32),
            shift_mlp.astype(jnp.float32),
        )
        grad_input, attn_gain_grad, attn_shift_grad, mlp_gain_grad, mlp_shift_grad = norm_pull(
            (grad_normed_attn, grad_normed_mlp)
        )
        grad_stream = grad_stream + grad_input
        summed = (
            lax.psum_scatter(
                flatten_rows(qkv_weight_grad), ("dp", "cp"), scatter_dimension=0, tiled=True
            ),
            lax.psum_scatter(qkv_bias_grad, ("dp", "cp"), scatter_dimension=0, tiled=True),
            lax.psum_scatter(
                flatten_rows(attn_weight_grad), ("dp", "cp"), scatter_dimension=0, tiled=True
            ),
            lax.psum_scatter(bias_grad, ("dp", "cp"), scatter_dimension=0, tiled=True),
            lax.psum_scatter(
                flatten_rows(up_weight_grad), ("dp", "cp"), scatter_dimension=0, tiled=True
            ),
            lax.psum_scatter(up_bias_grad, ("dp", "cp"), scatter_dimension=0, tiled=True),
            lax.psum_scatter(
                flatten_rows(down_weight_grad), ("dp", "cp"), scatter_dimension=0, tiled=True
            ),
            lax.psum_scatter(bias_grad, ("dp", "cp"), scatter_dimension=0, tiled=True),
            lax.psum_scatter(attn_gain_grad, ("dp", "cp"), scatter_dimension=0, tiled=True),
            lax.psum_scatter(attn_shift_grad, ("dp", "cp"), scatter_dimension=0, tiled=True),
            lax.psum_scatter(mlp_gain_grad, ("dp", "cp"), scatter_dimension=0, tiled=True),
            lax.psum_scatter(mlp_shift_grad, ("dp", "cp"), scatter_dimension=0, tiled=True),
        )
        per_layer[depth] = (
            summed[0].reshape(-1, 3 * D),
            summed[1],
            summed[2].reshape(-1, D),
            summed[3],
            summed[4].reshape(-1, FF),
            summed[5],
            summed[6].reshape(-1, D),
            summed[7],
            summed[8],
            summed[9],
            summed[10],
            summed[11],
        )
    stacked = [stack_layers(per_layer, member) for member in range(12)]
    return (
        stream.astype(jnp.bfloat16),
        grad_stream,
        stacked[0],
        stacked[1],
        stacked[2],
        stacked[3],
        stacked[4],
        stacked[5],
        stacked[6],
        stacked[7],
        stacked[8],
        stacked[9],
        stacked[10],
        stacked[11],
    )


TEAM = 4
TEAM_AXES = ("core", "x")
LINE_AXES = ("z", "y")
LINE = 4
MINE = (3 * D) // TEAM
HCOLS = D // TEAM
UCOLS = FF // TEAM
VMEM_BYTES = 56 * 1024 * 1024
BF = jnp.bfloat16
F32 = jnp.float32


def call(body, out_shape, name, operands, scratch=()):
    return pl.pallas_call(
        body,
        out_shape=out_shape,
        scratch_shapes=list(scratch),
        compiler_params=pltpu.CompilerParams(vmem_limit_bytes=VMEM_BYTES),
        name=name,
    )(*operands)


def shape(dims, kind):
    return jax.ShapeDtypeStruct(dims, kind)


def mm(left, right):
    return jnp.dot(left, right, preferred_element_type=F32)


def mm_t(left, right):
    return lax.dot_general(left, right, (((1,), (1,)), ((), ())), preferred_element_type=F32)


def t_mm(left, right):
    return lax.dot_general(left, right, (((0,), (0,)), ((), ())), preferred_element_type=F32)


def pick(member, pieces, wanted):
    chosen = pieces[0]
    for s in range(1, TEAM):
        chosen = jnp.where((member ^ s) == wanted, pieces[s], chosen)
    return chosen


def small_rows(vectors, depth):
    rows = []
    for vector in vectors:
        values = vector[depth : depth + 1].astype(F32)
        rows.append(
            jnp.concatenate([values, jnp.zeros((1, 128 - values.shape[1]), F32)], axis=1)
        )
    return jnp.concatenate(rows, axis=0)


def pack_body(me_ref, qkv_ref, up_ref, *refs):
    vectors, outs = [r[...] for r in refs[:8]], refs[8:]
    me = me_ref[0]
    small = jnp.concatenate([small_rows(vectors, depth) for depth in range(LAYERS)], axis=0)
    small = jnp.concatenate([small, jnp.zeros((small.shape[0], UCOLS - 128), F32)], axis=1)
    parts = [[] for _ in range(TEAM)]
    for depth in range(LAYERS):
        rows = qkv_ref.shape[1]
        qkv = qkv_ref[depth].astype(F32)
        up = up_ref[depth].astype(F32)
        blocks = up.shape[1] // (TEAM * 96)
        for p in range(TEAM):
            parts[p].append(
                jnp.concatenate(
                    [up[:, 96 * (TEAM * b + p) : 96 * (TEAM * b + p + 1)] for b in range(blocks)],
                    axis=1,
                )
            )
            parts[p].append(
                jnp.concatenate(
                    [qkv[:, D * t + HCOLS * p : D * t + HCOLS * (p + 1)] for t in range(3)]
                    + [jnp.zeros((rows, UCOLS - MINE), F32)],
                    axis=1,
                )
            )
    parts = [jnp.concatenate(group, axis=0) for group in parts]
    for s in range(TEAM):
        chosen = parts[0]
        for p in range(1, TEAM):
            chosen = jnp.where((me ^ s) == p, parts[p], chosen)
        outs[s][...] = jnp.concatenate([chosen, small], axis=0).astype(BF)


def assemble_body(me_ref, p0, p1, p2, p3, attn_ref, down_ref, *outs):
    me = me_ref[0]
    slots = [r[...].astype(F32) for r in (p0, p1, p2, p3)]
    ordered = [pick(me, slots, p) for p in range(TEAM)]
    for depth, out in enumerate(outs):
        base = 48 * depth
        up = jnp.concatenate([piece[base : base + 24] for piece in ordered], axis=0)
        qkv = jnp.concatenate([piece[base + 24 : base + 48] for piece in ordered], axis=0)
        attn = attn_ref[depth].astype(F32)
        side = jnp.concatenate([attn[:, HCOLS * n : HCOLS * (n + 1)] for n in range(4)], axis=0)
        out[0:96] = up.astype(BF)
        out[96:192] = down_ref[depth]
        out[192:288] = jnp.concatenate([qkv[:, :MINE], side], axis=1).astype(BF)
        if out.shape[0] > 288:
            small = jnp.concatenate(
                [piece[96:112, :128] for piece in ordered] + [jnp.zeros((16, D - 4 * 128), F32)],
                axis=1,
            )
            out[288:304] = small.astype(BF)


def source_team(me_ref, index):
    shift, flip = index % LINE, index // LINE
    return 2 * lax.rem(me_ref[1] + LINE - shift, LINE) + (me_ref[2] ^ flip)


def target_team(me_ref, index):
    shift, flip = index % LINE, index // LINE
    return 2 * lax.rem(me_ref[1] + shift, LINE) + (me_ref[2] ^ flip)


def place(me_ref, pieces, whole):
    for index, piece in enumerate(pieces):
        whole[source_team(me_ref, index)] = piece[...]


def hand_out(me_ref, whole, keep, sends, order):
    for s in range(LINE):
        keep[s] = whole[target_team(me_ref, s)]
    for send, slots in zip(sends, order):
        for n, s in enumerate(slots):
            send[n] = whole[target_team(me_ref, LINE + s)]


ALL_SLOTS = (tuple(range(LINE)),)
HALVES = ((1, 3), (2, 0))


def add_body(slots, places, me_ref, keep, received, *outs):
    for s, n, out in zip(slots, places, outs):
        out[...] = (keep[s].astype(F32) + received[n].astype(F32)).astype(BF)


def line_sum_body(me_ref, own, r1, r2, r3, keep_ref, send_ref):
    for f, out in enumerate((keep_ref, send_ref)):
        total = own[f].astype(F32) + r1[f].astype(F32) + r2[f].astype(F32) + r3[f].astype(F32)
        out[...] = total.astype(out.dtype)


def layer_vectors(me_ref, whole, depth):
    me = me_ref[0]
    small = [whole[k].astype(F32) for k in range(2 * LINE)]
    fields = [block[8 * depth : 8 * (depth + 1)] for block in small]
    shared = jnp.concatenate(
        [block[2:8, 128 * p : 128 * p + 24] for block in fields for p in range(TEAM)], axis=1
    )
    up_rows, qkv_rows = [], []
    qkv = jnp.concatenate(
        [block[0:1, 128 * p : 128 * p + 72] for block in fields for p in range(TEAM)], axis=1
    )
    for p in range(TEAM):
        up_rows.append(
            jnp.concatenate([block[1:2, 128 * p : 128 * p + 96] for block in fields], axis=1)
        )
        qkv_rows.append(
            jnp.concatenate(
                [qkv[:, D * t + HCOLS * p : D * t + HCOLS * (p + 1)] for t in range(3)]
                + [jnp.zeros((1, D - MINE), F32)],
                axis=1,
            )
        )
    up_mine, qkv_mine = up_rows[0], qkv_rows[0]
    for p in range(1, TEAM):
        up_mine = jnp.where(me == p, up_rows[p], up_mine)
        qkv_mine = jnp.where(me == p, qkv_rows[p], qkv_mine)
    return jnp.concatenate([shared, up_mine, qkv_mine], axis=0)


def attn_weights(whole):
    qkv = whole[:, 0:96, :][:, :, :MINE].reshape(D, MINE)
    side = whole[:, 0:96, MINE:].astype(F32)
    out = jnp.concatenate(
        [side[:, 24 * n : 24 * (n + 1), :].reshape(HCOLS, HCOLS) for n in range(4)], axis=1
    )
    return qkv, out.astype(BF)


def project(scaled, vec, weight, cosine, sine):
    normed = (scaled * vec[0:1] + vec[1:2]).astype(BF)
    projected = mm(normed, weight) + vec[7:8, :MINE]
    turned = turn(projected[:, : 2 * HCOLS], cosine, sine)
    queries = (turned[:, :HCOLS] * 0.125).astype(BF)
    keys = turned[:, HCOLS:].astype(BF)
    values = projected[:, 2 * HCOLS :].astype(BF)
    return normed, queries, keys, values


def attend_body(me_ref, x0, x1, x2, x3, *refs):
    pieces, smalls = refs[:8], refs[8:16]
    cos_ref, sin_ref, mask_ref, y_ref, vec_ref, whole, small = refs[16:]
    place(me_ref, pieces, whole)
    place(me_ref, smalls, small)
    for depth in range(LAYERS):
        vec_ref[depth] = layer_vectors(me_ref, small, depth)
    vec = vec_ref[0]
    weight, out_weight = attn_weights(whole)
    for g, (first, second) in enumerate(((x0, x1), (x2, x3))):
        rows = pl.ds(PAIR * g, PAIR)
        scaled, _ = norm_parts(two_slots(first[...], second[...]))
        _, queries, keys, values = project(scaled, vec, weight, cos_ref[rows, :], sin_ref[rows, :])
        total = jnp.zeros((PAIR, HCOLS), F32)
        for head in range(HEADS // TEAM):
            owned = head_mask(PAIR, head)
            scores = mm_t(jnp.where(owned, queries, jnp.zeros_like(queries)), keys) + mask_ref[g]
            weights = jnp.exp(scores - jnp.max(scores, axis=-1, keepdims=True))
            below = jnp.sum(weights, axis=-1, keepdims=True)
            total = total + jnp.where(owned, mm(weights.astype(BF), values) / below, 0.0)
        y_ref[rows, :] = mm(total.astype(BF), out_weight)


def store_pair(g, result, own, near, far):
    if g == 0:
        own[...] = result[0:TOK]
        near[...] = result[TOK:]
    else:
        far[...] = result.astype(BF)


def mlp_body(me_ref, x0, x1, x2, x3, *refs):
    pieces, (vec_ref, a_ref, y0, y1, y23, whole) = refs[:8], refs[8:]
    place(me_ref, pieces, whole)
    vec = vec_ref[0]
    up = whole[:, 0:96, :].reshape(D, UCOLS)
    down = whole[:, 96:192, :].reshape(UCOLS, D)
    for g, (first, second) in enumerate(((x0, x1), (x2, x3))):
        rows = pl.ds(PAIR * g, PAIR)
        scaled, _ = norm_parts(two_slots(first[...], second[...]))
        normed = (scaled * vec[2:3] + vec[3:4]).astype(BF)
        before = mm(normed, up) + vec[6:7]
        hidden = (before * (0.5 * (1.0 + lax.erf(before * (1.0 / math.sqrt(2.0)))))).astype(BF)
        result = mm(hidden, down) + a_ref[rows, :]
        store_pair(g, result, y0, y1, y23)


def mlp_both_body(depth, last, me_ref, x0, x1, x2, x3, g0, g1, g2, g3, *refs):
    pieces, vec_ref, (dn_ref, sum_ref), refs = refs[:8], refs[8], refs[9:11], refs[11:]
    if last:
        y_ref, refs = refs[0], refs[1:]
    whole, grads, c_s, hid_s, du_s, gb_s = refs[-6:]
    place(me_ref, pieces, whole)
    vec = vec_ref[depth]
    up = whole[:, 0:96, :].reshape(D, UCOLS)
    down = whole[:, 96:192, :].reshape(UCOLS, D)
    gain_sum = jnp.zeros((1, D), F32)
    shift_sum = jnp.zeros((1, D), F32)
    bias_sum = jnp.zeros((1, D), F32)
    up_sum = jnp.zeros((1, UCOLS), F32)
    for g, (first, second, g_first, g_second) in enumerate(((x0, x1, g0, g1), (x2, x3, g2, g3))):
        rows = pl.ds(PAIR * g, PAIR)
        scaled, _ = norm_parts(two_slots(first[...], second[...]))
        normed = (scaled * vec[2:3] + vec[3:4]).astype(BF)
        c_s[rows, :] = normed
        low = jnp.concatenate([g_first[...], g_second[...]], axis=0)
        gb_s[rows, :] = low
        hidden, slope = gelu_parts(mm(normed, up) + vec[6:7])
        hidden = hidden.astype(BF)
        hid_s[rows, :] = hidden
        if last:
            y_ref[rows, :] = mm(hidden, down)
        du = (mm_t(low, down) * slope).astype(BF)
        du_s[rows, :] = du
        dc = mm_t(du, up)
        dn_ref[rows, :] = dc * vec[2:3]
        gain_sum = gain_sum + jnp.sum(dc * scaled, axis=0, keepdims=True)
        shift_sum = shift_sum + jnp.sum(dc, axis=0, keepdims=True)
        bias_sum = bias_sum + jnp.sum(low.astype(F32), axis=0, keepdims=True)
        up_sum = up_sum + jnp.sum(du.astype(F32), axis=0, keepdims=True)
    grads[:, 0:96, :] = t_mm(c_s[...], du_s[...]).reshape(-1, 96, UCOLS).astype(BF)
    grads[:, 96:192, :] = t_mm(hid_s[...], gb_s[...]).reshape(-1, 96, D).astype(BF)
    if last:
        for s, out in enumerate(refs[0:LINE]):
            for f in range(2):
                out[f] = grads[target_team(me_ref, LINE * f + s), 0:EARLY, :]
        keep, send = refs[LINE : LINE + 2]
        for s in range(LINE):
            keep[s] = grads[target_team(me_ref, s), EARLY:192, :]
            send[s] = grads[target_team(me_ref, LINE + s), EARLY:192, :]
    else:
        hand_out(me_ref, grads, refs[0], refs[1:3], HALVES)
    sum_ref[...] = jnp.concatenate(
        [bias_sum, up_sum, gain_sum, shift_sum, jnp.zeros((4, D), F32)], axis=0
    )


def attend_both_body(depth, last, me_ref, x0, x1, x2, x3, g0, g1, g2, g3, *refs):
    pieces, (vec_ref, cos_ref, sin_ref, mask_ref, dn_ref, sum_ref) = refs[:8], refs[8:14]
    refs = refs[14:]
    if last:
        y_ref, refs = refs[0], refs[1:]
    blocks, (n0, n1, n23) = refs[:2], refs[2:5]
    whole, grads, a_s, dp_s, o_s, gb_s = refs[-6:]
    place(me_ref, pieces, whole)
    vec = vec_ref[depth]
    weight, out_weight = attn_weights(whole)
    gain_sum = jnp.zeros((1, D), F32)
    shift_sum = jnp.zeros((1, D), F32)
    bias_sum = jnp.zeros((1, MINE), F32)
    for g, (first, second, g_first, g_second) in enumerate(((x0, x1, g0, g1), (x2, x3, g2, g3))):
        rows = pl.ds(PAIR * g, PAIR)
        cosine, sine = cos_ref[rows, :], sin_ref[rows, :]
        scaled, _ = norm_parts(two_slots(first[...], second[...]))
        normed, queries, keys, values = project(scaled, vec, weight, cosine, sine)
        a_s[rows, :] = normed
        low = jnp.concatenate([g_first[...], g_second[...]], axis=0)
        gb_s[rows, :] = low
        grad_o = mm_t(low, out_weight).astype(BF)
        zero = jnp.zeros_like(queries)
        out = jnp.zeros((PAIR, HCOLS), F32)
        dq = jnp.zeros((PAIR, HCOLS), F32)
        dk = jnp.zeros((PAIR, HCOLS), F32)
        dv = jnp.zeros((PAIR, HCOLS), F32)
        for head in range(HEADS // TEAM):
            owned = head_mask(PAIR, head)
            scores = mm_t(jnp.where(owned, queries, zero), keys) + mask_ref[g]
            weights = jnp.exp(scores - jnp.max(scores, axis=-1, keepdims=True))
            weights = weights / jnp.sum(weights, axis=-1, keepdims=True)
            rounded = weights.astype(BF)
            dweights = mm_t(jnp.where(owned, grad_o, zero), values)
            delta = jnp.sum(weights * dweights, axis=-1, keepdims=True)
            dscores = (weights * (dweights - delta)).astype(BF)
            out = out + jnp.where(owned, mm(rounded, values), 0.0)
            dq = dq + jnp.where(owned, mm(dscores, keys), 0.0)
            dk = dk + jnp.where(owned, t_mm(dscores, queries), 0.0)
            dv = dv + jnp.where(owned, t_mm(rounded, grad_o), 0.0)
        o_s[rows, :] = out.astype(BF)
        both = turn(jnp.concatenate([dq * 0.125, dk], axis=1), cosine, -sine)
        dproj = jnp.concatenate([both, dv], axis=1).astype(BF)
        dp_s[rows, :] = dproj
        bias_sum = bias_sum + jnp.sum(dproj.astype(F32), axis=0, keepdims=True)
        da = mm_t(dproj, weight)
        gain_sum = gain_sum + jnp.sum(da * scaled, axis=0, keepdims=True)
        shift_sum = shift_sum + jnp.sum(da, axis=0, keepdims=True)
        dn = dn_ref[rows, :] + da * vec[0:1]
        store_pair(g, dn, n0, n1, n23)
        if last:
            result = y_ref[rows, :] + mm(out.astype(BF), out_weight)
            store_pair(g, result, *refs[5:8])
    qkv_grad = t_mm(a_s[...], dp_s[...]).reshape(-1, 96, MINE)
    out_grad = t_mm(o_s[...], gb_s[...])
    side = jnp.concatenate(
        [out_grad[:, HCOLS * n : HCOLS * (n + 1)].reshape(-1, 24, HCOLS) for n in range(4)], axis=1
    )
    grads[:, 0:96, :] = jnp.concatenate([qkv_grad, side], axis=2).astype(BF)
    sums = sum_ref[...]
    vectors = jnp.concatenate([sums[0:2], gain_sum, shift_sum, sums[2:4]], axis=0)
    me = me_ref[0]
    spread = jnp.concatenate(
        [
            jnp.where(me == p, bias_sum[:, HCOLS * t : HCOLS * (t + 1)], 0.0)
            for t in range(3)
            for p in range(TEAM)
        ],
        axis=1,
    )
    for k in range(2 * LINE):
        shared = jnp.concatenate(
            [vectors[:, 96 * k : 96 * (k + 1)], jnp.zeros((6, D - 96), F32)], axis=1
        )
        bias = jnp.concatenate(
            [spread[:, 288 * k : 288 * (k + 1)], jnp.zeros((1, D - 288), F32)], axis=1
        )
        grads[k, 96:112, :] = jnp.concatenate([shared, bias, jnp.zeros((9, D), F32)], axis=0).astype(BF)
    hand_out(me_ref, grads, blocks[0], blocks[1:], ALL_SLOTS)


def residual_body(me_ref, x_ref, y0, y1, y2, vec_ref, out_ref, low_ref):
    depth = 0 if x_ref.dtype == BF else 1
    total = y0[...] + y1[...].astype(F32) + y2[...].astype(F32)
    result = x_ref[...].astype(F32) + total + (vec_ref[depth, 4:5] + vec_ref[depth, 5:6])
    out_ref[...] = result
    low_ref[...] = result.astype(BF)

def norm_parts(stream):
    centered = stream - jnp.mean(stream, axis=-1, keepdims=True)
    spread = jnp.mean(centered * centered, axis=-1, keepdims=True)
    inverse = lax.rsqrt(spread + 1e-05)
    return centered * inverse, inverse


def two_slots(first, second):
    return jnp.concatenate([first[0:TOK].astype(F32), second[0:TOK].astype(F32)], axis=0)


TOK = 128
EARLY = 48
PAIR = 2 * TOK


def turn(block, cosine, sine):
    lane = lax.broadcasted_iota(jnp.int32, (block.shape[0], 128), 1) % HEAD
    tiles = []
    for t in range(block.shape[1] // 128):
        tile = block[:, 128 * t : 128 * (t + 1)]
        swapped = jnp.where(
            lane < ROT // 2, pltpu.roll(tile, 128 - ROT // 2, 1), pltpu.roll(tile, ROT // 2, 1)
        )
        tiles.append(tile * cosine + swapped * sine)
    return jnp.concatenate(tiles, axis=1)


def head_mask(rows, head):
    lane = lax.broadcasted_iota(jnp.int32, (rows, HCOLS), 1)
    return (lane >= head * HEAD) & (lane < (head + 1) * HEAD)


def gelu_parts(u):
    cdf = 0.5 * (1.0 + lax.erf(u * (1.0 / math.sqrt(2.0))))
    density = jnp.exp(-0.5 * u * u) * (1.0 / math.sqrt(2.0 * math.pi))
    return u * cdf, cdf + u * density


def norm_back_body(me_ref, x_ref, g_ref, n0, n1, n2, out_ref, low_ref):
    scaled, inverse = norm_parts(x_ref[...].astype(F32))
    dn = n0[...] + n1[...].astype(F32) + n2[...].astype(F32)
    centered = dn - jnp.mean(dn, axis=-1, keepdims=True)
    moment = jnp.mean(dn * scaled, axis=-1, keepdims=True)
    result = g_ref[...].astype(F32) + inverse * (centered - scaled * moment)
    out_ref[...] = result
    low_ref[...] = result.astype(BF)


def total(group):
    result = group[0].astype(F32)
    for term in group[1:]:
        result = result + term.astype(F32)
    return result


def by_owner(me_ref, parts, outs, start):
    me = me_ref[0]
    for s, out in enumerate(outs):
        piece = parts[0]
        for p in range(1, TEAM):
            piece = jnp.where((me ^ s) == p, parts[p], piece)
        out[start : start + 32] = piece.astype(BF)


def split_body(early, me_ref, *refs):
    outs, (down_ref, attn_ref, small_ref), refs = refs[-7:-3], refs[-3:], refs[:-7]
    split_attend(me_ref, refs[:5], outs, attn_ref, small_ref)
    refs = refs[5:]
    rest = total([refs[0][0], refs[1][0], refs[2][...], refs[3][...], refs[4][...]])
    if early:
        rest = jnp.concatenate([total([refs[5][...], refs[6][...]]), rest], axis=0)
    down_ref[...] = rest[96:192]
    blank = jnp.zeros((8, D), F32)
    parts = [
        jnp.concatenate([rest[24 * p : 24 * (p + 1)], blank], axis=0) for p in range(TEAM)
    ]
    by_owner(me_ref, parts, outs, 0)


def split_attend(me_ref, refs, outs, attn_ref, small_ref):
    me = me_ref[0]
    attn = total([refs[0][0], refs[1][0], refs[2][...], refs[3][...], refs[4][...]])
    side = attn[0:96, MINE:]
    attn_ref[...] = jnp.concatenate(
        [side[24 * n : 24 * (n + 1)] for n in range(4)], axis=1
    ).astype(BF)
    qkv = jnp.concatenate([attn[0:96, :MINE], jnp.zeros((96, UCOLS - MINE), F32)], axis=1)
    small = attn[96:112]
    parts, bias = [], jnp.zeros((1, 24), F32)
    for p in range(TEAM):
        rows = slice(24 * p, 24 * (p + 1))
        gains = jnp.concatenate([small[2:6, rows], jnp.zeros((4, D - 24), F32)], axis=1)
        qkv_bias = jnp.concatenate(
            [small[6:7, 72 * p : 72 * (p + 1)], jnp.zeros((1, D - 72), F32)], axis=1
        )
        parts.append(jnp.concatenate([qkv[rows], gains, qkv_bias, jnp.zeros((3, D), F32)], axis=0))
        bias = jnp.where(me == p, small[0:1, rows], bias)
    small_ref[...] = jnp.concatenate(
        [
            jnp.concatenate([bias, jnp.zeros((1, 104), F32)], axis=1),
            small[1:2, :128],
            jnp.zeros((6, 128), F32),
        ],
        axis=0,
    )
    by_owner(me_ref, parts, outs, 32)


def unpack_body(me_ref, *refs):
    me = me_ref[0]
    (
        qkv_ref, qkv_b_ref, attn_ref, attn_b_ref, up_ref, up_b_ref, down_ref,
        ga_ref, sa_ref, gm_ref, sm_ref,
    ) = refs[7 * LAYERS :]
    gain_refs = (ga_ref, sa_ref, gm_ref, sm_ref)
    for depth in range(LAYERS):
        group = refs[7 * depth : 7 * (depth + 1)]
        down_rows, own_small, attn_rows = group[TEAM:]
        slots = [r[...].astype(F32) for r in group[:TEAM]]
        ordered = [pick(me, slots, p) for p in range(TEAM)]
        blocks = FF // (96 * TEAM)
        up_ref[depth] = jnp.concatenate(
            [ordered[p][0:24, 96 * b : 96 * (b + 1)] for b in range(blocks) for p in range(TEAM)],
            axis=1,
        )
        qkv_ref[depth] = jnp.concatenate(
            [
                ordered[p][32:56, HCOLS * t : HCOLS * (t + 1)]
                for t in range(3)
                for p in range(TEAM)
            ],
            axis=1,
        )
        attn_ref[depth] = attn_rows[...].astype(F32)
        down_ref[depth] = down_rows[...]
        small = slots[0][56:64, :128] + slots[1][56:64, :128]
        small = small + slots[2][56:64, :128] + slots[3][56:64, :128]
        for n, ref in enumerate(gain_refs):
            ref[depth : depth + 1] = small[n : n + 1, :24]
        qkv_b_ref[depth : depth + 1] = small[4:5, :72]
        attn_b_ref[depth : depth + 1] = own_small[0:1, :24]
        up_b_ref[depth : depth + 1] = own_small[1:2, :96]


def team_send(piece, slot):
    flips = [(m, m ^ slot) for m in range(TEAM)]
    return lax.ppermute(piece, TEAM_AXES, flips)


def line_shift(piece, shift):
    size = lax.axis_size("z")
    return lax.ppermute(piece, "z", [(i, (i + shift) % size) for i in range(size)])


def line_flip(piece):
    return lax.ppermute(piece, "y", [(0, 1), (1, 0)])


def after(value, *others):
    return lax.optimization_barrier((value, *others))[0]


def line_near(piece):
    first = line_shift(piece, 1)
    third = line_shift(piece, 3)
    return [piece, first, line_shift(after(piece, first, third), 2), third]


def local_team(
    tokens, segment_ids, cotangent, qkv_weight, qkv_bias, attn_weight, attn_bias,
    up_weight, up_bias, down_weight, down_bias, attn_gain, attn_shift, mlp_gain, mlp_shift,
):
    lines = lax.axis_size("z") * lax.axis_size("y")
    world = lines * TEAM
    member = lax.axis_index("core") * 2 + lax.axis_index("x")
    me = jnp.stack([member, lax.axis_index("z"), lax.axis_index("y")]).astype(jnp.int32)
    everywhere = LINE_AXES + TEAM_AXES
    tok_all = TEAM * TOK
    whole_spec = pl.BlockSpec(memory_space=pltpu.VMEM)

    def run(body, out_shape, name, operands, scratch=()):
        specs = [whole_spec if isinstance(x, jax.Array) else x[1] for x in operands]
        return pl.pallas_call(
            body,
            grid=(1,),
            out_shape=out_shape,
            in_specs=[pl.BlockSpec(memory_space=pltpu.SMEM)] + specs,
            scratch_shapes=[pltpu.VMEM(dims, kind) for dims, kind in scratch],
            compiler_params=pltpu.CompilerParams(vmem_limit_bytes=VMEM_BYTES),
            name=name,
        )(me, *[x if isinstance(x, jax.Array) else x[0] for x in operands])

    def part(rows, start):
        return pl.BlockSpec((rows, D), lambda i: (start // rows, 0))

    def one_of(array, index):
        return (array, pl.BlockSpec((1,) + array.shape[1:], lambda i: (index, 0, 0)))

    def exchange(blocks):
        return [blocks[0]] + [team_send(blocks[s], s) for s in range(1, TEAM)]

    small = (
        qkv_bias, up_bias, attn_gain, attn_shift, mlp_gain, mlp_shift, attn_bias, down_bias
    )
    packed = run(
        pack_body, [shape((112, D), BF)] * TEAM, "pack_weights", (qkv_weight, up_weight, *small)
    )
    spread = [(i, TEAM * (i % lines) + i // lines) for i in range(world)]
    gather_back = [(b, a) for a, b in spread]
    attn_piece = lax.ppermute(attn_weight, everywhere, spread)
    chunks = run(
        assemble_body,
        [shape((304, D), BF), shape((288, D), BF)],
        "assemble_weights",
        (*exchange(packed), attn_piece, down_weight),
    )
    near = line_near(chunks[0])
    pieces = [near + [line_flip(p) for p in near]]
    near = line_near(after(chunks[1], near[2], pieces[0][5], pieces[0][7]))
    pieces.append(near + [line_flip(p) for p in near])
    m_parts = [[(p, part(192, 0)) for p in group] for group in pieces]
    a_parts = [[(p, part(96, 192)) for p in group] for group in pieces]
    small_parts = [(p, part(16, 288)) for p in pieces[0]]

    def gather_team(piece, *others):
        other = after(team_send(piece, 1), *others)
        return piece, other, team_send(jnp.concatenate([piece, other], axis=0), 2)

    def slots_of(gathered, start=0):
        piece, other, far = gathered
        size = piece.shape[0]
        return [
            (piece, part(TOK, start)), (other, part(TOK, start)),
            (far, part(TOK, start)), (far, part(TOK, size + start)),
        ]

    def sum_team(own, near, far, *others):
        other = after(team_send(far, 2), *others)
        both = (near + other[TOK:].astype(F32)).astype(BF)
        return own, (other, part(TOK, 0)), team_send(both, 1)

    ids_rows = jnp.pad(segment_ids.astype(BF)[None, :], ((0, TOK - 1), (0, D - TOK)))
    load = jnp.concatenate([tokens, cotangent, ids_rows], axis=0)
    loads = gather_team(after(load, pieces[0][1], pieces[0][3], pieces[0][4]), pieces[0][2], pieces[0][5], pieces[0][7])
    token_slots = slots_of(loads)
    here = lax.axis_index("x")
    rows = jnp.arange(TOK, dtype=jnp.int32)
    places = jnp.concatenate([here * TOK + rows, (1 - here) * TOK + rows])
    masks, cosines, sines = [], [], []
    lane = jnp.arange(128, dtype=jnp.int32) % HEAD
    inverse = 10000.0 ** (-(lane % (ROT // 2) * 2).astype(F32) / ROT)
    id_rows = [
        loads[0][2 * TOK, :TOK], loads[1][2 * TOK, :TOK],
        loads[2][2 * TOK, :TOK], loads[2][5 * TOK, :TOK],
    ]
    for g in range(2):
        ids = jnp.concatenate(id_rows[2 * g : 2 * g + 2]).astype(F32)
        visible = (places[None, :] <= places[:, None]) & (ids[None, :] == ids[:, None])
        masks.append(jnp.where(visible, 0.0, -1e30).astype(F32))
        position = places - jnp.sum((ids[None, :] < ids[:, None]).astype(jnp.int32), axis=1)
        phases = position.astype(F32)[:, None] * inverse[None, :]
        cosines.append(jnp.where(lane[None, :] < ROT, jnp.cos(phases), 1.0))
        sign = jnp.where(lane < ROT // 2, -1.0, jnp.where(lane < ROT, 1.0, 0.0))
        sines.append(jnp.sin(phases) * sign[None, :])
    mask = jnp.stack(masks)
    cosine, sine = jnp.concatenate(cosines), jnp.concatenate(sines)

    partials = [shape((TOK, D), F32)] * 2 + [shape((PAIR, D), BF)]
    stream_pair = [shape((TOK, D), F32), shape((TOK, D), BF)]
    wide = ((tok_all, D), BF)

    attn_out, vec = run(
        attend_body,
        [shape((tok_all, D), F32), shape((LAYERS, 8, D), F32)],
        "attend_forward",
        (*token_slots, *a_parts[0], *small_parts, cosine, sine, mask),
        [((lines, 96, D), BF), ((lines, 16, D), BF)],
    )
    y = run(
        mlp_body,
        partials,
        "mlp_forward",
        (*token_slots, *m_parts[0], vec, attn_out),
        [((lines, 192, D), BF)],
    )

    def residual(stream, blocks):
        return run(residual_body, stream_pair, "residual", (stream, *sum_team(*blocks), vec))

    stream, low = residual(tokens, (after(y[0], pieces[1][4]), *y[1:]))
    streams = [tokens, stream]
    slots = [token_slots, slots_of(gather_team(low, pieces[1][5], pieces[1][7]))]

    grad = cotangent
    grad_slots = slots_of(loads, TOK)
    outs = [None] * LAYERS
    block_m, block_a = shape((192, D), BF), shape((112, D), BF)

    def mlp_back(depth, slots, grad_slots, grads):
        last = depth == LAYERS - 1
        return run(
            partial(mlp_both_body, depth, last),
            [shape((tok_all, D), F32), shape((8, D), F32)]
            + ([shape((tok_all, D), F32)] if last else [])
            + grads,
            "mlp_both",
            (*slots, *grad_slots, *m_parts[depth], vec),
            [((lines, 192, D), BF), ((lines, 192, D), BF), wide, wide, wide, wide],
        )

    def attend_back(depth, slots, grad_slots, rest, *others):
        last = depth == LAYERS - 1
        result = run(
            partial(attend_both_body, depth, last),
            [shape((4, 112, D), BF)] * 2 + partials + (partials if last else []),
            "attend_both",
            (*slots, *grad_slots, *a_parts[depth], vec, cosine, sine, mask, *rest),
            [
                ((lines, 96, D), BF),
                ((lines, 112, D), BF),
                wide,
                ((tok_all, MINE), BF),
                ((tok_all, HCOLS), BF),
                wide,
            ],
        )
        return result[0], line_flip(after(result[1], *others)), result[2:5], result[5:]

    def norm_back(depth, grad, received):
        return run(
            norm_back_body, stream_pair, "norm_backward", (streams[depth], grad, *received)
        )

    def add(kind, keep, other, slots, places, name):
        return run(partial(add_body, slots, places), [kind] * len(slots), name, (keep, other))

    def shifts(sums):
        return [line_shift(piece, s + 1) for s, piece in enumerate(sums)]

    def split(attend, mlp, early=()):
        keep, other, *sums = attend
        m_keep, m_other, *m_sums = mlp
        mine = run(
            partial(split_body, bool(early)),
            [shape((64, D), BF)] * TEAM
            + [shape((96, D), F32), shape((24, D), BF), shape((8, 128), F32)],
            "split_gradients",
            (one_of(keep, 0), one_of(other, 0), *sums, one_of(m_keep, 0), m_other, *m_sums, *early),
        )
        attn_rows = lax.ppermute(mine[TEAM + 1], everywhere, gather_back)
        return exchange(mine[:TEAM]) + [mine[TEAM], mine[TEAM + 2], attn_rows]

    early_block, late_four = shape((2, EARLY, D), BF), shape((4, 192 - EARLY, D), BF)
    dn, sum_m, y_part, e0, e1, e2, e3, m_keep1, m_send1 = mlp_back(
        1, slots[1], grad_slots, [early_block] * 4 + [late_four] * 2
    )
    early = shifts((e1, e2, e3))
    m_other1 = line_flip(m_send1)
    a_keep1, a_other1, ns, ys = attend_back(1, slots[1], grad_slots, (dn, sum_m, y_part))
    ns = (ns[0], ns[1], after(ns[2], *early))
    grad, low = norm_back(1, grad, sum_team(*ns, m_other1))
    m_added1 = add(
        shape((192 - EARLY, D), BF), m_keep1, after(m_other1, low), (1, 2, 3), (1, 2, 3), "add_mlp"
    )
    m_sums1 = shifts(m_added1)
    gathered = gather_team(low)
    grad_slots = slots_of((after(gathered[0], *m_added1), *gathered[1:]))
    dn, sum_m, m_keep0, m_first0, m_second0 = mlp_back(
        0, slots[0], grad_slots, [shape((4, 192, D), BF)] + [shape((2, 192, D), BF)] * 2
    )
    a_added1 = add(block_a, a_keep1, after(a_other1, dn, *m_sums1), (1, 2, 3), (1, 2, 3), "add_attend")
    a_sums1 = shifts(a_added1)
    m_first0 = line_flip(after(m_first0, *a_added1))
    m_second0 = line_flip(after(m_second0, *a_added1))
    a_keep0, a_other0, ns, _ = attend_back(
        0, slots[0], grad_slots, (after(dn, *a_added1), sum_m), m_second0
    )
    m1, m3 = add(
        block_m, m_keep0, after(m_first0, a_keep0, *a_sums1), HALVES[0], (0, 1), "add_first"
    )
    first_added = m1
    m1, m3 = line_shift(m1, 1), line_shift(m3, 3)
    (m2,) = add(block_m, m_keep0, after(m_second0, m1, m3), HALVES[1][:1], (0,), "add_second")
    grad, _ = norm_back(0, grad, sum_team(*ns))
    _, activations = residual(streams[1], (ys[0], ys[1], after(ys[2], first_added)))
    e_keep, e_send = run(
        line_sum_body,
        [shape((EARLY, D), F32), shape((EARLY, D), BF)],
        "line_sum",
        (e0, after(early[0], first_added), early[1], early[2]),
    )
    outs[1] = split(
        (a_keep1, a_other1, *a_sums1),
        (m_keep1, one_of(m_other1, 0), *m_sums1),
        (e_keep, line_flip(e_send)),
    )
    a_added0 = add(
        block_a,
        a_keep0,
        after(a_other0, m2, grad, activations, outs[1][0]),
        (1, 2, 3),
        (1, 2, 3),
        "add_attend",
    )
    m2 = line_shift(m2, 2)
    a_sums0 = shifts(a_added0)
    outs[0] = split((a_keep0, a_other0, *a_sums0), (m_keep0, one_of(m_second0, 1), m1, m2, m3))
    row_24 = shape((LAYERS, 24), F32)
    final = run(
        unpack_body,
        [
            shape((LAYERS, 24, 3 * D), F32), shape((LAYERS, 72), F32),
            shape((LAYERS, 24, D), F32), row_24,
            shape((LAYERS, 24, FF), F32), shape((LAYERS, 96), F32),
            shape((LAYERS, 96, D), F32), row_24, row_24, row_24, row_24,
        ],
        "unpack_gradients",
        [array for group in outs for array in group],
    )
    return (activations, grad, *final[:7], final[3], *final[7:])


def whole_mesh_solution(mesh):
    in_specs = (
        P(("dp", "cp"), None),
        P(("dp", "cp")),
        P(("dp", "cp"), None),
        P(None, ("dp", "cp"), None),
        P(None, ("dp", "cp")),
        P(None, ("dp", "cp"), None),
        P(None, ("dp", "cp")),
        P(None, ("dp", "cp"), None),
        P(None, ("dp", "cp")),
        P(None, ("dp", "cp"), None),
        P(None, ("dp", "cp")),
        P(None, ("dp", "cp")),
        P(None, ("dp", "cp")),
        P(None, ("dp", "cp")),
        P(None, ("dp", "cp")),
    )
    out_specs = (
        P(("dp", "cp"), None),
        P(("dp", "cp"), None),
        P(None, ("dp", "cp"), None),
        P(None, ("dp", "cp")),
        P(None, ("dp", "cp"), None),
        P(None, ("dp", "cp")),
        P(None, ("dp", "cp"), None),
        P(None, ("dp", "cp")),
        P(None, ("dp", "cp"), None),
        P(None, ("dp", "cp")),
        P(None, ("dp", "cp")),
        P(None, ("dp", "cp")),
        P(None, ("dp", "cp")),
        P(None, ("dp", "cp")),
    )
    return jax.shard_map(local, mesh=mesh, in_specs=in_specs, out_specs=out_specs, check_vma=False)


def solution(mesh):
    teams = mesh.shape["dp"] // 2
    if mesh.shape["cp"] != 2 or teams != 2 * LINE or teams * TEAM * 24 != D:
        return whole_mesh_solution(mesh)
    split_mesh = Mesh(mesh.devices.reshape(teams // 2, 2, 2, 2), ("z", "y", "core", "x"))
    every = ("z", "y", "core", "x")
    row = P(every, None)
    matrix, vector = P(None, every, None), P(None, every)
    in_specs = (row, P(every), row) + (matrix, vector) * 4 + (vector,) * 4
    out_specs = (row, row) + (matrix, vector) * 4 + (vector,) * 4
    return jax.shard_map(
        local_team, mesh=split_mesh, in_specs=in_specs, out_specs=out_specs, check_vma=False
    )
```

```python
from functools import partial
import math

import jax
import jax.numpy as jnp
from jax import lax
from jax.experimental import pallas as pl
from jax.experimental.pallas import tpu as pltpu
from jax.sharding import Mesh, PartitionSpec as P

D = 768
HEADS = 12
HEAD = 64
FF = 3072
ROT = 16
LAYERS = 2


def layer_norm(stream, norm_gain, norm_shift):
    centered = stream - jnp.mean(stream, axis=-1, keepdims=True)
    spread = jnp.mean(centered * centered, axis=-1, keepdims=True)
    return centered * lax.rsqrt(spread + 1e-05) * norm_gain + norm_shift


def both_norms(stream, gain_attn, shift_attn, gain_mlp, shift_mlp):
    return (layer_norm(stream, gain_attn, shift_attn), layer_norm(stream, gain_mlp, shift_mlp))


def angles(positions):
    inverse = 10000.0 ** (-jnp.arange(0, ROT, 2, dtype=jnp.float32) / ROT)
    phases = positions.astype(jnp.float32)[:, None] * inverse[None, :]
    return (jnp.cos(phases)[:, None, :], jnp.sin(phases)[:, None, :])


def rotate(heads_in, cosine_table, sine_table):
    half_rot = cosine_table.shape[-1]
    first_half = heads_in[..., :half_rot]
    second_half = heads_in[..., half_rot : 2 * half_rot]
    untouched = heads_in[..., 2 * half_rot :]
    return jnp.concatenate(
        [
            first_half * cosine_table - second_half * sine_table,
            second_half * cosine_table + first_half * sine_table,
            untouched,
        ],
        axis=-1,
    )


def split_blocks(update, running, key_piece, value_piece, offset):
    piece_rows = key_piece.shape[0]
    block_rows = 512 if piece_rows > 512 and piece_rows % 512 == 0 else piece_rows
    block_count = piece_rows // block_rows
    if block_count == 1:
        return update(running, key_piece, value_piece, offset)

    def advance(state, inputs):
        key_block, value_block, start = inputs
        return (update(state, key_block, value_block, offset + start), None)

    starts = jnp.arange(block_count, dtype=jnp.int32) * block_rows
    state, _ = lax.scan(
        advance,
        running,
        (
            key_piece.reshape(block_count, block_rows, -1),
            value_piece.reshape(block_count, block_rows, -1),
            starts,
        ),
    )
    return state


def stack_layers(per_layer, member):
    return jnp.stack([layer_entry[member] for layer_entry in per_layer])


def flatten_rows(matrix):
    return matrix.reshape(matrix.shape[:-2] + (-1, 128))


def local(
    tokens,
    segment_ids,
    cotangent,
    qkv_weight,
    qkv_bias,
    attn_weight,
    attn_bias,
    up_weight,
    up_bias,
    down_weight,
    down_bias,
    attn_gain,
    attn_shift,
    mlp_gain,
    mlp_shift,
):
    tok_rows = tokens.shape[0]
    group_rows = tok_rows * lax.axis_size("cp")
    score_scale = 1.0 / math.sqrt(HEAD)
    all_segments = lax.all_gather(segment_ids, "cp", axis=0, tiled=True)
    row_index = lax.axis_index("cp") * tok_rows + jnp.arange(tok_rows, dtype=jnp.int32)
    positions = row_index - jnp.sum(
        (all_segments[None, :] < segment_ids[:, None]).astype(jnp.int32), axis=1
    )
    cosine_table, sine_table = angles(positions)

    def visible_mask(offset, block_rows):
        key_index = offset + jnp.arange(block_rows, dtype=jnp.int32)
        key_segment = lax.dynamic_slice_in_dim(all_segments, offset, block_rows)
        return (key_index[None, :] <= row_index[:, None]) & (
            key_segment[None, :] == segment_ids[:, None]
        )

    def online_step(query_heads, running, key_block, value_block, offset):
        row_max, denominator, weighted = running
        block_rows = key_block.shape[0]
        key_heads = key_block.reshape(block_rows, HEADS, HEAD)
        value_heads = value_block.reshape(block_rows, HEADS, HEAD)
        scores = (
            jnp.einsum("qhd,khd->hqk", query_heads, key_heads, preferred_element_type=jnp.float32)
            * score_scale
        )
        visible = visible_mask(offset, block_rows)
        scores = jnp.where(visible[None], scores, -1e30)
        new_max = jnp.maximum(row_max, jnp.max(scores, axis=-1))
        rescale = jnp.exp(row_max - new_max)
        weights = jnp.where(visible[None], jnp.exp(scores - new_max[..., None]), 0.0)
        denominator = denominator * rescale + jnp.sum(weights, axis=-1)
        weighted = weighted * rescale[..., None] + jnp.einsum(
            "hqk,khd->hqd",
            weights.astype(jnp.bfloat16),
            value_heads,
            preferred_element_type=jnp.float32,
        )
        return (new_max, denominator, weighted)

    stream = tokens.astype(jnp.float32)
    stored = []
    for depth in range(LAYERS):
        params = (
            lax.all_gather(qkv_weight[depth], ("dp", "cp"), axis=0, tiled=True),
            lax.all_gather(qkv_bias[depth], ("dp", "cp"), axis=0, tiled=True),
            lax.all_gather(attn_weight[depth], ("dp", "cp"), axis=0, tiled=True),
            lax.all_gather(attn_bias[depth], ("dp", "cp"), axis=0, tiled=True),
            lax.all_gather(up_weight[depth], ("dp", "cp"), axis=0, tiled=True),
            lax.all_gather(up_bias[depth], ("dp", "cp"), axis=0, tiled=True),
            lax.all_gather(down_weight[depth], ("dp", "cp"), axis=0, tiled=True),
            lax.all_gather(down_bias[depth], ("dp", "cp"), axis=0, tiled=True),
            lax.all_gather(attn_gain[depth], ("dp", "cp"), axis=0, tiled=True),
            lax.all_gather(attn_shift[depth], ("dp", "cp"), axis=0, tiled=True),
            lax.all_gather(mlp_gain[depth], ("dp", "cp"), axis=0, tiled=True),
            lax.all_gather(mlp_shift[depth], ("dp", "cp"), axis=0, tiled=True),
        )
        (
            proj_qkv,
            bias_qkv,
            proj_attn,
            bias_attn,
            proj_up,
            bias_up,
            proj_down,
            bias_down,
            gain_attn,
            shift_attn,
            gain_mlp,
            shift_mlp,
        ) = params
        normed_attn, normed_mlp = both_norms(
            stream,
            gain_attn.astype(jnp.float32),
            shift_attn.astype(jnp.float32),
            gain_mlp.astype(jnp.float32),
            shift_mlp.astype(jnp.float32),
        )
        normed_attn = normed_attn.astype(jnp.bfloat16)
        normed_mlp = normed_mlp.astype(jnp.bfloat16)
        projected = jnp.dot(
            normed_attn, proj_qkv, preferred_element_type=jnp.float32
        ) + bias_qkv.astype(jnp.float32)
        queries = rotate(
            projected[:, :D].reshape(tok_rows, HEADS, HEAD), cosine_table, sine_table
        ).astype(jnp.bfloat16)
        key_rows = (
            rotate(projected[:, D : 2 * D].reshape(tok_rows, HEADS, HEAD), cosine_table, sine_table)
            .astype(jnp.bfloat16)
            .reshape(tok_rows, D)
        )
        values = projected[:, 2 * D :].astype(jnp.bfloat16)
        initial = (
            jnp.full((HEADS, tok_rows), -1e30, jnp.float32),
            jnp.zeros((HEADS, tok_rows), jnp.float32),
            jnp.zeros((HEADS, tok_rows, HEAD), jnp.float32),
        )
        row_max, denominator, weighted = split_blocks(
            partial(online_step, queries),
            initial,
            lax.all_gather(key_rows, "cp", axis=0, tiled=True),
            lax.all_gather(values, "cp", axis=0, tiled=True),
            jnp.int32(0),
        )
        attended = jnp.transpose(weighted / denominator[..., None], (1, 0, 2)).reshape(tok_rows, D)
        log_total = row_max + jnp.log(denominator)
        attended_low = attended.astype(jnp.bfloat16)
        attn_branch = jnp.dot(
            attended_low, proj_attn, preferred_element_type=jnp.float32
        ) + bias_attn.astype(jnp.float32)
        hidden_pre = jnp.dot(
            normed_mlp, proj_up, preferred_element_type=jnp.float32
        ) + bias_up.astype(jnp.float32)
        hidden = jax.nn.gelu(hidden_pre, approximate=False).astype(jnp.bfloat16)
        mlp_branch = jnp.dot(
            hidden, proj_down, preferred_element_type=jnp.float32
        ) + bias_down.astype(jnp.float32)
        stored.append(
            (
                stream,
                normed_attn,
                normed_mlp,
                queries,
                key_rows,
                values,
                attended,
                attended_low,
                log_total,
                hidden_pre,
                hidden,
            )
        )
        stream = stream + attn_branch + mlp_branch
    grad_stream = cotangent.astype(jnp.float32)
    per_layer = [None] * LAYERS
    for depth in reversed(range(LAYERS)):
        (
            saved_stream,
            normed_attn,
            normed_mlp,
            queries,
            key_rows,
            values,
            attended,
            attended_low,
            log_total,
            hidden_pre,
            hidden,
        ) = stored[depth]
        params = (
            lax.all_gather(qkv_weight[depth], ("dp", "cp"), axis=0, tiled=True),
            lax.all_gather(qkv_bias[depth], ("dp", "cp"), axis=0, tiled=True),
            lax.all_gather(attn_weight[depth], ("dp", "cp"), axis=0, tiled=True),
            lax.all_gather(attn_bias[depth], ("dp", "cp"), axis=0, tiled=True),
            lax.all_gather(up_weight[depth], ("dp", "cp"), axis=0, tiled=True),
            lax.all_gather(up_bias[depth], ("dp", "cp"), axis=0, tiled=True),
            lax.all_gather(down_weight[depth], ("dp", "cp"), axis=0, tiled=True),
            lax.all_gather(down_bias[depth], ("dp", "cp"), axis=0, tiled=True),
            lax.all_gather(attn_gain[depth], ("dp", "cp"), axis=0, tiled=True),
            lax.all_gather(attn_shift[depth], ("dp", "cp"), axis=0, tiled=True),
            lax.all_gather(mlp_gain[depth], ("dp", "cp"), axis=0, tiled=True),
            lax.all_gather(mlp_shift[depth], ("dp", "cp"), axis=0, tiled=True),
        )
        (
            proj_qkv,
            bias_qkv,
            proj_attn,
            bias_attn,
            proj_up,
            bias_up,
            proj_down,
            bias_down,
            gain_attn,
            shift_attn,
            gain_mlp,
            shift_mlp,
        ) = params
        grad_low = grad_stream.astype(jnp.bfloat16)
        bias_grad = jnp.sum(grad_low.astype(jnp.float32), axis=0)
        attn_weight_grad = jnp.einsum(
            "td,te->de", attended_low, grad_low, preferred_element_type=jnp.float32
        )
        down_weight_grad = jnp.einsum(
            "tf,te->fe", hidden, grad_low, preferred_element_type=jnp.float32
        )
        grad_attended = jnp.einsum(
            "te,de->td", grad_low, proj_attn, preferred_element_type=jnp.float32
        ).astype(jnp.bfloat16)
        grad_hidden = jnp.einsum(
            "te,fe->tf", grad_low, proj_down, preferred_element_type=jnp.float32
        )
        _, gelu_pull = jax.vjp(partial(jax.nn.gelu, approximate=False), hidden_pre)
        grad_pre = gelu_pull(grad_hidden)[0].astype(jnp.bfloat16)
        up_weight_grad = jnp.einsum(
            "td,tf->df", normed_mlp, grad_pre, preferred_element_type=jnp.float32
        )
        up_bias_grad = jnp.sum(grad_pre.astype(jnp.float32), axis=0)
        grad_normed_mlp = jnp.einsum(
            "tf,df->td", grad_pre, proj_up, preferred_element_type=jnp.float32
        )
        all_keys, all_values = (
            lax.all_gather(key_rows, "cp", axis=0, tiled=True),
            lax.all_gather(values, "cp", axis=0, tiled=True),
        )
        grad_heads = grad_attended.reshape(tok_rows, HEADS, HEAD)
        row_dot = jnp.transpose(
            jnp.sum(
                grad_heads.astype(jnp.float32) * attended.reshape(tok_rows, HEADS, HEAD), axis=-1
            )
        )
        block_rows = 512 if group_rows > 512 and group_rows % 512 == 0 else group_rows
        block_count = group_rows // block_rows
        starts = jnp.arange(block_count, dtype=jnp.int32) * block_rows

        def back_step(grad_query, inputs):
            key_block, value_block, offset = inputs
            key_heads = key_block.reshape(block_rows, HEADS, HEAD)
            value_heads = value_block.reshape(block_rows, HEADS, HEAD)
            scores = (
                jnp.einsum("qhd,khd->hqk", queries, key_heads, preferred_element_type=jnp.float32)
                * score_scale
            )
            visible = visible_mask(offset, block_rows)
            weights = jnp.where(visible[None], jnp.exp(scores - log_total[..., None]), 0.0)
            grad_weights = jnp.einsum(
                "qhd,khd->hqk", grad_heads, value_heads, preferred_element_type=jnp.float32
            )
            grad_scores = (weights * (grad_weights - row_dot[..., None])).astype(jnp.bfloat16)
            grad_query = grad_query + jnp.einsum(
                "hqk,khd->hqd", grad_scores, key_heads, preferred_element_type=jnp.float32
            )
            key_grad = (
                jnp.einsum("hqk,qhd->khd", grad_scores, queries, preferred_element_type=jnp.float32)
                * score_scale
            )
            value_grad = jnp.einsum(
                "hqk,qhd->khd",
                weights.astype(jnp.bfloat16),
                grad_heads,
                preferred_element_type=jnp.float32,
            )
            return (
                grad_query,
                (key_grad.reshape(block_rows, D), value_grad.reshape(block_rows, D)),
            )

        grad_query, (key_grads, value_grads) = lax.scan(
            back_step,
            jnp.zeros((HEADS, tok_rows, HEAD), jnp.float32),
            (
                all_keys.reshape(block_count, block_rows, D),
                all_values.reshape(block_count, block_rows, D),
                starts,
            ),
        )
        local_key_grad, local_value_grad = (
            lax.psum_scatter(
                key_grads.reshape(group_rows, D).astype(jnp.bfloat16),
                "cp",
                scatter_dimension=0,
                tiled=True,
            ).astype(jnp.float32),
            lax.psum_scatter(
                value_grads.reshape(group_rows, D).astype(jnp.bfloat16),
                "cp",
                scatter_dimension=0,
                tiled=True,
            ).astype(jnp.float32),
        )
        query_raw = rotate(
            jnp.transpose(grad_query * score_scale, (1, 0, 2)), cosine_table, -sine_table
        )
        key_raw = rotate(local_key_grad.reshape(tok_rows, HEADS, HEAD), cosine_table, -sine_table)
        grad_projected = jnp.concatenate(
            [query_raw.reshape(tok_rows, D), key_raw.reshape(tok_rows, D), local_value_grad], axis=1
        ).astype(jnp.bfloat16)
        qkv_weight_grad = jnp.einsum(
            "td,te->de", normed_attn, grad_projected, preferred_element_type=jnp.float32
        )
        qkv_bias_grad = jnp.sum(grad_projected.astype(jnp.float32), axis=0)
        grad_normed_attn = jnp.einsum(
            "te,de->td", grad_projected, proj_qkv, preferred_element_type=jnp.float32
        )
        _, norm_pull = jax.vjp(
            both_norms,
            saved_stream,
            gain_attn.astype(jnp.float32),
            shift_attn.astype(jnp.float32),
            gain_mlp.astype(jnp.float32),
            shift_mlp.astype(jnp.float32),
        )
        grad_input, attn_gain_grad, attn_shift_grad, mlp_gain_grad, mlp_shift_grad = norm_pull(
            (grad_normed_attn, grad_normed_mlp)
        )
        grad_stream = grad_stream + grad_input
        summed = (
            lax.psum_scatter(
                flatten_rows(qkv_weight_grad), ("dp", "cp"), scatter_dimension=0, tiled=True
            ),
            lax.psum_scatter(qkv_bias_grad, ("dp", "cp"), scatter_dimension=0, tiled=True),
            lax.psum_scatter(
                flatten_rows(attn_weight_grad), ("dp", "cp"), scatter_dimension=0, tiled=True
            ),
            lax.psum_scatter(bias_grad, ("dp", "cp"), scatter_dimension=0, tiled=True),
            lax.psum_scatter(
                flatten_rows(up_weight_grad), ("dp", "cp"), scatter_dimension=0, tiled=True
            ),
            lax.psum_scatter(up_bias_grad, ("dp", "cp"), scatter_dimension=0, tiled=True),
            lax.psum_scatter(
                flatten_rows(down_weight_grad), ("dp", "cp"), scatter_dimension=0, tiled=True
            ),
            lax.psum_scatter(bias_grad, ("dp", "cp"), scatter_dimension=0, tiled=True),
            lax.psum_scatter(attn_gain_grad, ("dp", "cp"), scatter_dimension=0, tiled=True),
            lax.psum_scatter(attn_shift_grad, ("dp", "cp"), scatter_dimension=0, tiled=True),
            lax.psum_scatter(mlp_gain_grad, ("dp", "cp"), scatter_dimension=0, tiled=True),
            lax.psum_scatter(mlp_shift_grad, ("dp", "cp"), scatter_dimension=0, tiled=True),
        )
        per_layer[depth] = (
            summed[0].reshape(-1, 3 * D),
            summed[1],
            summed[2].reshape(-1, D),
            summed[3],
            summed[4].reshape(-1, FF),
            summed[5],
            summed[6].reshape(-1, D),
            summed[7],
            summed[8],
            summed[9],
            summed[10],
            summed[11],
        )
    stacked = [stack_layers(per_layer, member) for member in range(12)]
    return (
        stream.astype(jnp.bfloat16),
        grad_stream,
        stacked[0],
        stacked[1],
        stacked[2],
        stacked[3],
        stacked[4],
        stacked[5],
        stacked[6],
        stacked[7],
        stacked[8],
        stacked[9],
        stacked[10],
        stacked[11],
    )


TEAM = 4
TEAM_AXES = ("core", "x")
LINE_AXES = ("z", "y")
LINE = 4
MINE = (3 * D) // TEAM
HCOLS = D // TEAM
UCOLS = FF // TEAM
VMEM_BYTES = 56 * 1024 * 1024
BF = jnp.bfloat16
F32 = jnp.float32


def call(body, out_shape, name, operands, scratch=()):
    return pl.pallas_call(
        body,
        out_shape=out_shape,
        scratch_shapes=list(scratch),
        compiler_params=pltpu.CompilerParams(vmem_limit_bytes=VMEM_BYTES),
        name=name,
    )(*operands)


def shape(dims, kind):
    return jax.ShapeDtypeStruct(dims, kind)


def mm(left, right):
    return jnp.dot(left, right, preferred_element_type=F32)


def mm_t(left, right):
    return lax.dot_general(left, right, (((1,), (1,)), ((), ())), preferred_element_type=F32)


def t_mm(left, right):
    return lax.dot_general(left, right, (((0,), (0,)), ((), ())), preferred_element_type=F32)


def pick(member, pieces, wanted):
    chosen = pieces[0]
    for s in range(1, TEAM):
        chosen = jnp.where((member ^ s) == wanted, pieces[s], chosen)
    return chosen


def small_rows(vectors, depth):
    rows = []
    for vector in vectors:
        values = vector[depth : depth + 1].astype(F32)
        rows.append(
            jnp.concatenate([values, jnp.zeros((1, 128 - values.shape[1]), F32)], axis=1)
        )
    return jnp.concatenate(rows, axis=0)


def pack_body(me_ref, qkv_ref, up_ref, *refs):
    vectors, outs = [r[...] for r in refs[:8]], refs[8:]
    me = me_ref[0]
    small = jnp.concatenate([small_rows(vectors, depth) for depth in range(LAYERS)], axis=0)
    small = jnp.concatenate([small, jnp.zeros((small.shape[0], UCOLS - 128), F32)], axis=1)
    parts = [[] for _ in range(TEAM)]
    for depth in range(LAYERS):
        rows = qkv_ref.shape[1]
        qkv = qkv_ref[depth].astype(F32)
        up = up_ref[depth].astype(F32)
        blocks = up.shape[1] // (TEAM * 96)
        for p in range(TEAM):
            parts[p].append(
                jnp.concatenate(
                    [up[:, 96 * (TEAM * b + p) : 96 * (TEAM * b + p + 1)] for b in range(blocks)],
                    axis=1,
                )
            )
            parts[p].append(
                jnp.concatenate(
                    [qkv[:, D * t + HCOLS * p : D * t + HCOLS * (p + 1)] for t in range(3)]
                    + [jnp.zeros((rows, UCOLS - MINE), F32)],
                    axis=1,
                )
            )
    parts = [jnp.concatenate(group, axis=0) for group in parts]
    for s in range(TEAM):
        chosen = parts[0]
        for p in range(1, TEAM):
            chosen = jnp.where((me ^ s) == p, parts[p], chosen)
        outs[s][...] = jnp.concatenate([chosen, small], axis=0).astype(BF)


def assemble_body(me_ref, p0, p1, p2, p3, attn_ref, down_ref, *outs):
    me = me_ref[0]
    slots = [r[...].astype(F32) for r in (p0, p1, p2, p3)]
    ordered = [pick(me, slots, p) for p in range(TEAM)]
    for depth, out in enumerate(outs):
        base = 48 * depth
        up = jnp.concatenate([piece[base : base + 24] for piece in ordered], axis=0)
        qkv = jnp.concatenate([piece[base + 24 : base + 48] for piece in ordered], axis=0)
        attn = attn_ref[depth].astype(F32)
        side = jnp.concatenate([attn[:, HCOLS * n : HCOLS * (n + 1)] for n in range(4)], axis=0)
        out[0:96] = up.astype(BF)
        out[96:192] = down_ref[depth]
        out[192:288] = jnp.concatenate([qkv[:, :MINE], side], axis=1).astype(BF)
        if out.shape[0] > 288:
            small = jnp.concatenate(
                [piece[96:112, :128] for piece in ordered] + [jnp.zeros((16, D - 4 * 128), F32)],
                axis=1,
            )
            out[288:304] = small.astype(BF)


def source_team(me_ref, index):
    shift, flip = index % LINE, index // LINE
    return 2 * lax.rem(me_ref[1] + LINE - shift, LINE) + (me_ref[2] ^ flip)


def target_team(me_ref, index):
    shift, flip = index % LINE, index // LINE
    return 2 * lax.rem(me_ref[1] + shift, LINE) + (me_ref[2] ^ flip)


def place(me_ref, pieces, whole):
    for index, piece in enumerate(pieces):
        whole[source_team(me_ref, index)] = piece[...]


def hand_out(me_ref, whole, keep, sends, order):
    for s in range(LINE):
        keep[s] = whole[target_team(me_ref, s)]
    for send, slots in zip(sends, order):
        for n, s in enumerate(slots):
            send[n] = whole[target_team(me_ref, LINE + s)]


ALL_SLOTS = (tuple(range(LINE)),)
HALVES = ((1, 3), (2, 0))


def add_body(slots, places, me_ref, keep, received, *outs):
    for s, n, out in zip(slots, places, outs):
        out[...] = (keep[s].astype(F32) + received[n].astype(F32)).astype(BF)


def line_sum_body(me_ref, own, r1, r2, r3, keep_ref, send_ref):
    for f, out in enumerate((keep_ref, send_ref)):
        total = own[f].astype(F32) + r1[f].astype(F32) + r2[f].astype(F32) + r3[f].astype(F32)
        out[...] = total.astype(out.dtype)


def layer_vectors(me_ref, whole, depth):
    me = me_ref[0]
    small = [whole[k].astype(F32) for k in range(2 * LINE)]
    fields = [block[8 * depth : 8 * (depth + 1)] for block in small]
    shared = jnp.concatenate(
        [block[2:8, 128 * p : 128 * p + 24] for block in fields for p in range(TEAM)], axis=1
    )
    up_rows, qkv_rows = [], []
    qkv = jnp.concatenate(
        [block[0:1, 128 * p : 128 * p + 72] for block in fields for p in range(TEAM)], axis=1
    )
    for p in range(TEAM):
        up_rows.append(
            jnp.concatenate([block[1:2, 128 * p : 128 * p + 96] for block in fields], axis=1)
        )
        qkv_rows.append(
            jnp.concatenate(
                [qkv[:, D * t + HCOLS * p : D * t + HCOLS * (p + 1)] for t in range(3)]
                + [jnp.zeros((1, D - MINE), F32)],
                axis=1,
            )
        )
    up_mine, qkv_mine = up_rows[0], qkv_rows[0]
    for p in range(1, TEAM):
        up_mine = jnp.where(me == p, up_rows[p], up_mine)
        qkv_mine = jnp.where(me == p, qkv_rows[p], qkv_mine)
    return jnp.concatenate([shared, up_mine, qkv_mine], axis=0)


def attn_weights(whole):
    qkv = whole[:, 0:96, :][:, :, :MINE].reshape(D, MINE)
    side = whole[:, 0:96, MINE:].astype(F32)
    out = jnp.concatenate(
        [side[:, 24 * n : 24 * (n + 1), :].reshape(HCOLS, HCOLS) for n in range(4)], axis=1
    )
    return qkv, out.astype(BF)


def project(scaled, vec, weight, cosine, sine):
    normed = (scaled * vec[0:1] + vec[1:2]).astype(BF)
    projected = mm(normed, weight) + vec[7:8, :MINE]
    turned = turn(projected[:, : 2 * HCOLS], cosine, sine)
    queries = (turned[:, :HCOLS] * 0.125).astype(BF)
    keys = turned[:, HCOLS:].astype(BF)
    values = projected[:, 2 * HCOLS :].astype(BF)
    return normed, queries, keys, values


def attend_body(me_ref, x0, x1, x2, x3, *refs):
    pieces, smalls = refs[:8], refs[8:16]
    cos_ref, sin_ref, mask_ref, y_ref, vec_ref, whole, small = refs[16:]
    place(me_ref, pieces, whole)
    place(me_ref, smalls, small)
    for depth in range(LAYERS):
        vec_ref[depth] = layer_vectors(me_ref, small, depth)
    vec = vec_ref[0]
    weight, out_weight = attn_weights(whole)
    for g, (first, second) in enumerate(((x0, x1), (x2, x3))):
        rows = pl.ds(PAIR * g, PAIR)
        scaled, _ = norm_parts(two_slots(first[...], second[...]))
        _, queries, keys, values = project(scaled, vec, weight, cos_ref[rows, :], sin_ref[rows, :])
        total = jnp.zeros((PAIR, HCOLS), F32)
        for head in range(HEADS // TEAM):
            owned = head_mask(PAIR, head)
            scores = mm_t(jnp.where(owned, queries, jnp.zeros_like(queries)), keys) + mask_ref[g]
            weights = jnp.exp(scores - jnp.max(scores, axis=-1, keepdims=True))
            below = jnp.sum(weights, axis=-1, keepdims=True)
            total = total + jnp.where(owned, mm(weights.astype(BF), values) / below, 0.0)
        y_ref[rows, :] = mm(total.astype(BF), out_weight)


def store_pair(g, result, own, near, far):
    if g == 0:
        own[...] = result[0:TOK]
        near[...] = result[TOK:]
    else:
        far[...] = result.astype(BF)


def mlp_body(me_ref, x0, x1, x2, x3, *refs):
    pieces, (vec_ref, a_ref, y0, y1, y23, whole) = refs[:8], refs[8:]
    place(me_ref, pieces, whole)
    vec = vec_ref[0]
    up = whole[:, 0:96, :].reshape(D, UCOLS)
    down = whole[:, 96:192, :].reshape(UCOLS, D)
    for g, (first, second) in enumerate(((x0, x1), (x2, x3))):
        rows = pl.ds(PAIR * g, PAIR)
        scaled, _ = norm_parts(two_slots(first[...], second[...]))
        normed = (scaled * vec[2:3] + vec[3:4]).astype(BF)
        before = mm(normed, up) + vec[6:7]
        hidden = (before * (0.5 * (1.0 + lax.erf(before * (1.0 / math.sqrt(2.0)))))).astype(BF)
        result = mm(hidden, down) + a_ref[rows, :]
        store_pair(g, result, y0, y1, y23)


def mlp_both_body(depth, last, me_ref, x0, x1, x2, x3, g0, g1, g2, g3, *refs):
    pieces, vec_ref, (dn_ref, sum_ref), refs = refs[:8], refs[8], refs[9:11], refs[11:]
    if last:
        y_ref, refs = refs[0], refs[1:]
    whole, grads, c_s, hid_s, du_s, gb_s = refs[-6:]
    place(me_ref, pieces, whole)
    vec = vec_ref[depth]
    up = whole[:, 0:96, :].reshape(D, UCOLS)
    down = whole[:, 96:192, :].reshape(UCOLS, D)
    gain_sum = jnp.zeros((1, D), F32)
    shift_sum = jnp.zeros((1, D), F32)
    bias_sum = jnp.zeros((1, D), F32)
    up_sum = jnp.zeros((1, UCOLS), F32)
    for g, (first, second, g_first, g_second) in enumerate(((x0, x1, g0, g1), (x2, x3, g2, g3))):
        rows = pl.ds(PAIR * g, PAIR)
        scaled, _ = norm_parts(two_slots(first[...], second[...]))
        normed = (scaled * vec[2:3] + vec[3:4]).astype(BF)
        c_s[rows, :] = normed
        low = jnp.concatenate([g_first[...], g_second[...]], axis=0)
        gb_s[rows, :] = low
        hidden, slope = gelu_parts(mm(normed, up) + vec[6:7])
        hidden = hidden.astype(BF)
        hid_s[rows, :] = hidden
        if last:
            y_ref[rows, :] = mm(hidden, down)
        du = (mm_t(low, down) * slope).astype(BF)
        du_s[rows, :] = du
        dc = mm_t(du, up)
        dn_ref[rows, :] = dc * vec[2:3]
        gain_sum = gain_sum + jnp.sum(dc * scaled, axis=0, keepdims=True)
        shift_sum = shift_sum + jnp.sum(dc, axis=0, keepdims=True)
        bias_sum = bias_sum + jnp.sum(low.astype(F32), axis=0, keepdims=True)
        up_sum = up_sum + jnp.sum(du.astype(F32), axis=0, keepdims=True)
    grads[:, 0:96, :] = t_mm(c_s[...], du_s[...]).reshape(-1, 96, UCOLS).astype(BF)
    grads[:, 96:192, :] = t_mm(hid_s[...], gb_s[...]).reshape(-1, 96, D).astype(BF)
    if last:
        for s, out in enumerate(refs[0:LINE]):
            for f in range(2):
                out[f] = grads[target_team(me_ref, LINE * f + s), 0:EARLY, :]
        keep, send = refs[LINE : LINE + 2]
        for s in range(LINE):
            keep[s] = grads[target_team(me_ref, s), EARLY:192, :]
            send[s] = grads[target_team(me_ref, LINE + s), EARLY:192, :]
    else:
        hand_out(me_ref, grads, refs[0], refs[1:3], HALVES)
    sum_ref[...] = jnp.concatenate(
        [bias_sum, up_sum, gain_sum, shift_sum, jnp.zeros((4, D), F32)], axis=0
    )


def attend_both_body(depth, last, me_ref, x0, x1, x2, x3, g0, g1, g2, g3, *refs):
    pieces, (vec_ref, cos_ref, sin_ref, mask_ref, dn_ref, sum_ref) = refs[:8], refs[8:14]
    refs = refs[14:]
    if last:
        y_ref, refs = refs[0], refs[1:]
    blocks, (n0, n1, n23) = refs[:2], refs[2:5]
    whole, grads, a_s, dp_s, o_s, gb_s = refs[-6:]
    place(me_ref, pieces, whole)
    vec = vec_ref[depth]
    weight, out_weight = attn_weights(whole)
    gain_sum = jnp.zeros((1, D), F32)
    shift_sum = jnp.zeros((1, D), F32)
    bias_sum = jnp.zeros((1, MINE), F32)
    for g, (first, second, g_first, g_second) in enumerate(((x0, x1, g0, g1), (x2, x3, g2, g3))):
        rows = pl.ds(PAIR * g, PAIR)
        cosine, sine = cos_ref[rows, :], sin_ref[rows, :]
        scaled, _ = norm_parts(two_slots(first[...], second[...]))
        normed, queries, keys, values = project(scaled, vec, weight, cosine, sine)
        a_s[rows, :] = normed
        low = jnp.concatenate([g_first[...], g_second[...]], axis=0)
        gb_s[rows, :] = low
        grad_o = mm_t(low, out_weight).astype(BF)
        zero = jnp.zeros_like(queries)
        out = jnp.zeros((PAIR, HCOLS), F32)
        dq = jnp.zeros((PAIR, HCOLS), F32)
        dk = jnp.zeros((PAIR, HCOLS), F32)
        dv = jnp.zeros((PAIR, HCOLS), F32)
        for head in range(HEADS // TEAM):
            owned = head_mask(PAIR, head)
            scores = mm_t(jnp.where(owned, queries, zero), keys) + mask_ref[g]
            weights = jnp.exp(scores - jnp.max(scores, axis=-1, keepdims=True))
            weights = weights / jnp.sum(weights, axis=-1, keepdims=True)
            rounded = weights.astype(BF)
            dweights = mm_t(jnp.where(owned, grad_o, zero), values)
            delta = jnp.sum(weights * dweights, axis=-1, keepdims=True)
            dscores = (weights * (dweights - delta)).astype(BF)
            out = out + jnp.where(owned, mm(rounded, values), 0.0)
            dq = dq + jnp.where(owned, mm(dscores, keys), 0.0)
            dk = dk + jnp.where(owned, t_mm(dscores, queries), 0.0)
            dv = dv + jnp.where(owned, t_mm(rounded, grad_o), 0.0)
        o_s[rows, :] = out.astype(BF)
        both = turn(jnp.concatenate([dq * 0.125, dk], axis=1), cosine, -sine)
        dproj = jnp.concatenate([both, dv], axis=1).astype(BF)
        dp_s[rows, :] = dproj
        bias_sum = bias_sum + jnp.sum(dproj.astype(F32), axis=0, keepdims=True)
        da = mm_t(dproj, weight)
        gain_sum = gain_sum + jnp.sum(da * scaled, axis=0, keepdims=True)
        shift_sum = shift_sum + jnp.sum(da, axis=0, keepdims=True)
        dn = dn_ref[rows, :] + da * vec[0:1]
        store_pair(g, dn, n0, n1, n23)
        if last:
            result = y_ref[rows, :] + mm(out.astype(BF), out_weight)
            store_pair(g, result, *refs[5:8])
    qkv_grad = t_mm(a_s[...], dp_s[...]).reshape(-1, 96, MINE)
    out_grad = t_mm(o_s[...], gb_s[...])
    side = jnp.concatenate(
        [out_grad[:, HCOLS * n : HCOLS * (n + 1)].reshape(-1, 24, HCOLS) for n in range(4)], axis=1
    )
    grads[:, 0:96, :] = jnp.concatenate([qkv_grad, side], axis=2).astype(BF)
    sums = sum_ref[...]
    vectors = jnp.concatenate([sums[0:2], gain_sum, shift_sum, sums[2:4]], axis=0)
    me = me_ref[0]
    spread = jnp.concatenate(
        [
            jnp.where(me == p, bias_sum[:, HCOLS * t : HCOLS * (t + 1)], 0.0)
            for t in range(3)
            for p in range(TEAM)
        ],
        axis=1,
    )
    for k in range(2 * LINE):
        shared = jnp.concatenate(
            [vectors[:, 96 * k : 96 * (k + 1)], jnp.zeros((6, D - 96), F32)], axis=1
        )
        bias = jnp.concatenate(
            [spread[:, 288 * k : 288 * (k + 1)], jnp.zeros((1, D - 288), F32)], axis=1
        )
        grads[k, 96:112, :] = jnp.concatenate([shared, bias, jnp.zeros((9, D), F32)], axis=0).astype(BF)
    hand_out(me_ref, grads, blocks[0], blocks[1:], ALL_SLOTS)


def residual_body(me_ref, x_ref, y0, y1, y2, vec_ref, out_ref, low_ref):
    depth = 0 if x_ref.dtype == BF else 1
    total = y0[...] + y1[...].astype(F32) + y2[...].astype(F32)
    result = x_ref[...].astype(F32) + total + (vec_ref[depth, 4:5] + vec_ref[depth, 5:6])
    out_ref[...] = result
    low_ref[...] = result.astype(BF)

def norm_parts(stream):
    centered = stream - jnp.mean(stream, axis=-1, keepdims=True)
    spread = jnp.mean(centered * centered, axis=-1, keepdims=True)
    inverse = lax.rsqrt(spread + 1e-05)
    return centered * inverse, inverse


def two_slots(first, second):
    return jnp.concatenate([first[0:TOK].astype(F32), second[0:TOK].astype(F32)], axis=0)


TOK = 128
EARLY = 48
PAIR = 2 * TOK


def turn(block, cosine, sine):
    lane = lax.broadcasted_iota(jnp.int32, (block.shape[0], 128), 1) % HEAD
    tiles = []
    for t in range(block.shape[1] // 128):
        tile = block[:, 128 * t : 128 * (t + 1)]
        swapped = jnp.where(
            lane < ROT // 2, pltpu.roll(tile, 128 - ROT // 2, 1), pltpu.roll(tile, ROT // 2, 1)
        )
        tiles.append(tile * cosine + swapped * sine)
    return jnp.concatenate(tiles, axis=1)


def head_mask(rows, head):
    lane = lax.broadcasted_iota(jnp.int32, (rows, HCOLS), 1)
    return (lane >= head * HEAD) & (lane < (head + 1) * HEAD)


def gelu_parts(u):
    cdf = 0.5 * (1.0 + lax.erf(u * (1.0 / math.sqrt(2.0))))
    density = jnp.exp(-0.5 * u * u) * (1.0 / math.sqrt(2.0 * math.pi))
    return u * cdf, cdf + u * density


def norm_back_body(me_ref, x_ref, g_ref, n0, n1, n2, out_ref, low_ref):
    scaled, inverse = norm_parts(x_ref[...].astype(F32))
    dn = n0[...] + n1[...].astype(F32) + n2[...].astype(F32)
    centered = dn - jnp.mean(dn, axis=-1, keepdims=True)
    moment = jnp.mean(dn * scaled, axis=-1, keepdims=True)
    result = g_ref[...].astype(F32) + inverse * (centered - scaled * moment)
    out_ref[...] = result
    low_ref[...] = result.astype(BF)


def total(group):
    result = group[0].astype(F32)
    for term in group[1:]:
        result = result + term.astype(F32)
    return result


def by_owner(me_ref, parts, outs, start):
    me = me_ref[0]
    for s, out in enumerate(outs):
        piece = parts[0]
        for p in range(1, TEAM):
            piece = jnp.where((me ^ s) == p, parts[p], piece)
        out[start : start + 32] = piece.astype(BF)


def split_body(early, me_ref, *refs):
    outs, (down_ref, attn_ref, small_ref), refs = refs[-7:-3], refs[-3:], refs[:-7]
    split_attend(me_ref, refs[:5], outs, attn_ref, small_ref)
    refs = refs[5:]
    rest = total([refs[0][0], refs[1][0], refs[2][...], refs[3][...], refs[4][...]])
    if early:
        rest = jnp.concatenate([total([refs[5][...], refs[6][...]]), rest], axis=0)
    down_ref[...] = rest[96:192]
    blank = jnp.zeros((8, D), F32)
    parts = [
        jnp.concatenate([rest[24 * p : 24 * (p + 1)], blank], axis=0) for p in range(TEAM)
    ]
    by_owner(me_ref, parts, outs, 0)


def split_attend(me_ref, refs, outs, attn_ref, small_ref):
    me = me_ref[0]
    attn = total([refs[0][0], refs[1][0], refs[2][...], refs[3][...], refs[4][...]])
    side = attn[0:96, MINE:]
    attn_ref[...] = jnp.concatenate(
        [side[24 * n : 24 * (n + 1)] for n in range(4)], axis=1
    ).astype(BF)
    qkv = jnp.concatenate([attn[0:96, :MINE], jnp.zeros((96, UCOLS - MINE), F32)], axis=1)
    small = attn[96:112]
    parts, bias = [], jnp.zeros((1, 24), F32)
    for p in range(TEAM):
        rows = slice(24 * p, 24 * (p + 1))
        gains = jnp.concatenate([small[2:6, rows], jnp.zeros((4, D - 24), F32)], axis=1)
        qkv_bias = jnp.concatenate(
            [small[6:7, 72 * p : 72 * (p + 1)], jnp.zeros((1, D - 72), F32)], axis=1
        )
        parts.append(jnp.concatenate([qkv[rows], gains, qkv_bias, jnp.zeros((3, D), F32)], axis=0))
        bias = jnp.where(me == p, small[0:1, rows], bias)
    small_ref[...] = jnp.concatenate(
        [
            jnp.concatenate([bias, jnp.zeros((1, 104), F32)], axis=1),
            small[1:2, :128],
            jnp.zeros((6, 128), F32),
        ],
        axis=0,
    )
    by_owner(me_ref, parts, outs, 32)


def unpack_body(me_ref, *refs):
    me = me_ref[0]
    (
        qkv_ref, qkv_b_ref, attn_ref, attn_b_ref, up_ref, up_b_ref, down_ref,
        ga_ref, sa_ref, gm_ref, sm_ref,
    ) = refs[7 * LAYERS :]
    gain_refs = (ga_ref, sa_ref, gm_ref, sm_ref)
    for depth in range(LAYERS):
        group = refs[7 * depth : 7 * (depth + 1)]
        down_rows, own_small, attn_rows = group[TEAM:]
        slots = [r[...].astype(F32) for r in group[:TEAM]]
        ordered = [pick(me, slots, p) for p in range(TEAM)]
        blocks = FF // (96 * TEAM)
        up_ref[depth] = jnp.concatenate(
            [ordered[p][0:24, 96 * b : 96 * (b + 1)] for b in range(blocks) for p in range(TEAM)],
            axis=1,
        )
        qkv_ref[depth] = jnp.concatenate(
            [
                ordered[p][32:56, HCOLS * t : HCOLS * (t + 1)]
                for t in range(3)
                for p in range(TEAM)
            ],
            axis=1,
        )
        attn_ref[depth] = attn_rows[...].astype(F32)
        down_ref[depth] = down_rows[...]
        small = slots[0][56:64, :128] + slots[1][56:64, :128]
        small = small + slots[2][56:64, :128] + slots[3][56:64, :128]
        for n, ref in enumerate(gain_refs):
            ref[depth : depth + 1] = small[n : n + 1, :24]
        qkv_b_ref[depth : depth + 1] = small[4:5, :72]
        attn_b_ref[depth : depth + 1] = own_small[0:1, :24]
        up_b_ref[depth : depth + 1] = own_small[1:2, :96]


def team_send(piece, slot):
    flips = [(m, m ^ slot) for m in range(TEAM)]
    return lax.ppermute(piece, TEAM_AXES, flips)


def line_shift(piece, shift):
    size = lax.axis_size("z")
    return lax.ppermute(piece, "z", [(i, (i + shift) % size) for i in range(size)])


def line_flip(piece):
    return lax.ppermute(piece, "y", [(0, 1), (1, 0)])


def after(value, *others):
    return lax.optimization_barrier((value, *others))[0]


def line_near(piece):
    first = line_shift(piece, 1)
    third = line_shift(piece, 3)
    return [piece, first, line_shift(after(piece, first, third), 2), third]


def local_team(
    tokens, segment_ids, cotangent, qkv_weight, qkv_bias, attn_weight, attn_bias,
    up_weight, up_bias, down_weight, down_bias, attn_gain, attn_shift, mlp_gain, mlp_shift,
):
    lines = lax.axis_size("z") * lax.axis_size("y")
    world = lines * TEAM
    member = lax.axis_index("core") * 2 + lax.axis_index("x")
    me = jnp.stack([member, lax.axis_index("z"), lax.axis_index("y")]).astype(jnp.int32)
    everywhere = LINE_AXES + TEAM_AXES
    tok_all = TEAM * TOK
    whole_spec = pl.BlockSpec(memory_space=pltpu.VMEM)

    def run(body, out_shape, name, operands, scratch=()):
        specs = [whole_spec if isinstance(x, jax.Array) else x[1] for x in operands]
        return pl.pallas_call(
            body,
            grid=(1,),
            out_shape=out_shape,
            in_specs=[pl.BlockSpec(memory_space=pltpu.SMEM)] + specs,
            scratch_shapes=[pltpu.VMEM(dims, kind) for dims, kind in scratch],
            compiler_params=pltpu.CompilerParams(vmem_limit_bytes=VMEM_BYTES),
            name=name,
        )(me, *[x if isinstance(x, jax.Array) else x[0] for x in operands])

    def part(rows, start):
        return pl.BlockSpec((rows, D), lambda i: (start // rows, 0))

    def one_of(array, index):
        return (array, pl.BlockSpec((1,) + array.shape[1:], lambda i: (index, 0, 0)))

    def exchange(blocks):
        return [blocks[0]] + [team_send(blocks[s], s) for s in range(1, TEAM)]

    small = (
        qkv_bias, up_bias, attn_gain, attn_shift, mlp_gain, mlp_shift, attn_bias, down_bias
    )
    packed = run(
        pack_body, [shape((112, D), BF)] * TEAM, "pack_weights", (qkv_weight, up_weight, *small)
    )
    spread = [(i, TEAM * (i % lines) + i // lines) for i in range(world)]
    gather_back = [(b, a) for a, b in spread]
    attn_piece = lax.ppermute(attn_weight, everywhere, spread)
    chunks = run(
        assemble_body,
        [shape((304, D), BF), shape((288, D), BF)],
        "assemble_weights",
        (*exchange(packed), attn_piece, down_weight),
    )
    near = line_near(chunks[0])
    pieces = [near + [line_flip(p) for p in near]]
    near = line_near(after(chunks[1], near[2], pieces[0][5], pieces[0][7]))
    pieces.append(near + [line_flip(p) for p in (chunks[1], *near[1:])])
    m_parts = [[(p, part(192, 0)) for p in group] for group in pieces]
    a_parts = [[(p, part(96, 192)) for p in group] for group in pieces]
    small_parts = [(p, part(16, 288)) for p in pieces[0]]

    def gather_team(piece, *others):
        other = after(team_send(piece, 1), *others)
        return piece, other, team_send(jnp.concatenate([piece, other], axis=0), 2)

    def slots_of(gathered, start=0):
        piece, other, far = gathered
        size = piece.shape[0]
        return [
            (piece, part(TOK, start)), (other, part(TOK, start)),
            (far, part(TOK, start)), (far, part(TOK, size + start)),
        ]

    def sum_team(own, near, far, *others):
        other = after(team_send(far, 2), *others)
        both = (near + other[TOK:].astype(F32)).astype(BF)
        return own, (other, part(TOK, 0)), team_send(both, 1)

    ids_rows = jnp.pad(segment_ids.astype(BF)[None, :], ((0, TOK - 1), (0, D - TOK)))
    load = jnp.concatenate([tokens, cotangent, ids_rows], axis=0)
    loads = gather_team(after(load, pieces[0][1], pieces[0][3], pieces[0][4], pieces[1][4]), pieces[0][2], pieces[0][5], pieces[0][7])
    token_slots = slots_of(loads)
    here = lax.axis_index("x")
    rows = jnp.arange(TOK, dtype=jnp.int32)
    places = jnp.concatenate([here * TOK + rows, (1 - here) * TOK + rows])
    masks, cosines, sines = [], [], []
    lane = jnp.arange(128, dtype=jnp.int32) % HEAD
    inverse = 10000.0 ** (-(lane % (ROT // 2) * 2).astype(F32) / ROT)
    id_rows = [
        loads[0][2 * TOK, :TOK], loads[1][2 * TOK, :TOK],
        loads[2][2 * TOK, :TOK], loads[2][5 * TOK, :TOK],
    ]
    for g in range(2):
        ids = jnp.concatenate(id_rows[2 * g : 2 * g + 2]).astype(F32)
        visible = (places[None, :] <= places[:, None]) & (ids[None, :] == ids[:, None])
        masks.append(jnp.where(visible, 0.0, -1e30).astype(F32))
        position = places - jnp.sum((ids[None, :] < ids[:, None]).astype(jnp.int32), axis=1)
        phases = position.astype(F32)[:, None] * inverse[None, :]
        cosines.append(jnp.where(lane[None, :] < ROT, jnp.cos(phases), 1.0))
        sign = jnp.where(lane < ROT // 2, -1.0, jnp.where(lane < ROT, 1.0, 0.0))
        sines.append(jnp.sin(phases) * sign[None, :])
    mask = jnp.stack(masks)
    cosine, sine = jnp.concatenate(cosines), jnp.concatenate(sines)

    partials = [shape((TOK, D), F32)] * 2 + [shape((PAIR, D), BF)]
    stream_pair = [shape((TOK, D), F32), shape((TOK, D), BF)]
    wide = ((tok_all, D), BF)

    attn_out, vec = run(
        attend_body,
        [shape((tok_all, D), F32), shape((LAYERS, 8, D), F32)],
        "attend_forward",
        (*token_slots, *a_parts[0], *small_parts, cosine, sine, mask),
        [((lines, 96, D), BF), ((lines, 16, D), BF)],
    )
    y = run(
        mlp_body,
        partials,
        "mlp_forward",
        (*token_slots, *m_parts[0], vec, attn_out),
        [((lines, 192, D), BF)],
    )

    def residual(stream, blocks):
        return run(residual_body, stream_pair, "residual", (stream, *sum_team(*blocks), vec))

    stream, low = residual(tokens, (after(y[0], pieces[1][4]), *y[1:]))
    streams = [tokens, stream]
    slots = [token_slots, slots_of(gather_team(low, pieces[1][5], pieces[1][7]))]

    grad = cotangent
    grad_slots = slots_of(loads, TOK)
    outs = [None] * LAYERS
    block_m, block_a = shape((192, D), BF), shape((112, D), BF)

    def mlp_back(depth, slots, grad_slots, grads):
        last = depth == LAYERS - 1
        return run(
            partial(mlp_both_body, depth, last),
            [shape((tok_all, D), F32), shape((8, D), F32)]
            + ([shape((tok_all, D), F32)] if last else [])
            + grads,
            "mlp_both",
            (*slots, *grad_slots, *m_parts[depth], vec),
            [((lines, 192, D), BF), ((lines, 192, D), BF), wide, wide, wide, wide],
        )

    def attend_back(depth, slots, grad_slots, rest, *others):
        last = depth == LAYERS - 1
        result = run(
            partial(attend_both_body, depth, last),
            [shape((4, 112, D), BF)] * 2 + partials + (partials if last else []),
            "attend_both",
            (*slots, *grad_slots, *a_parts[depth], vec, cosine, sine, mask, *rest),
            [
                ((lines, 96, D), BF),
                ((lines, 112, D), BF),
                wide,
                ((tok_all, MINE), BF),
                ((tok_all, HCOLS), BF),
                wide,
            ],
        )
        return result[0], line_flip(after(result[1], *others)), result[2:5], result[5:]

    def norm_back(depth, grad, received):
        return run(
            norm_back_body, stream_pair, "norm_backward", (streams[depth], grad, *received)
        )

    def add(kind, keep, other, slots, places, name):
        return run(partial(add_body, slots, places), [kind] * len(slots), name, (keep, other))

    def shifts(sums):
        return [line_shift(piece, s + 1) for s, piece in enumerate(sums)]

    def split(attend, mlp, early=()):
        keep, other, *sums = attend
        m_keep, m_other, *m_sums = mlp
        mine = run(
            partial(split_body, bool(early)),
            [shape((64, D), BF)] * TEAM
            + [shape((96, D), F32), shape((24, D), BF), shape((8, 128), F32)],
            "split_gradients",
            (one_of(keep, 0), one_of(other, 0), *sums, one_of(m_keep, 0), m_other, *m_sums, *early),
        )
        attn_rows = lax.ppermute(mine[TEAM + 1], everywhere, gather_back)
        return exchange(mine[:TEAM]) + [mine[TEAM], mine[TEAM + 2], attn_rows]

    early_block, late_four = shape((2, EARLY, D), BF), shape((4, 192 - EARLY, D), BF)
    dn, sum_m, y_part, e0, e1, e2, e3, m_keep1, m_send1 = mlp_back(
        1, slots[1], grad_slots, [early_block] * 4 + [late_four] * 2
    )
    early = shifts((e1, e2, e3))
    m_other1 = line_flip(m_send1)
    a_keep1, a_other1, ns, ys = attend_back(1, slots[1], grad_slots, (dn, sum_m, y_part))
    ns = (ns[0], ns[1], after(ns[2], *early))
    grad, low = norm_back(1, grad, sum_team(*ns, m_other1))
    m_added1 = add(
        shape((192 - EARLY, D), BF), m_keep1, after(m_other1, low), (1, 2, 3), (1, 2, 3), "add_mlp"
    )
    m_sums1 = shifts(m_added1)
    gathered = gather_team(low)
    grad_slots = slots_of((after(gathered[0], *m_added1), *gathered[1:]))
    dn, sum_m, m_keep0, m_first0, m_second0 = mlp_back(
        0, slots[0], grad_slots, [shape((4, 192, D), BF)] + [shape((2, 192, D), BF)] * 2
    )
    m_first0 = line_flip(after(m_first0, m_sums1[0]))
    m_second0 = line_flip(after(m_second0, m_sums1[0]))
    a_keep0, a_other0, ns, _ = attend_back(
        0, slots[0], grad_slots, (after(dn, m_sums1[0]), sum_m), m_second0
    )
    a_added1 = add(
        block_a,
        a_keep1,
        after(a_other1, a_keep0, m_first0, *m_sums1),
        (1, 2, 3),
        (1, 2, 3),
        "add_attend",
    )
    a_sums1 = shifts(a_added1)
    m1, m3 = add(block_m, m_keep0, after(m_first0, *a_sums1), HALVES[0], (0, 1), "add_first")
    first_added = m1
    m1, m3 = line_shift(m1, 1), line_shift(m3, 3)
    (m2,) = add(block_m, m_keep0, after(m_second0, m1, m3), HALVES[1][:1], (0,), "add_second")
    grad, _ = norm_back(0, grad, sum_team(ns[0], ns[1], after(ns[2], a_added1[0])))
    _, activations = residual(streams[1], (ys[0], ys[1], after(ys[2], a_added1[0])))
    e_keep, e_send = run(
        line_sum_body,
        [shape((EARLY, D), F32), shape((EARLY, D), BF)],
        "line_sum",
        (e0, after(early[0], a_added1[0]), early[1], early[2]),
    )
    outs[1] = split(
        (after(a_keep1, first_added), a_other1, *a_sums1),
        (m_keep1, one_of(m_other1, 0), *m_sums1),
        (e_keep, line_flip(e_send)),
    )
    a_added0 = add(
        block_a,
        a_keep0,
        after(a_other0, m2, grad, activations, outs[1][0]),
        (1, 2, 3),
        (1, 2, 3),
        "add_attend",
    )
    m2 = line_shift(m2, 2)
    a_sums0 = shifts(a_added0)
    outs[0] = split((a_keep0, a_other0, *a_sums0), (m_keep0, one_of(m_second0, 1), m1, m2, m3))
    row_24 = shape((LAYERS, 24), F32)
    final = run(
        unpack_body,
        [
            shape((LAYERS, 24, 3 * D), F32), shape((LAYERS, 72), F32),
            shape((LAYERS, 24, D), F32), row_24,
            shape((LAYERS, 24, FF), F32), shape((LAYERS, 96), F32),
            shape((LAYERS, 96, D), F32), row_24, row_24, row_24, row_24,
        ],
        "unpack_gradients",
        [array for group in outs for array in group],
    )
    return (activations, grad, *final[:7], final[3], *final[7:])


def whole_mesh_solution(mesh):
    in_specs = (
        P(("dp", "cp"), None),
        P(("dp", "cp")),
        P(("dp", "cp"), None),
        P(None, ("dp", "cp"), None),
        P(None, ("dp", "cp")),
        P(None, ("dp", "cp"), None),
        P(None, ("dp", "cp")),
        P(None, ("dp", "cp"), None),
        P(None, ("dp", "cp")),
        P(None, ("dp", "cp"), None),
        P(None, ("dp", "cp")),
        P(None, ("dp", "cp")),
        P(None, ("dp", "cp")),
        P(None, ("dp", "cp")),
        P(None, ("dp", "cp")),
    )
    out_specs = (
        P(("dp", "cp"), None),
        P(("dp", "cp"), None),
        P(None, ("dp", "cp"), None),
        P(None, ("dp", "cp")),
        P(None, ("dp", "cp"), None),
        P(None, ("dp", "cp")),
        P(None, ("dp", "cp"), None),
        P(None, ("dp", "cp")),
        P(None, ("dp", "cp"), None),
        P(None, ("dp", "cp")),
        P(None, ("dp", "cp")),
        P(None, ("dp", "cp")),
        P(None, ("dp", "cp")),
        P(None, ("dp", "cp")),
    )
    return jax.shard_map(local, mesh=mesh, in_specs=in_specs, out_specs=out_specs, check_vma=False)


def solution(mesh):
    teams = mesh.shape["dp"] // 2
    if mesh.shape["cp"] != 2 or teams != 2 * LINE or teams * TEAM * 24 != D:
        return whole_mesh_solution(mesh)
    split_mesh = Mesh(mesh.devices.reshape(teams // 2, 2, 2, 2), ("z", "y", "core", "x"))
    every = ("z", "y", "core", "x")
    row = P(every, None)
    matrix, vector = P(None, every, None), P(None, every)
    in_specs = (row, P(every), row) + (matrix, vector) * 4 + (vector,) * 4
    out_specs = (row, row) + (matrix, vector) * 4 + (vector,) * 4
    return jax.shard_map(
        local_team, mesh=split_mesh, in_specs=in_specs, out_specs=out_specs, check_vma=False
    )
```

```python
from functools import partial
import math

import jax
import jax.numpy as jnp
from jax import lax
from jax.experimental import pallas as pl
from jax.experimental.pallas import tpu as pltpu
from jax.sharding import Mesh, PartitionSpec as P

D = 768
HEADS = 12
HEAD = 64
FF = 3072
ROT = 16
LAYERS = 2


def layer_norm(stream, norm_gain, norm_shift):
    centered = stream - jnp.mean(stream, axis=-1, keepdims=True)
    spread = jnp.mean(centered * centered, axis=-1, keepdims=True)
    return centered * lax.rsqrt(spread + 1e-05) * norm_gain + norm_shift


def both_norms(stream, gain_attn, shift_attn, gain_mlp, shift_mlp):
    return (layer_norm(stream, gain_attn, shift_attn), layer_norm(stream, gain_mlp, shift_mlp))


def angles(positions):
    inverse = 10000.0 ** (-jnp.arange(0, ROT, 2, dtype=jnp.float32) / ROT)
    phases = positions.astype(jnp.float32)[:, None] * inverse[None, :]
    return (jnp.cos(phases)[:, None, :], jnp.sin(phases)[:, None, :])


def rotate(heads_in, cosine_table, sine_table):
    half_rot = cosine_table.shape[-1]
    first_half = heads_in[..., :half_rot]
    second_half = heads_in[..., half_rot : 2 * half_rot]
    untouched = heads_in[..., 2 * half_rot :]
    return jnp.concatenate(
        [
            first_half * cosine_table - second_half * sine_table,
            second_half * cosine_table + first_half * sine_table,
            untouched,
        ],
        axis=-1,
    )


def split_blocks(update, running, key_piece, value_piece, offset):
    piece_rows = key_piece.shape[0]
    block_rows = 512 if piece_rows > 512 and piece_rows % 512 == 0 else piece_rows
    block_count = piece_rows // block_rows
    if block_count == 1:
        return update(running, key_piece, value_piece, offset)

    def advance(state, inputs):
        key_block, value_block, start = inputs
        return (update(state, key_block, value_block, offset + start), None)

    starts = jnp.arange(block_count, dtype=jnp.int32) * block_rows
    state, _ = lax.scan(
        advance,
        running,
        (
            key_piece.reshape(block_count, block_rows, -1),
            value_piece.reshape(block_count, block_rows, -1),
            starts,
        ),
    )
    return state


def stack_layers(per_layer, member):
    return jnp.stack([layer_entry[member] for layer_entry in per_layer])


def flatten_rows(matrix):
    return matrix.reshape(matrix.shape[:-2] + (-1, 128))


def local(
    tokens,
    segment_ids,
    cotangent,
    qkv_weight,
    qkv_bias,
    attn_weight,
    attn_bias,
    up_weight,
    up_bias,
    down_weight,
    down_bias,
    attn_gain,
    attn_shift,
    mlp_gain,
    mlp_shift,
):
    tok_rows = tokens.shape[0]
    group_rows = tok_rows * lax.axis_size("cp")
    score_scale = 1.0 / math.sqrt(HEAD)
    all_segments = lax.all_gather(segment_ids, "cp", axis=0, tiled=True)
    row_index = lax.axis_index("cp") * tok_rows + jnp.arange(tok_rows, dtype=jnp.int32)
    positions = row_index - jnp.sum(
        (all_segments[None, :] < segment_ids[:, None]).astype(jnp.int32), axis=1
    )
    cosine_table, sine_table = angles(positions)

    def visible_mask(offset, block_rows):
        key_index = offset + jnp.arange(block_rows, dtype=jnp.int32)
        key_segment = lax.dynamic_slice_in_dim(all_segments, offset, block_rows)
        return (key_index[None, :] <= row_index[:, None]) & (
            key_segment[None, :] == segment_ids[:, None]
        )

    def online_step(query_heads, running, key_block, value_block, offset):
        row_max, denominator, weighted = running
        block_rows = key_block.shape[0]
        key_heads = key_block.reshape(block_rows, HEADS, HEAD)
        value_heads = value_block.reshape(block_rows, HEADS, HEAD)
        scores = (
            jnp.einsum("qhd,khd->hqk", query_heads, key_heads, preferred_element_type=jnp.float32)
            * score_scale
        )
        visible = visible_mask(offset, block_rows)
        scores = jnp.where(visible[None], scores, -1e30)
        new_max = jnp.maximum(row_max, jnp.max(scores, axis=-1))
        rescale = jnp.exp(row_max - new_max)
        weights = jnp.where(visible[None], jnp.exp(scores - new_max[..., None]), 0.0)
        denominator = denominator * rescale + jnp.sum(weights, axis=-1)
        weighted = weighted * rescale[..., None] + jnp.einsum(
            "hqk,khd->hqd",
            weights.astype(jnp.bfloat16),
            value_heads,
            preferred_element_type=jnp.float32,
        )
        return (new_max, denominator, weighted)

    stream = tokens.astype(jnp.float32)
    stored = []
    for depth in range(LAYERS):
        params = (
            lax.all_gather(qkv_weight[depth], ("dp", "cp"), axis=0, tiled=True),
            lax.all_gather(qkv_bias[depth], ("dp", "cp"), axis=0, tiled=True),
            lax.all_gather(attn_weight[depth], ("dp", "cp"), axis=0, tiled=True),
            lax.all_gather(attn_bias[depth], ("dp", "cp"), axis=0, tiled=True),
            lax.all_gather(up_weight[depth], ("dp", "cp"), axis=0, tiled=True),
            lax.all_gather(up_bias[depth], ("dp", "cp"), axis=0, tiled=True),
            lax.all_gather(down_weight[depth], ("dp", "cp"), axis=0, tiled=True),
            lax.all_gather(down_bias[depth], ("dp", "cp"), axis=0, tiled=True),
            lax.all_gather(attn_gain[depth], ("dp", "cp"), axis=0, tiled=True),
            lax.all_gather(attn_shift[depth], ("dp", "cp"), axis=0, tiled=True),
            lax.all_gather(mlp_gain[depth], ("dp", "cp"), axis=0, tiled=True),
            lax.all_gather(mlp_shift[depth], ("dp", "cp"), axis=0, tiled=True),
        )
        (
            proj_qkv,
            bias_qkv,
            proj_attn,
            bias_attn,
            proj_up,
            bias_up,
            proj_down,
            bias_down,
            gain_attn,
            shift_attn,
            gain_mlp,
            shift_mlp,
        ) = params
        normed_attn, normed_mlp = both_norms(
            stream,
            gain_attn.astype(jnp.float32),
            shift_attn.astype(jnp.float32),
            gain_mlp.astype(jnp.float32),
            shift_mlp.astype(jnp.float32),
        )
        normed_attn = normed_attn.astype(jnp.bfloat16)
        normed_mlp = normed_mlp.astype(jnp.bfloat16)
        projected = jnp.dot(
            normed_attn, proj_qkv, preferred_element_type=jnp.float32
        ) + bias_qkv.astype(jnp.float32)
        queries = rotate(
            projected[:, :D].reshape(tok_rows, HEADS, HEAD), cosine_table, sine_table
        ).astype(jnp.bfloat16)
        key_rows = (
            rotate(projected[:, D : 2 * D].reshape(tok_rows, HEADS, HEAD), cosine_table, sine_table)
            .astype(jnp.bfloat16)
            .reshape(tok_rows, D)
        )
        values = projected[:, 2 * D :].astype(jnp.bfloat16)
        initial = (
            jnp.full((HEADS, tok_rows), -1e30, jnp.float32),
            jnp.zeros((HEADS, tok_rows), jnp.float32),
            jnp.zeros((HEADS, tok_rows, HEAD), jnp.float32),
        )
        row_max, denominator, weighted = split_blocks(
            partial(online_step, queries),
            initial,
            lax.all_gather(key_rows, "cp", axis=0, tiled=True),
            lax.all_gather(values, "cp", axis=0, tiled=True),
            jnp.int32(0),
        )
        attended = jnp.transpose(weighted / denominator[..., None], (1, 0, 2)).reshape(tok_rows, D)
        log_total = row_max + jnp.log(denominator)
        attended_low = attended.astype(jnp.bfloat16)
        attn_branch = jnp.dot(
            attended_low, proj_attn, preferred_element_type=jnp.float32
        ) + bias_attn.astype(jnp.float32)
        hidden_pre = jnp.dot(
            normed_mlp, proj_up, preferred_element_type=jnp.float32
        ) + bias_up.astype(jnp.float32)
        hidden = jax.nn.gelu(hidden_pre, approximate=False).astype(jnp.bfloat16)
        mlp_branch = jnp.dot(
            hidden, proj_down, preferred_element_type=jnp.float32
        ) + bias_down.astype(jnp.float32)
        stored.append(
            (
                stream,
                normed_attn,
                normed_mlp,
                queries,
                key_rows,
                values,
                attended,
                attended_low,
                log_total,
                hidden_pre,
                hidden,
            )
        )
        stream = stream + attn_branch + mlp_branch
    grad_stream = cotangent.astype(jnp.float32)
    per_layer = [None] * LAYERS
    for depth in reversed(range(LAYERS)):
        (
            saved_stream,
            normed_attn,
            normed_mlp,
            queries,
            key_rows,
            values,
            attended,
            attended_low,
            log_total,
            hidden_pre,
            hidden,
        ) = stored[depth]
        params = (
            lax.all_gather(qkv_weight[depth], ("dp", "cp"), axis=0, tiled=True),
            lax.all_gather(qkv_bias[depth], ("dp", "cp"), axis=0, tiled=True),
            lax.all_gather(attn_weight[depth], ("dp", "cp"), axis=0, tiled=True),
            lax.all_gather(attn_bias[depth], ("dp", "cp"), axis=0, tiled=True),
            lax.all_gather(up_weight[depth], ("dp", "cp"), axis=0, tiled=True),
            lax.all_gather(up_bias[depth], ("dp", "cp"), axis=0, tiled=True),
            lax.all_gather(down_weight[depth], ("dp", "cp"), axis=0, tiled=True),
            lax.all_gather(down_bias[depth], ("dp", "cp"), axis=0, tiled=True),
            lax.all_gather(attn_gain[depth], ("dp", "cp"), axis=0, tiled=True),
            lax.all_gather(attn_shift[depth], ("dp", "cp"), axis=0, tiled=True),
            lax.all_gather(mlp_gain[depth], ("dp", "cp"), axis=0, tiled=True),
            lax.all_gather(mlp_shift[depth], ("dp", "cp"), axis=0, tiled=True),
        )
        (
            proj_qkv,
            bias_qkv,
            proj_attn,
            bias_attn,
            proj_up,
            bias_up,
            proj_down,
            bias_down,
            gain_attn,
            shift_attn,
            gain_mlp,
            shift_mlp,
        ) = params
        grad_low = grad_stream.astype(jnp.bfloat16)
        bias_grad = jnp.sum(grad_low.astype(jnp.float32), axis=0)
        attn_weight_grad = jnp.einsum(
            "td,te->de", attended_low, grad_low, preferred_element_type=jnp.float32
        )
        down_weight_grad = jnp.einsum(
            "tf,te->fe", hidden, grad_low, preferred_element_type=jnp.float32
        )
        grad_attended = jnp.einsum(
            "te,de->td", grad_low, proj_attn, preferred_element_type=jnp.float32
        ).astype(jnp.bfloat16)
        grad_hidden = jnp.einsum(
            "te,fe->tf", grad_low, proj_down, preferred_element_type=jnp.float32
        )
        _, gelu_pull = jax.vjp(partial(jax.nn.gelu, approximate=False), hidden_pre)
        grad_pre = gelu_pull(grad_hidden)[0].astype(jnp.bfloat16)
        up_weight_grad = jnp.einsum(
            "td,tf->df", normed_mlp, grad_pre, preferred_element_type=jnp.float32
        )
        up_bias_grad = jnp.sum(grad_pre.astype(jnp.float32), axis=0)
        grad_normed_mlp = jnp.einsum(
            "tf,df->td", grad_pre, proj_up, preferred_element_type=jnp.float32
        )
        all_keys, all_values = (
            lax.all_gather(key_rows, "cp", axis=0, tiled=True),
            lax.all_gather(values, "cp", axis=0, tiled=True),
        )
        grad_heads = grad_attended.reshape(tok_rows, HEADS, HEAD)
        row_dot = jnp.transpose(
            jnp.sum(
                grad_heads.astype(jnp.float32) * attended.reshape(tok_rows, HEADS, HEAD), axis=-1
            )
        )
        block_rows = 512 if group_rows > 512 and group_rows % 512 == 0 else group_rows
        block_count = group_rows // block_rows
        starts = jnp.arange(block_count, dtype=jnp.int32) * block_rows

        def back_step(grad_query, inputs):
            key_block, value_block, offset = inputs
            key_heads = key_block.reshape(block_rows, HEADS, HEAD)
            value_heads = value_block.reshape(block_rows, HEADS, HEAD)
            scores = (
                jnp.einsum("qhd,khd->hqk", queries, key_heads, preferred_element_type=jnp.float32)
                * score_scale
            )
            visible = visible_mask(offset, block_rows)
            weights = jnp.where(visible[None], jnp.exp(scores - log_total[..., None]), 0.0)
            grad_weights = jnp.einsum(
                "qhd,khd->hqk", grad_heads, value_heads, preferred_element_type=jnp.float32
            )
            grad_scores = (weights * (grad_weights - row_dot[..., None])).astype(jnp.bfloat16)
            grad_query = grad_query + jnp.einsum(
                "hqk,khd->hqd", grad_scores, key_heads, preferred_element_type=jnp.float32
            )
            key_grad = (
                jnp.einsum("hqk,qhd->khd", grad_scores, queries, preferred_element_type=jnp.float32)
                * score_scale
            )
            value_grad = jnp.einsum(
                "hqk,qhd->khd",
                weights.astype(jnp.bfloat16),
                grad_heads,
                preferred_element_type=jnp.float32,
            )
            return (
                grad_query,
                (key_grad.reshape(block_rows, D), value_grad.reshape(block_rows, D)),
            )

        grad_query, (key_grads, value_grads) = lax.scan(
            back_step,
            jnp.zeros((HEADS, tok_rows, HEAD), jnp.float32),
            (
                all_keys.reshape(block_count, block_rows, D),
                all_values.reshape(block_count, block_rows, D),
                starts,
            ),
        )
        local_key_grad, local_value_grad = (
            lax.psum_scatter(
                key_grads.reshape(group_rows, D).astype(jnp.bfloat16),
                "cp",
                scatter_dimension=0,
                tiled=True,
            ).astype(jnp.float32),
            lax.psum_scatter(
                value_grads.reshape(group_rows, D).astype(jnp.bfloat16),
                "cp",
                scatter_dimension=0,
                tiled=True,
            ).astype(jnp.float32),
        )
        query_raw = rotate(
            jnp.transpose(grad_query * score_scale, (1, 0, 2)), cosine_table, -sine_table
        )
        key_raw = rotate(local_key_grad.reshape(tok_rows, HEADS, HEAD), cosine_table, -sine_table)
        grad_projected = jnp.concatenate(
            [query_raw.reshape(tok_rows, D), key_raw.reshape(tok_rows, D), local_value_grad], axis=1
        ).astype(jnp.bfloat16)
        qkv_weight_grad = jnp.einsum(
            "td,te->de", normed_attn, grad_projected, preferred_element_type=jnp.float32
        )
        qkv_bias_grad = jnp.sum(grad_projected.astype(jnp.float32), axis=0)
        grad_normed_attn = jnp.einsum(
            "te,de->td", grad_projected, proj_qkv, preferred_element_type=jnp.float32
        )
        _, norm_pull = jax.vjp(
            both_norms,
            saved_stream,
            gain_attn.astype(jnp.float32),
            shift_attn.astype(jnp.float32),
            gain_mlp.astype(jnp.float32),
            shift_mlp.astype(jnp.float32),
        )
        grad_input, attn_gain_grad, attn_shift_grad, mlp_gain_grad, mlp_shift_grad = norm_pull(
            (grad_normed_attn, grad_normed_mlp)
        )
        grad_stream = grad_stream + grad_input
        summed = (
            lax.psum_scatter(
                flatten_rows(qkv_weight_grad), ("dp", "cp"), scatter_dimension=0, tiled=True
            ),
            lax.psum_scatter(qkv_bias_grad, ("dp", "cp"), scatter_dimension=0, tiled=True),
            lax.psum_scatter(
                flatten_rows(attn_weight_grad), ("dp", "cp"), scatter_dimension=0, tiled=True
            ),
            lax.psum_scatter(bias_grad, ("dp", "cp"), scatter_dimension=0, tiled=True),
            lax.psum_scatter(
                flatten_rows(up_weight_grad), ("dp", "cp"), scatter_dimension=0, tiled=True
            ),
            lax.psum_scatter(up_bias_grad, ("dp", "cp"), scatter_dimension=0, tiled=True),
            lax.psum_scatter(
                flatten_rows(down_weight_grad), ("dp", "cp"), scatter_dimension=0, tiled=True
            ),
            lax.psum_scatter(bias_grad, ("dp", "cp"), scatter_dimension=0, tiled=True),
            lax.psum_scatter(attn_gain_grad, ("dp", "cp"), scatter_dimension=0, tiled=True),
            lax.psum_scatter(attn_shift_grad, ("dp", "cp"), scatter_dimension=0, tiled=True),
            lax.psum_scatter(mlp_gain_grad, ("dp", "cp"), scatter_dimension=0, tiled=True),
            lax.psum_scatter(mlp_shift_grad, ("dp", "cp"), scatter_dimension=0, tiled=True),
        )
        per_layer[depth] = (
            summed[0].reshape(-1, 3 * D),
            summed[1],
            summed[2].reshape(-1, D),
            summed[3],
            summed[4].reshape(-1, FF),
            summed[5],
            summed[6].reshape(-1, D),
            summed[7],
            summed[8],
            summed[9],
            summed[10],
            summed[11],
        )
    stacked = [stack_layers(per_layer, member) for member in range(12)]
    return (
        stream.astype(jnp.bfloat16),
        grad_stream,
        stacked[0],
        stacked[1],
        stacked[2],
        stacked[3],
        stacked[4],
        stacked[5],
        stacked[6],
        stacked[7],
        stacked[8],
        stacked[9],
        stacked[10],
        stacked[11],
    )


TEAM = 4
TEAM_AXES = ("core", "x")
LINE_AXES = ("z", "y")
LINE = 4
MINE = (3 * D) // TEAM
HCOLS = D // TEAM
UCOLS = FF // TEAM
VMEM_BYTES = 56 * 1024 * 1024
BF = jnp.bfloat16
F32 = jnp.float32


def call(body, out_shape, name, operands, scratch=()):
    return pl.pallas_call(
        body,
        out_shape=out_shape,
        scratch_shapes=list(scratch),
        compiler_params=pltpu.CompilerParams(vmem_limit_bytes=VMEM_BYTES),
        name=name,
    )(*operands)


def shape(dims, kind):
    return jax.ShapeDtypeStruct(dims, kind)


def mm(left, right):
    return jnp.dot(left, right, preferred_element_type=F32)


def mm_t(left, right):
    return lax.dot_general(left, right, (((1,), (1,)), ((), ())), preferred_element_type=F32)


def t_mm(left, right):
    return lax.dot_general(left, right, (((0,), (0,)), ((), ())), preferred_element_type=F32)


def pick(member, pieces, wanted):
    chosen = pieces[0]
    for s in range(1, TEAM):
        chosen = jnp.where((member ^ s) == wanted, pieces[s], chosen)
    return chosen


def small_rows(vectors, depth):
    rows = []
    for vector in vectors:
        values = vector[depth : depth + 1].astype(F32)
        rows.append(
            jnp.concatenate([values, jnp.zeros((1, 128 - values.shape[1]), F32)], axis=1)
        )
    return jnp.concatenate(rows, axis=0)


def pack_body(me_ref, qkv_ref, up_ref, *refs):
    vectors, outs = [r[...] for r in refs[:8]], refs[8:]
    me = me_ref[0]
    small = jnp.concatenate([small_rows(vectors, depth) for depth in range(LAYERS)], axis=0)
    small = jnp.concatenate([small, jnp.zeros((small.shape[0], UCOLS - 128), F32)], axis=1)
    parts = [[] for _ in range(TEAM)]
    for depth in range(LAYERS):
        rows = qkv_ref.shape[1]
        qkv = qkv_ref[depth].astype(F32)
        up = up_ref[depth].astype(F32)
        blocks = up.shape[1] // (TEAM * 96)
        for p in range(TEAM):
            parts[p].append(
                jnp.concatenate(
                    [up[:, 96 * (TEAM * b + p) : 96 * (TEAM * b + p + 1)] for b in range(blocks)],
                    axis=1,
                )
            )
            parts[p].append(
                jnp.concatenate(
                    [qkv[:, D * t + HCOLS * p : D * t + HCOLS * (p + 1)] for t in range(3)]
                    + [jnp.zeros((rows, UCOLS - MINE), F32)],
                    axis=1,
                )
            )
    parts = [jnp.concatenate(group, axis=0) for group in parts]
    for s in range(TEAM):
        chosen = parts[0]
        for p in range(1, TEAM):
            chosen = jnp.where((me ^ s) == p, parts[p], chosen)
        outs[s][...] = jnp.concatenate([chosen, small], axis=0).astype(BF)


def assemble_body(me_ref, p0, p1, p2, p3, attn_ref, down_ref, *outs):
    me = me_ref[0]
    slots = [r[...].astype(F32) for r in (p0, p1, p2, p3)]
    ordered = [pick(me, slots, p) for p in range(TEAM)]
    for depth, out in enumerate(outs):
        base = 48 * depth
        up = jnp.concatenate([piece[base : base + 24] for piece in ordered], axis=0)
        qkv = jnp.concatenate([piece[base + 24 : base + 48] for piece in ordered], axis=0)
        attn = attn_ref[depth].astype(F32)
        side = jnp.concatenate([attn[:, HCOLS * n : HCOLS * (n + 1)] for n in range(4)], axis=0)
        out[0:96] = up.astype(BF)
        out[96:192] = down_ref[depth]
        out[192:288] = jnp.concatenate([qkv[:, :MINE], side], axis=1).astype(BF)
        if out.shape[0] > 288:
            small = jnp.concatenate(
                [piece[96:112, :128] for piece in ordered] + [jnp.zeros((16, D - 4 * 128), F32)],
                axis=1,
            )
            out[288:304] = small.astype(BF)


def source_team(me_ref, index):
    shift, flip = index % LINE, index // LINE
    return 2 * lax.rem(me_ref[1] + LINE - shift, LINE) + (me_ref[2] ^ flip)


def target_team(me_ref, index):
    shift, flip = index % LINE, index // LINE
    return 2 * lax.rem(me_ref[1] + shift, LINE) + (me_ref[2] ^ flip)


def place(me_ref, pieces, whole):
    for index, piece in enumerate(pieces):
        whole[source_team(me_ref, index)] = piece[...]


def hand_out(me_ref, whole, keep, sends, order):
    for s in range(LINE):
        keep[s] = whole[target_team(me_ref, s)]
    for send, slots in zip(sends, order):
        for n, s in enumerate(slots):
            send[n] = whole[target_team(me_ref, LINE + s)]


ALL_SLOTS = (tuple(range(LINE)),)
HALVES = ((1, 3), (2, 0))


def add_body(slots, places, me_ref, keep, received, *outs):
    for s, n, out in zip(slots, places, outs):
        out[...] = (keep[s].astype(F32) + received[n].astype(F32)).astype(BF)


def add_both_body(slots, places, me_ref, m_keep, m_received, a_keep, a_received, *outs):
    for s, n, out in zip(slots, places, outs):
        out[0:192] = (m_keep[s].astype(F32) + m_received[n].astype(F32)).astype(BF)
        out[192:304] = (a_keep[s].astype(F32) + a_received[s].astype(F32)).astype(BF)


def line_sum_body(me_ref, own, r1, r2, r3, keep_ref, send_ref):
    for f, out in enumerate((keep_ref, send_ref)):
        total = own[f].astype(F32) + r1[f].astype(F32) + r2[f].astype(F32) + r3[f].astype(F32)
        out[...] = total.astype(out.dtype)


def layer_vectors(me_ref, whole, depth):
    me = me_ref[0]
    small = [whole[k].astype(F32) for k in range(2 * LINE)]
    fields = [block[8 * depth : 8 * (depth + 1)] for block in small]
    shared = jnp.concatenate(
        [block[2:8, 128 * p : 128 * p + 24] for block in fields for p in range(TEAM)], axis=1
    )
    up_rows, qkv_rows = [], []
    qkv = jnp.concatenate(
        [block[0:1, 128 * p : 128 * p + 72] for block in fields for p in range(TEAM)], axis=1
    )
    for p in range(TEAM):
        up_rows.append(
            jnp.concatenate([block[1:2, 128 * p : 128 * p + 96] for block in fields], axis=1)
        )
        qkv_rows.append(
            jnp.concatenate(
                [qkv[:, D * t + HCOLS * p : D * t + HCOLS * (p + 1)] for t in range(3)]
                + [jnp.zeros((1, D - MINE), F32)],
                axis=1,
            )
        )
    up_mine, qkv_mine = up_rows[0], qkv_rows[0]
    for p in range(1, TEAM):
        up_mine = jnp.where(me == p, up_rows[p], up_mine)
        qkv_mine = jnp.where(me == p, qkv_rows[p], qkv_mine)
    return jnp.concatenate([shared, up_mine, qkv_mine], axis=0)


def attn_weights(whole):
    qkv = whole[:, 0:96, :][:, :, :MINE].reshape(D, MINE)
    side = whole[:, 0:96, MINE:].astype(F32)
    out = jnp.concatenate(
        [side[:, 24 * n : 24 * (n + 1), :].reshape(HCOLS, HCOLS) for n in range(4)], axis=1
    )
    return qkv, out.astype(BF)


def project(scaled, vec, weight, cosine, sine):
    normed = (scaled * vec[0:1] + vec[1:2]).astype(BF)
    projected = mm(normed, weight) + vec[7:8, :MINE]
    turned = turn(projected[:, : 2 * HCOLS], cosine, sine)
    queries = (turned[:, :HCOLS] * 0.125).astype(BF)
    keys = turned[:, HCOLS:].astype(BF)
    values = projected[:, 2 * HCOLS :].astype(BF)
    return normed, queries, keys, values


def attend_body(me_ref, x0, x1, x2, x3, *refs):
    pieces, smalls = refs[:8], refs[8:16]
    cos_ref, sin_ref, mask_ref, y_ref, vec_ref, whole, small = refs[16:]
    place(me_ref, pieces, whole)
    place(me_ref, smalls, small)
    for depth in range(LAYERS):
        vec_ref[depth] = layer_vectors(me_ref, small, depth)
    vec = vec_ref[0]
    weight, out_weight = attn_weights(whole)
    for g, (first, second) in enumerate(((x0, x1), (x2, x3))):
        rows = pl.ds(PAIR * g, PAIR)
        scaled, _ = norm_parts(two_slots(first[...], second[...]))
        _, queries, keys, values = project(scaled, vec, weight, cos_ref[rows, :], sin_ref[rows, :])
        total = jnp.zeros((PAIR, HCOLS), F32)
        for head in range(HEADS // TEAM):
            owned = head_mask(PAIR, head)
            scores = mm_t(jnp.where(owned, queries, jnp.zeros_like(queries)), keys) + mask_ref[g]
            weights = jnp.exp(scores - jnp.max(scores, axis=-1, keepdims=True))
            below = jnp.sum(weights, axis=-1, keepdims=True)
            total = total + jnp.where(owned, mm(weights.astype(BF), values) / below, 0.0)
        y_ref[rows, :] = mm(total.astype(BF), out_weight)


def store_pair(g, result, own, near, far):
    if g == 0:
        own[...] = result[0:TOK]
        near[...] = result[TOK:]
    else:
        far[...] = result.astype(BF)


def mlp_body(me_ref, x0, x1, x2, x3, *refs):
    pieces, (vec_ref, a_ref, y0, y1, y23, whole) = refs[:8], refs[8:]
    place(me_ref, pieces, whole)
    vec = vec_ref[0]
    up = whole[:, 0:96, :].reshape(D, UCOLS)
    down = whole[:, 96:192, :].reshape(UCOLS, D)
    for g, (first, second) in enumerate(((x0, x1), (x2, x3))):
        rows = pl.ds(PAIR * g, PAIR)
        scaled, _ = norm_parts(two_slots(first[...], second[...]))
        normed = (scaled * vec[2:3] + vec[3:4]).astype(BF)
        before = mm(normed, up) + vec[6:7]
        hidden = (before * (0.5 * (1.0 + lax.erf(before * (1.0 / math.sqrt(2.0)))))).astype(BF)
        result = mm(hidden, down) + a_ref[rows, :]
        store_pair(g, result, y0, y1, y23)


def mlp_both_body(depth, last, me_ref, x0, x1, x2, x3, g0, g1, g2, g3, *refs):
    pieces, vec_ref, (dn_ref, sum_ref), refs = refs[:8], refs[8], refs[9:11], refs[11:]
    if last:
        y_ref, refs = refs[0], refs[1:]
    whole, grads, c_s, hid_s, du_s, gb_s = refs[-6:]
    place(me_ref, pieces, whole)
    vec = vec_ref[depth]
    up = whole[:, 0:96, :].reshape(D, UCOLS)
    down = whole[:, 96:192, :].reshape(UCOLS, D)
    gain_sum = jnp.zeros((1, D), F32)
    shift_sum = jnp.zeros((1, D), F32)
    bias_sum = jnp.zeros((1, D), F32)
    up_sum = jnp.zeros((1, UCOLS), F32)
    for g, (first, second, g_first, g_second) in enumerate(((x0, x1, g0, g1), (x2, x3, g2, g3))):
        rows = pl.ds(PAIR * g, PAIR)
        scaled, _ = norm_parts(two_slots(first[...], second[...]))
        normed = (scaled * vec[2:3] + vec[3:4]).astype(BF)
        c_s[rows, :] = normed
        low = jnp.concatenate([g_first[...], g_second[...]], axis=0)
        gb_s[rows, :] = low
        hidden, slope = gelu_parts(mm(normed, up) + vec[6:7])
        hidden = hidden.astype(BF)
        hid_s[rows, :] = hidden
        if last:
            y_ref[rows, :] = mm(hidden, down)
        du = (mm_t(low, down) * slope).astype(BF)
        du_s[rows, :] = du
        dc = mm_t(du, up)
        dn_ref[rows, :] = dc * vec[2:3]
        gain_sum = gain_sum + jnp.sum(dc * scaled, axis=0, keepdims=True)
        shift_sum = shift_sum + jnp.sum(dc, axis=0, keepdims=True)
        bias_sum = bias_sum + jnp.sum(low.astype(F32), axis=0, keepdims=True)
        up_sum = up_sum + jnp.sum(du.astype(F32), axis=0, keepdims=True)
    grads[:, 0:96, :] = t_mm(c_s[...], du_s[...]).reshape(-1, 96, UCOLS).astype(BF)
    grads[:, 96:192, :] = t_mm(hid_s[...], gb_s[...]).reshape(-1, 96, D).astype(BF)
    if last:
        for s, out in enumerate(refs[0:LINE]):
            for f in range(2):
                out[f] = grads[target_team(me_ref, LINE * f + s), 0:EARLY, :]
        keep, send = refs[LINE : LINE + 2]
        for s in range(LINE):
            keep[s] = grads[target_team(me_ref, s), EARLY:192, :]
            send[s] = grads[target_team(me_ref, LINE + s), EARLY:192, :]
    else:
        hand_out(me_ref, grads, refs[0], refs[1:3], HALVES)
    sum_ref[...] = jnp.concatenate(
        [bias_sum, up_sum, gain_sum, shift_sum, jnp.zeros((4, D), F32)], axis=0
    )


def attend_both_body(depth, last, me_ref, x0, x1, x2, x3, g0, g1, g2, g3, *refs):
    pieces, (vec_ref, cos_ref, sin_ref, mask_ref, dn_ref, sum_ref) = refs[:8], refs[8:14]
    refs = refs[14:]
    if last:
        y_ref, refs = refs[0], refs[1:]
    blocks, (n0, n1, n23) = refs[:2], refs[2:5]
    whole, grads, a_s, dp_s, o_s, gb_s = refs[-6:]
    place(me_ref, pieces, whole)
    vec = vec_ref[depth]
    weight, out_weight = attn_weights(whole)
    gain_sum = jnp.zeros((1, D), F32)
    shift_sum = jnp.zeros((1, D), F32)
    bias_sum = jnp.zeros((1, MINE), F32)
    for g, (first, second, g_first, g_second) in enumerate(((x0, x1, g0, g1), (x2, x3, g2, g3))):
        rows = pl.ds(PAIR * g, PAIR)
        cosine, sine = cos_ref[rows, :], sin_ref[rows, :]
        scaled, _ = norm_parts(two_slots(first[...], second[...]))
        normed, queries, keys, values = project(scaled, vec, weight, cosine, sine)
        a_s[rows, :] = normed
        low = jnp.concatenate([g_first[...], g_second[...]], axis=0)
        gb_s[rows, :] = low
        grad_o = mm_t(low, out_weight).astype(BF)
        zero = jnp.zeros_like(queries)
        out = jnp.zeros((PAIR, HCOLS), F32)
        dq = jnp.zeros((PAIR, HCOLS), F32)
        dk = jnp.zeros((PAIR, HCOLS), F32)
        dv = jnp.zeros((PAIR, HCOLS), F32)
        for head in range(HEADS // TEAM):
            owned = head_mask(PAIR, head)
            scores = mm_t(jnp.where(owned, queries, zero), keys) + mask_ref[g]
            weights = jnp.exp(scores - jnp.max(scores, axis=-1, keepdims=True))
            weights = weights / jnp.sum(weights, axis=-1, keepdims=True)
            rounded = weights.astype(BF)
            dweights = mm_t(jnp.where(owned, grad_o, zero), values)
            delta = jnp.sum(weights * dweights, axis=-1, keepdims=True)
            dscores = (weights * (dweights - delta)).astype(BF)
            out = out + jnp.where(owned, mm(rounded, values), 0.0)
            dq = dq + jnp.where(owned, mm(dscores, keys), 0.0)
            dk = dk + jnp.where(owned, t_mm(dscores, queries), 0.0)
            dv = dv + jnp.where(owned, t_mm(rounded, grad_o), 0.0)
        o_s[rows, :] = out.astype(BF)
        both = turn(jnp.concatenate([dq * 0.125, dk], axis=1), cosine, -sine)
        dproj = jnp.concatenate([both, dv], axis=1).astype(BF)
        dp_s[rows, :] = dproj
        bias_sum = bias_sum + jnp.sum(dproj.astype(F32), axis=0, keepdims=True)
        da = mm_t(dproj, weight)
        gain_sum = gain_sum + jnp.sum(da * scaled, axis=0, keepdims=True)
        shift_sum = shift_sum + jnp.sum(da, axis=0, keepdims=True)
        dn = dn_ref[rows, :] + da * vec[0:1]
        store_pair(g, dn, n0, n1, n23)
        if last:
            result = y_ref[rows, :] + mm(out.astype(BF), out_weight)
            store_pair(g, result, *refs[5:8])
    qkv_grad = t_mm(a_s[...], dp_s[...]).reshape(-1, 96, MINE)
    out_grad = t_mm(o_s[...], gb_s[...])
    side = jnp.concatenate(
        [out_grad[:, HCOLS * n : HCOLS * (n + 1)].reshape(-1, 24, HCOLS) for n in range(4)], axis=1
    )
    grads[:, 0:96, :] = jnp.concatenate([qkv_grad, side], axis=2).astype(BF)
    sums = sum_ref[...]
    vectors = jnp.concatenate([sums[0:2], gain_sum, shift_sum, sums[2:4]], axis=0)
    me = me_ref[0]
    spread = jnp.concatenate(
        [
            jnp.where(me == p, bias_sum[:, HCOLS * t : HCOLS * (t + 1)], 0.0)
            for t in range(3)
            for p in range(TEAM)
        ],
        axis=1,
    )
    for k in range(2 * LINE):
        shared = jnp.concatenate(
            [vectors[:, 96 * k : 96 * (k + 1)], jnp.zeros((6, D - 96), F32)], axis=1
        )
        bias = jnp.concatenate(
            [spread[:, 288 * k : 288 * (k + 1)], jnp.zeros((1, D - 288), F32)], axis=1
        )
        grads[k, 96:112, :] = jnp.concatenate([shared, bias, jnp.zeros((9, D), F32)], axis=0).astype(BF)
    hand_out(me_ref, grads, blocks[0], blocks[1:], ALL_SLOTS)


def residual_body(me_ref, x_ref, y0, y1, y2, vec_ref, out_ref, low_ref):
    depth = 0 if x_ref.dtype == BF else 1
    total = y0[...] + y1[...].astype(F32) + y2[...].astype(F32)
    result = x_ref[...].astype(F32) + total + (vec_ref[depth, 4:5] + vec_ref[depth, 5:6])
    out_ref[...] = result
    low_ref[...] = result.astype(BF)

def norm_parts(stream):
    centered = stream - jnp.mean(stream, axis=-1, keepdims=True)
    spread = jnp.mean(centered * centered, axis=-1, keepdims=True)
    inverse = lax.rsqrt(spread + 1e-05)
    return centered * inverse, inverse


def two_slots(first, second):
    return jnp.concatenate([first[0:TOK].astype(F32), second[0:TOK].astype(F32)], axis=0)


TOK = 128
EARLY = 48
PAIR = 2 * TOK


def turn(block, cosine, sine):
    lane = lax.broadcasted_iota(jnp.int32, (block.shape[0], 128), 1) % HEAD
    tiles = []
    for t in range(block.shape[1] // 128):
        tile = block[:, 128 * t : 128 * (t + 1)]
        swapped = jnp.where(
            lane < ROT // 2, pltpu.roll(tile, 128 - ROT // 2, 1), pltpu.roll(tile, ROT // 2, 1)
        )
        tiles.append(tile * cosine + swapped * sine)
    return jnp.concatenate(tiles, axis=1)


def head_mask(rows, head):
    lane = lax.broadcasted_iota(jnp.int32, (rows, HCOLS), 1)
    return (lane >= head * HEAD) & (lane < (head + 1) * HEAD)


def gelu_parts(u):
    cdf = 0.5 * (1.0 + lax.erf(u * (1.0 / math.sqrt(2.0))))
    density = jnp.exp(-0.5 * u * u) * (1.0 / math.sqrt(2.0 * math.pi))
    return u * cdf, cdf + u * density


def norm_back_body(me_ref, x_ref, g_ref, n0, n1, n2, out_ref, low_ref):
    scaled, inverse = norm_parts(x_ref[...].astype(F32))
    dn = n0[...] + n1[...].astype(F32) + n2[...].astype(F32)
    centered = dn - jnp.mean(dn, axis=-1, keepdims=True)
    moment = jnp.mean(dn * scaled, axis=-1, keepdims=True)
    result = g_ref[...].astype(F32) + inverse * (centered - scaled * moment)
    out_ref[...] = result
    low_ref[...] = result.astype(BF)


def total(group):
    result = group[0].astype(F32)
    for term in group[1:]:
        result = result + term.astype(F32)
    return result


def by_owner(me_ref, parts, outs, start):
    me = me_ref[0]
    for s, out in enumerate(outs):
        piece = parts[0]
        for p in range(1, TEAM):
            piece = jnp.where((me ^ s) == p, parts[p], piece)
        out[start : start + 32] = piece.astype(BF)


def split_body(early, me_ref, *refs):
    outs, (down_ref, attn_ref, small_ref), refs = refs[-7:-3], refs[-3:], refs[:-7]
    split_attend(me_ref, refs[:5], outs, attn_ref, small_ref)
    refs = refs[5:]
    size = refs[0].shape[1]
    rest = total([refs[0][0], refs[1][0]] + [ref[0:size, :] for ref in refs[2:5]])
    if early:
        rest = jnp.concatenate([total([refs[5][...], refs[6][...]]), rest], axis=0)
    down_ref[...] = rest[96:192]
    blank = jnp.zeros((8, D), F32)
    parts = [
        jnp.concatenate([rest[24 * p : 24 * (p + 1)], blank], axis=0) for p in range(TEAM)
    ]
    by_owner(me_ref, parts, outs, 0)


def split_attend(me_ref, refs, outs, attn_ref, small_ref):
    me = me_ref[0]
    attn = total([refs[0][0], refs[1][0]] + [ref[-112:, :] for ref in refs[2:]])
    side = attn[0:96, MINE:]
    attn_ref[...] = jnp.concatenate(
        [side[24 * n : 24 * (n + 1)] for n in range(4)], axis=1
    ).astype(BF)
    qkv = jnp.concatenate([attn[0:96, :MINE], jnp.zeros((96, UCOLS - MINE), F32)], axis=1)
    small = attn[96:112]
    parts, bias = [], jnp.zeros((1, 24), F32)
    for p in range(TEAM):
        rows = slice(24 * p, 24 * (p + 1))
        gains = jnp.concatenate([small[2:6, rows], jnp.zeros((4, D - 24), F32)], axis=1)
        qkv_bias = jnp.concatenate(
            [small[6:7, 72 * p : 72 * (p + 1)], jnp.zeros((1, D - 72), F32)], axis=1
        )
        parts.append(jnp.concatenate([qkv[rows], gains, qkv_bias, jnp.zeros((3, D), F32)], axis=0))
        bias = jnp.where(me == p, small[0:1, rows], bias)
    small_ref[...] = jnp.concatenate(
        [
            jnp.concatenate([bias, jnp.zeros((1, 104), F32)], axis=1),
            small[1:2, :128],
            jnp.zeros((6, 128), F32),
        ],
        axis=0,
    )
    by_owner(me_ref, parts, outs, 32)


def unpack_body(me_ref, *refs):
    me = me_ref[0]
    (
        qkv_ref, qkv_b_ref, attn_ref, attn_b_ref, up_ref, up_b_ref, down_ref,
        ga_ref, sa_ref, gm_ref, sm_ref,
    ) = refs[7 * LAYERS :]
    gain_refs = (ga_ref, sa_ref, gm_ref, sm_ref)
    for depth in range(LAYERS):
        group = refs[7 * depth : 7 * (depth + 1)]
        down_rows, own_small, attn_rows = group[TEAM:]
        slots = [r[...].astype(F32) for r in group[:TEAM]]
        ordered = [pick(me, slots, p) for p in range(TEAM)]
        blocks = FF // (96 * TEAM)
        up_ref[depth] = jnp.concatenate(
            [ordered[p][0:24, 96 * b : 96 * (b + 1)] for b in range(blocks) for p in range(TEAM)],
            axis=1,
        )
        qkv_ref[depth] = jnp.concatenate(
            [
                ordered[p][32:56, HCOLS * t : HCOLS * (t + 1)]
                for t in range(3)
                for p in range(TEAM)
            ],
            axis=1,
        )
        attn_ref[depth] = attn_rows[...].astype(F32)
        down_ref[depth] = down_rows[...]
        small = slots[0][56:64, :128] + slots[1][56:64, :128]
        small = small + slots[2][56:64, :128] + slots[3][56:64, :128]
        for n, ref in enumerate(gain_refs):
            ref[depth : depth + 1] = small[n : n + 1, :24]
        qkv_b_ref[depth : depth + 1] = small[4:5, :72]
        attn_b_ref[depth : depth + 1] = own_small[0:1, :24]
        up_b_ref[depth : depth + 1] = own_small[1:2, :96]


def team_send(piece, slot):
    flips = [(m, m ^ slot) for m in range(TEAM)]
    return lax.ppermute(piece, TEAM_AXES, flips)


def line_shift(piece, shift):
    size = lax.axis_size("z")
    return lax.ppermute(piece, "z", [(i, (i + shift) % size) for i in range(size)])


def line_flip(piece):
    return lax.ppermute(piece, "y", [(0, 1), (1, 0)])


def after(value, *others):
    return lax.optimization_barrier((value, *others))[0]


def line_near(piece):
    first = line_shift(piece, 1)
    third = line_shift(piece, 3)
    return [piece, first, line_shift(after(piece, first, third), 2), third]


def local_team(
    tokens, segment_ids, cotangent, qkv_weight, qkv_bias, attn_weight, attn_bias,
    up_weight, up_bias, down_weight, down_bias, attn_gain, attn_shift, mlp_gain, mlp_shift,
):
    lines = lax.axis_size("z") * lax.axis_size("y")
    world = lines * TEAM
    member = lax.axis_index("core") * 2 + lax.axis_index("x")
    me = jnp.stack([member, lax.axis_index("z"), lax.axis_index("y")]).astype(jnp.int32)
    everywhere = LINE_AXES + TEAM_AXES
    tok_all = TEAM * TOK
    whole_spec = pl.BlockSpec(memory_space=pltpu.VMEM)

    def run(body, out_shape, name, operands, scratch=()):
        specs = [whole_spec if isinstance(x, jax.Array) else x[1] for x in operands]
        return pl.pallas_call(
            body,
            grid=(1,),
            out_shape=out_shape,
            in_specs=[pl.BlockSpec(memory_space=pltpu.SMEM)] + specs,
            scratch_shapes=[pltpu.VMEM(dims, kind) for dims, kind in scratch],
            compiler_params=pltpu.CompilerParams(vmem_limit_bytes=VMEM_BYTES),
            name=name,
        )(me, *[x if isinstance(x, jax.Array) else x[0] for x in operands])

    def part(rows, start):
        return pl.BlockSpec((rows, D), lambda i: (start // rows, 0))

    def one_of(array, index):
        return (array, pl.BlockSpec((1,) + array.shape[1:], lambda i: (index, 0, 0)))

    def exchange(blocks):
        return [blocks[0]] + [team_send(blocks[s], s) for s in range(1, TEAM)]

    small = (
        qkv_bias, up_bias, attn_gain, attn_shift, mlp_gain, mlp_shift, attn_bias, down_bias
    )
    packed = run(
        pack_body, [shape((112, D), BF)] * TEAM, "pack_weights", (qkv_weight, up_weight, *small)
    )
    spread = [(i, TEAM * (i % lines) + i // lines) for i in range(world)]
    gather_back = [(b, a) for a, b in spread]
    attn_piece = lax.ppermute(attn_weight, everywhere, spread)
    chunks = run(
        assemble_body,
        [shape((304, D), BF), shape((288, D), BF)],
        "assemble_weights",
        (*exchange(packed), attn_piece, down_weight),
    )
    near = line_near(chunks[0])
    pieces = [near + [line_flip(p) for p in near]]
    near = line_near(after(chunks[1], near[2], pieces[0][5], pieces[0][7]))
    pieces.append(near + [line_flip(p) for p in (chunks[1], *near[1:])])
    m_parts = [[(p, part(192, 0)) for p in group] for group in pieces]
    a_parts = [[(p, part(96, 192)) for p in group] for group in pieces]
    small_parts = [(p, part(16, 288)) for p in pieces[0]]

    def gather_team(piece, *others):
        other = after(team_send(piece, 1), *others)
        return piece, other, team_send(jnp.concatenate([piece, other], axis=0), 2)

    def slots_of(gathered, start=0):
        piece, other, far = gathered
        size = piece.shape[0]
        return [
            (piece, part(TOK, start)), (other, part(TOK, start)),
            (far, part(TOK, start)), (far, part(TOK, size + start)),
        ]

    def sum_team(own, near, far, *others):
        other = after(team_send(far, 2), *others)
        both = (near + other[TOK:].astype(F32)).astype(BF)
        return own, (other, part(TOK, 0)), team_send(both, 1)

    ids_rows = jnp.pad(segment_ids.astype(BF)[None, :], ((0, TOK - 1), (0, D - TOK)))
    load = jnp.concatenate([tokens, cotangent, ids_rows], axis=0)
    loads = gather_team(after(load, pieces[0][1], pieces[0][3], pieces[0][4], pieces[1][4]), pieces[0][2], pieces[0][5], pieces[0][7])
    token_slots = slots_of(loads)
    here = lax.axis_index("x")
    rows = jnp.arange(TOK, dtype=jnp.int32)
    places = jnp.concatenate([here * TOK + rows, (1 - here) * TOK + rows])
    masks, cosines, sines = [], [], []
    lane = jnp.arange(128, dtype=jnp.int32) % HEAD
    inverse = 10000.0 ** (-(lane % (ROT // 2) * 2).astype(F32) / ROT)
    id_rows = [
        loads[0][2 * TOK, :TOK], loads[1][2 * TOK, :TOK],
        loads[2][2 * TOK, :TOK], loads[2][5 * TOK, :TOK],
    ]
    for g in range(2):
        ids = jnp.concatenate(id_rows[2 * g : 2 * g + 2]).astype(F32)
        visible = (places[None, :] <= places[:, None]) & (ids[None, :] == ids[:, None])
        masks.append(jnp.where(visible, 0.0, -1e30).astype(F32))
        position = places - jnp.sum((ids[None, :] < ids[:, None]).astype(jnp.int32), axis=1)
        phases = position.astype(F32)[:, None] * inverse[None, :]
        cosines.append(jnp.where(lane[None, :] < ROT, jnp.cos(phases), 1.0))
        sign = jnp.where(lane < ROT // 2, -1.0, jnp.where(lane < ROT, 1.0, 0.0))
        sines.append(jnp.sin(phases) * sign[None, :])
    mask = jnp.stack(masks)
    cosine, sine = jnp.concatenate(cosines), jnp.concatenate(sines)

    partials = [shape((TOK, D), F32)] * 2 + [shape((PAIR, D), BF)]
    stream_pair = [shape((TOK, D), F32), shape((TOK, D), BF)]
    wide = ((tok_all, D), BF)

    attn_out, vec = run(
        attend_body,
        [shape((tok_all, D), F32), shape((LAYERS, 8, D), F32)],
        "attend_forward",
        (*token_slots, *a_parts[0], *small_parts, cosine, sine, mask),
        [((lines, 96, D), BF), ((lines, 16, D), BF)],
    )
    y = run(
        mlp_body,
        partials,
        "mlp_forward",
        (*token_slots, *m_parts[0], vec, attn_out),
        [((lines, 192, D), BF)],
    )

    def residual(stream, blocks):
        return run(residual_body, stream_pair, "residual", (stream, *sum_team(*blocks), vec))

    stream, low = residual(tokens, (after(y[0], pieces[1][4]), *y[1:]))
    streams = [tokens, stream]
    slots = [token_slots, slots_of(gather_team(low, pieces[1][5], pieces[1][7]))]

    grad = cotangent
    grad_slots = slots_of(loads, TOK)
    outs = [None] * LAYERS
    block_m, block_a = shape((192, D), BF), shape((112, D), BF)

    def mlp_back(depth, slots, grad_slots, grads):
        last = depth == LAYERS - 1
        return run(
            partial(mlp_both_body, depth, last),
            [shape((tok_all, D), F32), shape((8, D), F32)]
            + ([shape((tok_all, D), F32)] if last else [])
            + grads,
            "mlp_both",
            (*slots, *grad_slots, *m_parts[depth], vec),
            [((lines, 192, D), BF), ((lines, 192, D), BF), wide, wide, wide, wide],
        )

    def attend_back(depth, slots, grad_slots, rest, *others):
        last = depth == LAYERS - 1
        result = run(
            partial(attend_both_body, depth, last),
            [shape((4, 112, D), BF)] * 2 + partials + (partials if last else []),
            "attend_both",
            (*slots, *grad_slots, *a_parts[depth], vec, cosine, sine, mask, *rest),
            [
                ((lines, 96, D), BF),
                ((lines, 112, D), BF),
                wide,
                ((tok_all, MINE), BF),
                ((tok_all, HCOLS), BF),
                wide,
            ],
        )
        return result[0], line_flip(after(result[1], *others)), result[2:5], result[5:]

    def norm_back(depth, grad, received):
        return run(
            norm_back_body, stream_pair, "norm_backward", (streams[depth], grad, *received)
        )

    def add(kind, keep, other, slots, places, name):
        return run(partial(add_body, slots, places), [kind] * len(slots), name, (keep, other))

    def shifts(sums):
        return [line_shift(piece, s + 1) for s, piece in enumerate(sums)]

    def split(attend, mlp, early=()):
        keep, other, *sums = attend
        m_keep, m_other, *m_sums = mlp
        mine = run(
            partial(split_body, bool(early)),
            [shape((64, D), BF)] * TEAM
            + [shape((96, D), F32), shape((24, D), BF), shape((8, 128), F32)],
            "split_gradients",
            (one_of(keep, 0), one_of(other, 0), *sums, one_of(m_keep, 0), m_other, *m_sums, *early),
        )
        attn_rows = lax.ppermute(mine[TEAM + 1], everywhere, gather_back)
        return exchange(mine[:TEAM]) + [mine[TEAM], mine[TEAM + 2], attn_rows]

    early_block, late_four = shape((2, EARLY, D), BF), shape((4, 192 - EARLY, D), BF)
    dn, sum_m, y_part, e0, e1, e2, e3, m_keep1, m_send1 = mlp_back(
        1, slots[1], grad_slots, [early_block] * 4 + [late_four] * 2
    )
    early = shifts((e1, e2, e3))
    m_other1 = line_flip(m_send1)
    a_keep1, a_other1, ns, ys = attend_back(1, slots[1], grad_slots, (dn, sum_m, y_part))
    ns = (ns[0], ns[1], after(ns[2], *early))
    grad, low = norm_back(1, grad, sum_team(*ns, m_other1))
    m_added1 = add(
        shape((192 - EARLY, D), BF), m_keep1, after(m_other1, low), (1, 2, 3), (1, 2, 3), "add_mlp"
    )
    m_sums1 = shifts(m_added1)
    gathered = gather_team(low)
    grad_slots = slots_of((after(gathered[0], *m_added1), *gathered[1:]))
    dn, sum_m, m_keep0, m_first0, m_second0 = mlp_back(
        0, slots[0], grad_slots, [shape((4, 192, D), BF)] + [shape((2, 192, D), BF)] * 2
    )
    m_first0 = line_flip(after(m_first0, m_sums1[0]))
    m_second0 = line_flip(after(m_second0, m_sums1[0]))
    a_keep0, a_other0, ns, _ = attend_back(
        0, slots[0], grad_slots, (after(dn, m_sums1[0]), sum_m)
    )
    block_both = shape((304, D), BF)

    def add_both(other, slots, places, name):
        return run(
            partial(add_both_body, slots, places),
            [block_both] * len(slots),
            name,
            (m_keep0, other, a_keep1, a_other1),
        )

    both1, both3 = add_both(after(m_first0, a_keep0, a_other1, *m_sums1), HALVES[0], (0, 1), "add_first")
    first_added = both1
    both1, both3 = line_shift(both1, 1), line_shift(both3, 3)
    grad, _ = norm_back(0, grad, sum_team(ns[0], ns[1], after(ns[2], first_added)))
    _, activations = residual(streams[1], (ys[0], ys[1], after(ys[2], first_added)))
    e_keep, e_send = run(
        line_sum_body,
        [shape((EARLY, D), F32), shape((EARLY, D), BF)],
        "line_sum",
        (e0, after(early[0], first_added), early[1], early[2]),
    )
    e_other = line_flip(e_send)
    (both2,) = add_both(
        after(m_second0, both1, both3, grad, activations, e_other), HALVES[1][:1], (0,), "add_second"
    )
    a_added0 = add(
        block_a, a_keep0, after(a_other0, both2), (1, 2, 3), (1, 2, 3), "add_attend"
    )
    both2 = line_shift(both2, 2)
    a_sums0 = shifts([after(piece, both2) for piece in a_added0])
    both = (both1, both2, both3)
    outs[1] = split(
        (a_keep1, a_other1, *both), (m_keep1, one_of(m_other1, 0), *m_sums1), (e_keep, e_other)
    )
    outs[0] = split(
        (a_keep0, after(a_other0, outs[1][0]), *a_sums0), (m_keep0, one_of(m_second0, 1), *both)
    )
    row_24 = shape((LAYERS, 24), F32)
    final = run(
        unpack_body,
        [
            shape((LAYERS, 24, 3 * D), F32), shape((LAYERS, 72), F32),
            shape((LAYERS, 24, D), F32), row_24,
            shape((LAYERS, 24, FF), F32), shape((LAYERS, 96), F32),
            shape((LAYERS, 96, D), F32), row_24, row_24, row_24, row_24,
        ],
        "unpack_gradients",
        [array for group in outs for array in group],
    )
    return (activations, grad, *final[:7], final[3], *final[7:])


def whole_mesh_solution(mesh):
    in_specs = (
        P(("dp", "cp"), None),
        P(("dp", "cp")),
        P(("dp", "cp"), None),
        P(None, ("dp", "cp"), None),
        P(None, ("dp", "cp")),
        P(None, ("dp", "cp"), None),
        P(None, ("dp", "cp")),
        P(None, ("dp", "cp"), None),
        P(None, ("dp", "cp")),
        P(None, ("dp", "cp"), None),
        P(None, ("dp", "cp")),
        P(None, ("dp", "cp")),
        P(None, ("dp", "cp")),
        P(None, ("dp", "cp")),
        P(None, ("dp", "cp")),
    )
    out_specs = (
        P(("dp", "cp"), None),
        P(("dp", "cp"), None),
        P(None, ("dp", "cp"), None),
        P(None, ("dp", "cp")),
        P(None, ("dp", "cp"), None),
        P(None, ("dp", "cp")),
        P(None, ("dp", "cp"), None),
        P(None, ("dp", "cp")),
        P(None, ("dp", "cp"), None),
        P(None, ("dp", "cp")),
        P(None, ("dp", "cp")),
        P(None, ("dp", "cp")),
        P(None, ("dp", "cp")),
        P(None, ("dp", "cp")),
    )
    return jax.shard_map(local, mesh=mesh, in_specs=in_specs, out_specs=out_specs, check_vma=False)


def solution(mesh):
    teams = mesh.shape["dp"] // 2
    if mesh.shape["cp"] != 2 or teams != 2 * LINE or teams * TEAM * 24 != D:
        return whole_mesh_solution(mesh)
    split_mesh = Mesh(mesh.devices.reshape(teams // 2, 2, 2, 2), ("z", "y", "core", "x"))
    every = ("z", "y", "core", "x")
    row = P(every, None)
    matrix, vector = P(None, every, None), P(None, every)
    in_specs = (row, P(every), row) + (matrix, vector) * 4 + (vector,) * 4
    out_specs = (row, row) + (matrix, vector) * 4 + (vector,) * 4
    return jax.shard_map(
        local_team, mesh=split_mesh, in_specs=in_specs, out_specs=out_specs, check_vma=False
    )
```

```python
from functools import partial
import math

import jax
import jax.numpy as jnp
from jax import lax
from jax.experimental import pallas as pl
from jax.experimental.pallas import tpu as pltpu
from jax.sharding import Mesh, PartitionSpec as P

D = 768
HEADS = 12
HEAD = 64
FF = 3072
ROT = 16
LAYERS = 2


def layer_norm(stream, norm_gain, norm_shift):
    centered = stream - jnp.mean(stream, axis=-1, keepdims=True)
    spread = jnp.mean(centered * centered, axis=-1, keepdims=True)
    return centered * lax.rsqrt(spread + 1e-05) * norm_gain + norm_shift


def both_norms(stream, gain_attn, shift_attn, gain_mlp, shift_mlp):
    return (layer_norm(stream, gain_attn, shift_attn), layer_norm(stream, gain_mlp, shift_mlp))


def angles(positions):
    inverse = 10000.0 ** (-jnp.arange(0, ROT, 2, dtype=jnp.float32) / ROT)
    phases = positions.astype(jnp.float32)[:, None] * inverse[None, :]
    return (jnp.cos(phases)[:, None, :], jnp.sin(phases)[:, None, :])


def rotate(heads_in, cosine_table, sine_table):
    half_rot = cosine_table.shape[-1]
    first_half = heads_in[..., :half_rot]
    second_half = heads_in[..., half_rot : 2 * half_rot]
    untouched = heads_in[..., 2 * half_rot :]
    return jnp.concatenate(
        [
            first_half * cosine_table - second_half * sine_table,
            second_half * cosine_table + first_half * sine_table,
            untouched,
        ],
        axis=-1,
    )


def split_blocks(update, running, key_piece, value_piece, offset):
    piece_rows = key_piece.shape[0]
    block_rows = 512 if piece_rows > 512 and piece_rows % 512 == 0 else piece_rows
    block_count = piece_rows // block_rows
    if block_count == 1:
        return update(running, key_piece, value_piece, offset)

    def advance(state, inputs):
        key_block, value_block, start = inputs
        return (update(state, key_block, value_block, offset + start), None)

    starts = jnp.arange(block_count, dtype=jnp.int32) * block_rows
    state, _ = lax.scan(
        advance,
        running,
        (
            key_piece.reshape(block_count, block_rows, -1),
            value_piece.reshape(block_count, block_rows, -1),
            starts,
        ),
    )
    return state


def stack_layers(per_layer, member):
    return jnp.stack([layer_entry[member] for layer_entry in per_layer])


def flatten_rows(matrix):
    return matrix.reshape(matrix.shape[:-2] + (-1, 128))


def local(
    tokens,
    segment_ids,
    cotangent,
    qkv_weight,
    qkv_bias,
    attn_weight,
    attn_bias,
    up_weight,
    up_bias,
    down_weight,
    down_bias,
    attn_gain,
    attn_shift,
    mlp_gain,
    mlp_shift,
):
    tok_rows = tokens.shape[0]
    group_rows = tok_rows * lax.axis_size("cp")
    score_scale = 1.0 / math.sqrt(HEAD)
    all_segments = lax.all_gather(segment_ids, "cp", axis=0, tiled=True)
    row_index = lax.axis_index("cp") * tok_rows + jnp.arange(tok_rows, dtype=jnp.int32)
    positions = row_index - jnp.sum(
        (all_segments[None, :] < segment_ids[:, None]).astype(jnp.int32), axis=1
    )
    cosine_table, sine_table = angles(positions)

    def visible_mask(offset, block_rows):
        key_index = offset + jnp.arange(block_rows, dtype=jnp.int32)
        key_segment = lax.dynamic_slice_in_dim(all_segments, offset, block_rows)
        return (key_index[None, :] <= row_index[:, None]) & (
            key_segment[None, :] == segment_ids[:, None]
        )

    def online_step(query_heads, running, key_block, value_block, offset):
        row_max, denominator, weighted = running
        block_rows = key_block.shape[0]
        key_heads = key_block.reshape(block_rows, HEADS, HEAD)
        value_heads = value_block.reshape(block_rows, HEADS, HEAD)
        scores = (
            jnp.einsum("qhd,khd->hqk", query_heads, key_heads, preferred_element_type=jnp.float32)
            * score_scale
        )
        visible = visible_mask(offset, block_rows)
        scores = jnp.where(visible[None], scores, -1e30)
        new_max = jnp.maximum(row_max, jnp.max(scores, axis=-1))
        rescale = jnp.exp(row_max - new_max)
        weights = jnp.where(visible[None], jnp.exp(scores - new_max[..., None]), 0.0)
        denominator = denominator * rescale + jnp.sum(weights, axis=-1)
        weighted = weighted * rescale[..., None] + jnp.einsum(
            "hqk,khd->hqd",
            weights.astype(jnp.bfloat16),
            value_heads,
            preferred_element_type=jnp.float32,
        )
        return (new_max, denominator, weighted)

    stream = tokens.astype(jnp.float32)
    stored = []
    for depth in range(LAYERS):
        params = (
            lax.all_gather(qkv_weight[depth], ("dp", "cp"), axis=0, tiled=True),
            lax.all_gather(qkv_bias[depth], ("dp", "cp"), axis=0, tiled=True),
            lax.all_gather(attn_weight[depth], ("dp", "cp"), axis=0, tiled=True),
            lax.all_gather(attn_bias[depth], ("dp", "cp"), axis=0, tiled=True),
            lax.all_gather(up_weight[depth], ("dp", "cp"), axis=0, tiled=True),
            lax.all_gather(up_bias[depth], ("dp", "cp"), axis=0, tiled=True),
            lax.all_gather(down_weight[depth], ("dp", "cp"), axis=0, tiled=True),
            lax.all_gather(down_bias[depth], ("dp", "cp"), axis=0, tiled=True),
            lax.all_gather(attn_gain[depth], ("dp", "cp"), axis=0, tiled=True),
            lax.all_gather(attn_shift[depth], ("dp", "cp"), axis=0, tiled=True),
            lax.all_gather(mlp_gain[depth], ("dp", "cp"), axis=0, tiled=True),
            lax.all_gather(mlp_shift[depth], ("dp", "cp"), axis=0, tiled=True),
        )
        (
            proj_qkv,
            bias_qkv,
            proj_attn,
            bias_attn,
            proj_up,
            bias_up,
            proj_down,
            bias_down,
            gain_attn,
            shift_attn,
            gain_mlp,
            shift_mlp,
        ) = params
        normed_attn, normed_mlp = both_norms(
            stream,
            gain_attn.astype(jnp.float32),
            shift_attn.astype(jnp.float32),
            gain_mlp.astype(jnp.float32),
            shift_mlp.astype(jnp.float32),
        )
        normed_attn = normed_attn.astype(jnp.bfloat16)
        normed_mlp = normed_mlp.astype(jnp.bfloat16)
        projected = jnp.dot(
            normed_attn, proj_qkv, preferred_element_type=jnp.float32
        ) + bias_qkv.astype(jnp.float32)
        queries = rotate(
            projected[:, :D].reshape(tok_rows, HEADS, HEAD), cosine_table, sine_table
        ).astype(jnp.bfloat16)
        key_rows = (
            rotate(projected[:, D : 2 * D].reshape(tok_rows, HEADS, HEAD), cosine_table, sine_table)
            .astype(jnp.bfloat16)
            .reshape(tok_rows, D)
        )
        values = projected[:, 2 * D :].astype(jnp.bfloat16)
        initial = (
            jnp.full((HEADS, tok_rows), -1e30, jnp.float32),
            jnp.zeros((HEADS, tok_rows), jnp.float32),
            jnp.zeros((HEADS, tok_rows, HEAD), jnp.float32),
        )
        row_max, denominator, weighted = split_blocks(
            partial(online_step, queries),
            initial,
            lax.all_gather(key_rows, "cp", axis=0, tiled=True),
            lax.all_gather(values, "cp", axis=0, tiled=True),
            jnp.int32(0),
        )
        attended = jnp.transpose(weighted / denominator[..., None], (1, 0, 2)).reshape(tok_rows, D)
        log_total = row_max + jnp.log(denominator)
        attended_low = attended.astype(jnp.bfloat16)
        attn_branch = jnp.dot(
            attended_low, proj_attn, preferred_element_type=jnp.float32
        ) + bias_attn.astype(jnp.float32)
        hidden_pre = jnp.dot(
            normed_mlp, proj_up, preferred_element_type=jnp.float32
        ) + bias_up.astype(jnp.float32)
        hidden = jax.nn.gelu(hidden_pre, approximate=False).astype(jnp.bfloat16)
        mlp_branch = jnp.dot(
            hidden, proj_down, preferred_element_type=jnp.float32
        ) + bias_down.astype(jnp.float32)
        stored.append(
            (
                stream,
                normed_attn,
                normed_mlp,
                queries,
                key_rows,
                values,
                attended,
                attended_low,
                log_total,
                hidden_pre,
                hidden,
            )
        )
        stream = stream + attn_branch + mlp_branch
    grad_stream = cotangent.astype(jnp.float32)
    per_layer = [None] * LAYERS
    for depth in reversed(range(LAYERS)):
        (
            saved_stream,
            normed_attn,
            normed_mlp,
            queries,
            key_rows,
            values,
            attended,
            attended_low,
            log_total,
            hidden_pre,
            hidden,
        ) = stored[depth]
        params = (
            lax.all_gather(qkv_weight[depth], ("dp", "cp"), axis=0, tiled=True),
            lax.all_gather(qkv_bias[depth], ("dp", "cp"), axis=0, tiled=True),
            lax.all_gather(attn_weight[depth], ("dp", "cp"), axis=0, tiled=True),
            lax.all_gather(attn_bias[depth], ("dp", "cp"), axis=0, tiled=True),
            lax.all_gather(up_weight[depth], ("dp", "cp"), axis=0, tiled=True),
            lax.all_gather(up_bias[depth], ("dp", "cp"), axis=0, tiled=True),
            lax.all_gather(down_weight[depth], ("dp", "cp"), axis=0, tiled=True),
            lax.all_gather(down_bias[depth], ("dp", "cp"), axis=0, tiled=True),
            lax.all_gather(attn_gain[depth], ("dp", "cp"), axis=0, tiled=True),
            lax.all_gather(attn_shift[depth], ("dp", "cp"), axis=0, tiled=True),
            lax.all_gather(mlp_gain[depth], ("dp", "cp"), axis=0, tiled=True),
            lax.all_gather(mlp_shift[depth], ("dp", "cp"), axis=0, tiled=True),
        )
        (
            proj_qkv,
            bias_qkv,
            proj_attn,
            bias_attn,
            proj_up,
            bias_up,
            proj_down,
            bias_down,
            gain_attn,
            shift_attn,
            gain_mlp,
            shift_mlp,
        ) = params
        grad_low = grad_stream.astype(jnp.bfloat16)
        bias_grad = jnp.sum(grad_low.astype(jnp.float32), axis=0)
        attn_weight_grad = jnp.einsum(
            "td,te->de", attended_low, grad_low, preferred_element_type=jnp.float32
        )
        down_weight_grad = jnp.einsum(
            "tf,te->fe", hidden, grad_low, preferred_element_type=jnp.float32
        )
        grad_attended = jnp.einsum(
            "te,de->td", grad_low, proj_attn, preferred_element_type=jnp.float32
        ).astype(jnp.bfloat16)
        grad_hidden = jnp.einsum(
            "te,fe->tf", grad_low, proj_down, preferred_element_type=jnp.float32
        )
        _, gelu_pull = jax.vjp(partial(jax.nn.gelu, approximate=False), hidden_pre)
        grad_pre = gelu_pull(grad_hidden)[0].astype(jnp.bfloat16)
        up_weight_grad = jnp.einsum(
            "td,tf->df", normed_mlp, grad_pre, preferred_element_type=jnp.float32
        )
        up_bias_grad = jnp.sum(grad_pre.astype(jnp.float32), axis=0)
        grad_normed_mlp = jnp.einsum(
            "tf,df->td", grad_pre, proj_up, preferred_element_type=jnp.float32
        )
        all_keys, all_values = (
            lax.all_gather(key_rows, "cp", axis=0, tiled=True),
            lax.all_gather(values, "cp", axis=0, tiled=True),
        )
        grad_heads = grad_attended.reshape(tok_rows, HEADS, HEAD)
        row_dot = jnp.transpose(
            jnp.sum(
                grad_heads.astype(jnp.float32) * attended.reshape(tok_rows, HEADS, HEAD), axis=-1
            )
        )
        block_rows = 512 if group_rows > 512 and group_rows % 512 == 0 else group_rows
        block_count = group_rows // block_rows
        starts = jnp.arange(block_count, dtype=jnp.int32) * block_rows

        def back_step(grad_query, inputs):
            key_block, value_block, offset = inputs
            key_heads = key_block.reshape(block_rows, HEADS, HEAD)
            value_heads = value_block.reshape(block_rows, HEADS, HEAD)
            scores = (
                jnp.einsum("qhd,khd->hqk", queries, key_heads, preferred_element_type=jnp.float32)
                * score_scale
            )
            visible = visible_mask(offset, block_rows)
            weights = jnp.where(visible[None], jnp.exp(scores - log_total[..., None]), 0.0)
            grad_weights = jnp.einsum(
                "qhd,khd->hqk", grad_heads, value_heads, preferred_element_type=jnp.float32
            )
            grad_scores = (weights * (grad_weights - row_dot[..., None])).astype(jnp.bfloat16)
            grad_query = grad_query + jnp.einsum(
                "hqk,khd->hqd", grad_scores, key_heads, preferred_element_type=jnp.float32
            )
            key_grad = (
                jnp.einsum("hqk,qhd->khd", grad_scores, queries, preferred_element_type=jnp.float32)
                * score_scale
            )
            value_grad = jnp.einsum(
                "hqk,qhd->khd",
                weights.astype(jnp.bfloat16),
                grad_heads,
                preferred_element_type=jnp.float32,
            )
            return (
                grad_query,
                (key_grad.reshape(block_rows, D), value_grad.reshape(block_rows, D)),
            )

        grad_query, (key_grads, value_grads) = lax.scan(
            back_step,
            jnp.zeros((HEADS, tok_rows, HEAD), jnp.float32),
            (
                all_keys.reshape(block_count, block_rows, D),
                all_values.reshape(block_count, block_rows, D),
                starts,
            ),
        )
        local_key_grad, local_value_grad = (
            lax.psum_scatter(
                key_grads.reshape(group_rows, D).astype(jnp.bfloat16),
                "cp",
                scatter_dimension=0,
                tiled=True,
            ).astype(jnp.float32),
            lax.psum_scatter(
                value_grads.reshape(group_rows, D).astype(jnp.bfloat16),
                "cp",
                scatter_dimension=0,
                tiled=True,
            ).astype(jnp.float32),
        )
        query_raw = rotate(
            jnp.transpose(grad_query * score_scale, (1, 0, 2)), cosine_table, -sine_table
        )
        key_raw = rotate(local_key_grad.reshape(tok_rows, HEADS, HEAD), cosine_table, -sine_table)
        grad_projected = jnp.concatenate(
            [query_raw.reshape(tok_rows, D), key_raw.reshape(tok_rows, D), local_value_grad], axis=1
        ).astype(jnp.bfloat16)
        qkv_weight_grad = jnp.einsum(
            "td,te->de", normed_attn, grad_projected, preferred_element_type=jnp.float32
        )
        qkv_bias_grad = jnp.sum(grad_projected.astype(jnp.float32), axis=0)
        grad_normed_attn = jnp.einsum(
            "te,de->td", grad_projected, proj_qkv, preferred_element_type=jnp.float32
        )
        _, norm_pull = jax.vjp(
            both_norms,
            saved_stream,
            gain_attn.astype(jnp.float32),
            shift_attn.astype(jnp.float32),
            gain_mlp.astype(jnp.float32),
            shift_mlp.astype(jnp.float32),
        )
        grad_input, attn_gain_grad, attn_shift_grad, mlp_gain_grad, mlp_shift_grad = norm_pull(
            (grad_normed_attn, grad_normed_mlp)
        )
        grad_stream = grad_stream + grad_input
        summed = (
            lax.psum_scatter(
                flatten_rows(qkv_weight_grad), ("dp", "cp"), scatter_dimension=0, tiled=True
            ),
            lax.psum_scatter(qkv_bias_grad, ("dp", "cp"), scatter_dimension=0, tiled=True),
            lax.psum_scatter(
                flatten_rows(attn_weight_grad), ("dp", "cp"), scatter_dimension=0, tiled=True
            ),
            lax.psum_scatter(bias_grad, ("dp", "cp"), scatter_dimension=0, tiled=True),
            lax.psum_scatter(
                flatten_rows(up_weight_grad), ("dp", "cp"), scatter_dimension=0, tiled=True
            ),
            lax.psum_scatter(up_bias_grad, ("dp", "cp"), scatter_dimension=0, tiled=True),
            lax.psum_scatter(
                flatten_rows(down_weight_grad), ("dp", "cp"), scatter_dimension=0, tiled=True
            ),
            lax.psum_scatter(bias_grad, ("dp", "cp"), scatter_dimension=0, tiled=True),
            lax.psum_scatter(attn_gain_grad, ("dp", "cp"), scatter_dimension=0, tiled=True),
            lax.psum_scatter(attn_shift_grad, ("dp", "cp"), scatter_dimension=0, tiled=True),
            lax.psum_scatter(mlp_gain_grad, ("dp", "cp"), scatter_dimension=0, tiled=True),
            lax.psum_scatter(mlp_shift_grad, ("dp", "cp"), scatter_dimension=0, tiled=True),
        )
        per_layer[depth] = (
            summed[0].reshape(-1, 3 * D),
            summed[1],
            summed[2].reshape(-1, D),
            summed[3],
            summed[4].reshape(-1, FF),
            summed[5],
            summed[6].reshape(-1, D),
            summed[7],
            summed[8],
            summed[9],
            summed[10],
            summed[11],
        )
    stacked = [stack_layers(per_layer, member) for member in range(12)]
    return (
        stream.astype(jnp.bfloat16),
        grad_stream,
        stacked[0],
        stacked[1],
        stacked[2],
        stacked[3],
        stacked[4],
        stacked[5],
        stacked[6],
        stacked[7],
        stacked[8],
        stacked[9],
        stacked[10],
        stacked[11],
    )


TEAM = 4
TEAM_AXES = ("core", "x")
LINE_AXES = ("z", "y")
LINE = 4
MINE = (3 * D) // TEAM
HCOLS = D // TEAM
UCOLS = FF // TEAM
VMEM_BYTES = 56 * 1024 * 1024
BF = jnp.bfloat16
F32 = jnp.float32


def call(body, out_shape, name, operands, scratch=()):
    return pl.pallas_call(
        body,
        out_shape=out_shape,
        scratch_shapes=list(scratch),
        compiler_params=pltpu.CompilerParams(vmem_limit_bytes=VMEM_BYTES),
        name=name,
    )(*operands)


def shape(dims, kind):
    return jax.ShapeDtypeStruct(dims, kind)


def mm(left, right):
    return jnp.dot(left, right, preferred_element_type=F32)


def mm_t(left, right):
    return lax.dot_general(left, right, (((1,), (1,)), ((), ())), preferred_element_type=F32)


def t_mm(left, right):
    return lax.dot_general(left, right, (((0,), (0,)), ((), ())), preferred_element_type=F32)


def pick(member, pieces, wanted):
    chosen = pieces[0]
    for s in range(1, TEAM):
        chosen = jnp.where((member ^ s) == wanted, pieces[s], chosen)
    return chosen


def small_rows(vectors, depth):
    rows = []
    for vector in vectors:
        values = vector[depth : depth + 1].astype(F32)
        rows.append(
            jnp.concatenate([values, jnp.zeros((1, 128 - values.shape[1]), F32)], axis=1)
        )
    return jnp.concatenate(rows, axis=0)


def pack_body(me_ref, qkv_ref, up_ref, *refs):
    vectors, outs = [r[...] for r in refs[:8]], refs[8:]
    me = me_ref[0]
    small = jnp.concatenate([small_rows(vectors, depth) for depth in range(LAYERS)], axis=0)
    small = jnp.concatenate([small, jnp.zeros((small.shape[0], UCOLS - 128), F32)], axis=1)
    parts = [[] for _ in range(TEAM)]
    for depth in range(LAYERS):
        rows = qkv_ref.shape[1]
        qkv = qkv_ref[depth].astype(F32)
        up = up_ref[depth].astype(F32)
        blocks = up.shape[1] // (TEAM * 96)
        for p in range(TEAM):
            parts[p].append(
                jnp.concatenate(
                    [up[:, 96 * (TEAM * b + p) : 96 * (TEAM * b + p + 1)] for b in range(blocks)],
                    axis=1,
                )
            )
            parts[p].append(
                jnp.concatenate(
                    [qkv[:, D * t + HCOLS * p : D * t + HCOLS * (p + 1)] for t in range(3)]
                    + [jnp.zeros((rows, UCOLS - MINE), F32)],
                    axis=1,
                )
            )
    parts = [jnp.concatenate(group, axis=0) for group in parts]
    for s in range(TEAM):
        chosen = parts[0]
        for p in range(1, TEAM):
            chosen = jnp.where((me ^ s) == p, parts[p], chosen)
        outs[s][...] = jnp.concatenate([chosen, small], axis=0).astype(BF)


def assemble_body(me_ref, p0, p1, p2, p3, attn_ref, down_ref, *outs):
    me = me_ref[0]
    slots = [r[...].astype(F32) for r in (p0, p1, p2, p3)]
    ordered = [pick(me, slots, p) for p in range(TEAM)]
    for depth, out in enumerate(outs):
        base = 48 * depth
        up = jnp.concatenate([piece[base : base + 24] for piece in ordered], axis=0)
        qkv = jnp.concatenate([piece[base + 24 : base + 48] for piece in ordered], axis=0)
        attn = attn_ref[depth].astype(F32)
        side = jnp.concatenate([attn[:, HCOLS * n : HCOLS * (n + 1)] for n in range(4)], axis=0)
        out[0:96] = up.astype(BF)
        out[96:192] = down_ref[depth]
        out[192:288] = jnp.concatenate([qkv[:, :MINE], side], axis=1).astype(BF)
        if out.shape[0] > 288:
            small = jnp.concatenate(
                [piece[96:112, :128] for piece in ordered] + [jnp.zeros((16, D - 4 * 128), F32)],
                axis=1,
            )
            out[288:304] = small.astype(BF)


def source_team(me_ref, index):
    shift, flip = index % LINE, index // LINE
    return 2 * lax.rem(me_ref[1] + LINE - shift, LINE) + (me_ref[2] ^ flip)


def target_team(me_ref, index):
    shift, flip = index % LINE, index // LINE
    return 2 * lax.rem(me_ref[1] + shift, LINE) + (me_ref[2] ^ flip)


def place(me_ref, pieces, whole):
    for index, piece in enumerate(pieces):
        whole[source_team(me_ref, index)] = piece[...]


def hand_out(me_ref, whole, keep, sends, order):
    for s in range(LINE):
        keep[s] = whole[target_team(me_ref, s)]
    for send, slots in zip(sends, order):
        for n, s in enumerate(slots):
            send[n] = whole[target_team(me_ref, LINE + s)]


ALL_SLOTS = (tuple(range(LINE)),)
HALVES = ((1, 3), (2, 0))


def add_body(slots, places, me_ref, keep, received, *outs):
    for s, n, out in zip(slots, places, outs):
        out[...] = (keep[s].astype(F32) + received[n].astype(F32)).astype(BF)


def add_both_body(slots, places, me_ref, m_keep, m_received, a_keep, a_received, *outs):
    for s, n, out in zip(slots, places, outs):
        out[0:192] = (m_keep[s].astype(F32) + m_received[n].astype(F32)).astype(BF)
        out[192:304] = (a_keep[s].astype(F32) + a_received[s].astype(F32)).astype(BF)


def line_sum_body(me_ref, own, r1, r2, r3, keep_ref, send_ref):
    for f, out in enumerate((keep_ref, send_ref)):
        total = own[f].astype(F32) + r1[f].astype(F32) + r2[f].astype(F32) + r3[f].astype(F32)
        out[...] = total.astype(out.dtype)


def layer_vectors(me_ref, whole, depth):
    me = me_ref[0]
    small = [whole[k].astype(F32) for k in range(2 * LINE)]
    fields = [block[8 * depth : 8 * (depth + 1)] for block in small]
    shared = jnp.concatenate(
        [block[2:8, 128 * p : 128 * p + 24] for block in fields for p in range(TEAM)], axis=1
    )
    up_rows, qkv_rows = [], []
    qkv = jnp.concatenate(
        [block[0:1, 128 * p : 128 * p + 72] for block in fields for p in range(TEAM)], axis=1
    )
    for p in range(TEAM):
        up_rows.append(
            jnp.concatenate([block[1:2, 128 * p : 128 * p + 96] for block in fields], axis=1)
        )
        qkv_rows.append(
            jnp.concatenate(
                [qkv[:, D * t + HCOLS * p : D * t + HCOLS * (p + 1)] for t in range(3)]
                + [jnp.zeros((1, D - MINE), F32)],
                axis=1,
            )
        )
    up_mine, qkv_mine = up_rows[0], qkv_rows[0]
    for p in range(1, TEAM):
        up_mine = jnp.where(me == p, up_rows[p], up_mine)
        qkv_mine = jnp.where(me == p, qkv_rows[p], qkv_mine)
    return jnp.concatenate([shared, up_mine, qkv_mine], axis=0)


def attn_weights(whole):
    qkv = whole[:, 0:96, :][:, :, :MINE].reshape(D, MINE)
    side = whole[:, 0:96, MINE:].astype(F32)
    out = jnp.concatenate(
        [side[:, 24 * n : 24 * (n + 1), :].reshape(HCOLS, HCOLS) for n in range(4)], axis=1
    )
    return qkv, out.astype(BF)


def project(scaled, vec, weight, cosine, sine):
    normed = (scaled * vec[0:1] + vec[1:2]).astype(BF)
    projected = mm(normed, weight) + vec[7:8, :MINE]
    turned = turn(projected[:, : 2 * HCOLS], cosine, sine)
    queries = (turned[:, :HCOLS] * 0.125).astype(BF)
    keys = turned[:, HCOLS:].astype(BF)
    values = projected[:, 2 * HCOLS :].astype(BF)
    return normed, queries, keys, values


def attend_body(me_ref, x0, x1, x2, x3, *refs):
    pieces, smalls = refs[:8], refs[8:16]
    cos_ref, sin_ref, mask_ref, y_ref, vec_ref, whole, small = refs[16:]
    place(me_ref, pieces, whole)
    place(me_ref, smalls, small)
    for depth in range(LAYERS):
        vec_ref[depth] = layer_vectors(me_ref, small, depth)
    vec = vec_ref[0]
    weight, out_weight = attn_weights(whole)
    for g, (first, second) in enumerate(((x0, x1), (x2, x3))):
        rows = pl.ds(PAIR * g, PAIR)
        scaled, _ = norm_parts(two_slots(first[...], second[...]))
        _, queries, keys, values = project(scaled, vec, weight, cos_ref[rows, :], sin_ref[rows, :])
        total = jnp.zeros((PAIR, HCOLS), F32)
        for head in range(HEADS // TEAM):
            owned = head_mask(PAIR, head)
            scores = mm_t(jnp.where(owned, queries, jnp.zeros_like(queries)), keys) + mask_ref[g]
            weights = jnp.exp(scores - jnp.max(scores, axis=-1, keepdims=True))
            below = jnp.sum(weights, axis=-1, keepdims=True)
            total = total + jnp.where(owned, mm(weights.astype(BF), values) / below, 0.0)
        y_ref[rows, :] = mm(total.astype(BF), out_weight)


def store_pair(g, result, own, near, far):
    if g == 0:
        own[...] = result[0:TOK]
        near[...] = result[TOK:]
    else:
        far[...] = result.astype(BF)


def mlp_body(me_ref, x0, x1, x2, x3, *refs):
    pieces, (vec_ref, a_ref, y0, y1, y23, whole) = refs[:8], refs[8:]
    place(me_ref, pieces, whole)
    vec = vec_ref[0]
    up = whole[:, 0:96, :].reshape(D, UCOLS)
    down = whole[:, 96:192, :].reshape(UCOLS, D)
    for g, (first, second) in enumerate(((x0, x1), (x2, x3))):
        rows = pl.ds(PAIR * g, PAIR)
        scaled, _ = norm_parts(two_slots(first[...], second[...]))
        normed = (scaled * vec[2:3] + vec[3:4]).astype(BF)
        before = mm(normed, up) + vec[6:7]
        hidden = (before * (0.5 * (1.0 + lax.erf(before * (1.0 / math.sqrt(2.0)))))).astype(BF)
        result = mm(hidden, down) + a_ref[rows, :]
        store_pair(g, result, y0, y1, y23)


def mlp_both_body(depth, last, me_ref, x0, x1, x2, x3, g0, g1, g2, g3, *refs):
    pieces, vec_ref, (dn_ref, sum_ref), refs = refs[:8], refs[8], refs[9:11], refs[11:]
    if last:
        y_ref, refs = refs[0], refs[1:]
    whole, grads, c_s, hid_s, du_s, gb_s = refs[-6:]
    place(me_ref, pieces, whole)
    vec = vec_ref[depth]
    up = whole[:, 0:96, :].reshape(D, UCOLS)
    down = whole[:, 96:192, :].reshape(UCOLS, D)
    gain_sum = jnp.zeros((1, D), F32)
    shift_sum = jnp.zeros((1, D), F32)
    bias_sum = jnp.zeros((1, D), F32)
    up_sum = jnp.zeros((1, UCOLS), F32)
    for g, (first, second, g_first, g_second) in enumerate(((x0, x1, g0, g1), (x2, x3, g2, g3))):
        rows = pl.ds(PAIR * g, PAIR)
        scaled, _ = norm_parts(two_slots(first[...], second[...]))
        normed = (scaled * vec[2:3] + vec[3:4]).astype(BF)
        c_s[rows, :] = normed
        low = jnp.concatenate([g_first[...], g_second[...]], axis=0)
        gb_s[rows, :] = low
        hidden, slope = gelu_parts(mm(normed, up) + vec[6:7])
        hidden = hidden.astype(BF)
        hid_s[rows, :] = hidden
        if last:
            y_ref[rows, :] = mm(hidden, down)
        du = (mm_t(low, down) * slope).astype(BF)
        du_s[rows, :] = du
        dc = mm_t(du, up)
        dn_ref[rows, :] = dc * vec[2:3]
        gain_sum = gain_sum + jnp.sum(dc * scaled, axis=0, keepdims=True)
        shift_sum = shift_sum + jnp.sum(dc, axis=0, keepdims=True)
        bias_sum = bias_sum + jnp.sum(low.astype(F32), axis=0, keepdims=True)
        up_sum = up_sum + jnp.sum(du.astype(F32), axis=0, keepdims=True)
    grads[:, 0:96, :] = t_mm(c_s[...], du_s[...]).reshape(-1, 96, UCOLS).astype(BF)
    grads[:, 96:192, :] = t_mm(hid_s[...], gb_s[...]).reshape(-1, 96, D).astype(BF)
    if last:
        for s, out in enumerate(refs[0:LINE]):
            for f in range(2):
                out[f] = grads[target_team(me_ref, LINE * f + s), 0:EARLY, :]
        keep, send = refs[LINE : LINE + 2]
        for s in range(LINE):
            keep[s] = grads[target_team(me_ref, s), EARLY:192, :]
            send[s] = grads[target_team(me_ref, LINE + s), EARLY:192, :]
    else:
        hand_out(me_ref, grads, refs[0], refs[1:3], HALVES)
    sum_ref[...] = jnp.concatenate(
        [bias_sum, up_sum, gain_sum, shift_sum, jnp.zeros((4, D), F32)], axis=0
    )


def attend_both_body(depth, last, me_ref, x0, x1, x2, x3, g0, g1, g2, g3, *refs):
    pieces, (vec_ref, cos_ref, sin_ref, mask_ref, dn_ref, sum_ref) = refs[:8], refs[8:14]
    refs = refs[14:]
    if last:
        y_ref, refs = refs[0], refs[1:]
    blocks, (n0, n1, n23) = refs[:2], refs[2:5]
    whole, grads, a_s, dp_s, o_s, gb_s = refs[-6:]
    place(me_ref, pieces, whole)
    vec = vec_ref[depth]
    weight, out_weight = attn_weights(whole)
    gain_sum = jnp.zeros((1, D), F32)
    shift_sum = jnp.zeros((1, D), F32)
    bias_sum = jnp.zeros((1, MINE), F32)
    for g, (first, second, g_first, g_second) in enumerate(((x0, x1, g0, g1), (x2, x3, g2, g3))):
        rows = pl.ds(PAIR * g, PAIR)
        cosine, sine = cos_ref[rows, :], sin_ref[rows, :]
        scaled, _ = norm_parts(two_slots(first[...], second[...]))
        normed, queries, keys, values = project(scaled, vec, weight, cosine, sine)
        a_s[rows, :] = normed
        low = jnp.concatenate([g_first[...], g_second[...]], axis=0)
        gb_s[rows, :] = low
        grad_o = mm_t(low, out_weight).astype(BF)
        zero = jnp.zeros_like(queries)
        out = jnp.zeros((PAIR, HCOLS), F32)
        dq = jnp.zeros((PAIR, HCOLS), F32)
        dk = jnp.zeros((PAIR, HCOLS), F32)
        dv = jnp.zeros((PAIR, HCOLS), F32)
        for head in range(HEADS // TEAM):
            owned = head_mask(PAIR, head)
            scores = mm_t(jnp.where(owned, queries, zero), keys) + mask_ref[g]
            weights = jnp.exp(scores - jnp.max(scores, axis=-1, keepdims=True))
            weights = weights / jnp.sum(weights, axis=-1, keepdims=True)
            rounded = weights.astype(BF)
            dweights = mm_t(jnp.where(owned, grad_o, zero), values)
            delta = jnp.sum(weights * dweights, axis=-1, keepdims=True)
            dscores = (weights * (dweights - delta)).astype(BF)
            out = out + jnp.where(owned, mm(rounded, values), 0.0)
            dq = dq + jnp.where(owned, mm(dscores, keys), 0.0)
            dk = dk + jnp.where(owned, t_mm(dscores, queries), 0.0)
            dv = dv + jnp.where(owned, t_mm(rounded, grad_o), 0.0)
        o_s[rows, :] = out.astype(BF)
        both = turn(jnp.concatenate([dq * 0.125, dk], axis=1), cosine, -sine)
        dproj = jnp.concatenate([both, dv], axis=1).astype(BF)
        dp_s[rows, :] = dproj
        bias_sum = bias_sum + jnp.sum(dproj.astype(F32), axis=0, keepdims=True)
        da = mm_t(dproj, weight)
        gain_sum = gain_sum + jnp.sum(da * scaled, axis=0, keepdims=True)
        shift_sum = shift_sum + jnp.sum(da, axis=0, keepdims=True)
        dn = dn_ref[rows, :] + da * vec[0:1]
        store_pair(g, dn, n0, n1, n23)
        if last:
            result = y_ref[rows, :] + mm(out.astype(BF), out_weight)
            store_pair(g, result, *refs[5:8])
    qkv_grad = t_mm(a_s[...], dp_s[...]).reshape(-1, 96, MINE)
    out_grad = t_mm(o_s[...], gb_s[...])
    side = jnp.concatenate(
        [out_grad[:, HCOLS * n : HCOLS * (n + 1)].reshape(-1, 24, HCOLS) for n in range(4)], axis=1
    )
    grads[:, 0:96, :] = jnp.concatenate([qkv_grad, side], axis=2).astype(BF)
    sums = sum_ref[...]
    vectors = jnp.concatenate([sums[0:2], gain_sum, shift_sum, sums[2:4]], axis=0)
    me = me_ref[0]
    spread = jnp.concatenate(
        [
            jnp.where(me == p, bias_sum[:, HCOLS * t : HCOLS * (t + 1)], 0.0)
            for t in range(3)
            for p in range(TEAM)
        ],
        axis=1,
    )
    for k in range(2 * LINE):
        shared = jnp.concatenate(
            [vectors[:, 96 * k : 96 * (k + 1)], jnp.zeros((6, D - 96), F32)], axis=1
        )
        bias = jnp.concatenate(
            [spread[:, 288 * k : 288 * (k + 1)], jnp.zeros((1, D - 288), F32)], axis=1
        )
        grads[k, 96:112, :] = jnp.concatenate([shared, bias, jnp.zeros((9, D), F32)], axis=0).astype(BF)
    hand_out(me_ref, grads, blocks[0], blocks[1:], ALL_SLOTS)


def residual_body(me_ref, x_ref, y0, y1, y2, vec_ref, out_ref, low_ref):
    depth = 0 if x_ref.dtype == BF else 1
    total = y0[...] + y1[...].astype(F32) + y2[...].astype(F32)
    result = x_ref[...].astype(F32) + total + (vec_ref[depth, 4:5] + vec_ref[depth, 5:6])
    out_ref[...] = result
    low_ref[...] = result.astype(BF)

def norm_parts(stream):
    centered = stream - jnp.mean(stream, axis=-1, keepdims=True)
    spread = jnp.mean(centered * centered, axis=-1, keepdims=True)
    inverse = lax.rsqrt(spread + 1e-05)
    return centered * inverse, inverse


def two_slots(first, second):
    return jnp.concatenate([first[0:TOK].astype(F32), second[0:TOK].astype(F32)], axis=0)


TOK = 128
EARLY = 48
PAIR = 2 * TOK


def turn(block, cosine, sine):
    lane = lax.broadcasted_iota(jnp.int32, (block.shape[0], 128), 1) % HEAD
    tiles = []
    for t in range(block.shape[1] // 128):
        tile = block[:, 128 * t : 128 * (t + 1)]
        swapped = jnp.where(
            lane < ROT // 2, pltpu.roll(tile, 128 - ROT // 2, 1), pltpu.roll(tile, ROT // 2, 1)
        )
        tiles.append(tile * cosine + swapped * sine)
    return jnp.concatenate(tiles, axis=1)


def head_mask(rows, head):
    lane = lax.broadcasted_iota(jnp.int32, (rows, HCOLS), 1)
    return (lane >= head * HEAD) & (lane < (head + 1) * HEAD)


def gelu_parts(u):
    cdf = 0.5 * (1.0 + lax.erf(u * (1.0 / math.sqrt(2.0))))
    density = jnp.exp(-0.5 * u * u) * (1.0 / math.sqrt(2.0 * math.pi))
    return u * cdf, cdf + u * density


def norm_back_body(me_ref, x_ref, g_ref, n0, n1, n2, out_ref, low_ref):
    scaled, inverse = norm_parts(x_ref[...].astype(F32))
    dn = n0[...] + n1[...].astype(F32) + n2[...].astype(F32)
    centered = dn - jnp.mean(dn, axis=-1, keepdims=True)
    moment = jnp.mean(dn * scaled, axis=-1, keepdims=True)
    result = g_ref[...].astype(F32) + inverse * (centered - scaled * moment)
    out_ref[...] = result
    low_ref[...] = result.astype(BF)


def total(group):
    result = group[0].astype(F32)
    for term in group[1:]:
        result = result + term.astype(F32)
    return result


def by_owner(me_ref, parts, outs, start):
    me = me_ref[0]
    for s, out in enumerate(outs):
        piece = parts[0]
        for p in range(1, TEAM):
            piece = jnp.where((me ^ s) == p, parts[p], piece)
        out[start : start + 32] = piece.astype(BF)


def split_body(early, me_ref, *refs):
    outs, (down_ref, attn_ref, small_ref), refs = refs[-7:-3], refs[-3:], refs[:-7]
    split_attend(me_ref, refs[:5], outs, attn_ref, small_ref)
    refs = refs[5:]
    size = refs[0].shape[1]
    rest = total([refs[0][0], refs[1][0]] + [ref[0:size, :] for ref in refs[2:5]])
    if early:
        rest = jnp.concatenate([total([refs[5][...], refs[6][...]]), rest], axis=0)
    down_ref[...] = rest[96:192]
    blank = jnp.zeros((8, D), F32)
    parts = [
        jnp.concatenate([rest[24 * p : 24 * (p + 1)], blank], axis=0) for p in range(TEAM)
    ]
    by_owner(me_ref, parts, outs, 0)


def split_attend(me_ref, refs, outs, attn_ref, small_ref):
    me = me_ref[0]
    attn = total([refs[0][0], refs[1][0]] + [ref[-112:, :] for ref in refs[2:]])
    side = attn[0:96, MINE:]
    attn_ref[...] = jnp.concatenate(
        [side[24 * n : 24 * (n + 1)] for n in range(4)], axis=1
    ).astype(BF)
    qkv = jnp.concatenate([attn[0:96, :MINE], jnp.zeros((96, UCOLS - MINE), F32)], axis=1)
    small = attn[96:112]
    parts, bias = [], jnp.zeros((1, 24), F32)
    for p in range(TEAM):
        rows = slice(24 * p, 24 * (p + 1))
        gains = jnp.concatenate([small[2:6, rows], jnp.zeros((4, D - 24), F32)], axis=1)
        qkv_bias = jnp.concatenate(
            [small[6:7, 72 * p : 72 * (p + 1)], jnp.zeros((1, D - 72), F32)], axis=1
        )
        parts.append(jnp.concatenate([qkv[rows], gains, qkv_bias, jnp.zeros((3, D), F32)], axis=0))
        bias = jnp.where(me == p, small[0:1, rows], bias)
    small_ref[...] = jnp.concatenate(
        [
            jnp.concatenate([bias, jnp.zeros((1, 104), F32)], axis=1),
            small[1:2, :128],
            jnp.zeros((6, 128), F32),
        ],
        axis=0,
    )
    by_owner(me_ref, parts, outs, 32)


def unpack_body(me_ref, *refs):
    me = me_ref[0]
    (
        qkv_ref, qkv_b_ref, attn_ref, attn_b_ref, up_ref, up_b_ref, down_ref,
        down_b_ref, ga_ref, sa_ref, gm_ref, sm_ref,
    ) = refs[7 * LAYERS :]
    gain_refs = (ga_ref, sa_ref, gm_ref, sm_ref)
    for depth in range(LAYERS):
        group = refs[7 * depth : 7 * (depth + 1)]
        down_rows, own_small, attn_rows = group[TEAM:]
        slots = [r[...].astype(F32) for r in group[:TEAM]]
        ordered = [pick(me, slots, p) for p in range(TEAM)]
        blocks = FF // (96 * TEAM)
        up_ref[depth] = jnp.concatenate(
            [ordered[p][0:24, 96 * b : 96 * (b + 1)] for b in range(blocks) for p in range(TEAM)],
            axis=1,
        )
        qkv_ref[depth] = jnp.concatenate(
            [
                ordered[p][32:56, HCOLS * t : HCOLS * (t + 1)]
                for t in range(3)
                for p in range(TEAM)
            ],
            axis=1,
        )
        attn_ref[depth] = attn_rows[...].astype(F32)
        down_ref[depth] = down_rows[...]
        small = slots[0][56:64, :128] + slots[1][56:64, :128]
        small = small + slots[2][56:64, :128] + slots[3][56:64, :128]
        for n, ref in enumerate(gain_refs):
            ref[depth : depth + 1] = small[n : n + 1, :24]
        qkv_b_ref[depth : depth + 1] = small[4:5, :72]
        attn_b_ref[depth : depth + 1] = own_small[0:1, :24]
        down_b_ref[depth : depth + 1] = own_small[0:1, :24]
        up_b_ref[depth : depth + 1] = own_small[1:2, :96]


def team_send(piece, slot):
    flips = [(m, m ^ slot) for m in range(TEAM)]
    return lax.ppermute(piece, TEAM_AXES, flips)


def line_shift(piece, shift):
    size = lax.axis_size("z")
    return lax.ppermute(piece, "z", [(i, (i + shift) % size) for i in range(size)])


def line_flip(piece):
    return lax.ppermute(piece, "y", [(0, 1), (1, 0)])


def after(value, *others):
    return lax.optimization_barrier((value, *others))[0]


def line_near(piece):
    first = line_shift(piece, 1)
    third = line_shift(piece, 3)
    return [piece, first, line_shift(after(piece, first, third), 2), third]


def local_team(
    tokens, segment_ids, cotangent, qkv_weight, qkv_bias, attn_weight, attn_bias,
    up_weight, up_bias, down_weight, down_bias, attn_gain, attn_shift, mlp_gain, mlp_shift,
):
    lines = lax.axis_size("z") * lax.axis_size("y")
    world = lines * TEAM
    member = lax.axis_index("core") * 2 + lax.axis_index("x")
    me = jnp.stack([member, lax.axis_index("z"), lax.axis_index("y")]).astype(jnp.int32)
    everywhere = LINE_AXES + TEAM_AXES
    tok_all = TEAM * TOK
    whole_spec = pl.BlockSpec(memory_space=pltpu.VMEM)

    def run(body, out_shape, name, operands, scratch=()):
        specs = [whole_spec if isinstance(x, jax.Array) else x[1] for x in operands]
        return pl.pallas_call(
            body,
            grid=(1,),
            out_shape=out_shape,
            in_specs=[pl.BlockSpec(memory_space=pltpu.SMEM)] + specs,
            scratch_shapes=[pltpu.VMEM(dims, kind) for dims, kind in scratch],
            compiler_params=pltpu.CompilerParams(vmem_limit_bytes=VMEM_BYTES),
            name=name,
        )(me, *[x if isinstance(x, jax.Array) else x[0] for x in operands])

    def part(rows, start):
        return pl.BlockSpec((rows, D), lambda i: (start // rows, 0))

    def one_of(array, index):
        return (array, pl.BlockSpec((1,) + array.shape[1:], lambda i: (index, 0, 0)))

    def exchange(blocks):
        return [blocks[0]] + [team_send(blocks[s], s) for s in range(1, TEAM)]

    small = (
        qkv_bias, up_bias, attn_gain, attn_shift, mlp_gain, mlp_shift, attn_bias, down_bias
    )
    packed = run(
        pack_body, [shape((112, D), BF)] * TEAM, "pack_weights", (qkv_weight, up_weight, *small)
    )
    spread = [(i, TEAM * (i % lines) + i // lines) for i in range(world)]
    gather_back = [(b, a) for a, b in spread]
    attn_piece = lax.ppermute(attn_weight, everywhere, spread)
    chunks = run(
        assemble_body,
        [shape((304, D), BF), shape((288, D), BF)],
        "assemble_weights",
        (*exchange(packed), attn_piece, down_weight),
    )
    near = line_near(chunks[0])
    pieces = [near + [line_flip(p) for p in near]]
    near = line_near(after(chunks[1], near[2], pieces[0][5], pieces[0][7]))
    pieces.append(near + [line_flip(p) for p in (chunks[1], *near[1:])])
    m_parts = [[(p, part(192, 0)) for p in group] for group in pieces]
    a_parts = [[(p, part(96, 192)) for p in group] for group in pieces]
    small_parts = [(p, part(16, 288)) for p in pieces[0]]

    def gather_team(piece, *others):
        other = after(team_send(piece, 1), *others)
        return piece, other, team_send(jnp.concatenate([piece, other], axis=0), 2)

    def slots_of(gathered, start=0):
        piece, other, far = gathered
        size = piece.shape[0]
        return [
            (piece, part(TOK, start)), (other, part(TOK, start)),
            (far, part(TOK, start)), (far, part(TOK, size + start)),
        ]

    def sum_team(own, near, far, *others):
        other = after(team_send(far, 2), *others)
        both = (near + other[TOK:].astype(F32)).astype(BF)
        return own, (other, part(TOK, 0)), team_send(both, 1)

    ids_rows = jnp.pad(segment_ids.astype(BF)[None, :], ((0, TOK - 1), (0, D - TOK)))
    load = jnp.concatenate([tokens, cotangent, ids_rows], axis=0)
    loads = gather_team(after(load, pieces[0][1], pieces[0][3], pieces[0][4], pieces[1][4]), pieces[0][2], pieces[0][5], pieces[0][7])
    token_slots = slots_of(loads)
    here = lax.axis_index("x")
    rows = jnp.arange(TOK, dtype=jnp.int32)
    places = jnp.concatenate([here * TOK + rows, (1 - here) * TOK + rows])
    masks, cosines, sines = [], [], []
    lane = jnp.arange(128, dtype=jnp.int32) % HEAD
    inverse = 10000.0 ** (-(lane % (ROT // 2) * 2).astype(F32) / ROT)
    id_rows = [
        loads[0][2 * TOK, :TOK], loads[1][2 * TOK, :TOK],
        loads[2][2 * TOK, :TOK], loads[2][5 * TOK, :TOK],
    ]
    for g in range(2):
        ids = jnp.concatenate(id_rows[2 * g : 2 * g + 2]).astype(F32)
        visible = (places[None, :] <= places[:, None]) & (ids[None, :] == ids[:, None])
        masks.append(jnp.where(visible, 0.0, -1e30).astype(F32))
        position = places - jnp.sum((ids[None, :] < ids[:, None]).astype(jnp.int32), axis=1)
        phases = position.astype(F32)[:, None] * inverse[None, :]
        cosines.append(jnp.where(lane[None, :] < ROT, jnp.cos(phases), 1.0))
        sign = jnp.where(lane < ROT // 2, -1.0, jnp.where(lane < ROT, 1.0, 0.0))
        sines.append(jnp.sin(phases) * sign[None, :])
    mask = jnp.stack(masks)
    cosine, sine = jnp.concatenate(cosines), jnp.concatenate(sines)

    partials = [shape((TOK, D), F32)] * 2 + [shape((PAIR, D), BF)]
    stream_pair = [shape((TOK, D), F32), shape((TOK, D), BF)]
    wide = ((tok_all, D), BF)

    attn_out, vec = run(
        attend_body,
        [shape((tok_all, D), F32), shape((LAYERS, 8, D), F32)],
        "attend_forward",
        (*token_slots, *a_parts[0], *small_parts, cosine, sine, mask),
        [((lines, 96, D), BF), ((lines, 16, D), BF)],
    )
    y = run(
        mlp_body,
        partials,
        "mlp_forward",
        (*token_slots, *m_parts[0], vec, attn_out),
        [((lines, 192, D), BF)],
    )

    def residual(stream, blocks):
        return run(residual_body, stream_pair, "residual", (stream, *sum_team(*blocks), vec))

    stream, low = residual(tokens, (after(y[0], pieces[1][4]), *y[1:]))
    streams = [tokens, stream]
    slots = [token_slots, slots_of(gather_team(low, pieces[1][5], pieces[1][7]))]

    grad = cotangent
    grad_slots = slots_of(loads, TOK)
    outs = [None] * LAYERS
    block_m, block_a = shape((192, D), BF), shape((112, D), BF)

    def mlp_back(depth, slots, grad_slots, grads):
        last = depth == LAYERS - 1
        return run(
            partial(mlp_both_body, depth, last),
            [shape((tok_all, D), F32), shape((8, D), F32)]
            + ([shape((tok_all, D), F32)] if last else [])
            + grads,
            "mlp_both",
            (*slots, *grad_slots, *m_parts[depth], vec),
            [((lines, 192, D), BF), ((lines, 192, D), BF), wide, wide, wide, wide],
        )

    def attend_back(depth, slots, grad_slots, rest, *others):
        last = depth == LAYERS - 1
        result = run(
            partial(attend_both_body, depth, last),
            [shape((4, 112, D), BF)] * 2 + partials + (partials if last else []),
            "attend_both",
            (*slots, *grad_slots, *a_parts[depth], vec, cosine, sine, mask, *rest),
            [
                ((lines, 96, D), BF),
                ((lines, 112, D), BF),
                wide,
                ((tok_all, MINE), BF),
                ((tok_all, HCOLS), BF),
                wide,
            ],
        )
        return result[0], line_flip(after(result[1], *others)), result[2:5], result[5:]

    def norm_back(depth, grad, received):
        return run(
            norm_back_body, stream_pair, "norm_backward", (streams[depth], grad, *received)
        )

    def add(kind, keep, other, slots, places, name):
        return run(partial(add_body, slots, places), [kind] * len(slots), name, (keep, other))

    def shifts(sums):
        return [line_shift(piece, s + 1) for s, piece in enumerate(sums)]

    def split(attend, mlp, early=()):
        keep, other, *sums = attend
        m_keep, m_other, *m_sums = mlp
        mine = run(
            partial(split_body, bool(early)),
            [shape((64, D), BF)] * TEAM
            + [shape((96, D), F32), shape((24, D), BF), shape((8, 128), F32)],
            "split_gradients",
            (one_of(keep, 0), one_of(other, 0), *sums, one_of(m_keep, 0), m_other, *m_sums, *early),
        )
        attn_rows = lax.ppermute(mine[TEAM + 1], everywhere, gather_back)
        return exchange(mine[:TEAM]) + [mine[TEAM], mine[TEAM + 2], attn_rows]

    early_block, late_four = shape((2, EARLY, D), BF), shape((4, 192 - EARLY, D), BF)
    dn, sum_m, y_part, e0, e1, e2, e3, m_keep1, m_send1 = mlp_back(
        1, slots[1], grad_slots, [early_block] * 4 + [late_four] * 2
    )
    early = shifts((e1, e2, e3))
    m_other1 = line_flip(m_send1)
    a_keep1, a_other1, ns, ys = attend_back(1, slots[1], grad_slots, (dn, sum_m, y_part))
    ns = (ns[0], ns[1], after(ns[2], *early))
    grad, low = norm_back(1, grad, sum_team(*ns, m_other1))
    m_added1 = add(
        shape((192 - EARLY, D), BF), m_keep1, after(m_other1, low), (1, 2, 3), (1, 2, 3), "add_mlp"
    )
    m_sums1 = shifts(m_added1)
    gathered = gather_team(low)
    grad_slots = slots_of((after(gathered[0], *m_added1), *gathered[1:]))
    dn, sum_m, m_keep0, m_first0, m_second0 = mlp_back(
        0, slots[0], grad_slots, [shape((4, 192, D), BF)] + [shape((2, 192, D), BF)] * 2
    )
    m_first0 = line_flip(after(m_first0, m_sums1[0]))
    m_second0 = line_flip(after(m_second0, m_sums1[0]))
    a_keep0, a_other0, ns, _ = attend_back(
        0, slots[0], grad_slots, (after(dn, m_sums1[0]), sum_m)
    )
    block_both = shape((304, D), BF)

    def add_both(other, slots, places, name):
        return run(
            partial(add_both_body, slots, places),
            [block_both] * len(slots),
            name,
            (m_keep0, other, a_keep1, a_other1),
        )

    both1, both3 = add_both(after(m_first0, a_keep0, a_other1, *m_sums1), HALVES[0], (0, 1), "add_first")
    first_added = both1
    both1, both3 = line_shift(both1, 1), line_shift(both3, 3)
    grad, _ = norm_back(0, grad, sum_team(ns[0], ns[1], after(ns[2], first_added)))
    _, activations = residual(streams[1], (ys[0], ys[1], after(ys[2], first_added)))
    e_keep, e_send = run(
        line_sum_body,
        [shape((EARLY, D), F32), shape((EARLY, D), BF)],
        "line_sum",
        (e0, after(early[0], grad), early[1], early[2]),
    )
    e_other = line_flip(e_send)
    (both2,) = add_both(
        after(m_second0, both1, both3, grad, activations), HALVES[1][:1], (0,), "add_second"
    )
    a_added0 = add(
        block_a, a_keep0, after(a_other0, both2), (1, 2, 3), (1, 2, 3), "add_attend"
    )
    both2 = line_shift(both2, 2)
    a_sums0 = shifts([after(piece, both2) for piece in a_added0])
    both = (both1, both2, both3)
    outs[1] = split(
        (a_keep1, a_other1, *both), (m_keep1, one_of(m_other1, 0), *m_sums1), (e_keep, e_other)
    )
    outs[0] = split(
        (a_keep0, after(a_other0, outs[1][0]), *a_sums0), (m_keep0, one_of(m_second0, 1), *both)
    )
    row_24 = shape((LAYERS, 24), F32)
    final = run(
        unpack_body,
        [
            shape((LAYERS, 24, 3 * D), F32), shape((LAYERS, 72), F32),
            shape((LAYERS, 24, D), F32), row_24,
            shape((LAYERS, 24, FF), F32), shape((LAYERS, 96), F32),
            shape((LAYERS, 96, D), F32), row_24, row_24, row_24, row_24, row_24,
        ],
        "unpack_gradients",
        [array for group in outs for array in group],
    )
    return (activations, grad, *final)


def whole_mesh_solution(mesh):
    in_specs = (
        P(("dp", "cp"), None),
        P(("dp", "cp")),
        P(("dp", "cp"), None),
        P(None, ("dp", "cp"), None),
        P(None, ("dp", "cp")),
        P(None, ("dp", "cp"), None),
        P(None, ("dp", "cp")),
        P(None, ("dp", "cp"), None),
        P(None, ("dp", "cp")),
        P(None, ("dp", "cp"), None),
        P(None, ("dp", "cp")),
        P(None, ("dp", "cp")),
        P(None, ("dp", "cp")),
        P(None, ("dp", "cp")),
        P(None, ("dp", "cp")),
    )
    out_specs = (
        P(("dp", "cp"), None),
        P(("dp", "cp"), None),
        P(None, ("dp", "cp"), None),
        P(None, ("dp", "cp")),
        P(None, ("dp", "cp"), None),
        P(None, ("dp", "cp")),
        P(None, ("dp", "cp"), None),
        P(None, ("dp", "cp")),
        P(None, ("dp", "cp"), None),
        P(None, ("dp", "cp")),
        P(None, ("dp", "cp")),
        P(None, ("dp", "cp")),
        P(None, ("dp", "cp")),
        P(None, ("dp", "cp")),
    )
    return jax.shard_map(local, mesh=mesh, in_specs=in_specs, out_specs=out_specs, check_vma=False)


def solution(mesh):
    teams = mesh.shape["dp"] // 2
    if mesh.shape["cp"] != 2 or teams != 2 * LINE or teams * TEAM * 24 != D:
        return whole_mesh_solution(mesh)
    split_mesh = Mesh(mesh.devices.reshape(teams // 2, 2, 2, 2), ("z", "y", "core", "x"))
    every = ("z", "y", "core", "x")
    row = P(every, None)
    matrix, vector = P(None, every, None), P(None, every)
    in_specs = (row, P(every), row) + (matrix, vector) * 4 + (vector,) * 4
    out_specs = (row, row) + (matrix, vector) * 4 + (vector,) * 4
    return jax.shard_map(
        local_team, mesh=split_mesh, in_specs=in_specs, out_specs=out_specs, check_vma=False
    )
```

```python
from functools import partial
import math

import jax
import jax.numpy as jnp
from jax import lax
from jax.experimental import pallas as pl
from jax.experimental.pallas import tpu as pltpu
from jax.sharding import Mesh, PartitionSpec as P

D = 768
HEADS = 12
HEAD = 64
FF = 3072
ROT = 16
LAYERS = 2


def layer_norm(stream, norm_gain, norm_shift):
    centered = stream - jnp.mean(stream, axis=-1, keepdims=True)
    spread = jnp.mean(centered * centered, axis=-1, keepdims=True)
    return centered * lax.rsqrt(spread + 1e-05) * norm_gain + norm_shift


def both_norms(stream, gain_attn, shift_attn, gain_mlp, shift_mlp):
    return (layer_norm(stream, gain_attn, shift_attn), layer_norm(stream, gain_mlp, shift_mlp))


def angles(positions):
    inverse = 10000.0 ** (-jnp.arange(0, ROT, 2, dtype=jnp.float32) / ROT)
    phases = positions.astype(jnp.float32)[:, None] * inverse[None, :]
    return (jnp.cos(phases)[:, None, :], jnp.sin(phases)[:, None, :])


def rotate(heads_in, cosine_table, sine_table):
    half_rot = cosine_table.shape[-1]
    first_half = heads_in[..., :half_rot]
    second_half = heads_in[..., half_rot : 2 * half_rot]
    untouched = heads_in[..., 2 * half_rot :]
    return jnp.concatenate(
        [
            first_half * cosine_table - second_half * sine_table,
            second_half * cosine_table + first_half * sine_table,
            untouched,
        ],
        axis=-1,
    )


def split_blocks(update, running, key_piece, value_piece, offset):
    piece_rows = key_piece.shape[0]
    block_rows = 512 if piece_rows > 512 and piece_rows % 512 == 0 else piece_rows
    block_count = piece_rows // block_rows
    if block_count == 1:
        return update(running, key_piece, value_piece, offset)

    def advance(state, inputs):
        key_block, value_block, start = inputs
        return (update(state, key_block, value_block, offset + start), None)

    starts = jnp.arange(block_count, dtype=jnp.int32) * block_rows
    state, _ = lax.scan(
        advance,
        running,
        (
            key_piece.reshape(block_count, block_rows, -1),
            value_piece.reshape(block_count, block_rows, -1),
            starts,
        ),
    )
    return state


def stack_layers(per_layer, member):
    return jnp.stack([layer_entry[member] for layer_entry in per_layer])


def flatten_rows(matrix):
    return matrix.reshape(matrix.shape[:-2] + (-1, 128))


def local(
    tokens,
    segment_ids,
    cotangent,
    qkv_weight,
    qkv_bias,
    attn_weight,
    attn_bias,
    up_weight,
    up_bias,
    down_weight,
    down_bias,
    attn_gain,
    attn_shift,
    mlp_gain,
    mlp_shift,
):
    tok_rows = tokens.shape[0]
    group_rows = tok_rows * lax.axis_size("cp")
    score_scale = 1.0 / math.sqrt(HEAD)
    all_segments = lax.all_gather(segment_ids, "cp", axis=0, tiled=True)
    row_index = lax.axis_index("cp") * tok_rows + jnp.arange(tok_rows, dtype=jnp.int32)
    positions = row_index - jnp.sum(
        (all_segments[None, :] < segment_ids[:, None]).astype(jnp.int32), axis=1
    )
    cosine_table, sine_table = angles(positions)

    def visible_mask(offset, block_rows):
        key_index = offset + jnp.arange(block_rows, dtype=jnp.int32)
        key_segment = lax.dynamic_slice_in_dim(all_segments, offset, block_rows)
        return (key_index[None, :] <= row_index[:, None]) & (
            key_segment[None, :] == segment_ids[:, None]
        )

    def online_step(query_heads, running, key_block, value_block, offset):
        row_max, denominator, weighted = running
        block_rows = key_block.shape[0]
        key_heads = key_block.reshape(block_rows, HEADS, HEAD)
        value_heads = value_block.reshape(block_rows, HEADS, HEAD)
        scores = (
            jnp.einsum("qhd,khd->hqk", query_heads, key_heads, preferred_element_type=jnp.float32)
            * score_scale
        )
        visible = visible_mask(offset, block_rows)
        scores = jnp.where(visible[None], scores, -1e30)
        new_max = jnp.maximum(row_max, jnp.max(scores, axis=-1))
        rescale = jnp.exp(row_max - new_max)
        weights = jnp.where(visible[None], jnp.exp(scores - new_max[..., None]), 0.0)
        denominator = denominator * rescale + jnp.sum(weights, axis=-1)
        weighted = weighted * rescale[..., None] + jnp.einsum(
            "hqk,khd->hqd",
            weights.astype(jnp.bfloat16),
            value_heads,
            preferred_element_type=jnp.float32,
        )
        return (new_max, denominator, weighted)

    stream = tokens.astype(jnp.float32)
    stored = []
    for depth in range(LAYERS):
        params = (
            lax.all_gather(qkv_weight[depth], ("dp", "cp"), axis=0, tiled=True),
            lax.all_gather(qkv_bias[depth], ("dp", "cp"), axis=0, tiled=True),
            lax.all_gather(attn_weight[depth], ("dp", "cp"), axis=0, tiled=True),
            lax.all_gather(attn_bias[depth], ("dp", "cp"), axis=0, tiled=True),
            lax.all_gather(up_weight[depth], ("dp", "cp"), axis=0, tiled=True),
            lax.all_gather(up_bias[depth], ("dp", "cp"), axis=0, tiled=True),
            lax.all_gather(down_weight[depth], ("dp", "cp"), axis=0, tiled=True),
            lax.all_gather(down_bias[depth], ("dp", "cp"), axis=0, tiled=True),
            lax.all_gather(attn_gain[depth], ("dp", "cp"), axis=0, tiled=True),
            lax.all_gather(attn_shift[depth], ("dp", "cp"), axis=0, tiled=True),
            lax.all_gather(mlp_gain[depth], ("dp", "cp"), axis=0, tiled=True),
            lax.all_gather(mlp_shift[depth], ("dp", "cp"), axis=0, tiled=True),
        )
        (
            proj_qkv,
            bias_qkv,
            proj_attn,
            bias_attn,
            proj_up,
            bias_up,
            proj_down,
            bias_down,
            gain_attn,
            shift_attn,
            gain_mlp,
            shift_mlp,
        ) = params
        normed_attn, normed_mlp = both_norms(
            stream,
            gain_attn.astype(jnp.float32),
            shift_attn.astype(jnp.float32),
            gain_mlp.astype(jnp.float32),
            shift_mlp.astype(jnp.float32),
        )
        normed_attn = normed_attn.astype(jnp.bfloat16)
        normed_mlp = normed_mlp.astype(jnp.bfloat16)
        projected = jnp.dot(
            normed_attn, proj_qkv, preferred_element_type=jnp.float32
        ) + bias_qkv.astype(jnp.float32)
        queries = rotate(
            projected[:, :D].reshape(tok_rows, HEADS, HEAD), cosine_table, sine_table
        ).astype(jnp.bfloat16)
        key_rows = (
            rotate(projected[:, D : 2 * D].reshape(tok_rows, HEADS, HEAD), cosine_table, sine_table)
            .astype(jnp.bfloat16)
            .reshape(tok_rows, D)
        )
        values = projected[:, 2 * D :].astype(jnp.bfloat16)
        initial = (
            jnp.full((HEADS, tok_rows), -1e30, jnp.float32),
            jnp.zeros((HEADS, tok_rows), jnp.float32),
            jnp.zeros((HEADS, tok_rows, HEAD), jnp.float32),
        )
        row_max, denominator, weighted = split_blocks(
            partial(online_step, queries),
            initial,
            lax.all_gather(key_rows, "cp", axis=0, tiled=True),
            lax.all_gather(values, "cp", axis=0, tiled=True),
            jnp.int32(0),
        )
        attended = jnp.transpose(weighted / denominator[..., None], (1, 0, 2)).reshape(tok_rows, D)
        log_total = row_max + jnp.log(denominator)
        attended_low = attended.astype(jnp.bfloat16)
        attn_branch = jnp.dot(
            attended_low, proj_attn, preferred_element_type=jnp.float32
        ) + bias_attn.astype(jnp.float32)
        hidden_pre = jnp.dot(
            normed_mlp, proj_up, preferred_element_type=jnp.float32
        ) + bias_up.astype(jnp.float32)
        hidden = jax.nn.gelu(hidden_pre, approximate=False).astype(jnp.bfloat16)
        mlp_branch = jnp.dot(
            hidden, proj_down, preferred_element_type=jnp.float32
        ) + bias_down.astype(jnp.float32)
        stored.append(
            (
                stream,
                normed_attn,
                normed_mlp,
                queries,
                key_rows,
                values,
                attended,
                attended_low,
                log_total,
                hidden_pre,
                hidden,
            )
        )
        stream = stream + attn_branch + mlp_branch
    grad_stream = cotangent.astype(jnp.float32)
    per_layer = [None] * LAYERS
    for depth in reversed(range(LAYERS)):
        (
            saved_stream,
            normed_attn,
            normed_mlp,
            queries,
            key_rows,
            values,
            attended,
            attended_low,
            log_total,
            hidden_pre,
            hidden,
        ) = stored[depth]
        params = (
            lax.all_gather(qkv_weight[depth], ("dp", "cp"), axis=0, tiled=True),
            lax.all_gather(qkv_bias[depth], ("dp", "cp"), axis=0, tiled=True),
            lax.all_gather(attn_weight[depth], ("dp", "cp"), axis=0, tiled=True),
            lax.all_gather(attn_bias[depth], ("dp", "cp"), axis=0, tiled=True),
            lax.all_gather(up_weight[depth], ("dp", "cp"), axis=0, tiled=True),
            lax.all_gather(up_bias[depth], ("dp", "cp"), axis=0, tiled=True),
            lax.all_gather(down_weight[depth], ("dp", "cp"), axis=0, tiled=True),
            lax.all_gather(down_bias[depth], ("dp", "cp"), axis=0, tiled=True),
            lax.all_gather(attn_gain[depth], ("dp", "cp"), axis=0, tiled=True),
            lax.all_gather(attn_shift[depth], ("dp", "cp"), axis=0, tiled=True),
            lax.all_gather(mlp_gain[depth], ("dp", "cp"), axis=0, tiled=True),
            lax.all_gather(mlp_shift[depth], ("dp", "cp"), axis=0, tiled=True),
        )
        (
            proj_qkv,
            bias_qkv,
            proj_attn,
            bias_attn,
            proj_up,
            bias_up,
            proj_down,
            bias_down,
            gain_attn,
            shift_attn,
            gain_mlp,
            shift_mlp,
        ) = params
        grad_low = grad_stream.astype(jnp.bfloat16)
        bias_grad = jnp.sum(grad_low.astype(jnp.float32), axis=0)
        attn_weight_grad = jnp.einsum(
            "td,te->de", attended_low, grad_low, preferred_element_type=jnp.float32
        )
        down_weight_grad = jnp.einsum(
            "tf,te->fe", hidden, grad_low, preferred_element_type=jnp.float32
        )
        grad_attended = jnp.einsum(
            "te,de->td", grad_low, proj_attn, preferred_element_type=jnp.float32
        ).astype(jnp.bfloat16)
        grad_hidden = jnp.einsum(
            "te,fe->tf", grad_low, proj_down, preferred_element_type=jnp.float32
        )
        _, gelu_pull = jax.vjp(partial(jax.nn.gelu, approximate=False), hidden_pre)
        grad_pre = gelu_pull(grad_hidden)[0].astype(jnp.bfloat16)
        up_weight_grad = jnp.einsum(
            "td,tf->df", normed_mlp, grad_pre, preferred_element_type=jnp.float32
        )
        up_bias_grad = jnp.sum(grad_pre.astype(jnp.float32), axis=0)
        grad_normed_mlp = jnp.einsum(
            "tf,df->td", grad_pre, proj_up, preferred_element_type=jnp.float32
        )
        all_keys, all_values = (
            lax.all_gather(key_rows, "cp", axis=0, tiled=True),
            lax.all_gather(values, "cp", axis=0, tiled=True),
        )
        grad_heads = grad_attended.reshape(tok_rows, HEADS, HEAD)
        row_dot = jnp.transpose(
            jnp.sum(
                grad_heads.astype(jnp.float32) * attended.reshape(tok_rows, HEADS, HEAD), axis=-1
            )
        )
        block_rows = 512 if group_rows > 512 and group_rows % 512 == 0 else group_rows
        block_count = group_rows // block_rows
        starts = jnp.arange(block_count, dtype=jnp.int32) * block_rows

        def back_step(grad_query, inputs):
            key_block, value_block, offset = inputs
            key_heads = key_block.reshape(block_rows, HEADS, HEAD)
            value_heads = value_block.reshape(block_rows, HEADS, HEAD)
            scores = (
                jnp.einsum("qhd,khd->hqk", queries, key_heads, preferred_element_type=jnp.float32)
                * score_scale
            )
            visible = visible_mask(offset, block_rows)
            weights = jnp.where(visible[None], jnp.exp(scores - log_total[..., None]), 0.0)
            grad_weights = jnp.einsum(
                "qhd,khd->hqk", grad_heads, value_heads, preferred_element_type=jnp.float32
            )
            grad_scores = (weights * (grad_weights - row_dot[..., None])).astype(jnp.bfloat16)
            grad_query = grad_query + jnp.einsum(
                "hqk,khd->hqd", grad_scores, key_heads, preferred_element_type=jnp.float32
            )
            key_grad = (
                jnp.einsum("hqk,qhd->khd", grad_scores, queries, preferred_element_type=jnp.float32)
                * score_scale
            )
            value_grad = jnp.einsum(
                "hqk,qhd->khd",
                weights.astype(jnp.bfloat16),
                grad_heads,
                preferred_element_type=jnp.float32,
            )
            return (
                grad_query,
                (key_grad.reshape(block_rows, D), value_grad.reshape(block_rows, D)),
            )

        grad_query, (key_grads, value_grads) = lax.scan(
            back_step,
            jnp.zeros((HEADS, tok_rows, HEAD), jnp.float32),
            (
                all_keys.reshape(block_count, block_rows, D),
                all_values.reshape(block_count, block_rows, D),
                starts,
            ),
        )
        local_key_grad, local_value_grad = (
            lax.psum_scatter(
                key_grads.reshape(group_rows, D).astype(jnp.bfloat16),
                "cp",
                scatter_dimension=0,
                tiled=True,
            ).astype(jnp.float32),
            lax.psum_scatter(
                value_grads.reshape(group_rows, D).astype(jnp.bfloat16),
                "cp",
                scatter_dimension=0,
                tiled=True,
            ).astype(jnp.float32),
        )
        query_raw = rotate(
            jnp.transpose(grad_query * score_scale, (1, 0, 2)), cosine_table, -sine_table
        )
        key_raw = rotate(local_key_grad.reshape(tok_rows, HEADS, HEAD), cosine_table, -sine_table)
        grad_projected = jnp.concatenate(
            [query_raw.reshape(tok_rows, D), key_raw.reshape(tok_rows, D), local_value_grad], axis=1
        ).astype(jnp.bfloat16)
        qkv_weight_grad = jnp.einsum(
            "td,te->de", normed_attn, grad_projected, preferred_element_type=jnp.float32
        )
        qkv_bias_grad = jnp.sum(grad_projected.astype(jnp.float32), axis=0)
        grad_normed_attn = jnp.einsum(
            "te,de->td", grad_projected, proj_qkv, preferred_element_type=jnp.float32
        )
        _, norm_pull = jax.vjp(
            both_norms,
            saved_stream,
            gain_attn.astype(jnp.float32),
            shift_attn.astype(jnp.float32),
            gain_mlp.astype(jnp.float32),
            shift_mlp.astype(jnp.float32),
        )
        grad_input, attn_gain_grad, attn_shift_grad, mlp_gain_grad, mlp_shift_grad = norm_pull(
            (grad_normed_attn, grad_normed_mlp)
        )
        grad_stream = grad_stream + grad_input
        summed = (
            lax.psum_scatter(
                flatten_rows(qkv_weight_grad), ("dp", "cp"), scatter_dimension=0, tiled=True
            ),
            lax.psum_scatter(qkv_bias_grad, ("dp", "cp"), scatter_dimension=0, tiled=True),
            lax.psum_scatter(
                flatten_rows(attn_weight_grad), ("dp", "cp"), scatter_dimension=0, tiled=True
            ),
            lax.psum_scatter(bias_grad, ("dp", "cp"), scatter_dimension=0, tiled=True),
            lax.psum_scatter(
                flatten_rows(up_weight_grad), ("dp", "cp"), scatter_dimension=0, tiled=True
            ),
            lax.psum_scatter(up_bias_grad, ("dp", "cp"), scatter_dimension=0, tiled=True),
            lax.psum_scatter(
                flatten_rows(down_weight_grad), ("dp", "cp"), scatter_dimension=0, tiled=True
            ),
            lax.psum_scatter(bias_grad, ("dp", "cp"), scatter_dimension=0, tiled=True),
            lax.psum_scatter(attn_gain_grad, ("dp", "cp"), scatter_dimension=0, tiled=True),
            lax.psum_scatter(attn_shift_grad, ("dp", "cp"), scatter_dimension=0, tiled=True),
            lax.psum_scatter(mlp_gain_grad, ("dp", "cp"), scatter_dimension=0, tiled=True),
            lax.psum_scatter(mlp_shift_grad, ("dp", "cp"), scatter_dimension=0, tiled=True),
        )
        per_layer[depth] = (
            summed[0].reshape(-1, 3 * D),
            summed[1],
            summed[2].reshape(-1, D),
            summed[3],
            summed[4].reshape(-1, FF),
            summed[5],
            summed[6].reshape(-1, D),
            summed[7],
            summed[8],
            summed[9],
            summed[10],
            summed[11],
        )
    stacked = [stack_layers(per_layer, member) for member in range(12)]
    return (
        stream.astype(jnp.bfloat16),
        grad_stream,
        stacked[0],
        stacked[1],
        stacked[2],
        stacked[3],
        stacked[4],
        stacked[5],
        stacked[6],
        stacked[7],
        stacked[8],
        stacked[9],
        stacked[10],
        stacked[11],
    )


TEAM = 4
TEAM_AXES = ("core", "x")
LINE_AXES = ("z", "y")
LINE = 4
MINE = (3 * D) // TEAM
HCOLS = D // TEAM
UCOLS = FF // TEAM
VMEM_BYTES = 56 * 1024 * 1024
BF = jnp.bfloat16
F32 = jnp.float32


def call(body, out_shape, name, operands, scratch=()):
    return pl.pallas_call(
        body,
        out_shape=out_shape,
        scratch_shapes=list(scratch),
        compiler_params=pltpu.CompilerParams(vmem_limit_bytes=VMEM_BYTES),
        name=name,
    )(*operands)


def shape(dims, kind):
    return jax.ShapeDtypeStruct(dims, kind)


def mm(left, right):
    return jnp.dot(left, right, preferred_element_type=F32)


def mm_t(left, right):
    return lax.dot_general(left, right, (((1,), (1,)), ((), ())), preferred_element_type=F32)


def t_mm(left, right):
    return lax.dot_general(left, right, (((0,), (0,)), ((), ())), preferred_element_type=F32)


def pick(member, pieces, wanted):
    chosen = pieces[0]
    for s in range(1, TEAM):
        chosen = jnp.where((member ^ s) == wanted, pieces[s], chosen)
    return chosen


def small_rows(vectors, depth):
    rows = []
    for vector in vectors:
        values = vector[depth : depth + 1].astype(F32)
        rows.append(
            jnp.concatenate([values, jnp.zeros((1, 128 - values.shape[1]), F32)], axis=1)
        )
    return jnp.concatenate(rows, axis=0)


def pack_body(me_ref, qkv_ref, up_ref, *refs):
    vectors, outs = [r[...] for r in refs[:8]], refs[8:]
    me = me_ref[0]
    small = jnp.concatenate([small_rows(vectors, depth) for depth in range(LAYERS)], axis=0)
    small = jnp.concatenate([small, jnp.zeros((small.shape[0], UCOLS - 128), F32)], axis=1)
    parts = [[] for _ in range(TEAM)]
    for depth in range(LAYERS):
        rows = qkv_ref.shape[1]
        qkv = qkv_ref[depth].astype(F32)
        up = up_ref[depth].astype(F32)
        blocks = up.shape[1] // (TEAM * 96)
        for p in range(TEAM):
            parts[p].append(
                jnp.concatenate(
                    [up[:, 96 * (TEAM * b + p) : 96 * (TEAM * b + p + 1)] for b in range(blocks)],
                    axis=1,
                )
            )
            parts[p].append(
                jnp.concatenate(
                    [qkv[:, D * t + HCOLS * p : D * t + HCOLS * (p + 1)] for t in range(3)]
                    + [jnp.zeros((rows, UCOLS - MINE), F32)],
                    axis=1,
                )
            )
    parts = [jnp.concatenate(group, axis=0) for group in parts]
    for s in range(TEAM):
        chosen = parts[0]
        for p in range(1, TEAM):
            chosen = jnp.where((me ^ s) == p, parts[p], chosen)
        outs[s][...] = jnp.concatenate([chosen, small], axis=0).astype(BF)


def assemble_body(me_ref, p0, p1, p2, p3, attn_ref, down_ref, *outs):
    me = me_ref[0]
    slots = [r[...].astype(F32) for r in (p0, p1, p2, p3)]
    ordered = [pick(me, slots, p) for p in range(TEAM)]
    for depth, out in enumerate(outs):
        base = 48 * depth
        up = jnp.concatenate([piece[base : base + 24] for piece in ordered], axis=0)
        qkv = jnp.concatenate([piece[base + 24 : base + 48] for piece in ordered], axis=0)
        attn = attn_ref[depth].astype(F32)
        side = jnp.concatenate([attn[:, HCOLS * n : HCOLS * (n + 1)] for n in range(4)], axis=0)
        out[0:96] = up.astype(BF)
        out[96:192] = down_ref[depth]
        out[192:288] = jnp.concatenate([qkv[:, :MINE], side], axis=1).astype(BF)
        if out.shape[0] > 288:
            small = jnp.concatenate(
                [piece[96:112, :128] for piece in ordered] + [jnp.zeros((16, D - 4 * 128), F32)],
                axis=1,
            )
            out[288:304] = small.astype(BF)


def source_team(me_ref, index):
    shift, flip = index % LINE, index // LINE
    return 2 * lax.rem(me_ref[1] + LINE - shift, LINE) + (me_ref[2] ^ flip)


def target_team(me_ref, index):
    shift, flip = index % LINE, index // LINE
    return 2 * lax.rem(me_ref[1] + shift, LINE) + (me_ref[2] ^ flip)


def place(me_ref, pieces, whole):
    for index, piece in enumerate(pieces):
        whole[source_team(me_ref, index)] = piece[...]


def hand_out(me_ref, whole, keep, sends, order):
    for s in range(LINE):
        keep[s] = whole[target_team(me_ref, s)]
    for send, slots in zip(sends, order):
        for n, s in enumerate(slots):
            send[n] = whole[target_team(me_ref, LINE + s)]


ALL_SLOTS = (tuple(range(LINE)),)
HALVES = ((1, 3), (2, 0))


def add_body(slots, places, me_ref, keep, received, *outs):
    for s, n, out in zip(slots, places, outs):
        out[...] = (keep[s].astype(F32) + received[n].astype(F32)).astype(BF)


def add_both_body(slots, places, me_ref, m_keep, m_received, a_keep, a_received, *outs):
    for s, n, out in zip(slots, places, outs):
        out[0:192] = (m_keep[s].astype(F32) + m_received[n].astype(F32)).astype(BF)
        out[192:304] = (a_keep[s].astype(F32) + a_received[s].astype(F32)).astype(BF)


def line_sum_body(me_ref, own, r1, r2, r3, keep_ref, send_ref):
    for f, out in enumerate((keep_ref, send_ref)):
        total = own[f].astype(F32) + r1[f].astype(F32) + r2[f].astype(F32) + r3[f].astype(F32)
        out[...] = total.astype(out.dtype)


def layer_vectors(me_ref, whole, depth):
    me = me_ref[0]
    small = [whole[k].astype(F32) for k in range(2 * LINE)]
    fields = [block[8 * depth : 8 * (depth + 1)] for block in small]
    shared = jnp.concatenate(
        [block[2:8, 128 * p : 128 * p + 24] for block in fields for p in range(TEAM)], axis=1
    )
    up_rows, qkv_rows = [], []
    qkv = jnp.concatenate(
        [block[0:1, 128 * p : 128 * p + 72] for block in fields for p in range(TEAM)], axis=1
    )
    for p in range(TEAM):
        up_rows.append(
            jnp.concatenate([block[1:2, 128 * p : 128 * p + 96] for block in fields], axis=1)
        )
        qkv_rows.append(
            jnp.concatenate(
                [qkv[:, D * t + HCOLS * p : D * t + HCOLS * (p + 1)] for t in range(3)]
                + [jnp.zeros((1, D - MINE), F32)],
                axis=1,
            )
        )
    up_mine, qkv_mine = up_rows[0], qkv_rows[0]
    for p in range(1, TEAM):
        up_mine = jnp.where(me == p, up_rows[p], up_mine)
        qkv_mine = jnp.where(me == p, qkv_rows[p], qkv_mine)
    return jnp.concatenate([shared, up_mine, qkv_mine], axis=0)


def attn_weights(whole):
    qkv = whole[:, 0:96, :][:, :, :MINE].reshape(D, MINE)
    side = whole[:, 0:96, MINE:].astype(F32)
    out = jnp.concatenate(
        [side[:, 24 * n : 24 * (n + 1), :].reshape(HCOLS, HCOLS) for n in range(4)], axis=1
    )
    return qkv, out.astype(BF)


def project(scaled, vec, weight, cosine, sine):
    normed = (scaled * vec[0:1] + vec[1:2]).astype(BF)
    projected = mm(normed, weight) + vec[7:8, :MINE]
    turned = turn(projected[:, : 2 * HCOLS], cosine, sine)
    queries = (turned[:, :HCOLS] * 0.125).astype(BF)
    keys = turned[:, HCOLS:].astype(BF)
    values = projected[:, 2 * HCOLS :].astype(BF)
    return normed, queries, keys, values


def attend_body(me_ref, x0, x1, x2, x3, *refs):
    pieces, smalls = refs[:8], refs[8:16]
    cos_ref, sin_ref, mask_ref, y_ref, vec_ref, whole, small = refs[16:]
    place(me_ref, pieces, whole)
    place(me_ref, smalls, small)
    for depth in range(LAYERS):
        vec_ref[depth] = layer_vectors(me_ref, small, depth)
    vec = vec_ref[0]
    weight, out_weight = attn_weights(whole)
    for g, (first, second) in enumerate(((x0, x1), (x2, x3))):
        rows = pl.ds(PAIR * g, PAIR)
        scaled, _ = norm_parts(two_slots(first[...], second[...]))
        _, queries, keys, values = project(scaled, vec, weight, cos_ref[rows, :], sin_ref[rows, :])
        total = jnp.zeros((PAIR, HCOLS), F32)
        for head in range(HEADS // TEAM):
            owned = head_mask(PAIR, head)
            scores = mm_t(jnp.where(owned, queries, jnp.zeros_like(queries)), keys) + mask_ref[g]
            weights = jnp.exp(scores - jnp.max(scores, axis=-1, keepdims=True))
            below = jnp.sum(weights, axis=-1, keepdims=True)
            total = total + jnp.where(owned, mm(weights.astype(BF), values) / below, 0.0)
        y_ref[rows, :] = mm(total.astype(BF), out_weight)


def store_pair(g, result, own, near, far):
    if g == 0:
        own[...] = result[0:TOK]
        near[...] = result[TOK:]
    else:
        far[...] = result.astype(BF)


def mlp_body(me_ref, x0, x1, x2, x3, *refs):
    pieces, (vec_ref, a_ref, y0, y1, y23, whole) = refs[:8], refs[8:]
    place(me_ref, pieces, whole)
    vec = vec_ref[0]
    up = whole[:, 0:96, :].reshape(D, UCOLS)
    down = whole[:, 96:192, :].reshape(UCOLS, D)
    for g, (first, second) in enumerate(((x0, x1), (x2, x3))):
        rows = pl.ds(PAIR * g, PAIR)
        scaled, _ = norm_parts(two_slots(first[...], second[...]))
        normed = (scaled * vec[2:3] + vec[3:4]).astype(BF)
        before = mm(normed, up) + vec[6:7]
        hidden = (before * (0.5 * (1.0 + lax.erf(before * (1.0 / math.sqrt(2.0)))))).astype(BF)
        result = mm(hidden, down) + a_ref[rows, :]
        store_pair(g, result, y0, y1, y23)


def mlp_both_body(depth, last, me_ref, x0, x1, x2, x3, g0, g1, g2, g3, *refs):
    pieces, vec_ref, (dn_ref, sum_ref), refs = refs[:8], refs[8], refs[9:11], refs[11:]
    if last:
        y_ref, refs = refs[0], refs[1:]
    whole, grads, c_s, hid_s, du_s, gb_s = refs[-6:]
    place(me_ref, pieces, whole)
    vec = vec_ref[depth]
    up = whole[:, 0:96, :].reshape(D, UCOLS)
    down = whole[:, 96:192, :].reshape(UCOLS, D)
    gain_sum = jnp.zeros((1, D), F32)
    shift_sum = jnp.zeros((1, D), F32)
    bias_sum = jnp.zeros((1, D), F32)
    up_sum = jnp.zeros((1, UCOLS), F32)
    for g, (first, second, g_first, g_second) in enumerate(((x0, x1, g0, g1), (x2, x3, g2, g3))):
        rows = pl.ds(PAIR * g, PAIR)
        scaled, _ = norm_parts(two_slots(first[...], second[...]))
        normed = (scaled * vec[2:3] + vec[3:4]).astype(BF)
        c_s[rows, :] = normed
        low = jnp.concatenate([g_first[...], g_second[...]], axis=0)
        gb_s[rows, :] = low
        hidden, slope = gelu_parts(mm(normed, up) + vec[6:7])
        hidden = hidden.astype(BF)
        hid_s[rows, :] = hidden
        if last:
            y_ref[rows, :] = mm(hidden, down)
        du = (mm_t(low, down) * slope).astype(BF)
        du_s[rows, :] = du
        dc = mm_t(du, up)
        dn_ref[rows, :] = dc * vec[2:3]
        gain_sum = gain_sum + jnp.sum(dc * scaled, axis=0, keepdims=True)
        shift_sum = shift_sum + jnp.sum(dc, axis=0, keepdims=True)
        bias_sum = bias_sum + jnp.sum(low.astype(F32), axis=0, keepdims=True)
        up_sum = up_sum + jnp.sum(du.astype(F32), axis=0, keepdims=True)
    grads[:, 0:96, :] = t_mm(c_s[...], du_s[...]).reshape(-1, 96, UCOLS).astype(BF)
    grads[:, 96:192, :] = t_mm(hid_s[...], gb_s[...]).reshape(-1, 96, D).astype(BF)
    if last:
        for s, out in enumerate(refs[0:LINE]):
            for f in range(2):
                out[f] = grads[target_team(me_ref, LINE * f + s), 0:EARLY, :]
        keep, send = refs[LINE : LINE + 2]
        for s in range(LINE):
            keep[s] = grads[target_team(me_ref, s), EARLY:192, :]
            send[s] = grads[target_team(me_ref, LINE + s), EARLY:192, :]
    else:
        hand_out(me_ref, grads, refs[0], refs[1:3], HALVES)
    sum_ref[...] = jnp.concatenate(
        [bias_sum, up_sum, gain_sum, shift_sum, jnp.zeros((4, D), F32)], axis=0
    )


def attend_both_body(depth, last, me_ref, x0, x1, x2, x3, g0, g1, g2, g3, *refs):
    pieces, (vec_ref, cos_ref, sin_ref, mask_ref, dn_ref, sum_ref) = refs[:8], refs[8:14]
    refs = refs[14:]
    if last:
        y_ref, refs = refs[0], refs[1:]
    blocks, (n0, n1, n23) = refs[:2], refs[2:5]
    whole, grads, a_s, dp_s, o_s, gb_s = refs[-6:]
    place(me_ref, pieces, whole)
    vec = vec_ref[depth]
    weight, out_weight = attn_weights(whole)
    gain_sum = jnp.zeros((1, D), F32)
    shift_sum = jnp.zeros((1, D), F32)
    bias_sum = jnp.zeros((1, MINE), F32)
    for g, (first, second, g_first, g_second) in enumerate(((x0, x1, g0, g1), (x2, x3, g2, g3))):
        rows = pl.ds(PAIR * g, PAIR)
        cosine, sine = cos_ref[rows, :], sin_ref[rows, :]
        scaled, _ = norm_parts(two_slots(first[...], second[...]))
        normed, queries, keys, values = project(scaled, vec, weight, cosine, sine)
        a_s[rows, :] = normed
        low = jnp.concatenate([g_first[...], g_second[...]], axis=0)
        gb_s[rows, :] = low
        grad_o = mm_t(low, out_weight).astype(BF)
        zero = jnp.zeros_like(queries)
        out = jnp.zeros((PAIR, HCOLS), F32)
        dq = jnp.zeros((PAIR, HCOLS), F32)
        dk = jnp.zeros((PAIR, HCOLS), F32)
        dv = jnp.zeros((PAIR, HCOLS), F32)
        for head in range(HEADS // TEAM):
            owned = head_mask(PAIR, head)
            scores = mm_t(jnp.where(owned, queries, zero), keys) + mask_ref[g]
            weights = jnp.exp(scores - jnp.max(scores, axis=-1, keepdims=True))
            weights = weights / jnp.sum(weights, axis=-1, keepdims=True)
            rounded = weights.astype(BF)
            dweights = mm_t(jnp.where(owned, grad_o, zero), values)
            delta = jnp.sum(weights * dweights, axis=-1, keepdims=True)
            dscores = (weights * (dweights - delta)).astype(BF)
            out = out + jnp.where(owned, mm(rounded, values), 0.0)
            dq = dq + jnp.where(owned, mm(dscores, keys), 0.0)
            dk = dk + jnp.where(owned, t_mm(dscores, queries), 0.0)
            dv = dv + jnp.where(owned, t_mm(rounded, grad_o), 0.0)
        o_s[rows, :] = out.astype(BF)
        both = turn(jnp.concatenate([dq * 0.125, dk], axis=1), cosine, -sine)
        dproj = jnp.concatenate([both, dv], axis=1).astype(BF)
        dp_s[rows, :] = dproj
        bias_sum = bias_sum + jnp.sum(dproj.astype(F32), axis=0, keepdims=True)
        da = mm_t(dproj, weight)
        gain_sum = gain_sum + jnp.sum(da * scaled, axis=0, keepdims=True)
        shift_sum = shift_sum + jnp.sum(da, axis=0, keepdims=True)
        dn = dn_ref[rows, :] + da * vec[0:1]
        store_pair(g, dn, n0, n1, n23)
        if last:
            result = y_ref[rows, :] + mm(out.astype(BF), out_weight)
            store_pair(g, result, *refs[5:8])
    qkv_grad = t_mm(a_s[...], dp_s[...]).reshape(-1, 96, MINE)
    out_grad = t_mm(o_s[...], gb_s[...])
    side = jnp.concatenate(
        [out_grad[:, HCOLS * n : HCOLS * (n + 1)].reshape(-1, 24, HCOLS) for n in range(4)], axis=1
    )
    grads[:, 0:96, :] = jnp.concatenate([qkv_grad, side], axis=2).astype(BF)
    sums = sum_ref[...]
    vectors = jnp.concatenate([sums[0:2], gain_sum, shift_sum, sums[2:4]], axis=0)
    me = me_ref[0]
    spread = jnp.concatenate(
        [
            jnp.where(me == p, bias_sum[:, HCOLS * t : HCOLS * (t + 1)], 0.0)
            for t in range(3)
            for p in range(TEAM)
        ],
        axis=1,
    )
    for k in range(2 * LINE):
        shared = jnp.concatenate(
            [vectors[:, 96 * k : 96 * (k + 1)], jnp.zeros((6, D - 96), F32)], axis=1
        )
        bias = jnp.concatenate(
            [spread[:, 288 * k : 288 * (k + 1)], jnp.zeros((1, D - 288), F32)], axis=1
        )
        grads[k, 96:112, :] = jnp.concatenate([shared, bias, jnp.zeros((9, D), F32)], axis=0).astype(BF)
    hand_out(me_ref, grads, blocks[0], blocks[1:], ALL_SLOTS)


def residual_body(me_ref, x_ref, y0, y1, y2, vec_ref, out_ref, low_ref):
    depth = 0 if x_ref.dtype == BF else 1
    total = y0[...] + y1[...].astype(F32) + y2[...].astype(F32)
    result = x_ref[...].astype(F32) + total + (vec_ref[depth, 4:5] + vec_ref[depth, 5:6])
    out_ref[...] = result
    low_ref[...] = result.astype(BF)

def norm_parts(stream):
    centered = stream - jnp.mean(stream, axis=-1, keepdims=True)
    spread = jnp.mean(centered * centered, axis=-1, keepdims=True)
    inverse = lax.rsqrt(spread + 1e-05)
    return centered * inverse, inverse


def two_slots(first, second):
    return jnp.concatenate([first[0:TOK].astype(F32), second[0:TOK].astype(F32)], axis=0)


TOK = 128
EARLY = 48
PAIR = 2 * TOK


def turn(block, cosine, sine):
    lane = lax.broadcasted_iota(jnp.int32, (block.shape[0], 128), 1) % HEAD
    tiles = []
    for t in range(block.shape[1] // 128):
        tile = block[:, 128 * t : 128 * (t + 1)]
        swapped = jnp.where(
            lane < ROT // 2, pltpu.roll(tile, 128 - ROT // 2, 1), pltpu.roll(tile, ROT // 2, 1)
        )
        tiles.append(tile * cosine + swapped * sine)
    return jnp.concatenate(tiles, axis=1)


def head_mask(rows, head):
    lane = lax.broadcasted_iota(jnp.int32, (rows, HCOLS), 1)
    return (lane >= head * HEAD) & (lane < (head + 1) * HEAD)


def gelu_parts(u):
    cdf = 0.5 * (1.0 + lax.erf(u * (1.0 / math.sqrt(2.0))))
    density = jnp.exp(-0.5 * u * u) * (1.0 / math.sqrt(2.0 * math.pi))
    return u * cdf, cdf + u * density


def norm_back_body(me_ref, x_ref, g_ref, n0, n1, n2, out_ref, low_ref):
    scaled, inverse = norm_parts(x_ref[...].astype(F32))
    dn = n0[...] + n1[...].astype(F32) + n2[...].astype(F32)
    centered = dn - jnp.mean(dn, axis=-1, keepdims=True)
    moment = jnp.mean(dn * scaled, axis=-1, keepdims=True)
    result = g_ref[...].astype(F32) + inverse * (centered - scaled * moment)
    out_ref[...] = result
    low_ref[...] = result.astype(BF)


def total(group):
    result = group[0].astype(F32)
    for term in group[1:]:
        result = result + term.astype(F32)
    return result


def by_owner(me_ref, parts, outs, start):
    me = me_ref[0]
    for s, out in enumerate(outs):
        piece = parts[0]
        for p in range(1, TEAM):
            piece = jnp.where((me ^ s) == p, parts[p], piece)
        out[start : start + 32] = piece.astype(BF)


def split_body(early, me_ref, *refs):
    outs, (down_ref, attn_ref, small_ref), refs = refs[-7:-3], refs[-3:], refs[:-7]
    split_attend(me_ref, refs[:5], outs, attn_ref, small_ref)
    refs = refs[5:]
    size = refs[0].shape[1]
    rest = total([refs[0][0], refs[1][0]] + [ref[0:size, :] for ref in refs[2:5]])
    if early:
        rest = jnp.concatenate([total([refs[5][...], refs[6][...]]), rest], axis=0)
    down_ref[...] = rest[96:192]
    blank = jnp.zeros((8, D), F32)
    parts = [
        jnp.concatenate([rest[24 * p : 24 * (p + 1)], blank], axis=0) for p in range(TEAM)
    ]
    by_owner(me_ref, parts, outs, 0)


def split_attend(me_ref, refs, outs, attn_ref, small_ref):
    me = me_ref[0]
    attn = total([refs[0][0], refs[1][0]] + [ref[-112:, :] for ref in refs[2:]])
    side = attn[0:96, MINE:]
    attn_ref[...] = jnp.concatenate(
        [side[24 * n : 24 * (n + 1)] for n in range(4)], axis=1
    ).astype(BF)
    qkv = jnp.concatenate([attn[0:96, :MINE], jnp.zeros((96, UCOLS - MINE), F32)], axis=1)
    small = attn[96:112]
    parts, bias = [], jnp.zeros((1, 24), F32)
    for p in range(TEAM):
        rows = slice(24 * p, 24 * (p + 1))
        gains = jnp.concatenate([small[2:6, rows], jnp.zeros((4, D - 24), F32)], axis=1)
        qkv_bias = jnp.concatenate(
            [small[6:7, 72 * p : 72 * (p + 1)], jnp.zeros((1, D - 72), F32)], axis=1
        )
        parts.append(jnp.concatenate([qkv[rows], gains, qkv_bias, jnp.zeros((3, D), F32)], axis=0))
        bias = jnp.where(me == p, small[0:1, rows], bias)
    small_ref[...] = jnp.concatenate(
        [
            jnp.concatenate([bias, jnp.zeros((1, 104), F32)], axis=1),
            small[1:2, :128],
            jnp.zeros((6, 128), F32),
        ],
        axis=0,
    )
    by_owner(me_ref, parts, outs, 32)


def unpack_body(me_ref, *refs):
    me = me_ref[0]
    (
        qkv_ref, qkv_b_ref, attn_ref, attn_b_ref, up_ref, up_b_ref, down_ref,
        down_b_ref, ga_ref, sa_ref, gm_ref, sm_ref,
    ) = refs[7 * LAYERS :]
    gain_refs = (ga_ref, sa_ref, gm_ref, sm_ref)
    for depth in range(LAYERS):
        group = refs[7 * depth : 7 * (depth + 1)]
        down_rows, own_small, attn_rows = group[TEAM:]
        slots = [r[...].astype(F32) for r in group[:TEAM]]
        ordered = [pick(me, slots, p) for p in range(TEAM)]
        blocks = FF // (96 * TEAM)
        up_ref[depth] = jnp.concatenate(
            [ordered[p][0:24, 96 * b : 96 * (b + 1)] for b in range(blocks) for p in range(TEAM)],
            axis=1,
        )
        qkv_ref[depth] = jnp.concatenate(
            [
                ordered[p][32:56, HCOLS * t : HCOLS * (t + 1)]
                for t in range(3)
                for p in range(TEAM)
            ],
            axis=1,
        )
        attn_ref[depth] = attn_rows[...].astype(F32)
        down_ref[depth] = down_rows[...]
        small = slots[0][56:64, :128] + slots[1][56:64, :128]
        small = small + slots[2][56:64, :128] + slots[3][56:64, :128]
        for n, ref in enumerate(gain_refs):
            ref[depth : depth + 1] = small[n : n + 1, :24]
        qkv_b_ref[depth : depth + 1] = small[4:5, :72]
        attn_b_ref[depth : depth + 1] = own_small[0:1, :24]
        down_b_ref[depth : depth + 1] = own_small[0:1, :24]
        up_b_ref[depth : depth + 1] = own_small[1:2, :96]


def team_send(piece, slot):
    flips = [(m, m ^ slot) for m in range(TEAM)]
    return lax.ppermute(piece, TEAM_AXES, flips)


def line_shift(piece, shift):
    size = lax.axis_size("z")
    return lax.ppermute(piece, "z", [(i, (i + shift) % size) for i in range(size)])


def line_flip(piece):
    return lax.ppermute(piece, "y", [(0, 1), (1, 0)])


def after(value, *others):
    return lax.optimization_barrier((value, *others))[0]


def line_near(piece):
    first = line_shift(piece, 1)
    third = line_shift(piece, 3)
    return [piece, first, line_shift(after(piece, first, third), 2), third]


def local_team(
    tokens, segment_ids, cotangent, qkv_weight, qkv_bias, attn_weight, attn_bias,
    up_weight, up_bias, down_weight, down_bias, attn_gain, attn_shift, mlp_gain, mlp_shift,
):
    lines = lax.axis_size("z") * lax.axis_size("y")
    world = lines * TEAM
    member = lax.axis_index("core") * 2 + lax.axis_index("x")
    me = jnp.stack([member, lax.axis_index("z"), lax.axis_index("y")]).astype(jnp.int32)
    everywhere = LINE_AXES + TEAM_AXES
    tok_all = TEAM * TOK
    whole_spec = pl.BlockSpec(memory_space=pltpu.VMEM)

    def run(body, out_shape, name, operands, scratch=()):
        specs = [whole_spec if isinstance(x, jax.Array) else x[1] for x in operands]
        return pl.pallas_call(
            body,
            grid=(1,),
            out_shape=out_shape,
            in_specs=[pl.BlockSpec(memory_space=pltpu.SMEM)] + specs,
            scratch_shapes=[pltpu.VMEM(dims, kind) for dims, kind in scratch],
            compiler_params=pltpu.CompilerParams(vmem_limit_bytes=VMEM_BYTES),
            name=name,
        )(me, *[x if isinstance(x, jax.Array) else x[0] for x in operands])

    def part(rows, start):
        return pl.BlockSpec((rows, D), lambda i: (start // rows, 0))

    def one_of(array, index):
        return (array, pl.BlockSpec((1,) + array.shape[1:], lambda i: (index, 0, 0)))

    def exchange(blocks):
        return [blocks[0]] + [team_send(blocks[s], s) for s in range(1, TEAM)]

    small = (
        qkv_bias, up_bias, attn_gain, attn_shift, mlp_gain, mlp_shift, attn_bias, down_bias
    )
    packed = run(
        pack_body, [shape((112, D), BF)] * TEAM, "pack_weights", (qkv_weight, up_weight, *small)
    )
    spread = [(i, TEAM * (i % lines) + i // lines) for i in range(world)]
    gather_back = [(b, a) for a, b in spread]
    attn_piece = lax.ppermute(attn_weight, everywhere, spread)
    chunks = run(
        assemble_body,
        [shape((304, D), BF), shape((288, D), BF)],
        "assemble_weights",
        (*exchange(packed), attn_piece, down_weight),
    )
    near = line_near(chunks[0])
    pieces = [near + [line_flip(p) for p in near]]
    near = line_near(after(chunks[1], near[2], pieces[0][5], pieces[0][7]))
    pieces.append(near + [line_flip(p) for p in (chunks[1], *near[1:])])
    m_parts = [[(p, part(192, 0)) for p in group] for group in pieces]
    a_parts = [[(p, part(96, 192)) for p in group] for group in pieces]
    small_parts = [(p, part(16, 288)) for p in pieces[0]]

    def gather_team(piece, *others):
        other = after(team_send(piece, 1), *others)
        return piece, other, team_send(jnp.concatenate([piece, other], axis=0), 2)

    def slots_of(gathered, start=0):
        piece, other, far = gathered
        size = piece.shape[0]
        return [
            (piece, part(TOK, start)), (other, part(TOK, start)),
            (far, part(TOK, start)), (far, part(TOK, size + start)),
        ]

    def sum_team(own, near, far, *others):
        other = after(team_send(far, 2), *others)
        both = (near + other[TOK:].astype(F32)).astype(BF)
        return own, (other, part(TOK, 0)), team_send(both, 1)

    ids_rows = jnp.pad(segment_ids.astype(BF)[None, :], ((0, TOK - 1), (0, D - TOK)))
    load = jnp.concatenate([tokens, cotangent, ids_rows], axis=0)
    loads = gather_team(after(load, pieces[0][1], pieces[0][3], pieces[0][4], pieces[1][4]), pieces[0][2], pieces[0][5], pieces[0][7])
    token_slots = slots_of(loads)
    here = lax.axis_index("x")
    rows = jnp.arange(TOK, dtype=jnp.int32)
    places = jnp.concatenate([here * TOK + rows, (1 - here) * TOK + rows])
    masks, cosines, sines = [], [], []
    lane = jnp.arange(128, dtype=jnp.int32) % HEAD
    inverse = 10000.0 ** (-(lane % (ROT // 2) * 2).astype(F32) / ROT)
    id_rows = [
        loads[0][2 * TOK, :TOK], loads[1][2 * TOK, :TOK],
        loads[2][2 * TOK, :TOK], loads[2][5 * TOK, :TOK],
    ]
    for g in range(2):
        ids = jnp.concatenate(id_rows[2 * g : 2 * g + 2]).astype(F32)
        visible = (places[None, :] <= places[:, None]) & (ids[None, :] == ids[:, None])
        masks.append(jnp.where(visible, 0.0, -1e30).astype(F32))
        position = places - jnp.sum((ids[None, :] < ids[:, None]).astype(jnp.int32), axis=1)
        phases = position.astype(F32)[:, None] * inverse[None, :]
        cosines.append(jnp.where(lane[None, :] < ROT, jnp.cos(phases), 1.0))
        sign = jnp.where(lane < ROT // 2, -1.0, jnp.where(lane < ROT, 1.0, 0.0))
        sines.append(jnp.sin(phases) * sign[None, :])
    mask = jnp.stack(masks)
    cosine, sine = jnp.concatenate(cosines), jnp.concatenate(sines)

    partials = [shape((TOK, D), F32)] * 2 + [shape((PAIR, D), BF)]
    stream_pair = [shape((TOK, D), F32), shape((TOK, D), BF)]
    wide = ((tok_all, D), BF)

    attn_out, vec = run(
        attend_body,
        [shape((tok_all, D), F32), shape((LAYERS, 8, D), F32)],
        "attend_forward",
        (*token_slots, *a_parts[0], *small_parts, cosine, sine, mask),
        [((lines, 96, D), BF), ((lines, 16, D), BF)],
    )
    y = run(
        mlp_body,
        partials,
        "mlp_forward",
        (*token_slots, *m_parts[0], vec, attn_out),
        [((lines, 192, D), BF)],
    )

    def residual(stream, blocks):
        return run(residual_body, stream_pair, "residual", (stream, *sum_team(*blocks), vec))

    stream, low = residual(tokens, (after(y[0], pieces[1][4]), *y[1:]))
    streams = [tokens, stream]
    slots = [token_slots, slots_of(gather_team(low, pieces[1][5], pieces[1][7]))]

    grad = cotangent
    grad_slots = slots_of(loads, TOK)
    outs = [None] * LAYERS
    block_m, block_a = shape((192, D), BF), shape((112, D), BF)

    def mlp_back(depth, slots, grad_slots, grads):
        last = depth == LAYERS - 1
        return run(
            partial(mlp_both_body, depth, last),
            [shape((tok_all, D), F32), shape((8, D), F32)]
            + ([shape((tok_all, D), F32)] if last else [])
            + grads,
            "mlp_both",
            (*slots, *grad_slots, *m_parts[depth], vec),
            [((lines, 192, D), BF), ((lines, 192, D), BF), wide, wide, wide, wide],
        )

    def attend_back(depth, slots, grad_slots, rest, *others):
        last = depth == LAYERS - 1
        result = run(
            partial(attend_both_body, depth, last),
            [shape((4, 112, D), BF)] * 2 + partials + (partials if last else []),
            "attend_both",
            (*slots, *grad_slots, *a_parts[depth], vec, cosine, sine, mask, *rest),
            [
                ((lines, 96, D), BF),
                ((lines, 112, D), BF),
                wide,
                ((tok_all, MINE), BF),
                ((tok_all, HCOLS), BF),
                wide,
            ],
        )
        return result[0], line_flip(after(result[1], *others)), result[2:5], result[5:]

    def norm_back(depth, grad, received):
        return run(
            norm_back_body, stream_pair, "norm_backward", (streams[depth], grad, *received)
        )

    def add(kind, keep, other, slots, places, name):
        return run(partial(add_body, slots, places), [kind] * len(slots), name, (keep, other))

    def shifts(sums):
        return [line_shift(piece, s + 1) for s, piece in enumerate(sums)]

    def split(attend, mlp, early=()):
        keep, other, *sums = attend
        m_keep, m_other, *m_sums = mlp
        mine = run(
            partial(split_body, bool(early)),
            [shape((64, D), BF)] * TEAM
            + [shape((96, D), F32), shape((24, D), BF), shape((8, 128), F32)],
            "split_gradients",
            (one_of(keep, 0), one_of(other, 0), *sums, one_of(m_keep, 0), m_other, *m_sums, *early),
        )
        attn_rows = lax.ppermute(mine[TEAM + 1], everywhere, gather_back)
        return exchange(mine[:TEAM]) + [mine[TEAM], mine[TEAM + 2], attn_rows]

    early_block, late_four = shape((2, EARLY, D), BF), shape((4, 192 - EARLY, D), BF)
    dn, sum_m, y_part, e0, e1, e2, e3, m_keep1, m_send1 = mlp_back(
        1, slots[1], grad_slots, [early_block] * 4 + [late_four] * 2
    )
    early = shifts((e1, e2, e3))
    m_other1 = line_flip(m_send1)
    a_keep1, a_other1, ns, ys = attend_back(1, slots[1], grad_slots, (dn, sum_m, y_part))
    ns = (ns[0], ns[1], after(ns[2], *early))
    grad, low = norm_back(1, grad, sum_team(*ns, m_other1))
    m_added1 = add(
        shape((192 - EARLY, D), BF), m_keep1, after(m_other1, low), (1, 2, 3), (1, 2, 3), "add_mlp"
    )
    m_sums1 = shifts(m_added1)
    gathered = gather_team(low)
    grad_slots = slots_of((after(gathered[0], *m_added1), *gathered[1:]))
    dn, sum_m, m_keep0, m_first0, m_second0 = mlp_back(
        0, slots[0], grad_slots, [shape((4, 192, D), BF)] + [shape((2, 192, D), BF)] * 2
    )
    m_first0 = line_flip(after(m_first0, m_sums1[0]))
    m_second0 = line_flip(after(m_second0, m_sums1[0]))
    a_keep0, a_other0, ns, _ = attend_back(
        0, slots[0], grad_slots, (after(dn, m_sums1[0]), sum_m)
    )
    block_both = shape((304, D), BF)

    def add_both(other, slots, places, name):
        return run(
            partial(add_both_body, slots, places),
            [block_both] * len(slots),
            name,
            (m_keep0, other, a_keep1, a_other1),
        )

    both1, both3 = add_both(after(m_first0, a_keep0, a_other1, *m_sums1), HALVES[0], (0, 1), "add_first")
    first_added = both1
    both1, both3 = line_shift(both1, 1), line_shift(both3, 3)
    grad, _ = norm_back(0, grad, sum_team(ns[0], ns[1], after(ns[2], first_added)))
    _, activations = residual(streams[1], (ys[0], ys[1], after(ys[2], first_added)))
    e_keep, e_send = run(
        line_sum_body,
        [shape((EARLY, D), F32), shape((EARLY, D), BF)],
        "line_sum",
        (e0, after(early[0], grad), early[1], early[2]),
    )
    e_other = line_flip(e_send)
    (both2,) = add_both(
        after(m_second0, both1, both3, grad, activations), HALVES[1][:1], (0,), "add_second"
    )
    a_added0 = add(
        block_a, a_keep0, after(a_other0, both2, e_keep), (1, 2, 3), (1, 2, 3), "add_attend"
    )
    both2 = line_shift(both2, 2)
    a_sums0 = shifts([after(piece, both2, e_other) for piece in a_added0])
    both = (both1, both2, both3)
    outs[1] = split(
        (a_keep1, a_other1, *both), (m_keep1, one_of(m_other1, 0), *m_sums1), (e_keep, e_other)
    )
    outs[0] = split(
        (a_keep0, after(a_other0, outs[1][0]), *a_sums0), (m_keep0, one_of(m_second0, 1), *both)
    )
    row_24 = shape((LAYERS, 24), F32)
    final = run(
        unpack_body,
        [
            shape((LAYERS, 24, 3 * D), F32), shape((LAYERS, 72), F32),
            shape((LAYERS, 24, D), F32), row_24,
            shape((LAYERS, 24, FF), F32), shape((LAYERS, 96), F32),
            shape((LAYERS, 96, D), F32), row_24, row_24, row_24, row_24, row_24,
        ],
        "unpack_gradients",
        [array for group in outs for array in group],
    )
    return (activations, grad, *final)


def whole_mesh_solution(mesh):
    in_specs = (
        P(("dp", "cp"), None),
        P(("dp", "cp")),
        P(("dp", "cp"), None),
        P(None, ("dp", "cp"), None),
        P(None, ("dp", "cp")),
        P(None, ("dp", "cp"), None),
        P(None, ("dp", "cp")),
        P(None, ("dp", "cp"), None),
        P(None, ("dp", "cp")),
        P(None, ("dp", "cp"), None),
        P(None, ("dp", "cp")),
        P(None, ("dp", "cp")),
        P(None, ("dp", "cp")),
        P(None, ("dp", "cp")),
        P(None, ("dp", "cp")),
    )
    out_specs = (
        P(("dp", "cp"), None),
        P(("dp", "cp"), None),
        P(None, ("dp", "cp"), None),
        P(None, ("dp", "cp")),
        P(None, ("dp", "cp"), None),
        P(None, ("dp", "cp")),
        P(None, ("dp", "cp"), None),
        P(None, ("dp", "cp")),
        P(None, ("dp", "cp"), None),
        P(None, ("dp", "cp")),
        P(None, ("dp", "cp")),
        P(None, ("dp", "cp")),
        P(None, ("dp", "cp")),
        P(None, ("dp", "cp")),
    )
    return jax.shard_map(local, mesh=mesh, in_specs=in_specs, out_specs=out_specs, check_vma=False)


def solution(mesh):
    teams = mesh.shape["dp"] // 2
    if mesh.shape["cp"] != 2 or teams != 2 * LINE or teams * TEAM * 24 != D:
        return whole_mesh_solution(mesh)
    split_mesh = Mesh(mesh.devices.reshape(teams // 2, 2, 2, 2), ("z", "y", "core", "x"))
    every = ("z", "y", "core", "x")
    row = P(every, None)
    matrix, vector = P(None, every, None), P(None, every)
    in_specs = (row, P(every), row) + (matrix, vector) * 4 + (vector,) * 4
    out_specs = (row, row) + (matrix, vector) * 4 + (vector,) * 4
    return jax.shard_map(
        local_team, mesh=split_mesh, in_specs=in_specs, out_specs=out_specs, check_vma=False
    )
```
